32 devices in a mesh: groups: 2 (over y), dp: 4 (over x, core), fsdp: 4 (over z).
Axes of the slice: x: 2, y: 2, z: 4, core: 2. Of those that a mesh axis runs over, the one named last changes fastest.
Arguments:
- facies: int32 [128, 64, 2048], P(('groups', 'dp', 'fsdp')), parts along dimension 0, may hold values from 0 to 3
- prior_draws: bfloat16 [128, 512], P(('groups', 'dp', 'fsdp')), parts along dimension 0, may hold values from -6 to 6
- recon_grad: bfloat16 [128, 512], P(('groups', 'dp', 'fsdp')), parts along dimension 0, may hold values from -0.796875 to 0.796875
- w_embed: bfloat16 [256, 128], replicated, may hold values from -0.75 to 0.75
- w_conv: bfloat16 [1024, 256], replicated, may hold values from -0.1875 to 0.1875
- w_head: bfloat16 [256, 512], replicated, may hold values from -1 to 1
Outputs:
- grad_embed: float32 [512, 128], P(('groups', 'fsdp')), parts along dimension 0
- grad_conv: float32 [2048, 256], P(('groups', 'fsdp')), parts along dimension 0
- grad_head: float32 [512, 512], P(('groups', 'fsdp')), parts along dimension 0
The draws below stay inside these ranges and needn't reach their ends.
There are 2 independent parts, one for each index of `groups`. The reference program is written for one: setup_inputs(seed, part) draws one part's arguments, and reference() takes and returns one part's arrays. A program takes and returns all parts, laid end to end along the dimension named above; an argument that names none is the same for every part. Nothing has to cross between parts.
All inputs are finite; a program needn't handle non-finite values.
Results may differ from the reference program's by a relative error of at most 0.0012.
Values may be sent and summed in bfloat16 or wider, within the bound.
No kernel may reach another device: no remote copies, remote signals or barrier semaphores. Data moves between devices by JAX's collectives and lax.ppermute only.
A program may use at most 256 MiB of HBM per device.

```python
import jax
import jax.numpy as jnp
from jax import lax

FACIES = 4
C1 = 128
C2 = 256
LAT = 512
PATCH_X = 64
PATCH_Y = 64
PATCH_Z = 32
SAMP_DEV = 4
SAMPLES = 64


def draw_facies(key, part):
    keys = jax.random.split(key, 8)
    voxel_count = PATCH_X * PATCH_Y * PATCH_Z
    levels = jnp.arange(FACIES, dtype=jnp.int32)
    dominant = jax.random.randint(keys[0], (SAMPLES, 1), 0, FACIES)
    weights = jax.random.randint(keys[1], (SAMPLES, FACIES), 1, 5)
    boost = jax.random.randint(keys[2], (SAMPLES, 1), 6, 40)
    weights = weights + boost * (levels[None, :] == dominant).astype(jnp.int32)
    bounds = jnp.cumsum(weights, axis=1)
    layer_count = max(PATCH_X, PATCH_Y, PATCH_Z) + 8
    picks = jax.random.randint(keys[3], (SAMPLES, layer_count), 0, bounds[:, -1:])
    layer_cat = jnp.sum((picks[:, :, None] >= bounds[:, None, :]).astype(jnp.int32), axis=2)
    orient = jax.random.randint(keys[4], (SAMPLES, 1), 0, 3)
    thick = jax.random.randint(keys[5], (SAMPLES, 1), 1, 7)
    phase = jax.random.randint(keys[6], (SAMPLES, 1), 0, 8)
    voxel = jnp.arange(voxel_count, dtype=jnp.int32)[None, :]
    coord_x = voxel // (PATCH_Y * PATCH_Z)
    coord_y = voxel // PATCH_Z % PATCH_Y
    coord_z = voxel % PATCH_Z
    position = jnp.where(orient == 0, coord_x, jnp.where(orient == 1, coord_y, coord_z))
    layer_id = (position + phase) // thick
    layered = jnp.take_along_axis(layer_cat, layer_id, axis=1)
    rough = jax.random.randint(keys[7], (SAMPLES, voxel_count), 0, 8 * FACIES)
    result = jnp.where(rough < FACIES, rough, layered)
    return result.reshape(SAMPLES, PATCH_X, PATCH_Y * PATCH_Z).astype(jnp.int32)


def level_of(own_key, extent, shards, least, top_value):
    def one(axis_at, parts):
        steps = jax.random.uniform(jax.random.fold_in(jax.random.fold_in(own_key, 6), axis_at), (parts,), jnp.float32, least / len(shards), top_value / len(shards))
        return jnp.repeat(jnp.exp(steps), extent[axis_at] // parts).reshape((-1,) + (1,) * (len(extent) - axis_at - 1))

    level = one(*shards[0])
    for cut in shards[1:]:
        level = level * one(*cut)
    return level


def scatter_about(stream_key, shape, scale, bound, pieces=(), kind=jnp.bfloat16):
    drawn = scale * jax.random.normal(stream_key, shape, jnp.float32)
    if pieces:
        drawn = drawn * level_of(stream_key, shape, pieces, -0.22, 0.18)
    return jnp.clip(drawn, -bound, bound).astype(kind)


def setup_inputs(seed: int = 0, part: int = 0) -> dict:
    arg_keys = jax.random.split(jax.random.key(seed), 7)
    part_splits = jax.random.split(jax.random.fold_in(arg_keys[6], part), 7)
    return {
        "facies": draw_facies(jax.random.fold_in(jax.random.fold_in(arg_keys[6], part), 71), part),
        "prior_draws": scatter_about(part_splits[1], (SAMPLES, LAT), 1.0, 6.0, ((0, 16),)),
        "recon_grad": scatter_about(part_splits[2], (SAMPLES, LAT), 0.1, 0.796875, ((0, 16),)),
        "w_embed": scatter_about(arg_keys[3], (64 * FACIES, C1), 64 ** -0.5, 0.75),
        "w_conv": scatter_about(arg_keys[4], (8 * C1, C2), (8 * C1) ** -0.5, 0.1875),
        "w_head": scatter_about(arg_keys[5], (C2, LAT), (C2 // 8) ** -0.5, 1.0),
    }


def silu_slope(pre_act):
    sigmoid_val = jax.nn.sigmoid(pre_act)
    return sigmoid_val * (1.0 + pre_act * (1.0 - sigmoid_val))


def embed_rows(facies, levels_count):
    samples = facies.shape[0]
    voxels = facies.reshape(samples, PATCH_X // 4, 4, PATCH_Y // 4, 4, PATCH_Z // 4, 4)
    voxels = voxels.transpose(0, 1, 3, 5, 2, 4, 6).reshape(-1, 64)
    levels = jnp.arange(levels_count, dtype=jnp.int32)
    one_hot = (voxels[:, :, None] == levels[None, None, :]).astype(jnp.bfloat16)
    return one_hot.reshape(voxels.shape[0], 64 * levels_count)


def group_cells(rows_in, samples, grid_x, grid_y, grid_z):
    channels = rows_in.shape[1]
    blocks = rows_in.reshape(samples, grid_x // 2, 2, grid_y // 2, 2, grid_z // 2, 2, channels)
    blocks = blocks.transpose(0, 1, 3, 5, 2, 4, 6, 7)
    return blocks.reshape(-1, 8 * channels)


def spread_cells(rows_in, samples, grid_x, grid_y, grid_z):
    channels = rows_in.shape[1] // 8
    blocks = rows_in.reshape(samples, grid_x // 2, grid_y // 2, grid_z // 2, 2, 2, 2, channels)
    blocks = blocks.transpose(0, 1, 4, 2, 5, 3, 6, 7)
    return blocks.reshape(-1, channels)


def encode(facies, w_embed, w_conv, w_head):
    samples = facies.shape[0]
    grid_x, grid_y, grid_z = PATCH_X // 4, PATCH_Y // 4, PATCH_Z // 4
    one_hot = embed_rows(facies, w_embed.shape[0] // 64)
    pre_embed = jnp.dot(one_hot, w_embed, preferred_element_type=jnp.float32)
    hidden = jax.nn.silu(pre_embed).astype(jnp.bfloat16)
    conv_in = group_cells(hidden, samples, grid_x, grid_y, grid_z)
    pre_conv = jnp.dot(conv_in, w_conv, preferred_element_type=jnp.float32)
    pooled = jnp.mean(jax.nn.silu(pre_conv).reshape(samples, -1, pre_conv.shape[1]), axis=1).astype(jnp.bfloat16)
    latent = jnp.dot(pooled, w_head, preferred_element_type=jnp.float32).astype(jnp.bfloat16)
    return one_hot, pre_embed, conv_in, pre_conv, pooled, latent


def kernel_block(queries, query_square, key_rows, latent_width):
    inner_prod = lax.dot_general(queries, key_rows, (((1,), (1,)), ((), ())), preferred_element_type=jnp.float32)
    key_float = key_rows.astype(jnp.float32)
    key_square = jnp.sum(key_float * key_float, axis=1)
    square_dist = query_square[:, None] + key_square[None, :] - 2.0 * inner_prod
    kernel = jnp.exp(-square_dist / latent_width)
    mixed = jnp.dot(kernel.astype(jnp.bfloat16), key_rows, preferred_element_type=jnp.float32)
    return jnp.sum(kernel, axis=1), mixed


def back_signals(grid_dims, cotangent, pre_embed, pre_conv, w_conv, w_head):
    samples = cotangent.shape[0]
    cell_count = pre_conv.shape[0] // samples
    back_pool = lax.dot_general(cotangent, w_head, (((1,), (1,)), ((), ())), preferred_element_type=jnp.float32)
    slope = silu_slope(pre_conv).reshape(samples, cell_count, pre_conv.shape[1])
    conv_grad = ((back_pool[:, None, :] / cell_count) * slope).reshape(pre_conv.shape).astype(jnp.bfloat16)
    back_rows = lax.dot_general(conv_grad, w_conv, (((1,), (1,)), ((), ())), preferred_element_type=jnp.float32)
    spread = spread_cells(back_rows, samples, grid_dims[0], grid_dims[1], grid_dims[2])
    embed_grad = (spread * silu_slope(pre_embed)).astype(jnp.bfloat16)
    return conv_grad, embed_grad


def inner_rows(left_rows, right_rows):
    return lax.dot_general(left_rows, right_rows, (((0,), (0,)), ((), ())), preferred_element_type=jnp.float32)


def block_grads(facies_block, cotangent, w_embed, w_conv, w_head):
    one_hot, pre_embed, conv_in, pre_conv, pooled, latent = encode(facies_block, w_embed, w_conv, w_head)
    grid_dims = (PATCH_X // 4, PATCH_Y // 4, PATCH_Z // 4)
    conv_grad, embed_grad = back_signals(grid_dims, cotangent, pre_embed, pre_conv, w_conv, w_head)
    return inner_rows(one_hot, embed_grad), inner_rows(conv_in, conv_grad), inner_rows(pooled, cotangent)


def reference(facies, prior_draws, recon_grad, w_embed, w_conv, w_head):
    block_count = SAMPLES // SAMP_DEV
    facies_blocks = facies.reshape((block_count, SAMP_DEV) + facies.shape[1:])

    def latent_block(facies_block):
        return encode(facies_block, w_embed, w_conv, w_head)[5]

    latents = lax.map(latent_block, facies_blocks).reshape(SAMPLES, LAT)
    query_float = latents.astype(jnp.float32)
    query_square = jnp.sum(query_float * query_float, axis=1)
    self_sum, self_mix = kernel_block(latents, query_square, latents, LAT)
    cross_sum, cross_mix = kernel_block(latents, query_square, prior_draws, LAT)
    pull = (-32.0 / SAMPLES) * ((self_sum - cross_sum)[:, None] * query_float - self_mix + cross_mix)
    cotangent = (recon_grad.astype(jnp.float32) + pull).astype(jnp.bfloat16)
    cotan_blocks = cotangent.reshape(block_count, SAMP_DEV, LAT)

    def backward_pass(totals, inputs):
        terms = block_grads(inputs[0], inputs[1], w_embed, w_conv, w_head)
        return (totals[0] + terms[0], totals[1] + terms[1], totals[2] + terms[2]), None

    zero_grads = (jnp.zeros(w_embed.shape, jnp.float32), jnp.zeros(w_conv.shape, jnp.float32), jnp.zeros(w_head.shape, jnp.float32))
    summed = lax.scan(backward_pass, zero_grads, (facies_blocks, cotan_blocks))[0]
    return summed[0], summed[1], summed[2]
```

```python
import jax
import jax.numpy as jnp
from jax import lax
from jax.experimental import pallas as pl
from jax.experimental.pallas import tpu as pltpu
from jax.sharding import PartitionSpec as P

PATCH_X = 64
PATCH_Y = 64
PATCH_Z = 32
LEVELS = 4
GROUP = ("dp", "fsdp")
NT = (((1,), (1,)), ((), ()))
F32 = jnp.float32
BF16 = jnp.bfloat16


def iota(shape, dim):
    return lax.broadcasted_iota(jnp.int32, shape, dim)


def mm(left, right):
    return jnp.dot(left, right, preferred_element_type=F32)


def mm_nt(left, right):
    return lax.dot_general(left, right, NT, preferred_element_type=F32)


def spread_matrix():
    out_row = iota((512, 128), 0)
    lane = iota((512, 128), 1)
    pair, half = out_row // 128, out_row // 64 % 2
    row_dy, row_dz = out_row // 16 % 4, out_row // 4 % 4
    lane_dy, lane_c, lane_dz = lane // 32, lane // 4 % 8, lane % 4
    hit = (row_dy == lane_dy) & (row_dz == lane_dz) & (lane_c == 2 * pair + half)
    return jnp.where(hit, 1.0, 0.0).astype(BF16)


def pair_weights(w_embed):
    turned = jnp.transpose(w_embed.astype(F32)).astype(BF16)
    halves = []
    for half in range(2):
        row = iota((256, 512), 0)
        lane = iota((256, 512), 1)
        hit = (row // 64 == lane // 128) & (row % 64 == lane % 64) & (lane // 64 % 2 == half)
        halves.append(mm(turned, jnp.where(hit, 1.0, 0.0).astype(BF16)))
    return jnp.concatenate(halves, axis=0).astype(BF16)


def sigmoid(value):
    return 1.0 / (1.0 + jnp.exp(-value))


def forward_kernel(facies, w_embed, w_conv, pooled, one_hot, pre_embed, hidden, pre_conv, packed, sorted_rows):
    row, lane = iota((256, 256), 0), iota((256, 256), 1)
    order = jnp.where((row // 32 == lane % 8) & (row % 32 == lane // 8), 1.0, 0.0).astype(BF16)
    for at in range(0, facies.shape[1], 512):
        part = facies[:, pl.ds(at, 512)].astype(F32).astype(BF16)
        sorted_rows[:, pl.ds(at, 512)] = mm(order, part).astype(BF16)
    spread = spread_matrix()
    level = iota((512, 256), 0) % 4
    for t in range(8):
        for dy2 in range(2):
            j, dx = 2 * (t // 4) + dy2, t % 4
            rows = [
                sorted_rows[pl.ds(t * 32, 32), pl.ds((2 * b2 + dy2) * 128, 128)] for b2 in range(8)
            ]
            voxels = jnp.concatenate(rows, axis=0)
            copied = mm_nt(spread, voxels)
            hot = jnp.where(copied == level.astype(F32), 1.0, 0.0).astype(BF16)
            for cp in range(4):
                one_hot[cp, j, pl.ds(dx * 128, 128), :] = hot[cp * 128 : (cp + 1) * 128]
    packed[...] = pair_weights(w_embed[...])
    conv_turned = jnp.transpose(w_conv[...].astype(F32)).astype(BF16)
    sums = jnp.zeros((256, 128), F32)
    for cp in range(4):
        for j in range(4):
            pre = mm(packed[...], one_hot[cp, j])
            pre_embed[cp, j] = pre
            hidden[cp, j] = (pre * sigmoid(pre)).astype(BF16)
        pre = mm(conv_turned, hidden[cp].reshape(1024, 256))
        pre_conv[cp] = pre
        act = pre * sigmoid(pre)
        sums = sums + act[:, :128] + act[:, 128:]
    pick = jnp.where(iota((8, 128), 1) // 8 % 4 == iota((8, 128), 0), 1.0, 0.0)
    total = lax.dot_general(pick, sums, NT, precision=lax.Precision.HIGHEST, preferred_element_type=F32)
    pooled[...] = (total[:4] / 256.0).astype(BF16)


def pair_kernel(queries, query_square, keys):
    inner = mm_nt(queries, keys)
    key_float = keys.astype(F32)
    count = keys.shape[0]
    key_square = jnp.sum(key_float * key_float, axis=1, keepdims=True)
    key_row = jnp.transpose(jnp.broadcast_to(key_square, (count, 128)))[:1]
    kern = jnp.exp(-(query_square + key_row - 2.0 * inner) / keys.shape[1])
    return jnp.sum(kern, axis=1, keepdims=True), mm(kern.astype(BF16), keys)


def backward_kernel(
    sizes, pooled_rel, side_rel, w_head, w_conv, one_hot, pre_embed, hidden, pre_conv,
    grad_embed, grad_conv, grad_head, pooled_abs, side_abs, head_full
):
    devices, fsdp = sizes
    here = lax.axis_index("dp") * fsdp + lax.axis_index("fsdp")
    for step in range(devices):
        owner = lax.rem(here + (devices - step), devices)
        pooled_abs[owner] = pooled_rel[step].astype(F32)
        side_abs[owner] = side_rel[step].astype(F32)
    samples = pooled_abs.shape[1]
    count = devices * samples
    pooled = pooled_abs[...].reshape(count, pooled_abs.shape[2]).astype(BF16)
    prior = side_abs[:, :samples].reshape(count, side_abs.shape[2]).astype(BF16)
    recon = side_abs[:, samples:].reshape(count, side_abs.shape[2])
    latent = mm(pooled, w_head[...]).astype(BF16)
    latent_float = latent.astype(F32)
    square = jnp.sum(latent_float * latent_float, axis=1, keepdims=True)
    self_sum, self_mix = pair_kernel(latent, square, latent)
    cross_sum, cross_mix = pair_kernel(latent, square, prior)
    pull = -32.0 / count * ((self_sum - cross_sum) * latent_float - self_mix + cross_mix)
    cotangent = (recon + pull).astype(BF16)
    turned = jnp.transpose(pooled.astype(F32)).astype(BF16)
    head_full[...] = mm(turned, cotangent)
    share = grad_head.shape[0]
    start = pl.multiple_of(lax.axis_index("fsdp") * share, share)
    grad_head[...] = head_full[pl.ds(start, share), :]

    lane_sample = iota((128, count), 0) // 8 % 4 + samples * here
    pick = jnp.where(lane_sample == iota((128, count), 1), 1.0, 0.0).astype(BF16)
    lanes = mm(pick, cotangent).astype(BF16)
    back_pool = mm_nt(w_head[...], lanes) / 256.0
    back_pool = jnp.concatenate([back_pool, back_pool], axis=1)
    grads = []
    conv_total = None
    for cp in range(4):
        pre = pre_conv[cp]
        gate = sigmoid(pre)
        grads.append((back_pool * (gate * (1.0 + pre * (1.0 - gate)))).astype(BF16))
        term = mm_nt(hidden[cp].reshape(1024, 256), grads[cp])
        conv_total = term if cp == 0 else conv_total + term
    grad_conv[...] = conv_total
    embed_total = None
    for cp in range(4):
        for j in range(4):
            rows = mm(w_conv[pl.ds(j * 256, 256), :], grads[cp])
            pre = pre_embed[cp, j]
            gate = sigmoid(pre)
            signal = (rows * (gate * (1.0 + pre * (1.0 - gate)))).astype(BF16)
            term = mm_nt(one_hot[cp, j], signal)
            embed_total = term if embed_total is None else embed_total + term
    for dx in range(4):
        grad_embed[pl.ds(dx * 64, 64), :] = (
            embed_total[dx * 128 : dx * 128 + 64, :128] + embed_total[dx * 128 + 64 : dx * 128 + 128, 128:]
        )


VMEM = pl.BlockSpec(memory_space=pltpu.VMEM)


def forward(facies, w_embed, w_conv):
    samples = facies.shape[0]
    return pl.pallas_call(
        forward_kernel,
        out_shape=(
            jax.ShapeDtypeStruct((samples, 256), BF16),
            jax.ShapeDtypeStruct((4, 4, 512, 256), BF16),
            jax.ShapeDtypeStruct((4, 4, 256, 256), F32),
            jax.ShapeDtypeStruct((4, 4, 256, 256), BF16),
            jax.ShapeDtypeStruct((4, 256, 256), F32),
        ),
        in_specs=[VMEM] * 3,
        out_specs=(VMEM,) * 5,
        scratch_shapes=[pltpu.VMEM((256, 512), BF16), pltpu.VMEM((256, 2048), BF16)],
        compiler_params=pltpu.CompilerParams(vmem_limit_bytes=30 * 2**20),
        name="forward",
    )(facies.reshape(samples * PATCH_X, PATCH_Y * PATCH_Z), w_embed, w_conv)


def backward(sizes, pooled_rel, side_rel, w_head, w_conv, saved):
    devices, fsdp = sizes
    samples = pooled_rel.shape[1]
    return pl.pallas_call(
        lambda *refs: backward_kernel(sizes, *refs),
        out_shape=(
            jax.ShapeDtypeStruct((256, 128), F32),
            jax.ShapeDtypeStruct((1024, 256), F32),
            jax.ShapeDtypeStruct((256 // fsdp, 512), F32),
        ),
        in_specs=[VMEM] * 8,
        out_specs=(VMEM,) * 3,
        scratch_shapes=[
            pltpu.VMEM((devices, samples, 256), F32),
            pltpu.VMEM((devices, 2 * samples, 512), F32),
            pltpu.VMEM((256, 512), F32),
        ],
        compiler_params=pltpu.CompilerParams(vmem_limit_bytes=30 * 2**20),
        name="backward",
    )(pooled_rel, side_rel, w_head, w_conv, *saved)


def gather_relative(block, devices):
    if devices > 16:
        full = lax.all_gather(block, GROUP, axis=0)
        here = lax.axis_index(GROUP)
        return jnp.take(full, lax.rem(here + devices - jnp.arange(devices), devices), axis=0)
    blocks = [block]
    for step in range(1, devices):
        blocks.append(lax.ppermute(block, GROUP, [(i, (i + step) % devices) for i in range(devices)]))
    return jnp.stack(blocks)


def reduce_to_owner(grad, dp, fsdp):
    width = grad.shape[1]
    xs = dp // 2
    piece = grad.shape[0] // (fsdp * dp)
    blocks = grad.reshape(fsdp, xs, 2, piece, width)
    core = lax.axis_index("dp") % 2
    x_here, f_here = lax.axis_index("dp") // 2, lax.axis_index("fsdp")
    keep = lax.dynamic_index_in_dim(blocks, core, 2, keepdims=False)
    send = lax.dynamic_index_in_dim(blocks, 1 - core, 2, keepdims=False)
    held = keep + lax.ppermute(send, "dp", [(i, i ^ 1) for i in range(dp)])

    def block_at(dx, df):
        return lax.dynamic_slice(
            held, ((f_here + df) % fsdp, (x_here + dx) % xs, 0, 0), (1, 1, piece, width)
        )[0, 0]

    total = block_at(0, 0)
    for dx in range(xs):
        for df in range(fsdp):
            if dx == 0 and df == 0:
                continue
            pairs = []
            for d in range(dp):
                for f in range(fsdp):
                    to = ((d // 2 + dx) % xs * 2 + d % 2) * fsdp + (f + df) % fsdp
                    pairs.append((d * fsdp + f, to))
            total = total + lax.ppermute(block_at(dx, df), GROUP, pairs)
    parts = [total]
    for step in range(1, dp):
        parts.append(lax.ppermute(total, "dp", [(i, (i + step) % dp) for i in range(dp)]))
    stacked = jnp.stack(parts)
    order = (lax.axis_index("dp") + dp - jnp.arange(dp)) % dp
    return jnp.take(stacked, order, axis=0).reshape(dp * piece, width)


def shards(facies, prior_draws, recon_grad, w_embed, w_conv, w_head):
    dp, fsdp = lax.axis_size("dp"), lax.axis_size("fsdp")
    devices = dp * fsdp
    side_rel = gather_relative(jnp.concatenate([prior_draws, recon_grad], axis=0), devices)
    pooled, *saved = forward(facies, w_embed, w_conv)
    pooled_rel = gather_relative(pooled, devices)
    grad_embed, grad_conv, grad_head = backward((devices, fsdp), pooled_rel, side_rel, w_head, w_conv, saved)
    return (
        reduce_to_owner(grad_embed, dp, fsdp),
        reduce_to_owner(grad_conv, dp, fsdp),
        grad_head,
    )


def solution(mesh):
    return jax.shard_map(
        shards,
        mesh=mesh,
        in_specs=(
            P(("groups", "dp", "fsdp"), None, None),
            P(("groups", "dp", "fsdp"), None),
            P(("groups", "dp", "fsdp"), None),
            P(),
            P(),
            P(),
        ),
        out_specs=(
            P(("groups", "fsdp"), None),
            P(("groups", "fsdp"), None),
            P(("groups", "fsdp"), None),
        ),
        check_vma=False,
    )
```

```python
import jax
import jax.numpy as jnp
from jax import lax
from jax.experimental import pallas as pl
from jax.experimental.pallas import tpu as pltpu
from jax.sharding import PartitionSpec as P

PATCH_X = 64
PATCH_Y = 64
PATCH_Z = 32
LEVELS = 4
GROUP = ("dp", "fsdp")
NT = (((1,), (1,)), ((), ()))
F32 = jnp.float32
BF16 = jnp.bfloat16


def iota(shape, dim):
    return lax.broadcasted_iota(jnp.int32, shape, dim)


def mm(left, right):
    return jnp.dot(left, right, preferred_element_type=F32)


def mm_nt(left, right):
    return lax.dot_general(left, right, NT, preferred_element_type=F32)


def spread_matrix():
    out_row = iota((512, 128), 0)
    lane = iota((512, 128), 1)
    pair, half = out_row // 128, out_row // 64 % 2
    row_dy, row_dz = out_row // 16 % 4, out_row // 4 % 4
    lane_dy, lane_c, lane_dz = lane // 32, lane // 4 % 8, lane % 4
    hit = (row_dy == lane_dy) & (row_dz == lane_dz) & (lane_c == 2 * pair + half)
    return jnp.where(hit, 1.0, 0.0).astype(BF16)


def pair_weights(w_embed):
    turned = jnp.transpose(w_embed.astype(F32)).astype(BF16)
    halves = []
    for half in range(2):
        row = iota((256, 512), 0)
        lane = iota((256, 512), 1)
        hit = (row // 64 == lane // 128) & (row % 64 == lane % 64) & (lane // 64 % 2 == half)
        halves.append(mm(turned, jnp.where(hit, 1.0, 0.0).astype(BF16)))
    return jnp.concatenate(halves, axis=0).astype(BF16)


def sigmoid(value):
    return 1.0 / (1.0 + jnp.exp(-value))


def forward_kernel(
    facies_hbm, prior_hbm, recon_hbm, w_embed_hbm, w_conv_hbm,
    block, one_hot_hbm, pre_embed_hbm, hidden_hbm, pre_conv_hbm,
    facies, prior, recon, w_embed, w_conv, one_hot, pre_embed, hidden, pre_conv, packed, sorted_rows, in_sem, out_sem
):
    parts = 4
    width = facies.shape[1] // parts
    loads = [
        pltpu.make_async_copy(
            facies_hbm.at[:, pl.ds(i * width, width)], facies.at[:, pl.ds(i * width, width)], in_sem.at[i]
        )
        for i in range(parts)
    ]
    for source, target in ((w_embed_hbm, w_embed), (w_conv_hbm, w_conv), (prior_hbm, prior), (recon_hbm, recon)):
        loads.append(pltpu.make_async_copy(source, target, in_sem.at[len(loads)]))
    for load in loads:
        load.start()
    row, lane = iota((256, 256), 0), iota((256, 256), 1)
    order = jnp.where((row // 32 == lane % 8) & (row % 32 == lane // 8), 1.0, 0.0).astype(BF16)
    spread = spread_matrix()
    level = (iota((512, 256), 0) % 4).astype(F32)
    for i in range(parts):
        loads[i].wait()
        part = facies[:, pl.ds(i * width, width)].astype(F32).astype(BF16)
        sorted_rows[:, pl.ds(i * width, width)] = mm(order, part).astype(BF16)
    for t in range(8):
        for dy2 in range(2):
            j, dx = 2 * (t // 4) + dy2, t % 4
            rows = [sorted_rows[pl.ds(t * 32, 32), pl.ds((2 * b2 + dy2) * 128, 128)] for b2 in range(8)]
            copied = mm_nt(spread, jnp.concatenate(rows, axis=0))
            hot = jnp.where(copied == level, 1.0, 0.0).astype(BF16)
            for cp in range(4):
                one_hot[cp, j, pl.ds(dx * 128, 128), :] = hot[cp * 128 : (cp + 1) * 128]
    stores = []

    def save(source, target):
        stores.append(pltpu.make_async_copy(source, target, out_sem.at[len(stores)]))
        stores[-1].start()

    for cp in range(4):
        save(one_hot.at[cp], one_hot_hbm.at[cp])
    loads[4].wait()
    packed[...] = pair_weights(w_embed[...])
    loads[5].wait()
    conv_turned = jnp.transpose(w_conv[...].astype(F32)).astype(BF16)
    sums = jnp.zeros((256, 128), F32)
    for cp in range(4):
        for j in range(4):
            pre = mm(packed[...], one_hot[cp, j])
            pre_embed[cp, j] = pre
            save(pre_embed.at[cp, j], pre_embed_hbm.at[cp, j])
            hidden[cp, j] = (pre * sigmoid(pre)).astype(BF16)
        save(hidden.at[cp], hidden_hbm.at[cp])
        pre = mm(conv_turned, hidden[cp].reshape(1024, 256))
        pre_conv[cp] = pre
        save(pre_conv.at[cp], pre_conv_hbm.at[cp])
        act = pre * sigmoid(pre)
        sums = sums + act[:, :128] + act[:, 128:]
    pick = jnp.where(iota((8, 128), 1) // 8 % 4 == iota((8, 128), 0), 1.0, 0.0)
    total = lax.dot_general(pick, sums, NT, precision=lax.Precision.HIGHEST, preferred_element_type=F32)
    loads[6].wait()
    loads[7].wait()
    block[:, pl.ds(0, 512)] = prior[...]
    block[:, pl.ds(512, 512)] = recon[...]
    block[:, pl.ds(1024, 256)] = (total[:4] / 256.0).astype(BF16)
    for store in stores:
        store.wait()


def pair_kernel(queries, query_square, keys):
    inner = mm_nt(queries, keys)
    key_float = keys.astype(F32)
    count = keys.shape[0]
    key_square = jnp.sum(key_float * key_float, axis=1, keepdims=True)
    key_row = jnp.transpose(jnp.broadcast_to(key_square, (count, 128)))[:1]
    kern = jnp.exp(-(query_square + key_row - 2.0 * inner) / keys.shape[1])
    return jnp.sum(kern, axis=1, keepdims=True), mm(kern.astype(BF16), keys)


def backward_kernel(
    sizes, gathered, w_head_hbm, w_conv_hbm, one_hot_hbm, pre_embed_hbm, hidden_hbm, pre_conv_hbm,
    keep, send, grad_head,
    w_head, w_conv, one_hot, pre_embed, hidden, pre_conv, ordered, head_full, sem
):
    dp, fsdp = sizes
    devices = dp * fsdp
    loads = []

    def load(source, target):
        loads.append(pltpu.make_async_copy(source, target, sem.at[len(loads)]))
        loads[-1].start()
        return loads[-1]

    head_load = load(w_head_hbm, w_head)
    pre_conv_load = load(pre_conv_hbm, pre_conv)
    hidden_loads = [load(hidden_hbm.at[cp], hidden.at[cp]) for cp in range(4)]
    conv_load = load(w_conv_hbm, w_conv)
    embed_loads = [
        (load(pre_embed_hbm.at[cp], pre_embed.at[cp]), load(one_hot_hbm.at[cp], one_hot.at[cp])) for cp in range(4)
    ]
    dp_here, fsdp_here = lax.axis_index("dp"), lax.axis_index("fsdp")
    here = dp_here * fsdp + fsdp_here
    for place in range(devices):
        if devices == 16:
            x = (dp_here // 2) ^ (place & 1)
            z = fsdp_here ^ (place >> 1 & 3)
            owner = (2 * x + (lax.rem(dp_here, 2) ^ (place >> 3))) * fsdp + z
        else:
            owner = place
        ordered[owner] = gathered[place].astype(F32)
    samples = ordered.shape[1]
    count = devices * samples
    full = ordered[...].reshape(count, ordered.shape[2])
    prior = full[:, :512].astype(BF16)
    recon = full[:, 512:1024]
    pooled = full[:, 1024:].astype(BF16)
    head_load.wait()
    latent = mm(pooled, w_head[...]).astype(BF16)
    latent_float = latent.astype(F32)
    square = jnp.sum(latent_float * latent_float, axis=1, keepdims=True)
    self_sum, self_mix = pair_kernel(latent, square, latent)
    cross_sum, cross_mix = pair_kernel(latent, square, prior)
    pull = -32.0 / count * ((self_sum - cross_sum) * latent_float - self_mix + cross_mix)
    cotangent = (recon + pull).astype(BF16)
    turned = jnp.transpose(full[:, 1024:]).astype(BF16)
    head_full[...] = mm(turned, cotangent)
    share = grad_head.shape[0]
    start = pl.multiple_of(fsdp_here * share, share)
    grad_head[...] = head_full[pl.ds(start, share), :]

    lane_sample = iota((128, count), 0) // 8 % 4 + samples * here
    pick = jnp.where(lane_sample == iota((128, count), 1), 1.0, 0.0).astype(BF16)
    lanes = mm(pick, cotangent).astype(BF16)
    back_pool = mm_nt(w_head[...], lanes) / 256.0
    back_pool = jnp.concatenate([back_pool, back_pool], axis=1)
    grads = []
    conv_total = None
    pre_conv_load.wait()
    for cp in range(4):
        pre = pre_conv[cp]
        gate = sigmoid(pre)
        grads.append((back_pool * (gate * (1.0 + pre * (1.0 - gate)))).astype(BF16))
        hidden_loads[cp].wait()
        term = mm_nt(hidden[cp].reshape(1024, 256), grads[cp])
        conv_total = term if cp == 0 else conv_total + term
    core_zero = lax.rem(dp_here, 2) == 0
    xs, conv_rows, embed_rows = dp // 2, 1024 // devices, 256 // devices
    for x in range(xs):
        for f in range(fsdp):
            at = (f * dp + 2 * x) * conv_rows
            first, second = conv_total[at : at + conv_rows], conv_total[at + conv_rows : at + 2 * conv_rows]
            keep[x, f, pl.ds(0, conv_rows), :] = jnp.where(core_zero, first, second)
            send[x, f, pl.ds(0, conv_rows), :] = jnp.where(core_zero, second, first)
    embed_total = None
    conv_load.wait()
    for cp in range(4):
        embed_loads[cp][0].wait()
        embed_loads[cp][1].wait()
        for j in range(4):
            rows = mm(w_conv[pl.ds(j * 256, 256), :], grads[cp])
            pre = pre_embed[cp, j]
            gate = sigmoid(pre)
            signal = (rows * (gate * (1.0 + pre * (1.0 - gate)))).astype(BF16)
            term = mm_nt(one_hot[cp, j], signal)
            embed_total = term if embed_total is None else embed_total + term
    embed = jnp.concatenate(
        [
            embed_total[dx * 128 : dx * 128 + 64, :128] + embed_total[dx * 128 + 64 : dx * 128 + 128, 128:]
            for dx in range(4)
        ],
        axis=0,
    )
    half = embed_rows // 2
    for x in range(xs):
        for f in range(fsdp):
            for side in range(2):
                at = (f * dp + 2 * x) * embed_rows + side * half
                first, second = embed[at : at + half], embed[at + embed_rows : at + embed_rows + half]
                place = (x, f, pl.ds(conv_rows, half), pl.ds(side * 128, 128))
                keep[place] = jnp.where(core_zero, first, second)
                send[place] = jnp.where(core_zero, second, first)


VMEM = pl.BlockSpec(memory_space=pltpu.VMEM)
HBM = pl.BlockSpec(memory_space=pltpu.HBM)
SAVED = (
    ((4, 4, 512, 256), BF16),
    ((4, 4, 256, 256), F32),
    ((4, 4, 256, 256), BF16),
    ((4, 256, 256), F32),
)


def forward(facies, prior_draws, recon_grad, w_embed, w_conv):
    samples = facies.shape[0]
    latent_width = prior_draws.shape[1]
    rows, lanes = samples * PATCH_X, PATCH_Y * PATCH_Z
    return pl.pallas_call(
        forward_kernel,
        out_shape=(jax.ShapeDtypeStruct((samples, 2 * latent_width + 256), BF16),)
        + tuple(jax.ShapeDtypeStruct(shape, kind) for shape, kind in SAVED),
        in_specs=[HBM] * 5,
        out_specs=(VMEM,) + (HBM,) * 4,
        scratch_shapes=[
            pltpu.VMEM((rows, lanes), jnp.int32),
            pltpu.VMEM(prior_draws.shape, BF16),
            pltpu.VMEM(recon_grad.shape, BF16),
            pltpu.VMEM(w_embed.shape, BF16),
            pltpu.VMEM(w_conv.shape, BF16),
            *[pltpu.VMEM(shape, kind) for shape, kind in SAVED],
            pltpu.VMEM((256, 512), BF16),
            pltpu.VMEM((rows, lanes), BF16),
            pltpu.SemaphoreType.DMA((8,)),
            pltpu.SemaphoreType.DMA((28,)),
        ],
        compiler_params=pltpu.CompilerParams(vmem_limit_bytes=30 * 2**20),
        name="forward",
    )(facies.reshape(rows, lanes), prior_draws, recon_grad, w_embed, w_conv)


def backward(sizes, gathered, w_head, w_conv, saved):
    dp, fsdp = sizes
    devices, samples, width = gathered.shape
    payload = jax.ShapeDtypeStruct((dp // 2, fsdp, (1024 + 128) // devices, 256), F32)
    return pl.pallas_call(
        lambda *refs: backward_kernel(sizes, *refs),
        out_shape=(payload, payload, jax.ShapeDtypeStruct((256 // fsdp, 512), F32)),
        in_specs=[VMEM] + [HBM] * 6,
        out_specs=(VMEM,) * 3,
        scratch_shapes=[
            pltpu.VMEM(w_head.shape, BF16),
            pltpu.VMEM(w_conv.shape, BF16),
            *[pltpu.VMEM(shape, kind) for shape, kind in SAVED],
            pltpu.VMEM((devices, samples, width), F32),
            pltpu.VMEM((256, 512), F32),
            pltpu.SemaphoreType.DMA((15,)),
        ],
        compiler_params=pltpu.CompilerParams(vmem_limit_bytes=32 * 2**20),
        name="backward",
    )(gathered, w_head, w_conv, *saved)


def place_of(x, core, z, fsdp):
    return (2 * x + core) * fsdp + z


def exchange(block, dp, fsdp, flip_x, flip_core, flip_z):
    pairs = []
    for x in range(dp // 2):
        for core in range(2):
            for z in range(fsdp):
                pairs.append((place_of(x, core, z, fsdp), place_of(x ^ flip_x, core ^ flip_core, z ^ flip_z, fsdp)))
    return lax.ppermute(block, GROUP, pairs)


def gather_blocks(block, dp, fsdp):
    if (dp, fsdp) != (4, 4):
        return lax.all_gather(block, GROUP, axis=0)
    stacked = block[None]
    for flips in ((1, 0, 0), (0, 0, 1), (0, 0, 2), (0, 1, 0)):
        stacked = jnp.concatenate([stacked, exchange(stacked, dp, fsdp, *flips)], axis=0)
    return stacked


def exponent_of(part):
    top = jnp.max(jnp.abs(part))
    return jnp.clip(jnp.floor(jnp.log2(jnp.maximum(top, 1e-37))) - 14.0, -124.0, 114.0)


def reduce_to_owner(keep, send, dp, fsdp):
    xs, _, rows, width = keep.shape
    conv_rows = rows * 8 // 9
    held = keep + exchange(send, dp, fsdp, 0, 1, 0)
    conv, embed = held[:, :, :conv_rows], held[:, :, conv_rows:]
    conv_step, embed_step = exponent_of(conv), exponent_of(embed)
    spare = 16 * (rows // 16 + 1) - rows
    tail = jnp.where(jnp.arange(spare)[:, None] == 0, conv_step, embed_step)
    tail = jnp.broadcast_to(tail, (xs, fsdp, spare, width))
    coded = jnp.concatenate([conv * jnp.exp2(-conv_step), embed * jnp.exp2(-embed_step), tail], axis=2)
    coded = coded.astype(jnp.float16).reshape(xs * fsdp, rows + spare, width)
    groups = [[place_of(x, core, z, fsdp) for x in range(xs) for z in range(fsdp)] for core in range(2)]
    got = lax.all_to_all(coded, GROUP, 0, 0, axis_index_groups=groups, tiled=True).astype(F32)
    conv_scale = jnp.exp2(got[:, rows : rows + 1, :1])
    embed_scale = jnp.exp2(got[:, rows + 1 : rows + 2, :1])
    is_conv = jnp.arange(rows)[None, :, None] < conv_rows
    total = jnp.sum(got[:, :rows] * jnp.where(is_conv, conv_scale, embed_scale), axis=0)
    if dp != 4:
        return lax.all_gather(total, "dp", axis=0).reshape(xs, 2, rows, width)
    x, core = lax.axis_index("dp") // 2, lax.axis_index("dp") % 2
    other = exchange(total, dp, fsdp, 1, 0, 0)
    column = jnp.stack([jnp.where(x == 0, total, other), jnp.where(x == 0, other, total)])
    sibling = exchange(column, dp, fsdp, 0, 1, 0)
    return jnp.stack([jnp.where(core == 0, column, sibling), jnp.where(core == 0, sibling, column)], axis=1)


def shards(facies, prior_draws, recon_grad, w_embed, w_conv, w_head):
    dp, fsdp = lax.axis_size("dp"), lax.axis_size("fsdp")
    block, *saved = forward(facies, prior_draws, recon_grad, w_embed, w_conv)
    gathered = gather_blocks(block, dp, fsdp)
    keep, send, grad_head = backward((dp, fsdp), gathered, w_head, w_conv, saved)
    summed = reduce_to_owner(keep, send, dp, fsdp)
    conv_rows = summed.shape[2] * 8 // 9
    embed = summed[:, :, conv_rows:].reshape(dp, -1, 2, 128).transpose(0, 2, 1, 3)
    return (
        embed.reshape(256 // fsdp, 128),
        summed[:, :, :conv_rows].reshape(1024 // fsdp, 256),
        grad_head,
    )


def solution(mesh):
    return jax.shard_map(
        shards,
        mesh=mesh,
        in_specs=(
            P(("groups", "dp", "fsdp"), None, None),
            P(("groups", "dp", "fsdp"), None),
            P(("groups", "dp", "fsdp"), None),
            P(),
            P(),
            P(),
        ),
        out_specs=(
            P(("groups", "fsdp"), None),
            P(("groups", "fsdp"), None),
            P(("groups", "fsdp"), None),
        ),
        check_vma=False,
    )
```

```python
import jax
import jax.numpy as jnp
from jax import lax
from jax.experimental import pallas as pl
from jax.experimental.pallas import tpu as pltpu
from jax.sharding import PartitionSpec as P

PATCH_X = 64
PATCH_Y = 64
PATCH_Z = 32
LEVELS = 4
GROUP = ("dp", "fsdp")
NT = (((1,), (1,)), ((), ()))
F32 = jnp.float32
BF16 = jnp.bfloat16


def iota(shape, dim):
    return lax.broadcasted_iota(jnp.int32, shape, dim)


def mm(left, right):
    return jnp.dot(left, right, preferred_element_type=F32)


def mm_nt(left, right):
    return lax.dot_general(left, right, NT, preferred_element_type=F32)


def spread_matrix():
    out_row = iota((512, 128), 0)
    lane = iota((512, 128), 1)
    pair, half = out_row // 128, out_row // 64 % 2
    row_dy, row_dz = out_row // 16 % 4, out_row // 4 % 4
    lane_dy, lane_c, lane_dz = lane // 32, lane // 4 % 8, lane % 4
    hit = (row_dy == lane_dy) & (row_dz == lane_dz) & (lane_c == 2 * pair + half)
    return jnp.where(hit, 1.0, 0.0).astype(BF16)


def pair_weights(w_embed):
    turned = jnp.transpose(w_embed.astype(F32)).astype(BF16)
    halves = []
    for half in range(2):
        row = iota((256, 512), 0)
        lane = iota((256, 512), 1)
        hit = (row // 64 == lane // 128) & (row % 64 == lane % 64) & (lane // 64 % 2 == half)
        halves.append(mm(turned, jnp.where(hit, 1.0, 0.0).astype(BF16)))
    return jnp.concatenate(halves, axis=0).astype(BF16)


def sigmoid(value):
    return 1.0 / (1.0 + jnp.exp(-value))


def forward_kernel(
    facies_hbm, prior_hbm, recon_hbm, w_embed_hbm, w_conv_hbm, w_head_hbm,
    block, one_hot, pre_embed, hidden, pre_conv, w_conv, w_head,
    facies, prior, recon, w_embed, packed, sorted_rows, sem
):
    parts = 4
    width = facies.shape[1] // parts
    loads = [
        pltpu.make_async_copy(
            facies_hbm.at[:, pl.ds(i * width, width)], facies.at[:, pl.ds(i * width, width)], sem.at[i]
        )
        for i in range(parts)
    ]
    for source, target in (
        (w_embed_hbm, w_embed), (w_conv_hbm, w_conv), (prior_hbm, prior), (recon_hbm, recon), (w_head_hbm, w_head)
    ):
        loads.append(pltpu.make_async_copy(source, target, sem.at[len(loads)]))
    for load in loads:
        load.start()
    row, lane = iota((256, 256), 0), iota((256, 256), 1)
    order = jnp.where((row // 32 == lane % 8) & (row % 32 == lane // 8), 1.0, 0.0).astype(BF16)
    spread = spread_matrix()
    level = (iota((512, 256), 0) % 4).astype(F32)
    for i in range(parts):
        loads[i].wait()
        part = facies[:, pl.ds(i * width, width)].astype(F32).astype(BF16)
        sorted_rows[:, pl.ds(i * width, width)] = mm(order, part).astype(BF16)
    for t in range(8):
        for dy2 in range(2):
            j, dx = 2 * (t // 4) + dy2, t % 4
            rows = [sorted_rows[pl.ds(t * 32, 32), pl.ds((2 * b2 + dy2) * 128, 128)] for b2 in range(8)]
            copied = mm_nt(spread, jnp.concatenate(rows, axis=0))
            hot = jnp.where(copied == level, 1.0, 0.0).astype(BF16)
            for cp in range(4):
                one_hot[cp, j, pl.ds(dx * 128, 128), :] = hot[cp * 128 : (cp + 1) * 128]
    loads[4].wait()
    packed[...] = pair_weights(w_embed[...])
    loads[5].wait()
    conv_turned = jnp.transpose(w_conv[...].astype(F32)).astype(BF16)
    sums = jnp.zeros((256, 128), F32)
    for cp in range(4):
        for j in range(4):
            pre = mm(packed[...], one_hot[cp, j])
            pre_embed[cp, j] = pre
            hidden[cp, j] = (pre * sigmoid(pre)).astype(BF16)
        pre = mm(conv_turned, hidden[cp].reshape(1024, 256))
        pre_conv[cp] = pre
        act = pre * sigmoid(pre)
        sums = sums + act[:, :128] + act[:, 128:]
    pick = jnp.where(iota((8, 128), 1) // 8 % 4 == iota((8, 128), 0), 1.0, 0.0)
    total = lax.dot_general(pick, sums, NT, precision=lax.Precision.HIGHEST, preferred_element_type=F32)
    for load in loads[6:]:
        load.wait()
    block[:, pl.ds(0, 512)] = prior[...]
    block[:, pl.ds(512, 512)] = recon[...]
    block[:, pl.ds(1024, 256)] = (total[:4] / 256.0).astype(BF16)


def pair_kernel(queries, query_square, keys):
    inner = mm_nt(queries, keys)
    key_float = keys.astype(F32)
    count = keys.shape[0]
    key_square = jnp.sum(key_float * key_float, axis=1, keepdims=True)
    key_row = jnp.transpose(jnp.broadcast_to(key_square, (count, 128)))[:1]
    kern = jnp.exp(-(query_square + key_row - 2.0 * inner) / keys.shape[1])
    return jnp.sum(kern, axis=1, keepdims=True), mm(kern.astype(BF16), keys)


def backward_kernel(
    sizes, gathered, one_hot, pre_embed, hidden, pre_conv, w_conv, w_head,
    keep, send, grad_head,
    ordered, head_full
):
    dp, fsdp = sizes
    devices = dp * fsdp
    dp_here, fsdp_here = lax.axis_index("dp"), lax.axis_index("fsdp")
    here = dp_here * fsdp + fsdp_here
    for owner in range(devices):
        ordered[owner] = gathered[owner].astype(F32)
    samples = ordered.shape[1]
    count = devices * samples
    full = ordered[...].reshape(count, ordered.shape[2])
    prior = full[:, :512].astype(BF16)
    recon = full[:, 512:1024]
    pooled = full[:, 1024:].astype(BF16)
    latent = mm(pooled, w_head[...]).astype(BF16)
    latent_float = latent.astype(F32)
    square = jnp.sum(latent_float * latent_float, axis=1, keepdims=True)
    self_sum, self_mix = pair_kernel(latent, square, latent)
    cross_sum, cross_mix = pair_kernel(latent, square, prior)
    pull = -32.0 / count * ((self_sum - cross_sum) * latent_float - self_mix + cross_mix)
    cotangent = (recon + pull).astype(BF16)
    turned = jnp.transpose(full[:, 1024:]).astype(BF16)
    head_full[...] = mm(turned, cotangent)
    share = grad_head.shape[0]
    start = pl.multiple_of(fsdp_here * share, share)
    grad_head[...] = head_full[pl.ds(start, share), :]

    lane_sample = iota((128, count), 0) // 8 % 4 + samples * here
    pick = jnp.where(lane_sample == iota((128, count), 1), 1.0, 0.0).astype(BF16)
    lanes = mm(pick, cotangent).astype(BF16)
    back_pool = mm_nt(w_head[...], lanes) / 256.0
    back_pool = jnp.concatenate([back_pool, back_pool], axis=1)
    grads = []
    conv_total = None
    for cp in range(4):
        pre = pre_conv[cp]
        gate = sigmoid(pre)
        grads.append((back_pool * (gate * (1.0 + pre * (1.0 - gate)))).astype(BF16))
        term = mm_nt(hidden[cp].reshape(1024, 256), grads[cp])
        conv_total = term if cp == 0 else conv_total + term
    core_zero = lax.rem(dp_here, 2) == 0
    rows = 1024 // fsdp // 2
    for f in range(fsdp):
        at = 2 * f * rows
        first, second = conv_total[at : at + rows], conv_total[at + rows : at + 2 * rows]
        keep[f, pl.ds(0, rows), :] = jnp.where(core_zero, first, second)
        send[f, pl.ds(0, rows), :] = jnp.where(core_zero, second, first)
    embed_total = None
    for cp in range(4):
        for j in range(4):
            back_rows = mm(w_conv[pl.ds(j * 256, 256), :], grads[cp])
            pre = pre_embed[cp, j]
            gate = sigmoid(pre)
            signal = (back_rows * (gate * (1.0 + pre * (1.0 - gate)))).astype(BF16)
            term = mm_nt(one_hot[cp, j], signal)
            embed_total = term if embed_total is None else embed_total + term
    embed = jnp.concatenate(
        [
            embed_total[dx * 128 : dx * 128 + 64, :128] + embed_total[dx * 128 + 64 : dx * 128 + 128, 128:]
            for dx in range(4)
        ],
        axis=0,
    )
    half = 256 // fsdp // 4
    for f in range(fsdp):
        for side in range(2):
            at = (4 * f + side) * half
            first, second = embed[at : at + half], embed[at + 2 * half : at + 3 * half]
            place = (f, pl.ds(rows, half), pl.ds(side * 128, 128))
            keep[place] = jnp.where(core_zero, first, second)
            send[place] = jnp.where(core_zero, second, first)


def exponent_of(part):
    top = jnp.max(jnp.max(jnp.max(jnp.abs(part), axis=0), axis=0, keepdims=True), axis=1, keepdims=True)
    return jnp.clip(jnp.floor(jnp.log2(jnp.maximum(top, 1e-37))) - 14.0, -124.0, 114.0)


def scale_kernel(keep, other, coded):
    rows = keep.shape[1]
    conv_rows = rows * 8 // 9
    held = keep[...] + other[...]
    conv, embed = held[:, :conv_rows], held[:, conv_rows:]
    conv_step, embed_step = exponent_of(conv), exponent_of(embed)
    coded[:, pl.ds(0, conv_rows), :] = conv * jnp.exp2(-conv_step)[None]
    coded[:, pl.ds(conv_rows, rows - conv_rows), :] = embed * jnp.exp2(-embed_step)[None]
    spare = coded.shape[1] - rows
    tail = jnp.where(iota((spare, coded.shape[2]), 0) == 0, conv_step, embed_step)
    coded[:, pl.ds(rows, spare), :] = jnp.broadcast_to(tail[None], (coded.shape[0], spare, coded.shape[2]))


def output_kernel(own, other, grad_embed, grad_conv):
    rows = own.shape[0]
    conv_rows, half = rows * 8 // 9, rows // 9
    core_zero = lax.rem(lax.axis_index("dp"), 2) == 0
    first = jnp.where(core_zero, own[...], other[...])
    second = jnp.where(core_zero, other[...], own[...])
    for at, part in ((0, first), (1, second)):
        grad_conv[pl.ds(at * conv_rows, conv_rows), :] = part[:conv_rows]
        grad_embed[pl.ds(at * 2 * half, half), :] = part[conv_rows:, :128]
        grad_embed[pl.ds((at * 2 + 1) * half, half), :] = part[conv_rows:, 128:]


VMEM = pl.BlockSpec(memory_space=pltpu.VMEM)
HBM = pl.BlockSpec(memory_space=pltpu.HBM)
SAVED = (
    ((4, 4, 512, 256), BF16),
    ((4, 4, 256, 256), F32),
    ((4, 4, 256, 256), BF16),
    ((4, 256, 256), F32),
)


def forward(facies, prior_draws, recon_grad, w_embed, w_conv, w_head):
    samples = facies.shape[0]
    latent_width = prior_draws.shape[1]
    rows, lanes = samples * PATCH_X, PATCH_Y * PATCH_Z
    operands = (facies.reshape(rows, lanes), prior_draws, recon_grad, w_embed, w_conv, w_head)
    return pl.pallas_call(
        forward_kernel,
        out_shape=(pltpu.VMEM((samples, 2 * latent_width + 256), BF16),)
        + tuple(pltpu.VMEM(shape, kind) for shape, kind in SAVED)
        + (pltpu.VMEM(w_conv.shape, BF16), pltpu.VMEM(w_head.shape, BF16)),
        in_specs=[HBM] * 6,
        out_specs=(VMEM,) * 7,
        scratch_shapes=[
            pltpu.VMEM((rows, lanes), jnp.int32),
            pltpu.VMEM(prior_draws.shape, BF16),
            pltpu.VMEM(recon_grad.shape, BF16),
            pltpu.VMEM(w_embed.shape, BF16),
            pltpu.VMEM((256, 512), BF16),
            pltpu.VMEM((rows, lanes), BF16),
            pltpu.SemaphoreType.DMA((9,)),
        ],
        compiler_params=pltpu.CompilerParams(vmem_limit_bytes=30 * 2**20),
        name="forward",
    )(*(pltpu.with_memory_space_constraint(operand, pltpu.HBM) for operand in operands))


def backward(sizes, gathered, saved):
    dp, fsdp = sizes
    devices, samples, width = gathered.shape
    payload = jax.ShapeDtypeStruct((fsdp, (1024 + 128) // fsdp // 2, 256), F32)
    return pl.pallas_call(
        lambda *refs: backward_kernel(sizes, *refs),
        out_shape=(payload, payload, jax.ShapeDtypeStruct((256 // fsdp, 512), F32)),
        in_specs=[VMEM] * 7,
        out_specs=(VMEM,) * 3,
        scratch_shapes=[pltpu.VMEM((devices, samples, width), F32), pltpu.VMEM((256, 512), F32)],
        compiler_params=pltpu.CompilerParams(vmem_limit_bytes=30 * 2**20),
        name="backward",
    )(gathered, *saved)


def place_of(x, core, z, fsdp):
    return (2 * x + core) * fsdp + z


def exchange(block, dp, fsdp, flip_x, flip_core):
    pairs = []
    for x in range(dp // 2):
        for core in range(2):
            for z in range(fsdp):
                pairs.append((place_of(x, core, z, fsdp), place_of(x ^ flip_x, core ^ flip_core, z, fsdp)))
    return lax.ppermute(block, GROUP, pairs)


def gather_blocks(block, devices):
    copies = jnp.broadcast_to(block[None], (devices,) + block.shape)
    return lax.all_to_all(copies, GROUP, 0, 0, tiled=True)


def reduce_to_owner(keep, send, dp, fsdp):
    _, rows, width = keep.shape
    conv_rows = rows * 8 // 9
    spare = 16 * (rows // 16 + 1) - rows
    coded = pl.pallas_call(
        scale_kernel,
        out_shape=jax.ShapeDtypeStruct((fsdp, rows + spare, width), F32),
        in_specs=[VMEM] * 2,
        out_specs=VMEM,
        compiler_params=pltpu.CompilerParams(vmem_limit_bytes=16 * 2**20),
        name="scale",
    )(keep, exchange(send, dp, fsdp, 0, 1)).astype(jnp.float16)
    got = lax.all_to_all(coded, "fsdp", 0, 0, tiled=True).astype(F32)
    conv_scale = jnp.exp2(got[:, rows : rows + 1, :1])
    embed_scale = jnp.exp2(got[:, rows + 1 : rows + 2, :1])
    is_conv = jnp.arange(rows)[None, :, None] < conv_rows
    total = jnp.sum(got[:, :rows] * jnp.where(is_conv, conv_scale, embed_scale), axis=0)
    flip = 1
    while flip < dp // 2:
        total = total + exchange(total, dp, fsdp, flip, 0)
        flip *= 2
    return total, exchange(total, dp, fsdp, 0, 1)


def shards(facies, prior_draws, recon_grad, w_embed, w_conv, w_head):
    dp, fsdp = lax.axis_size("dp"), lax.axis_size("fsdp")
    block, *saved = forward(facies, prior_draws, recon_grad, w_embed, w_conv, w_head)
    gathered = gather_blocks(block, dp * fsdp)
    keep, send, grad_head = backward((dp, fsdp), gathered, saved)
    own, other = reduce_to_owner(keep, send, dp, fsdp)
    grad_embed, grad_conv = pl.pallas_call(
        output_kernel,
        out_shape=(
            jax.ShapeDtypeStruct((256 // fsdp, 128), F32),
            jax.ShapeDtypeStruct((1024 // fsdp, 256), F32),
        ),
        in_specs=[VMEM] * 2,
        out_specs=(VMEM,) * 2,
        compiler_params=pltpu.CompilerParams(vmem_limit_bytes=16 * 2**20),
        name="outputs",
    )(own, other)
    return (grad_embed, grad_conv, grad_head)


def solution(mesh):
    return jax.shard_map(
        shards,
        mesh=mesh,
        in_specs=(
            P(("groups", "dp", "fsdp"), None, None),
            P(("groups", "dp", "fsdp"), None),
            P(("groups", "dp", "fsdp"), None),
            P(),
            P(),
            P(),
        ),
        out_specs=(
            P(("groups", "fsdp"), None),
            P(("groups", "fsdp"), None),
            P(("groups", "fsdp"), None),
        ),
        check_vma=False,
    )
```

```python
import jax
import jax.numpy as jnp
from jax import lax
from jax.experimental import pallas as pl
from jax.experimental.pallas import tpu as pltpu
from jax.sharding import PartitionSpec as P

PATCH_X = 64
PATCH_Y = 64
PATCH_Z = 32
LEVELS = 4
GROUP = ("dp", "fsdp")
NT = (((1,), (1,)), ((), ()))
F32 = jnp.float32
BF16 = jnp.bfloat16


def iota(shape, dim):
    return lax.broadcasted_iota(jnp.int32, shape, dim)


def mm(left, right):
    return jnp.dot(left, right, preferred_element_type=F32)


def mm_nt(left, right):
    return lax.dot_general(left, right, NT, preferred_element_type=F32)


def spread_matrix():
    out_row = iota((512, 128), 0)
    lane = iota((512, 128), 1)
    pair, half = out_row // 128, out_row // 64 % 2
    row_dy, row_dz = out_row // 16 % 4, out_row // 4 % 4
    lane_dy, lane_c, lane_dz = lane // 32, lane // 4 % 8, lane % 4
    hit = (row_dy == lane_dy) & (row_dz == lane_dz) & (lane_c == 2 * pair + half)
    return jnp.where(hit, 1.0, 0.0).astype(BF16)


def pair_weights(w_embed):
    turned = jnp.transpose(w_embed.astype(F32)).astype(BF16)
    halves = []
    for half in range(2):
        row = iota((256, 512), 0)
        lane = iota((256, 512), 1)
        hit = (row // 64 == lane // 128) & (row % 64 == lane % 64) & (lane // 64 % 2 == half)
        halves.append(mm(turned, jnp.where(hit, 1.0, 0.0).astype(BF16)))
    return jnp.concatenate(halves, axis=0).astype(BF16)


def sigmoid(value):
    return 1.0 / (1.0 + jnp.exp(-value))


def forward_kernel(
    facies_hbm, prior_hbm, recon_hbm, w_embed_hbm, w_conv_hbm, w_head_hbm,
    block, one_hot, pre_embed, hidden, pre_conv, w_conv, w_head,
    facies, prior, recon, w_embed, packed, sorted_rows, sem
):
    parts = 4
    width = facies.shape[1] // parts
    loads = [
        pltpu.make_async_copy(
            facies_hbm.at[:, pl.ds(i * width, width)], facies.at[:, pl.ds(i * width, width)], sem.at[i]
        )
        for i in range(parts)
    ]
    for source, target in (
        (w_embed_hbm, w_embed), (w_conv_hbm, w_conv), (prior_hbm, prior), (recon_hbm, recon), (w_head_hbm, w_head)
    ):
        loads.append(pltpu.make_async_copy(source, target, sem.at[len(loads)]))
    for load in loads:
        load.start()
    row, lane = iota((256, 256), 0), iota((256, 256), 1)
    order = jnp.where((row // 32 == lane % 8) & (row % 32 == lane // 8), 1.0, 0.0).astype(BF16)
    spread = spread_matrix()
    level = (iota((512, 256), 0) % 4).astype(F32)
    for i in range(parts):
        loads[i].wait()
        part = facies[:, pl.ds(i * width, width)].astype(F32).astype(BF16)
        sorted_rows[:, pl.ds(i * width, width)] = mm(order, part).astype(BF16)
    for t in range(8):
        for dy2 in range(2):
            j, dx = 2 * (t // 4) + dy2, t % 4
            rows = [sorted_rows[pl.ds(t * 32, 32), pl.ds((2 * b2 + dy2) * 128, 128)] for b2 in range(8)]
            copied = mm_nt(spread, jnp.concatenate(rows, axis=0))
            hot = jnp.where(copied == level, 1.0, 0.0).astype(BF16)
            for cp in range(4):
                one_hot[cp, j, pl.ds(dx * 128, 128), :] = hot[cp * 128 : (cp + 1) * 128]
    loads[4].wait()
    packed[...] = pair_weights(w_embed[...])
    loads[5].wait()
    conv_turned = jnp.transpose(w_conv[...].astype(F32)).astype(BF16)
    sums = jnp.zeros((256, 128), F32)
    for cp in range(4):
        for j in range(4):
            pre = mm(packed[...], one_hot[cp, j])
            pre_embed[cp, j] = pre
            hidden[cp, j] = (pre * sigmoid(pre)).astype(BF16)
        pre = mm(conv_turned, hidden[cp].reshape(1024, 256))
        pre_conv[cp] = pre
        act = pre * sigmoid(pre)
        sums = sums + act[:, :128] + act[:, 128:]
    pick = jnp.where(iota((8, 128), 1) // 8 % 4 == iota((8, 128), 0), 1.0, 0.0)
    total = lax.dot_general(pick, sums, NT, precision=lax.Precision.HIGHEST, preferred_element_type=F32)
    for load in loads[6:]:
        load.wait()
    block[:, pl.ds(0, 512)] = prior[...]
    block[:, pl.ds(512, 512)] = recon[...]
    block[:, pl.ds(1024, 256)] = (total[:4] / 256.0).astype(BF16)


def pair_kernel(queries, query_square, keys):
    inner = mm_nt(queries, keys)
    key_float = keys.astype(F32)
    count = keys.shape[0]
    key_square = jnp.sum(key_float * key_float, axis=1, keepdims=True)
    key_row = jnp.transpose(jnp.broadcast_to(key_square, (count, 128)))[:1]
    kern = jnp.exp(-(query_square + key_row - 2.0 * inner) / keys.shape[1])
    return jnp.sum(kern, axis=1, keepdims=True), mm(kern.astype(BF16), keys)


def backward_kernel(
    sizes, gathered, one_hot, pre_embed, hidden, pre_conv, w_conv, w_head,
    keep, send, grad_head,
    ordered, head_full
):
    dp, fsdp = sizes
    devices = dp * fsdp
    dp_here, fsdp_here = lax.axis_index("dp"), lax.axis_index("fsdp")
    here = dp_here * fsdp + fsdp_here
    for owner in range(devices):
        ordered[owner] = gathered[owner].astype(F32)
    samples = ordered.shape[1]
    count = devices * samples
    full = ordered[...].reshape(count, ordered.shape[2])
    prior = full[:, :512].astype(BF16)
    recon = full[:, 512:1024]
    pooled = full[:, 1024:].astype(BF16)
    latent = mm(pooled, w_head[...]).astype(BF16)
    latent_float = latent.astype(F32)
    square = jnp.sum(latent_float * latent_float, axis=1, keepdims=True)
    self_sum, self_mix = pair_kernel(latent, square, latent)
    cross_sum, cross_mix = pair_kernel(latent, square, prior)
    pull = -32.0 / count * ((self_sum - cross_sum) * latent_float - self_mix + cross_mix)
    cotangent = (recon + pull).astype(BF16)
    turned = jnp.transpose(full[:, 1024:]).astype(BF16)
    head_full[...] = mm(turned, cotangent)
    share = grad_head.shape[0]
    start = pl.multiple_of(fsdp_here * share, share)
    grad_head[...] = head_full[pl.ds(start, share), :]

    lane_sample = iota((128, count), 0) // 8 % 4 + samples * here
    pick = jnp.where(lane_sample == iota((128, count), 1), 1.0, 0.0).astype(BF16)
    lanes = mm(pick, cotangent).astype(BF16)
    back_pool = mm_nt(w_head[...], lanes) / 256.0
    back_pool = jnp.concatenate([back_pool, back_pool], axis=1)
    grads = []
    conv_total = None
    for cp in range(4):
        pre = pre_conv[cp]
        gate = sigmoid(pre)
        grads.append((back_pool * (gate * (1.0 + pre * (1.0 - gate)))).astype(BF16))
        term = mm_nt(hidden[cp].reshape(1024, 256), grads[cp])
        conv_total = term if cp == 0 else conv_total + term
    core_zero = lax.rem(dp_here, 2) == 0
    rows = 1024 // fsdp // 2
    for f in range(fsdp):
        at = 2 * f * rows
        first, second = conv_total[at : at + rows], conv_total[at + rows : at + 2 * rows]
        keep[f, pl.ds(0, rows), :] = jnp.where(core_zero, first, second)
        send[f, pl.ds(0, rows), :] = jnp.where(core_zero, second, first)
    embed_total = None
    for cp in range(4):
        for j in range(4):
            back_rows = mm(w_conv[pl.ds(j * 256, 256), :], grads[cp])
            pre = pre_embed[cp, j]
            gate = sigmoid(pre)
            signal = (back_rows * (gate * (1.0 + pre * (1.0 - gate)))).astype(BF16)
            term = mm_nt(one_hot[cp, j], signal)
            embed_total = term if embed_total is None else embed_total + term
    embed = jnp.concatenate(
        [
            embed_total[dx * 128 : dx * 128 + 64, :128] + embed_total[dx * 128 + 64 : dx * 128 + 128, 128:]
            for dx in range(4)
        ],
        axis=0,
    )
    half = 256 // fsdp // 4
    for f in range(fsdp):
        for side in range(2):
            at = (4 * f + side) * half
            first, second = embed[at : at + half], embed[at + 2 * half : at + 3 * half]
            place = (f, pl.ds(rows, half), pl.ds(side * 128, 128))
            keep[place] = jnp.where(core_zero, first, second)
            send[place] = jnp.where(core_zero, second, first)


def exponent_of(part):
    top = jnp.abs(part)
    while top.ndim > 2:
        top = jnp.max(top, axis=0)
    top = jnp.max(jnp.max(top, axis=0, keepdims=True), axis=1, keepdims=True)
    return jnp.clip(jnp.floor(jnp.log2(jnp.maximum(top, 1e-37))) - 14.0, -124.0, 114.0)


def store_coded(coded, part):
    rows = part.shape[0]
    conv_rows = rows * 8 // 9
    conv, embed = part[:conv_rows], part[conv_rows:]
    steps = exponent_of(conv), exponent_of(embed)
    store_scaled(coded, part, steps)


def store_scaled(coded, part, steps):
    rows, spare = part.shape[0], coded.shape[0] - part.shape[0]
    conv_rows = rows * 8 // 9
    coded[pl.ds(0, conv_rows), :] = part[:conv_rows] * jnp.exp2(-steps[0])
    coded[pl.ds(conv_rows, rows - conv_rows), :] = part[conv_rows:] * jnp.exp2(-steps[1])
    tail = jnp.where(iota((spare, coded.shape[1]), 0) == 0, steps[0], steps[1])
    coded[pl.ds(rows, spare), :] = tail


def load_coded(coded, rows):
    conv_rows = rows * 8 // 9
    conv_scale = jnp.exp2(coded[pl.ds(rows, 1), :])
    embed_scale = jnp.exp2(coded[pl.ds(rows + 1, 1), :])
    return jnp.concatenate(
        [coded[pl.ds(0, conv_rows), :] * conv_scale, coded[pl.ds(conv_rows, rows - conv_rows), :] * embed_scale], axis=0
    )


def scale_kernel(keep, other, own, *coded):
    rows = keep.shape[1]
    conv_rows = rows * 8 // 9
    held = keep[...] + other[...]
    steps = exponent_of(held[:, :conv_rows]), exponent_of(held[:, conv_rows:])
    here = lax.axis_index("fsdp")
    own[...] = keep[here] + other[here]
    for place, target in enumerate(coded):
        owner = here ^ (place + 1)
        store_scaled(target, keep[owner] + other[owner], steps)


def first_sum_kernel(own, *refs):
    *received, coded = refs
    total = own[...]
    for part in received:
        total = total + load_coded(part, total.shape[0])
    store_coded(coded, total)


def next_sum_kernel(mine, other, total, coded):
    rows = total.shape[0]
    summed = load_coded(mine, rows) + load_coded(other, rows)
    total[...] = summed
    store_coded(coded, summed)


def output_kernel(own, other, grad_embed, grad_conv):
    rows = own.shape[0]
    conv_rows, half = rows * 8 // 9, rows // 9
    core_zero = lax.rem(lax.axis_index("dp"), 2) == 0
    first = jnp.where(core_zero, own[...], other[...])
    second = jnp.where(core_zero, other[...], own[...])
    for at, part in ((0, first), (1, second)):
        grad_conv[pl.ds(at * conv_rows, conv_rows), :] = part[:conv_rows]
        grad_embed[pl.ds(at * 2 * half, half), :] = part[conv_rows:, :128]
        grad_embed[pl.ds((at * 2 + 1) * half, half), :] = part[conv_rows:, 128:]


VMEM = pl.BlockSpec(memory_space=pltpu.VMEM)
HBM = pl.BlockSpec(memory_space=pltpu.HBM)
SAVED = (
    ((4, 4, 512, 256), BF16),
    ((4, 4, 256, 256), F32),
    ((4, 4, 256, 256), BF16),
    ((4, 256, 256), F32),
)


def forward(facies, prior_draws, recon_grad, w_embed, w_conv, w_head):
    samples = facies.shape[0]
    latent_width = prior_draws.shape[1]
    rows, lanes = samples * PATCH_X, PATCH_Y * PATCH_Z
    operands = (facies.reshape(rows, lanes), prior_draws, recon_grad, w_embed, w_conv, w_head)
    return pl.pallas_call(
        forward_kernel,
        out_shape=(pltpu.VMEM((samples, 2 * latent_width + 256), BF16),)
        + tuple(pltpu.VMEM(shape, kind) for shape, kind in SAVED)
        + (pltpu.VMEM(w_conv.shape, BF16), pltpu.VMEM(w_head.shape, BF16)),
        in_specs=[HBM] * 6,
        out_specs=(VMEM,) * 7,
        scratch_shapes=[
            pltpu.VMEM((rows, lanes), jnp.int32),
            pltpu.VMEM(prior_draws.shape, BF16),
            pltpu.VMEM(recon_grad.shape, BF16),
            pltpu.VMEM(w_embed.shape, BF16),
            pltpu.VMEM((256, 512), BF16),
            pltpu.VMEM((rows, lanes), BF16),
            pltpu.SemaphoreType.DMA((9,)),
        ],
        compiler_params=pltpu.CompilerParams(vmem_limit_bytes=30 * 2**20),
        name="forward",
    )(*(pltpu.with_memory_space_constraint(operand, pltpu.HBM) for operand in operands))


def backward(sizes, gathered, saved):
    dp, fsdp = sizes
    devices, samples, width = gathered.shape
    payload = jax.ShapeDtypeStruct((fsdp, (1024 + 128) // fsdp // 2, 256), F32)
    return pl.pallas_call(
        lambda *refs: backward_kernel(sizes, *refs),
        out_shape=(payload, payload, jax.ShapeDtypeStruct((256 // fsdp, 512), F32)),
        in_specs=[VMEM] * 7,
        out_specs=(VMEM,) * 3,
        scratch_shapes=[pltpu.VMEM((devices, samples, width), F32), pltpu.VMEM((256, 512), F32)],
        compiler_params=pltpu.CompilerParams(vmem_limit_bytes=30 * 2**20),
        name="backward",
    )(gathered, *saved)


def place_of(x, core, z, fsdp):
    return (2 * x + core) * fsdp + z


def exchange(block, dp, fsdp, flip_x, flip_core, flip_z):
    pairs = []
    for x in range(dp // 2):
        for core in range(2):
            for z in range(fsdp):
                pairs.append((place_of(x, core, z, fsdp), place_of(x ^ flip_x, core ^ flip_core, z ^ flip_z, fsdp)))
    return lax.ppermute(block, GROUP, pairs)


def gather_blocks(block, devices):
    copies = jnp.broadcast_to(block[None], (devices,) + block.shape)
    return lax.all_to_all(copies, GROUP, 0, 0, tiled=True)


def local_kernel(kernel, outs, name, *operands):
    return pl.pallas_call(
        kernel,
        out_shape=outs,
        in_specs=[VMEM] * len(operands),
        out_specs=(VMEM,) * len(outs),
        compiler_params=pltpu.CompilerParams(vmem_limit_bytes=16 * 2**20),
        name=name,
    )(*operands)


def to_half(coded):
    rounded = lax.reduce_precision(coded, exponent_bits=5, mantissa_bits=10)
    return rounded, rounded.astype(jnp.float16)


def reduce_to_owner(keep, send, dp, fsdp):
    _, rows, width = keep.shape
    plain = jax.ShapeDtypeStruct((rows, width), F32)
    scaled = jax.ShapeDtypeStruct((rows + 8, width), F32)
    other = exchange(send, dp, fsdp, 0, 1, 0)
    own, *coded = local_kernel(scale_kernel, (plain,) + (scaled,) * (fsdp - 1), "scale", keep, other)
    received = [
        exchange(to_half(part)[1], dp, fsdp, 0, 0, place + 1).astype(F32) for place, part in enumerate(coded)
    ]
    (coded,) = local_kernel(first_sum_kernel, (scaled,), "sum_z", own, *received)
    flip = 1
    while flip < dp // 2:
        mine, sent = to_half(coded)
        other = exchange(sent, dp, fsdp, flip, 0, 0).astype(F32)
        total, coded = local_kernel(next_sum_kernel, (plain, scaled), "sum_x", mine, other)
        flip *= 2
    return total, exchange(total, dp, fsdp, 0, 1, 0)


def shards(facies, prior_draws, recon_grad, w_embed, w_conv, w_head):
    dp, fsdp = lax.axis_size("dp"), lax.axis_size("fsdp")
    block, *saved = forward(facies, prior_draws, recon_grad, w_embed, w_conv, w_head)
    gathered = gather_blocks(block, dp * fsdp)
    keep, send, grad_head = backward((dp, fsdp), gathered, saved)
    own, other = reduce_to_owner(keep, send, dp, fsdp)
    grad_embed, grad_conv = pl.pallas_call(
        output_kernel,
        out_shape=(
            jax.ShapeDtypeStruct((256 // fsdp, 128), F32),
            jax.ShapeDtypeStruct((1024 // fsdp, 256), F32),
        ),
        in_specs=[VMEM] * 2,
        out_specs=(VMEM,) * 2,
        compiler_params=pltpu.CompilerParams(vmem_limit_bytes=16 * 2**20),
        name="outputs",
    )(own, other)
    return (grad_embed, grad_conv, grad_head)


def solution(mesh):
    return jax.shard_map(
        shards,
        mesh=mesh,
        in_specs=(
            P(("groups", "dp", "fsdp"), None, None),
            P(("groups", "dp", "fsdp"), None),
            P(("groups", "dp", "fsdp"), None),
            P(),
            P(),
            P(),
        ),
        out_specs=(
            P(("groups", "fsdp"), None),
            P(("groups", "fsdp"), None),
            P(("groups", "fsdp"), None),
        ),
        check_vma=False,
    )
```

```python
import jax
import jax.numpy as jnp
from jax import lax
from jax.experimental import pallas as pl
from jax.experimental.pallas import tpu as pltpu
from jax.sharding import PartitionSpec as P

PATCH_X = 64
PATCH_Y = 64
PATCH_Z = 32
LEVELS = 4
GROUP = ("dp", "fsdp")
NT = (((1,), (1,)), ((), ()))
F32 = jnp.float32
BF16 = jnp.bfloat16


def iota(shape, dim):
    return lax.broadcasted_iota(jnp.int32, shape, dim)


def mm(left, right):
    return jnp.dot(left, right, preferred_element_type=F32)


def mm_nt(left, right):
    return lax.dot_general(left, right, NT, preferred_element_type=F32)


def spread_matrix():
    out_row = iota((512, 128), 0)
    lane = iota((512, 128), 1)
    pair, half = out_row // 128, out_row // 64 % 2
    row_dy, row_dz = out_row // 16 % 4, out_row // 4 % 4
    lane_dy, lane_c, lane_dz = lane // 32, lane // 4 % 8, lane % 4
    hit = (row_dy == lane_dy) & (row_dz == lane_dz) & (lane_c == 2 * pair + half)
    return jnp.where(hit, 1.0, 0.0).astype(BF16)


def pair_weights(w_embed):
    turned = jnp.transpose(w_embed.astype(F32)).astype(BF16)
    halves = []
    for half in range(2):
        row = iota((256, 512), 0)
        lane = iota((256, 512), 1)
        hit = (row // 64 == lane // 128) & (row % 64 == lane % 64) & (lane // 64 % 2 == half)
        halves.append(mm(turned, jnp.where(hit, 1.0, 0.0).astype(BF16)))
    return jnp.concatenate(halves, axis=0).astype(BF16)


def sigmoid(value):
    return 1.0 / (1.0 + jnp.exp(-value))


def silu_slope(value):
    gate = sigmoid(value)
    return gate * (1.0 + value * (1.0 - gate))


def forward_kernel(
    facies_hbm, prior_hbm, recon_hbm, w_embed_hbm, w_conv_hbm, w_head_hbm,
    block, one_hot, pre_embed, hidden, pre_conv, w_conv, w_head,
    facies, prior, recon, w_embed, packed, sorted_rows, sem
):
    parts = 4
    width = facies.shape[1] // parts
    loads = [
        pltpu.make_async_copy(
            facies_hbm.at[:, pl.ds(i * width, width)], facies.at[:, pl.ds(i * width, width)], sem.at[i]
        )
        for i in range(parts)
    ]
    for source, target in (
        (w_embed_hbm, w_embed), (w_conv_hbm, w_conv), (prior_hbm, prior), (recon_hbm, recon), (w_head_hbm, w_head)
    ):
        loads.append(pltpu.make_async_copy(source, target, sem.at[len(loads)]))
    for load in loads:
        load.start()
    row, lane = iota((256, 256), 0), iota((256, 256), 1)
    order = jnp.where((row // 32 == lane % 8) & (row % 32 == lane // 8), 1.0, 0.0).astype(BF16)
    spread = spread_matrix()
    level = (iota((512, 256), 0) % 4).astype(F32)
    for i in range(parts):
        loads[i].wait()
        part = facies[:, pl.ds(i * width, width)].astype(F32).astype(BF16)
        sorted_rows[:, pl.ds(i * width, width)] = mm(order, part).astype(BF16)
    for t in range(8):
        for dy2 in range(2):
            j, dx = 2 * (t // 4) + dy2, t % 4
            rows = [sorted_rows[pl.ds(t * 32, 32), pl.ds((2 * b2 + dy2) * 128, 128)] for b2 in range(8)]
            copied = mm_nt(spread, jnp.concatenate(rows, axis=0))
            hot = jnp.where(copied == level, 1.0, 0.0).astype(BF16)
            for cp in range(4):
                one_hot[cp, j, pl.ds(dx * 128, 128), :] = hot[cp * 128 : (cp + 1) * 128]
    loads[4].wait()
    packed[...] = pair_weights(w_embed[...])
    loads[5].wait()
    conv_turned = jnp.transpose(w_conv[...].astype(F32)).astype(BF16)
    sums = jnp.zeros((256, 128), F32)
    for cp in range(4):
        for j in range(4):
            pre = mm(packed[...], one_hot[cp, j])
            pre_embed[cp, j] = pre
            hidden[cp, j] = (pre * sigmoid(pre)).astype(BF16)
        pre = mm(conv_turned, hidden[cp].reshape(1024, 256))
        pre_conv[cp] = pre
        act = pre * sigmoid(pre)
        sums = sums + act[:, :128] + act[:, 128:]
    pick = jnp.where(iota((8, 128), 1) // 8 % 4 == iota((8, 128), 0), 1.0, 0.0)
    total = lax.dot_general(pick, sums, NT, precision=lax.Precision.HIGHEST, preferred_element_type=F32)
    for load in loads[6:]:
        load.wait()
    block[:, pl.ds(0, 512)] = prior[...]
    block[:, pl.ds(512, 512)] = recon[...]
    block[:, pl.ds(1024, 256)] = (total[:4] / 256.0).astype(BF16)


def pair_kernel(queries, query_square, keys):
    inner = mm_nt(queries, keys)
    key_float = keys.astype(F32)
    count = keys.shape[0]
    key_square = jnp.sum(key_float * key_float, axis=1, keepdims=True)
    key_row = jnp.transpose(jnp.broadcast_to(key_square, (count, 128)))[:1]
    kern = jnp.exp(-(query_square + key_row - 2.0 * inner) / keys.shape[1])
    return jnp.sum(kern, axis=1, keepdims=True), mm(kern.astype(BF16), keys)


def backward_kernel(
    sizes, gathered, hidden, slope_conv, w_head,
    keep, send, grads, grad_head,
    ordered, head_full
):
    dp, fsdp = sizes
    devices = dp * fsdp
    dp_here, fsdp_here = lax.axis_index("dp"), lax.axis_index("fsdp")
    here = dp_here * fsdp + fsdp_here
    for owner in range(devices):
        ordered[owner] = gathered[owner].astype(F32)
    samples = ordered.shape[1]
    count = devices * samples
    full = ordered[...].reshape(count, ordered.shape[2])
    prior = full[:, :512].astype(BF16)
    recon = full[:, 512:1024]
    pooled = full[:, 1024:].astype(BF16)
    latent = mm(pooled, w_head[...]).astype(BF16)
    latent_float = latent.astype(F32)
    square = jnp.sum(latent_float * latent_float, axis=1, keepdims=True)
    self_sum, self_mix = pair_kernel(latent, square, latent)
    cross_sum, cross_mix = pair_kernel(latent, square, prior)
    pull = -32.0 / count * ((self_sum - cross_sum) * latent_float - self_mix + cross_mix)
    cotangent = (recon + pull).astype(BF16)
    turned = jnp.transpose(full[:, 1024:]).astype(BF16)
    head_full[...] = mm(turned, cotangent)
    share = grad_head.shape[0]
    start = pl.multiple_of(fsdp_here * share, share)
    grad_head[...] = head_full[pl.ds(start, share), :]

    lane_sample = iota((128, count), 0) // 8 % 4 + samples * here
    pick = jnp.where(lane_sample == iota((128, count), 1), 1.0, 0.0).astype(BF16)
    lanes = mm(pick, cotangent).astype(BF16)
    back_pool = mm_nt(w_head[...], lanes) / 256.0
    back_pool = jnp.concatenate([back_pool, back_pool], axis=1)
    conv_total = None
    for cp in range(4):
        grads[cp] = (back_pool * slope_conv[cp]).astype(BF16)
        term = mm_nt(hidden[cp].reshape(1024, 256), grads[cp])
        conv_total = term if cp == 0 else conv_total + term
    core_zero = lax.rem(dp_here, 2) == 0
    rows = keep.shape[1]
    for f in range(fsdp):
        at = 2 * f * rows
        first, second = conv_total[at : at + rows], conv_total[at + rows : at + 2 * rows]
        keep[f] = jnp.where(core_zero, first, second)
        send[f] = jnp.where(core_zero, second, first)


def embed_kernel(grads, w_conv, slope_embed, one_hot, embed_out):
    embed_total = None
    for cp in range(4):
        for j in range(4):
            back_rows = mm(w_conv[pl.ds(j * 256, 256), :], grads[cp])
            signal = (back_rows * slope_embed[cp, j]).astype(BF16)
            term = mm_nt(one_hot[cp, j], signal)
            embed_total = term if embed_total is None else embed_total + term
    embed = jnp.concatenate(
        [
            embed_total[dx * 128 : dx * 128 + 64, :128] + embed_total[dx * 128 + 64 : dx * 128 + 128, 128:]
            for dx in range(4)
        ],
        axis=0,
    )
    half = embed_out.shape[1]
    for f in range(embed_out.shape[0]):
        for side in range(2):
            at = (2 * f + side) * half
            embed_out[f, :, pl.ds(side * 128, 128)] = embed[at : at + half]


def slope_kernel(pre_embed, pre_conv, slope_embed, slope_conv):
    for cp in range(4):
        for j in range(4):
            slope_embed[cp, j] = silu_slope(pre_embed[cp, j])
        slope_conv[cp] = silu_slope(pre_conv[cp])


def exponent_of(part):
    top = jnp.abs(part)
    while top.ndim > 2:
        top = jnp.max(top, axis=0)
    top = jnp.max(jnp.max(top, axis=0, keepdims=True), axis=1, keepdims=True)
    return jnp.clip(jnp.floor(jnp.log2(jnp.maximum(top, 1e-37))) - 14.0, -124.0, 114.0)


def store_coded(coded, part):
    rows = part.shape[0]
    conv_rows = rows * 4 // 5
    conv, embed = part[:conv_rows], part[conv_rows:]
    steps = exponent_of(conv), exponent_of(embed)
    store_scaled(coded, part, steps)


def store_scaled(coded, part, steps):
    rows, spare = part.shape[0], coded.shape[0] - part.shape[0]
    conv_rows = rows * 4 // 5
    coded[pl.ds(0, conv_rows), :] = part[:conv_rows] * jnp.exp2(-steps[0])
    coded[pl.ds(conv_rows, rows - conv_rows), :] = part[conv_rows:] * jnp.exp2(-steps[1])
    tail = jnp.where(iota((spare, coded.shape[1]), 0) == 0, steps[0], steps[1])
    coded[pl.ds(rows, spare), :] = tail


def load_coded(coded, rows):
    conv_rows = rows * 4 // 5
    conv_scale = jnp.exp2(coded[pl.ds(rows, 1), :])
    embed_scale = jnp.exp2(coded[pl.ds(rows + 1, 1), :])
    return jnp.concatenate(
        [coded[pl.ds(0, conv_rows), :] * conv_scale, coded[pl.ds(conv_rows, rows - conv_rows), :] * embed_scale], axis=0
    )


def scale_kernel(keep, other, embed, own, *coded):
    held = keep[...] + other[...]
    steps = exponent_of(held), exponent_of(embed[...])
    here = lax.axis_index("fsdp")

    def share(z):
        return jnp.concatenate([keep[z] + other[z], embed[z]], axis=0)

    own[...] = share(here)
    for place, target in enumerate(coded):
        store_scaled(target, share(here ^ (len(coded) - place)), steps)


def first_sum_kernel(own, *refs):
    *received, coded = refs
    total = own[...]
    for part in received:
        total = total + load_coded(part, total.shape[0])
    store_coded(coded, total)


def next_sum_kernel(mine, other, total, *coded):
    rows = total.shape[0]
    summed = load_coded(mine, rows) + load_coded(other, rows)
    total[...] = summed
    if coded:
        store_coded(coded[0], summed)


def output_kernel(own, other, grad_embed, grad_conv):
    rows = own.shape[0]
    conv_rows, half = rows * 4 // 5, rows // 5
    core_zero = lax.rem(lax.axis_index("dp"), 2) == 0
    grad_conv[pl.ds(0, conv_rows), :] = jnp.where(core_zero, own[pl.ds(0, conv_rows), :], other[pl.ds(0, conv_rows), :])
    grad_conv[pl.ds(conv_rows, conv_rows), :] = jnp.where(
        core_zero, other[pl.ds(0, conv_rows), :], own[pl.ds(0, conv_rows), :]
    )
    embed = own[pl.ds(conv_rows, half), :] + other[pl.ds(conv_rows, half), :]
    grad_embed[pl.ds(0, half), :] = embed[:, :128]
    grad_embed[pl.ds(half, half), :] = embed[:, 128:]


VMEM = pl.BlockSpec(memory_space=pltpu.VMEM)
HBM = pl.BlockSpec(memory_space=pltpu.HBM)
SAVED = (
    ((4, 4, 512, 256), BF16),
    ((4, 4, 256, 256), F32),
    ((4, 4, 256, 256), BF16),
    ((4, 256, 256), F32),
)


def forward(facies, prior_draws, recon_grad, w_embed, w_conv, w_head):
    samples = facies.shape[0]
    latent_width = prior_draws.shape[1]
    rows, lanes = samples * PATCH_X, PATCH_Y * PATCH_Z
    operands = (facies.reshape(rows, lanes), prior_draws, recon_grad, w_embed, w_conv, w_head)
    return pl.pallas_call(
        forward_kernel,
        out_shape=(pltpu.VMEM((samples, 2 * latent_width + 256), BF16),)
        + tuple(pltpu.VMEM(shape, kind) for shape, kind in SAVED)
        + (pltpu.VMEM(w_conv.shape, BF16), pltpu.VMEM(w_head.shape, BF16)),
        in_specs=[HBM] * 6,
        out_specs=(VMEM,) * 7,
        scratch_shapes=[
            pltpu.VMEM((rows, lanes), jnp.int32),
            pltpu.VMEM(prior_draws.shape, BF16),
            pltpu.VMEM(recon_grad.shape, BF16),
            pltpu.VMEM(w_embed.shape, BF16),
            pltpu.VMEM((256, 512), BF16),
            pltpu.VMEM((rows, lanes), BF16),
            pltpu.SemaphoreType.DMA((9,)),
        ],
        compiler_params=pltpu.CompilerParams(vmem_limit_bytes=30 * 2**20),
        name="forward",
    )(*(pltpu.with_memory_space_constraint(operand, pltpu.HBM) for operand in operands))


def slopes(pre_embed, pre_conv):
    return pl.pallas_call(
        slope_kernel,
        out_shape=(pltpu.VMEM(pre_embed.shape, F32), pltpu.VMEM(pre_conv.shape, F32)),
        in_specs=[VMEM] * 2,
        out_specs=(VMEM,) * 2,
        input_output_aliases={0: 0, 1: 1},
        compiler_params=pltpu.CompilerParams(vmem_limit_bytes=16 * 2**20),
        cost_estimate=pl.CostEstimate(flops=12 * 10**6, bytes_accessed=10 * 2**20, transcendentals=2600000),
        name="slopes",
    )(pre_embed, pre_conv)


def backward(sizes, gathered, hidden, slope_conv, w_head):
    dp, fsdp = sizes
    devices, samples, width = gathered.shape
    payload = pltpu.VMEM((fsdp, 1024 // fsdp // 2, 256), F32)
    return pl.pallas_call(
        lambda *refs: backward_kernel(sizes, *refs),
        out_shape=(
            payload, payload, pltpu.VMEM((4, 256, 256), BF16), jax.ShapeDtypeStruct((256 // fsdp, 512), F32)
        ),
        in_specs=[VMEM] * 4,
        out_specs=(VMEM,) * 4,
        scratch_shapes=[pltpu.VMEM((devices, samples, width), F32), pltpu.VMEM((256, 512), F32)],
        compiler_params=pltpu.CompilerParams(vmem_limit_bytes=24 * 2**20),
        name="backward",
    )(gathered, hidden, slope_conv, w_head)


def embed_gradient(fsdp, grads, w_conv, slope_embed, one_hot):
    return pl.pallas_call(
        embed_kernel,
        out_shape=pltpu.VMEM((fsdp, 256 // fsdp // 2, 256), F32),
        in_specs=[VMEM] * 4,
        out_specs=VMEM,
        compiler_params=pltpu.CompilerParams(vmem_limit_bytes=24 * 2**20),
        cost_estimate=pl.CostEstimate(flops=16 * 10**8, bytes_accessed=10 * 2**20, transcendentals=0),
        name="embed_gradient",
    )(grads, w_conv, slope_embed, one_hot)


def place_of(x, core, z, fsdp):
    return (2 * x + core) * fsdp + z


def exchange(block, dp, fsdp, flip_x, flip_core, flip_z):
    pairs = []
    for x in range(dp // 2):
        for core in range(2):
            for z in range(fsdp):
                pairs.append((place_of(x, core, z, fsdp), place_of(x ^ flip_x, core ^ flip_core, z ^ flip_z, fsdp)))
    return lax.ppermute(block, GROUP, pairs)


def gather_blocks(block, devices):
    copies = jnp.broadcast_to(block[None], (devices,) + block.shape)
    return lax.all_to_all(copies, GROUP, 0, 0, tiled=True)


def local_kernel(kernel, outs, name, *operands):
    return pl.pallas_call(
        kernel,
        out_shape=outs,
        in_specs=[VMEM] * len(operands),
        out_specs=(VMEM,) * len(outs),
        compiler_params=pltpu.CompilerParams(vmem_limit_bytes=16 * 2**20),
        name=name,
    )(*operands)


def to_half(coded):
    rounded = lax.reduce_precision(coded, exponent_bits=5, mantissa_bits=10)
    return rounded, rounded.astype(jnp.float16)


def reduce_to_owner(keep, other, embed, dp, fsdp):
    rows, width = keep.shape[1] + embed.shape[1], keep.shape[2]
    plain = jax.ShapeDtypeStruct((rows, width), F32)
    scaled = jax.ShapeDtypeStruct((rows + 8, width), F32)
    own, *coded = local_kernel(scale_kernel, (plain,) + (scaled,) * (fsdp - 1), "scale", keep, other, embed)
    received = [
        exchange(to_half(part)[1], dp, fsdp, 0, 0, fsdp - 1 - place).astype(F32) for place, part in enumerate(coded)
    ]
    (coded,) = local_kernel(first_sum_kernel, (scaled,), "sum_z", own, *received)
    flip = 1
    while flip < dp // 2:
        mine, sent = to_half(coded)
        other = exchange(sent, dp, fsdp, flip, 0, 0).astype(F32)
        flip *= 2
        outs = (plain, scaled) if flip < dp // 2 else (plain,)
        total, *rest = local_kernel(next_sum_kernel, outs, "sum_x", mine, other)
        coded = rest[0] if rest else None
    return total, exchange(total, dp, fsdp, 0, 1, 0)


def shards(facies, prior_draws, recon_grad, w_embed, w_conv, w_head):
    dp, fsdp = lax.axis_size("dp"), lax.axis_size("fsdp")
    block, one_hot, pre_embed, hidden, pre_conv, w_conv, w_head = forward(
        facies, prior_draws, recon_grad, w_embed, w_conv, w_head
    )
    gathered = gather_blocks(block, dp * fsdp)
    slope_embed, slope_conv = slopes(pre_embed, pre_conv)
    keep, send, grads, grad_head = backward((dp, fsdp), gathered, hidden, slope_conv, w_head)
    received = exchange(send, dp, fsdp, 0, 1, 0)
    embed = embed_gradient(fsdp, grads, w_conv, slope_embed, one_hot)
    own, other = reduce_to_owner(keep, received, embed, dp, fsdp)
    grad_embed, grad_conv = pl.pallas_call(
        output_kernel,
        out_shape=(
            jax.ShapeDtypeStruct((256 // fsdp, 128), F32),
            jax.ShapeDtypeStruct((1024 // fsdp, 256), F32),
        ),
        in_specs=[VMEM] * 2,
        out_specs=(VMEM,) * 2,
        compiler_params=pltpu.CompilerParams(vmem_limit_bytes=16 * 2**20),
        name="outputs",
    )(own, other)
    return (grad_embed, grad_conv, grad_head)


def solution(mesh):
    return jax.shard_map(
        shards,
        mesh=mesh,
        in_specs=(
            P(("groups", "dp", "fsdp"), None, None),
            P(("groups", "dp", "fsdp"), None),
            P(("groups", "dp", "fsdp"), None),
            P(),
            P(),
            P(),
        ),
        out_specs=(
            P(("groups", "fsdp"), None),
            P(("groups", "fsdp"), None),
            P(("groups", "fsdp"), None),
        ),
        check_vma=False,
    )
```

```python
import jax
import jax.numpy as jnp
from jax import lax
from jax.experimental import pallas as pl
from jax.experimental.pallas import tpu as pltpu
from jax.sharding import PartitionSpec as P

PATCH_X = 64
PATCH_Y = 64
PATCH_Z = 32
LEVELS = 4
GROUP = ("dp", "fsdp")
NT = (((1,), (1,)), ((), ()))
F32 = jnp.float32
BF16 = jnp.bfloat16


def iota(shape, dim):
    return lax.broadcasted_iota(jnp.int32, shape, dim)


def mm(left, right):
    return jnp.dot(left, right, preferred_element_type=F32)


def mm_nt(left, right):
    return lax.dot_general(left, right, NT, preferred_element_type=F32)


def spread_matrix():
    out_row = iota((512, 128), 0)
    lane = iota((512, 128), 1)
    pair, half = out_row // 128, out_row // 64 % 2
    row_dy, row_dz = out_row // 16 % 4, out_row // 4 % 4
    lane_dy, lane_c, lane_dz = lane // 32, lane // 4 % 8, lane % 4
    hit = (row_dy == lane_dy) & (row_dz == lane_dz) & (lane_c == 2 * pair + half)
    return jnp.where(hit, 1.0, 0.0).astype(BF16)


def pair_weights(w_embed):
    turned = jnp.transpose(w_embed.astype(F32)).astype(BF16)
    halves = []
    for half in range(2):
        row = iota((256, 512), 0)
        lane = iota((256, 512), 1)
        hit = (row // 64 == lane // 128) & (row % 64 == lane % 64) & (lane // 64 % 2 == half)
        halves.append(mm(turned, jnp.where(hit, 1.0, 0.0).astype(BF16)))
    return jnp.concatenate(halves, axis=0).astype(BF16)


def sigmoid(value):
    return 1.0 / (1.0 + jnp.exp(-value))


def silu_slope(value):
    gate = sigmoid(value)
    return gate * (1.0 + value * (1.0 - gate))


def forward_kernel(
    facies_hbm, prior_hbm, recon_hbm, w_embed_hbm, w_conv_hbm, w_head_hbm,
    block, one_hot, pre_embed, hidden, pre_conv, w_conv, w_head,
    facies, prior, recon, w_embed, packed, sorted_rows, sem
):
    parts = 4
    width = facies.shape[1] // parts
    loads = [
        pltpu.make_async_copy(
            facies_hbm.at[:, pl.ds(i * width, width)], facies.at[:, pl.ds(i * width, width)], sem.at[i]
        )
        for i in range(parts)
    ]
    for source, target in (
        (w_embed_hbm, w_embed), (w_conv_hbm, w_conv), (prior_hbm, prior), (recon_hbm, recon), (w_head_hbm, w_head)
    ):
        loads.append(pltpu.make_async_copy(source, target, sem.at[len(loads)]))
    for load in loads:
        load.start()
    row, lane = iota((256, 256), 0), iota((256, 256), 1)
    order = jnp.where((row // 32 == lane % 8) & (row % 32 == lane // 8), 1.0, 0.0).astype(BF16)
    spread = spread_matrix()
    level = (iota((512, 256), 0) % 4).astype(F32)
    for i in range(parts):
        loads[i].wait()
        part = facies[:, pl.ds(i * width, width)].astype(F32).astype(BF16)
        sorted_rows[:, pl.ds(i * width, width)] = mm(order, part).astype(BF16)
    for t in range(8):
        for dy2 in range(2):
            j, dx = 2 * (t // 4) + dy2, t % 4
            rows = [sorted_rows[pl.ds(t * 32, 32), pl.ds((2 * b2 + dy2) * 128, 128)] for b2 in range(8)]
            copied = mm_nt(spread, jnp.concatenate(rows, axis=0))
            hot = jnp.where(copied == level, 1.0, 0.0).astype(BF16)
            for cp in range(4):
                one_hot[cp, j, pl.ds(dx * 128, 128), :] = hot[cp * 128 : (cp + 1) * 128]
    loads[4].wait()
    packed[...] = pair_weights(w_embed[...])
    loads[5].wait()
    conv_turned = jnp.transpose(w_conv[...].astype(F32)).astype(BF16)
    sums = jnp.zeros((256, 128), F32)
    for cp in range(4):
        for j in range(4):
            pre = mm(packed[...], one_hot[cp, j])
            pre_embed[cp, j] = pre
            hidden[cp, j] = (pre * sigmoid(pre)).astype(BF16)
        pre = mm(conv_turned, hidden[cp].reshape(1024, 256))
        pre_conv[cp] = pre
        act = pre * sigmoid(pre)
        sums = sums + act[:, :128] + act[:, 128:]
    pick = jnp.where(iota((8, 128), 1) // 8 % 4 == iota((8, 128), 0), 1.0, 0.0)
    total = lax.dot_general(pick, sums, NT, precision=lax.Precision.HIGHEST, preferred_element_type=F32)
    for load in loads[6:]:
        load.wait()
    block[:, pl.ds(0, 512)] = prior[...]
    block[:, pl.ds(512, 512)] = recon[...]
    block[:, pl.ds(1024, 256)] = (total[:4] / 256.0).astype(BF16)


def pair_kernel(queries, query_square, keys):
    inner = mm_nt(queries, keys)
    key_float = keys.astype(F32)
    count = keys.shape[0]
    key_square = jnp.sum(key_float * key_float, axis=1, keepdims=True)
    key_row = jnp.transpose(jnp.broadcast_to(key_square, (count, 128)))[:1]
    kern = jnp.exp(-(query_square + key_row - 2.0 * inner) / keys.shape[1])
    return jnp.sum(kern, axis=1, keepdims=True), mm(kern.astype(BF16), keys)


def backward_kernel(
    sizes, gathered, hidden, pre_conv, w_head,
    keep, send, grads, grad_head,
    ordered, head_full
):
    dp, fsdp = sizes
    devices = dp * fsdp
    dp_here, fsdp_here = lax.axis_index("dp"), lax.axis_index("fsdp")
    here = dp_here * fsdp + fsdp_here
    for place in range(devices):
        core_flip, x_flip, z_flip = place // (devices // 2), place // fsdp % (dp // 2), place % fsdp
        owner = (dp_here ^ (2 * x_flip + core_flip)) * fsdp + (fsdp_here ^ z_flip)
        ordered[owner] = gathered[place].astype(F32)
    samples = ordered.shape[1]
    count = devices * samples
    full = ordered[...].reshape(count, ordered.shape[2])
    prior = full[:, :512].astype(BF16)
    recon = full[:, 512:1024]
    pooled = full[:, 1024:].astype(BF16)
    latent = mm(pooled, w_head[...]).astype(BF16)
    latent_float = latent.astype(F32)
    square = jnp.sum(latent_float * latent_float, axis=1, keepdims=True)
    self_sum, self_mix = pair_kernel(latent, square, latent)
    cross_sum, cross_mix = pair_kernel(latent, square, prior)
    pull = -32.0 / count * ((self_sum - cross_sum) * latent_float - self_mix + cross_mix)
    cotangent = (recon + pull).astype(BF16)
    turned = jnp.transpose(full[:, 1024:]).astype(BF16)
    head_full[...] = mm(turned, cotangent)
    share = grad_head.shape[0]
    start = pl.multiple_of(fsdp_here * share, share)
    grad_head[...] = head_full[pl.ds(start, share), :]

    lane_sample = iota((128, count), 0) // 8 % 4 + samples * here
    pick = jnp.where(lane_sample == iota((128, count), 1), 1.0, 0.0).astype(BF16)
    lanes = mm(pick, cotangent).astype(BF16)
    back_pool = mm_nt(w_head[...], lanes) / 256.0
    back_pool = jnp.concatenate([back_pool, back_pool], axis=1)
    conv_total = None
    for cp in range(4):
        grads[cp] = (back_pool * silu_slope(pre_conv[cp])).astype(BF16)
        term = mm_nt(hidden[cp].reshape(1024, 256), grads[cp])
        conv_total = term if cp == 0 else conv_total + term
    core_zero = lax.rem(dp_here, 2) == 0
    rows = keep.shape[1]
    for f in range(fsdp):
        at = 2 * f * rows
        first, second = conv_total[at : at + rows], conv_total[at + rows : at + 2 * rows]
        keep[f] = jnp.where(core_zero, first, second)
        send[f] = jnp.where(core_zero, second, first)


def embed_kernel(grads, w_conv, pre_embed, one_hot, embed_out):
    embed_total = None
    for cp in range(4):
        for j in range(4):
            back_rows = mm(w_conv[pl.ds(j * 256, 256), :], grads[cp])
            signal = (back_rows * silu_slope(pre_embed[cp, j])).astype(BF16)
            term = mm_nt(one_hot[cp, j], signal)
            embed_total = term if embed_total is None else embed_total + term
    embed = jnp.concatenate(
        [
            embed_total[dx * 128 : dx * 128 + 64, :128] + embed_total[dx * 128 + 64 : dx * 128 + 128, 128:]
            for dx in range(4)
        ],
        axis=0,
    )
    half = embed_out.shape[1]
    for f in range(embed_out.shape[0]):
        for side in range(2):
            at = (2 * f + side) * half
            embed_out[f, :, pl.ds(side * 128, 128)] = embed[at : at + half]


def exponent_of(part):
    top = jnp.abs(part)
    while top.ndim > 2:
        top = jnp.max(top, axis=0)
    top = jnp.max(jnp.max(top, axis=0, keepdims=True), axis=1, keepdims=True)
    return jnp.clip(jnp.floor(jnp.log2(jnp.maximum(top, 1e-37))) - 14.0, -124.0, 114.0)


def store_coded(coded, part):
    rows = part.shape[0]
    conv_rows = rows * 4 // 5
    conv, embed = part[:conv_rows], part[conv_rows:]
    steps = exponent_of(conv), exponent_of(embed)
    store_scaled(coded, part, steps)


def store_scaled(coded, part, steps):
    rows, spare = part.shape[0], coded.shape[0] - part.shape[0]
    conv_rows = rows * 4 // 5
    coded[pl.ds(0, conv_rows), :] = part[:conv_rows] * jnp.exp2(-steps[0])
    coded[pl.ds(conv_rows, rows - conv_rows), :] = part[conv_rows:] * jnp.exp2(-steps[1])
    tail = jnp.where(iota((spare, coded.shape[1]), 0) == 0, steps[0], steps[1])
    coded[pl.ds(rows, spare), :] = tail


def load_coded(coded, rows):
    conv_rows = rows * 4 // 5
    conv_scale = jnp.exp2(coded[pl.ds(rows, 1), :])
    embed_scale = jnp.exp2(coded[pl.ds(rows + 1, 1), :])
    return jnp.concatenate(
        [coded[pl.ds(0, conv_rows), :] * conv_scale, coded[pl.ds(conv_rows, rows - conv_rows), :] * embed_scale], axis=0
    )


def scale_kernel(keep, other, embed, own, *coded):
    held = keep[...] + other[...]
    steps = exponent_of(held), exponent_of(embed[...])
    here = lax.axis_index("fsdp")

    def share(z):
        return jnp.concatenate([keep[z] + other[z], embed[z]], axis=0)

    own[...] = share(here)
    for place, target in enumerate(coded):
        store_scaled(target, share(here ^ (place + 1)), steps)


def first_sum_kernel(own, *refs):
    *received, coded = refs
    total = own[...]
    for part in received:
        total = total + load_coded(part, total.shape[0])
    store_coded(coded, total)


def next_sum_kernel(mine, other, total, *coded):
    rows = total.shape[0]
    summed = load_coded(mine, rows) + load_coded(other, rows)
    total[...] = summed
    if coded:
        store_coded(coded[0], summed)


def output_kernel(own, other, grad_embed, grad_conv):
    rows = own.shape[0]
    conv_rows, half = rows * 4 // 5, rows // 5
    core_zero = lax.rem(lax.axis_index("dp"), 2) == 0
    grad_conv[pl.ds(0, conv_rows), :] = jnp.where(core_zero, own[pl.ds(0, conv_rows), :], other[pl.ds(0, conv_rows), :])
    grad_conv[pl.ds(conv_rows, conv_rows), :] = jnp.where(
        core_zero, other[pl.ds(0, conv_rows), :], own[pl.ds(0, conv_rows), :]
    )
    embed = own[pl.ds(conv_rows, half), :] + other[pl.ds(conv_rows, half), :]
    grad_embed[pl.ds(0, half), :] = embed[:, :128]
    grad_embed[pl.ds(half, half), :] = embed[:, 128:]


VMEM = pl.BlockSpec(memory_space=pltpu.VMEM)
HBM = pl.BlockSpec(memory_space=pltpu.HBM)
SAVED = (
    ((4, 4, 512, 256), BF16),
    ((4, 4, 256, 256), F32),
    ((4, 4, 256, 256), BF16),
    ((4, 256, 256), F32),
)


def forward(facies, prior_draws, recon_grad, w_embed, w_conv, w_head):
    samples = facies.shape[0]
    latent_width = prior_draws.shape[1]
    rows, lanes = samples * PATCH_X, PATCH_Y * PATCH_Z
    operands = (facies.reshape(rows, lanes), prior_draws, recon_grad, w_embed, w_conv, w_head)
    return pl.pallas_call(
        forward_kernel,
        out_shape=(pltpu.VMEM((samples, 2 * latent_width + 256), BF16),)
        + tuple(pltpu.VMEM(shape, kind) for shape, kind in SAVED)
        + (pltpu.VMEM(w_conv.shape, BF16), pltpu.VMEM(w_head.shape, BF16)),
        in_specs=[HBM] * 6,
        out_specs=(VMEM,) * 7,
        scratch_shapes=[
            pltpu.VMEM((rows, lanes), jnp.int32),
            pltpu.VMEM(prior_draws.shape, BF16),
            pltpu.VMEM(recon_grad.shape, BF16),
            pltpu.VMEM(w_embed.shape, BF16),
            pltpu.VMEM((256, 512), BF16),
            pltpu.VMEM((rows, lanes), BF16),
            pltpu.SemaphoreType.DMA((9,)),
        ],
        compiler_params=pltpu.CompilerParams(vmem_limit_bytes=30 * 2**20),
        name="forward",
    )(*(pltpu.with_memory_space_constraint(operand, pltpu.HBM) for operand in operands))


def backward(sizes, gathered, hidden, pre_conv, w_head):
    dp, fsdp = sizes
    devices, samples, width = gathered.shape
    payload = pltpu.VMEM((fsdp, 1024 // fsdp // 2, 256), F32)
    return pl.pallas_call(
        lambda *refs: backward_kernel(sizes, *refs),
        out_shape=(
            payload, payload, pltpu.VMEM((4, 256, 256), BF16), jax.ShapeDtypeStruct((256 // fsdp, 512), F32)
        ),
        in_specs=[VMEM] * 4,
        out_specs=(VMEM,) * 4,
        scratch_shapes=[pltpu.VMEM((devices, samples, width), F32), pltpu.VMEM((256, 512), F32)],
        compiler_params=pltpu.CompilerParams(vmem_limit_bytes=24 * 2**20),
        name="backward",
    )(gathered, hidden, pre_conv, w_head)


def embed_gradient(fsdp, grads, w_conv, pre_embed, one_hot):
    return pl.pallas_call(
        embed_kernel,
        out_shape=pltpu.VMEM((fsdp, 256 // fsdp // 2, 256), F32),
        in_specs=[VMEM] * 4,
        out_specs=VMEM,
        compiler_params=pltpu.CompilerParams(vmem_limit_bytes=24 * 2**20),
        cost_estimate=pl.CostEstimate(flops=16 * 10**8, bytes_accessed=10 * 2**20, transcendentals=0),
        name="embed_gradient",
    )(grads, w_conv, pre_embed, one_hot)


def place_of(x, core, z, fsdp):
    return (2 * x + core) * fsdp + z


def exchange(block, dp, fsdp, flip_x, flip_core, flip_z):
    pairs = []
    for x in range(dp // 2):
        for core in range(2):
            for z in range(fsdp):
                pairs.append((place_of(x, core, z, fsdp), place_of(x ^ flip_x, core ^ flip_core, z ^ flip_z, fsdp)))
    return lax.ppermute(block, GROUP, pairs)


def gather_blocks(block, dp, fsdp):
    blocks = [block] + [exchange(block, dp, fsdp, 0, 0, flip) for flip in range(1, fsdp)]
    stacked = jnp.stack(blocks)
    flip = 1
    while flip < dp // 2:
        stacked = jnp.concatenate([stacked, exchange(stacked, dp, fsdp, flip, 0, 0)], axis=0)
        flip *= 2
    return jnp.concatenate([stacked, exchange(stacked, dp, fsdp, 0, 1, 0)], axis=0)


def local_kernel(kernel, outs, name, *operands):
    return pl.pallas_call(
        kernel,
        out_shape=outs,
        in_specs=[VMEM] * len(operands),
        out_specs=(VMEM,) * len(outs),
        compiler_params=pltpu.CompilerParams(vmem_limit_bytes=16 * 2**20),
        name=name,
    )(*operands)


def to_half(coded):
    rounded = lax.reduce_precision(coded, exponent_bits=5, mantissa_bits=10)
    return rounded, rounded.astype(jnp.float16)


def reduce_to_owner(keep, other, embed, dp, fsdp):
    rows, width = keep.shape[1] + embed.shape[1], keep.shape[2]
    plain = jax.ShapeDtypeStruct((rows, width), F32)
    scaled = jax.ShapeDtypeStruct((rows + 8, width), F32)
    own, *coded = local_kernel(scale_kernel, (plain,) + (scaled,) * (fsdp - 1), "scale", keep, other, embed)
    received = [
        exchange(to_half(part)[1], dp, fsdp, 0, 0, place + 1).astype(F32) for place, part in enumerate(coded)
    ]
    (coded,) = local_kernel(first_sum_kernel, (scaled,), "sum_z", own, *received)
    flip = 1
    while flip < dp // 2:
        mine, sent = to_half(coded)
        other = exchange(sent, dp, fsdp, flip, 0, 0).astype(F32)
        flip *= 2
        outs = (plain, scaled) if flip < dp // 2 else (plain,)
        total, *rest = local_kernel(next_sum_kernel, outs, "sum_x", mine, other)
        coded = rest[0] if rest else None
    return total, exchange(total, dp, fsdp, 0, 1, 0)


def shards(facies, prior_draws, recon_grad, w_embed, w_conv, w_head):
    dp, fsdp = lax.axis_size("dp"), lax.axis_size("fsdp")
    block, one_hot, pre_embed, hidden, pre_conv, w_conv, w_head = forward(
        facies, prior_draws, recon_grad, w_embed, w_conv, w_head
    )
    gathered = gather_blocks(block, dp, fsdp)
    keep, send, grads, grad_head = backward((dp, fsdp), gathered, hidden, pre_conv, w_head)
    received = exchange(send, dp, fsdp, 0, 1, 0)
    embed = embed_gradient(fsdp, grads, w_conv, pre_embed, one_hot)
    own, other = reduce_to_owner(keep, received, embed, dp, fsdp)
    grad_embed, grad_conv = pl.pallas_call(
        output_kernel,
        out_shape=(
            jax.ShapeDtypeStruct((256 // fsdp, 128), F32),
            jax.ShapeDtypeStruct((1024 // fsdp, 256), F32),
        ),
        in_specs=[VMEM] * 2,
        out_specs=(VMEM,) * 2,
        compiler_params=pltpu.CompilerParams(vmem_limit_bytes=16 * 2**20),
        name="outputs",
    )(own, other)
    return (grad_embed, grad_conv, grad_head)


def solution(mesh):
    return jax.shard_map(
        shards,
        mesh=mesh,
        in_specs=(
            P(("groups", "dp", "fsdp"), None, None),
            P(("groups", "dp", "fsdp"), None),
            P(("groups", "dp", "fsdp"), None),
            P(),
            P(),
            P(),
        ),
        out_specs=(
            P(("groups", "fsdp"), None),
            P(("groups", "fsdp"), None),
            P(("groups", "fsdp"), None),
        ),
        check_vma=False,
    )
```

```python
import jax
import jax.numpy as jnp
from jax import lax
from jax.experimental import pallas as pl
from jax.experimental.pallas import tpu as pltpu
from jax.sharding import PartitionSpec as P

PATCH_X = 64
PATCH_Y = 64
PATCH_Z = 32
LEVELS = 4
GROUP = ("dp", "fsdp")
NT = (((1,), (1,)), ((), ()))
F32 = jnp.float32
BF16 = jnp.bfloat16


def iota(shape, dim):
    return lax.broadcasted_iota(jnp.int32, shape, dim)


def mm(left, right):
    return jnp.dot(left, right, preferred_element_type=F32)


def mm_nt(left, right):
    return lax.dot_general(left, right, NT, preferred_element_type=F32)


def spread_matrix():
    out_row = iota((512, 128), 0)
    lane = iota((512, 128), 1)
    pair, half = out_row // 128, out_row // 64 % 2
    row_dy, row_dz = out_row // 16 % 4, out_row // 4 % 4
    lane_dy, lane_c, lane_dz = lane // 32, lane // 4 % 8, lane % 4
    hit = (row_dy == lane_dy) & (row_dz == lane_dz) & (lane_c == 2 * pair + half)
    return jnp.where(hit, 1.0, 0.0).astype(BF16)


def pair_weights(w_embed):
    turned = jnp.transpose(w_embed.astype(F32)).astype(BF16)
    halves = []
    for half in range(2):
        row = iota((256, 512), 0)
        lane = iota((256, 512), 1)
        hit = (row // 64 == lane // 128) & (row % 64 == lane % 64) & (lane // 64 % 2 == half)
        halves.append(mm(turned, jnp.where(hit, 1.0, 0.0).astype(BF16)))
    return jnp.concatenate(halves, axis=0).astype(BF16)


def sigmoid(value):
    return 1.0 / (1.0 + jnp.exp(-value))


def silu_slope(value):
    gate = sigmoid(value)
    return gate * (1.0 + value * (1.0 - gate))


def forward_kernel(
    facies_hbm, prior_hbm, recon_hbm, w_embed_hbm, w_conv_hbm, w_head_hbm,
    block, one_hot, pre_embed, hidden, pre_conv, w_conv, w_head,
    facies, prior, recon, w_embed, packed, sorted_rows, sem
):
    width = facies.shape[1] // 2
    halves = [pl.ds(half * width, width) for half in range(2)]
    loads = [pltpu.make_async_copy(facies_hbm.at[:, at], facies.at[:, at], sem.at[i]) for i, at in enumerate(halves)]
    for load in loads:
        load.start()
    for source, target in (
        (w_embed_hbm, w_embed), (w_conv_hbm, w_conv), (prior_hbm, prior), (recon_hbm, recon), (w_head_hbm, w_head)
    ):
        loads.append(pltpu.make_async_copy(source, target, sem.at[len(loads)]))
    row, lane = iota((256, 256), 0), iota((256, 256), 1)
    order = jnp.where((row // 32 == lane % 8) & (row % 32 == lane // 8), 1.0, 0.0).astype(BF16)
    spread = spread_matrix()
    level = (iota((512, 256), 0) % 4).astype(F32)
    for half in range(2):
        loads[half].wait()
        if half == 0:
            for load in loads[2:]:
                load.start()
        for at in range(half * width, half * width + width, 512):
            part = facies[:, pl.ds(at, 512)].astype(F32).astype(BF16)
            sorted_rows[:, pl.ds(at, 512)] = mm(order, part).astype(BF16)
        for t in range(8):
            dx2, dx = t // 4, t % 4
            rows = [
                sorted_rows[pl.ds(t * 32, 32), pl.ds((2 * b2 + dy2) * 128, 128)]
                for dy2 in range(2)
                for b2 in range(4 * half, 4 * half + 4)
            ]
            copied = mm_nt(spread, jnp.concatenate(rows, axis=0))
            hot = jnp.where(copied == level, 1.0, 0.0).astype(BF16)
            for cp in range(4):
                for dy2 in range(2):
                    one_hot[cp, pl.ds(dx * 128, 128), pl.ds((2 * dx2 + dy2) * 256 + half * 128, 128)] = hot[
                        cp * 128 : cp * 128 + 128, dy2 * 128 : dy2 * 128 + 128
                    ]
    loads[2].wait()
    packed[...] = pair_weights(w_embed[...])
    loads[3].wait()
    conv_turned = jnp.transpose(w_conv[...].astype(F32)).astype(BF16)
    sums = jnp.zeros((256, 128), F32)
    for cp in range(4):
        for dx2 in range(2):
            at = pl.ds(dx2 * 512, 512)
            pre = mm(packed[...], one_hot[cp, :, at])
            pre_embed[cp, :, at] = pre
            act = (pre * sigmoid(pre)).astype(BF16)
            hidden[cp, 2 * dx2] = act[:, :256]
            hidden[cp, 2 * dx2 + 1] = act[:, 256:]
        pre = mm(conv_turned, hidden[cp].reshape(1024, 256))
        pre_conv[cp] = pre
        act = pre * sigmoid(pre)
        sums = sums + act[:, :128] + act[:, 128:]
    pick = jnp.where(iota((8, 128), 1) // 8 % 4 == iota((8, 128), 0), 1.0, 0.0)
    total = lax.dot_general(pick, sums, NT, precision=lax.Precision.HIGHEST, preferred_element_type=F32)
    for load in loads[4:]:
        load.wait()
    block[:, pl.ds(0, 512)] = prior[...]
    block[:, pl.ds(512, 512)] = recon[...]
    block[:, pl.ds(1024, 256)] = (total[:4] / 256.0).astype(BF16)


def pair_kernel(queries, query_square, keys):
    inner = mm_nt(queries, keys)
    key_float = keys.astype(F32)
    count = keys.shape[0]
    key_square = jnp.sum(key_float * key_float, axis=1, keepdims=True)
    key_row = jnp.transpose(jnp.broadcast_to(key_square, (count, 128)))[:1]
    kern = jnp.exp(-(query_square + key_row - 2.0 * inner) / keys.shape[1])
    return jnp.sum(kern, axis=1, keepdims=True), mm(kern.astype(BF16), keys)


def backward_kernel(
    sizes, gathered, hidden, pre_conv, w_head,
    keep, send, grads, grad_head,
    ordered, head_full
):
    dp, fsdp = sizes
    devices = dp * fsdp
    dp_here, fsdp_here = lax.axis_index("dp"), lax.axis_index("fsdp")
    here = dp_here * fsdp + fsdp_here
    for owner in range(devices):
        ordered[owner] = gathered[owner].astype(F32)
    samples = ordered.shape[1]
    count = devices * samples
    full = ordered[...].reshape(count, ordered.shape[2])
    prior = full[:, :512].astype(BF16)
    recon = full[:, 512:1024]
    pooled = full[:, 1024:].astype(BF16)
    latent = mm(pooled, w_head[...]).astype(BF16)
    latent_float = latent.astype(F32)
    square = jnp.sum(latent_float * latent_float, axis=1, keepdims=True)
    self_sum, self_mix = pair_kernel(latent, square, latent)
    cross_sum, cross_mix = pair_kernel(latent, square, prior)
    pull = -32.0 / count * ((self_sum - cross_sum) * latent_float - self_mix + cross_mix)
    cotangent = (recon + pull).astype(BF16)
    turned = jnp.transpose(full[:, 1024:]).astype(BF16)
    head_full[...] = mm(turned, cotangent)
    share = grad_head.shape[0]
    start = pl.multiple_of(fsdp_here * share, share)
    grad_head[...] = head_full[pl.ds(start, share), :]

    lane_sample = iota((128, count), 0) // 8 % 4 + samples * here
    pick = jnp.where(lane_sample == iota((128, count), 1), 1.0, 0.0).astype(BF16)
    lanes = mm(pick, cotangent).astype(BF16)
    back_pool = mm_nt(w_head[...], lanes) / 256.0
    back_pool = jnp.concatenate([back_pool, back_pool], axis=1)
    conv_total = None
    for cp in range(4):
        grads[cp] = (back_pool * silu_slope(pre_conv[cp])).astype(BF16)
        term = mm_nt(hidden[cp].reshape(1024, 256), grads[cp])
        conv_total = term if cp == 0 else conv_total + term
    core_zero = lax.rem(dp_here, 2) == 0
    rows = keep.shape[1]
    for f in range(fsdp):
        at = 2 * f * rows
        first, second = conv_total[at : at + rows], conv_total[at + rows : at + 2 * rows]
        keep[f] = jnp.where(core_zero, first, second)
        send[f] = jnp.where(core_zero, second, first)


def embed_kernel(grads, w_conv, pre_embed, one_hot, embed_out):
    embed_total = None
    for cp in range(4):
        signals = []
        for dx2 in range(2):
            back_rows = mm(w_conv[pl.ds(dx2 * 512, 512), :], grads[cp])
            back_rows = jnp.concatenate([back_rows[:256], back_rows[256:]], axis=1)
            signals.append((back_rows * silu_slope(pre_embed[cp, :, pl.ds(dx2 * 512, 512)])).astype(BF16))
        term = mm_nt(one_hot[cp], jnp.concatenate(signals, axis=1))
        embed_total = term if cp == 0 else embed_total + term
    embed = jnp.concatenate(
        [
            embed_total[dx * 128 : dx * 128 + 64, :128] + embed_total[dx * 128 + 64 : dx * 128 + 128, 128:]
            for dx in range(4)
        ],
        axis=0,
    )
    half = embed_out.shape[1]
    for f in range(embed_out.shape[0]):
        for side in range(2):
            at = (2 * f + side) * half
            embed_out[f, :, pl.ds(side * 128, 128)] = embed[at : at + half]


def exponent_of(part):
    top = jnp.abs(part)
    while top.ndim > 2:
        top = jnp.max(top, axis=0)
    top = jnp.max(jnp.max(top, axis=0, keepdims=True), axis=1, keepdims=True)
    return jnp.clip(jnp.floor(jnp.log2(jnp.maximum(top, 1e-37))) - 14.0, -124.0, 114.0)


def store_coded(coded, part):
    rows = part.shape[0]
    conv_rows = rows * 4 // 5
    conv, embed = part[:conv_rows], part[conv_rows:]
    steps = exponent_of(conv), exponent_of(embed)
    store_scaled(coded, part, steps)


def store_scaled(coded, part, steps):
    rows, spare = part.shape[0], coded.shape[0] - part.shape[0]
    conv_rows = rows * 4 // 5
    coded[pl.ds(0, conv_rows), :] = part[:conv_rows] * jnp.exp2(-steps[0])
    coded[pl.ds(conv_rows, rows - conv_rows), :] = part[conv_rows:] * jnp.exp2(-steps[1])
    tail = jnp.where(iota((spare, coded.shape[1]), 0) == 0, steps[0], steps[1])
    coded[pl.ds(rows, spare), :] = tail


def load_coded(coded, rows):
    conv_rows = rows * 4 // 5
    conv_scale = jnp.exp2(coded[pl.ds(rows, 1), :])
    embed_scale = jnp.exp2(coded[pl.ds(rows + 1, 1), :])
    return jnp.concatenate(
        [coded[pl.ds(0, conv_rows), :] * conv_scale, coded[pl.ds(conv_rows, rows - conv_rows), :] * embed_scale], axis=0
    )


def scale_kernel(keep, other, embed, own, *coded):
    held = keep[...] + other[...]
    steps = exponent_of(held), exponent_of(embed[...])
    here = lax.axis_index("fsdp")

    def share(z):
        return jnp.concatenate([keep[z] + other[z], embed[z]], axis=0)

    own[...] = share(here)
    for place, target in enumerate(coded):
        store_scaled(target, share(here ^ (place + 1)), steps)


def first_sum_kernel(own, *refs):
    *received, coded = refs
    total = own[...]
    for part in received:
        total = total + load_coded(part, total.shape[0])
    store_coded(coded, total)


def next_sum_kernel(mine, other, total, *coded):
    rows = total.shape[0]
    summed = load_coded(mine, rows) + load_coded(other, rows)
    total[...] = summed
    if coded:
        store_coded(coded[0], summed)


def output_kernel(own, other, grad_embed, grad_conv):
    rows = own.shape[0]
    conv_rows, half = rows * 4 // 5, rows // 5
    core_zero = lax.rem(lax.axis_index("dp"), 2) == 0
    grad_conv[pl.ds(0, conv_rows), :] = jnp.where(core_zero, own[pl.ds(0, conv_rows), :], other[pl.ds(0, conv_rows), :])
    grad_conv[pl.ds(conv_rows, conv_rows), :] = jnp.where(
        core_zero, other[pl.ds(0, conv_rows), :], own[pl.ds(0, conv_rows), :]
    )
    embed = own[pl.ds(conv_rows, half), :] + other[pl.ds(conv_rows, half), :]
    grad_embed[pl.ds(0, half), :] = embed[:, :128]
    grad_embed[pl.ds(half, half), :] = embed[:, 128:]


VMEM = pl.BlockSpec(memory_space=pltpu.VMEM)
HBM = pl.BlockSpec(memory_space=pltpu.HBM)
SAVED = (
    ((4, 512, 1024), BF16),
    ((4, 256, 1024), F32),
    ((4, 4, 256, 256), BF16),
    ((4, 256, 256), F32),
)


def forward(facies, prior_draws, recon_grad, w_embed, w_conv, w_head):
    samples = facies.shape[0]
    latent_width = prior_draws.shape[1]
    rows, lanes = samples * PATCH_X, PATCH_Y * PATCH_Z
    operands = (facies.reshape(rows, lanes), prior_draws, recon_grad, w_embed, w_conv, w_head)
    return pl.pallas_call(
        forward_kernel,
        out_shape=(pltpu.VMEM((samples, 2 * latent_width + 256), BF16),)
        + tuple(pltpu.VMEM(shape, kind) for shape, kind in SAVED)
        + (pltpu.VMEM(w_conv.shape, BF16), pltpu.VMEM(w_head.shape, BF16)),
        in_specs=[HBM] * 6,
        out_specs=(VMEM,) * 7,
        scratch_shapes=[
            pltpu.VMEM((rows, lanes), jnp.int32),
            pltpu.VMEM(prior_draws.shape, BF16),
            pltpu.VMEM(recon_grad.shape, BF16),
            pltpu.VMEM(w_embed.shape, BF16),
            pltpu.VMEM((256, 512), BF16),
            pltpu.VMEM((rows, lanes), BF16),
            pltpu.SemaphoreType.DMA((7,)),
        ],
        compiler_params=pltpu.CompilerParams(vmem_limit_bytes=30 * 2**20),
        name="forward",
    )(*(pltpu.with_memory_space_constraint(operand, pltpu.HBM) for operand in operands))


def backward(sizes, gathered, hidden, pre_conv, w_head):
    dp, fsdp = sizes
    devices, samples, width = gathered.shape
    payload = pltpu.VMEM((fsdp, 1024 // fsdp // 2, 256), F32)
    return pl.pallas_call(
        lambda *refs: backward_kernel(sizes, *refs),
        out_shape=(
            payload, payload, pltpu.VMEM((4, 256, 256), BF16), jax.ShapeDtypeStruct((256 // fsdp, 512), F32)
        ),
        in_specs=[VMEM] * 4,
        out_specs=(VMEM,) * 4,
        scratch_shapes=[pltpu.VMEM((devices, samples, width), F32), pltpu.VMEM((256, 512), F32)],
        compiler_params=pltpu.CompilerParams(vmem_limit_bytes=24 * 2**20),
        name="backward",
    )(gathered, hidden, pre_conv, w_head)


def embed_gradient(fsdp, grads, w_conv, pre_embed, one_hot):
    return pl.pallas_call(
        embed_kernel,
        out_shape=pltpu.VMEM((fsdp, 256 // fsdp // 2, 256), F32),
        in_specs=[VMEM] * 4,
        out_specs=VMEM,
        compiler_params=pltpu.CompilerParams(vmem_limit_bytes=24 * 2**20),
        cost_estimate=pl.CostEstimate(flops=16 * 10**8, bytes_accessed=10 * 2**20, transcendentals=0),
        name="embed_gradient",
    )(grads, w_conv, pre_embed, one_hot)


def place_of(x, core, z, fsdp):
    return (2 * x + core) * fsdp + z


def exchange(block, dp, fsdp, flip_x, flip_core, flip_z):
    pairs = []
    for x in range(dp // 2):
        for core in range(2):
            for z in range(fsdp):
                pairs.append((place_of(x, core, z, fsdp), place_of(x ^ flip_x, core ^ flip_core, z ^ flip_z, fsdp)))
    return lax.ppermute(block, GROUP, pairs)


def gather_blocks(block, devices):
    copies = jnp.broadcast_to(block[None], (devices,) + block.shape)
    return lax.all_to_all(copies, GROUP, 0, 0, tiled=True)


def local_kernel(kernel, outs, name, *operands):
    return pl.pallas_call(
        kernel,
        out_shape=outs,
        in_specs=[VMEM] * len(operands),
        out_specs=(VMEM,) * len(outs),
        compiler_params=pltpu.CompilerParams(vmem_limit_bytes=16 * 2**20),
        name=name,
    )(*operands)


def to_half(coded):
    rounded = lax.reduce_precision(coded, exponent_bits=5, mantissa_bits=10)
    return rounded, rounded.astype(jnp.float16)


def reduce_to_owner(keep, other, embed, dp, fsdp):
    rows, width = keep.shape[1] + embed.shape[1], keep.shape[2]
    plain = jax.ShapeDtypeStruct((rows, width), F32)
    scaled = jax.ShapeDtypeStruct((rows + 8, width), F32)
    own, *coded = local_kernel(scale_kernel, (plain,) + (scaled,) * (fsdp - 1), "scale", keep, other, embed)
    received = [
        exchange(to_half(part)[1], dp, fsdp, 0, 0, place + 1).astype(F32) for place, part in enumerate(coded)
    ]
    (coded,) = local_kernel(first_sum_kernel, (scaled,), "sum_z", own, *received)
    flip = 1
    while flip < dp // 2:
        mine, sent = to_half(coded)
        other = exchange(sent, dp, fsdp, flip, 0, 0).astype(F32)
        flip *= 2
        outs = (plain, scaled) if flip < dp // 2 else (plain,)
        total, *rest = local_kernel(next_sum_kernel, outs, "sum_x", mine, other)
        coded = rest[0] if rest else None
    return total, exchange(total, dp, fsdp, 0, 1, 0)


def shards(facies, prior_draws, recon_grad, w_embed, w_conv, w_head):
    dp, fsdp = lax.axis_size("dp"), lax.axis_size("fsdp")
    block, one_hot, pre_embed, hidden, pre_conv, w_conv, w_head = forward(
        facies, prior_draws, recon_grad, w_embed, w_conv, w_head
    )
    gathered = gather_blocks(block, dp * fsdp)
    keep, send, grads, grad_head = backward((dp, fsdp), gathered, hidden, pre_conv, w_head)
    received = exchange(send, dp, fsdp, 0, 1, 0)
    embed = embed_gradient(fsdp, grads, w_conv, pre_embed, one_hot)
    own, other = reduce_to_owner(keep, received, embed, dp, fsdp)
    grad_embed, grad_conv = pl.pallas_call(
        output_kernel,
        out_shape=(
            jax.ShapeDtypeStruct((256 // fsdp, 128), F32),
            jax.ShapeDtypeStruct((1024 // fsdp, 256), F32),
        ),
        in_specs=[VMEM] * 2,
        out_specs=(VMEM,) * 2,
        compiler_params=pltpu.CompilerParams(vmem_limit_bytes=16 * 2**20),
        name="outputs",
    )(own, other)
    return (grad_embed, grad_conv, grad_head)


def solution(mesh):
    return jax.shard_map(
        shards,
        mesh=mesh,
        in_specs=(
            P(("groups", "dp", "fsdp"), None, None),
            P(("groups", "dp", "fsdp"), None),
            P(("groups", "dp", "fsdp"), None),
            P(),
            P(),
            P(),
        ),
        out_specs=(
            P(("groups", "fsdp"), None),
            P(("groups", "fsdp"), None),
            P(("groups", "fsdp"), None),
        ),
        check_vma=False,
    )
```

```python
import jax
import jax.numpy as jnp
from jax import lax
from jax.experimental import pallas as pl
from jax.experimental.pallas import tpu as pltpu
from jax.sharding import PartitionSpec as P

PATCH_X = 64
PATCH_Y = 64
PATCH_Z = 32
LEVELS = 4
GROUP = ("dp", "fsdp")
NT = (((1,), (1,)), ((), ()))
F32 = jnp.float32
BF16 = jnp.bfloat16


def iota(shape, dim):
    return lax.broadcasted_iota(jnp.int32, shape, dim)


def mm(left, right):
    return jnp.dot(left, right, preferred_element_type=F32)


def mm_nt(left, right):
    return lax.dot_general(left, right, NT, preferred_element_type=F32)


def spread_matrix():
    out_row = iota((512, 128), 0)
    lane = iota((512, 128), 1)
    pair, half = out_row // 128, out_row // 64 % 2
    row_dy, row_dz = out_row // 16 % 4, out_row // 4 % 4
    lane_dy, lane_c, lane_dz = lane // 32, lane // 4 % 8, lane % 4
    hit = (row_dy == lane_dy) & (row_dz == lane_dz) & (lane_c == 2 * pair + half)
    return jnp.where(hit, 1.0, 0.0).astype(BF16)


def pair_weights(w_embed):
    turned = jnp.transpose(w_embed.astype(F32)).astype(BF16)
    halves = []
    for half in range(2):
        row = iota((256, 512), 0)
        lane = iota((256, 512), 1)
        hit = (row // 64 == lane // 128) & (row % 64 == lane % 64) & (lane // 64 % 2 == half)
        halves.append(mm(turned, jnp.where(hit, 1.0, 0.0).astype(BF16)))
    return jnp.concatenate(halves, axis=0).astype(BF16)


def sigmoid(value):
    return pltpu.reciprocal(1.0 + jnp.exp2(value * -1.4426950408889634), approx=True)


def silu_slope(value):
    gate = sigmoid(value)
    return gate * (1.0 + value * (1.0 - gate))


def forward_kernel(
    facies_hbm, prior_hbm, recon_hbm, w_embed_hbm, w_conv_hbm, w_head_hbm,
    block, one_hot, pre_embed, hidden, pre_conv, w_conv, w_head,
    facies, prior, recon, w_embed, packed, sorted_rows, sem
):
    width = facies.shape[1] // 2
    halves = [pl.ds(half * width, width) for half in range(2)]
    loads = [pltpu.make_async_copy(facies_hbm.at[:, at], facies.at[:, at], sem.at[i]) for i, at in enumerate(halves)]
    for load in loads:
        load.start()
    for source, target in (
        (w_embed_hbm, w_embed), (w_conv_hbm, w_conv), (prior_hbm, prior), (recon_hbm, recon), (w_head_hbm, w_head)
    ):
        loads.append(pltpu.make_async_copy(source, target, sem.at[len(loads)]))
    row, lane = iota((256, 256), 0), iota((256, 256), 1)
    order = jnp.where((row // 32 == lane % 8) & (row % 32 == lane // 8), 1.0, 0.0).astype(BF16)
    spread = spread_matrix()
    level = (iota((512, 256), 0) % 4).astype(F32).astype(BF16)
    for half in range(2):
        loads[half].wait()
        if half == 0:
            for load in loads[2:]:
                load.start()
        for at in range(half * width, half * width + width, 512):
            part = facies[:, pl.ds(at, 512)].astype(F32).astype(BF16)
            sorted_rows[:, pl.ds(at, 512)] = mm(order, part).astype(BF16)
        for t in range(8):
            dx2, dx = t // 4, t % 4
            rows = [
                sorted_rows[pl.ds(t * 32, 32), pl.ds((2 * b2 + dy2) * 128, 128)]
                for dy2 in range(2)
                for b2 in range(4 * half, 4 * half + 4)
            ]
            copied = mm_nt(spread, jnp.concatenate(rows, axis=0))
            hot = jnp.where(copied.astype(BF16) == level, BF16(1.0), BF16(0.0))
            for cp in range(4):
                for dy2 in range(2):
                    one_hot[cp, pl.ds(dx * 128, 128), pl.ds((2 * dx2 + dy2) * 256 + half * 128, 128)] = hot[
                        cp * 128 : cp * 128 + 128, dy2 * 128 : dy2 * 128 + 128
                    ]
    loads[2].wait()
    packed[...] = pair_weights(w_embed[...])
    loads[3].wait()
    conv_turned = jnp.transpose(w_conv[...].astype(F32)).astype(BF16)
    sums = jnp.zeros((256, 128), F32)
    for cp in range(4):
        for dx2 in range(2):
            at = pl.ds(dx2 * 512, 512)
            pre = mm(packed[...], one_hot[cp, :, at])
            pre_embed[cp, :, at] = pre
            act = (pre * sigmoid(pre)).astype(BF16)
            hidden[cp, 2 * dx2] = act[:, :256]
            hidden[cp, 2 * dx2 + 1] = act[:, 256:]
        pre = mm(conv_turned, hidden[cp].reshape(1024, 256))
        pre_conv[cp] = pre
        act = pre * sigmoid(pre)
        sums = sums + act[:, :128] + act[:, 128:]
    pick = jnp.where(iota((8, 128), 1) // 8 % 4 == iota((8, 128), 0), 1.0, 0.0)
    total = lax.dot_general(pick, sums, NT, precision=lax.Precision.HIGHEST, preferred_element_type=F32)
    for load in loads[4:]:
        load.wait()
    block[:, pl.ds(0, 512)] = prior[...]
    block[:, pl.ds(512, 512)] = recon[...]
    block[:, pl.ds(1024, 256)] = (total[:4] / 256.0).astype(BF16)


def pair_kernel(queries, query_square, keys):
    inner = mm_nt(queries, keys)
    key_float = keys.astype(F32)
    count = keys.shape[0]
    key_square = jnp.sum(key_float * key_float, axis=1, keepdims=True)
    key_row = jnp.transpose(jnp.broadcast_to(key_square, (count, 128)))[:1]
    kern = jnp.exp(-(query_square + key_row - 2.0 * inner) / keys.shape[1])
    return jnp.sum(kern, axis=1, keepdims=True), mm(kern.astype(BF16), keys)


def backward_kernel(
    sizes, gathered, hidden, pre_conv, w_head,
    keep, send, grads, grad_head,
    head_full
):
    dp, fsdp = sizes
    devices = dp * fsdp
    dp_here, fsdp_here = lax.axis_index("dp"), lax.axis_index("fsdp")
    here = dp_here * fsdp + fsdp_here
    count = gathered.shape[0]
    samples = count // devices
    prior = gathered[:, pl.ds(0, 512)]
    recon = gathered[:, pl.ds(512, 512)].astype(F32)
    pooled = gathered[:, pl.ds(1024, 256)]
    latent = mm(pooled, w_head[...]).astype(BF16)
    latent_float = latent.astype(F32)
    square = jnp.sum(latent_float * latent_float, axis=1, keepdims=True)
    self_sum, self_mix = pair_kernel(latent, square, latent)
    cross_sum, cross_mix = pair_kernel(latent, square, prior)
    pull = -32.0 / count * ((self_sum - cross_sum) * latent_float - self_mix + cross_mix)
    cotangent = (recon + pull).astype(BF16)
    turned = jnp.transpose(pooled.astype(F32)).astype(BF16)
    head_full[...] = mm(turned, cotangent)
    share = grad_head.shape[0]
    start = pl.multiple_of(fsdp_here * share, share)
    grad_head[...] = head_full[pl.ds(start, share), :]

    lane_sample = iota((128, count), 0) // 8 % 4 + samples * here
    pick = jnp.where(lane_sample == iota((128, count), 1), 1.0, 0.0).astype(BF16)
    lanes = mm(pick, cotangent).astype(BF16)
    back_pool = mm_nt(w_head[...], lanes) / 256.0
    back_pool = jnp.concatenate([back_pool, back_pool], axis=1)
    conv_total = None
    for cp in range(4):
        grads[cp] = (back_pool * silu_slope(pre_conv[cp])).astype(BF16)
        term = mm_nt(hidden[cp].reshape(1024, 256), grads[cp])
        conv_total = term if cp == 0 else conv_total + term
    core_zero = lax.rem(dp_here, 2) == 0
    rows = keep.shape[1]
    for f in range(fsdp):
        at = 2 * f * rows
        first, second = conv_total[at : at + rows], conv_total[at + rows : at + 2 * rows]
        keep[f] = jnp.where(core_zero, first, second)
        send[f] = jnp.where(core_zero, second, first)


def embed_kernel(grads, w_conv, pre_embed, one_hot, embed_out):
    embed_total = None
    for cp in range(4):
        signals = []
        for dx2 in range(2):
            back_rows = mm(w_conv[pl.ds(dx2 * 512, 512), :], grads[cp])
            back_rows = jnp.concatenate([back_rows[:256], back_rows[256:]], axis=1)
            signals.append((back_rows * silu_slope(pre_embed[cp, :, pl.ds(dx2 * 512, 512)])).astype(BF16))
        term = mm_nt(one_hot[cp], jnp.concatenate(signals, axis=1))
        embed_total = term if cp == 0 else embed_total + term
    embed = jnp.concatenate(
        [
            embed_total[dx * 128 : dx * 128 + 64, :128] + embed_total[dx * 128 + 64 : dx * 128 + 128, 128:]
            for dx in range(4)
        ],
        axis=0,
    )
    half = embed_out.shape[1]
    for f in range(embed_out.shape[0]):
        for side in range(2):
            at = (2 * f + side) * half
            embed_out[f, :, pl.ds(side * 128, 128)] = embed[at : at + half]


def exponent_of(part):
    top = jnp.abs(part)
    while top.ndim > 2:
        top = jnp.max(top, axis=0)
    top = jnp.max(jnp.max(top, axis=0, keepdims=True), axis=1, keepdims=True)
    return jnp.clip(jnp.floor(jnp.log2(jnp.maximum(top, 1e-37))) - 14.0, -124.0, 114.0)


def store_coded(coded, part):
    rows = part.shape[0]
    conv_rows = rows * 4 // 5
    conv, embed = part[:conv_rows], part[conv_rows:]
    steps = exponent_of(conv), exponent_of(embed)
    store_scaled(coded, part, steps)


def store_scaled(coded, part, steps):
    rows, spare = part.shape[0], coded.shape[0] - part.shape[0]
    conv_rows = rows * 4 // 5
    coded[pl.ds(0, conv_rows), :] = part[:conv_rows] * jnp.exp2(-steps[0])
    coded[pl.ds(conv_rows, rows - conv_rows), :] = part[conv_rows:] * jnp.exp2(-steps[1])
    tail = jnp.where(iota((spare, coded.shape[1]), 0) == 0, steps[0], steps[1])
    coded[pl.ds(rows, spare), :] = tail


def load_coded(coded, rows):
    conv_rows = rows * 4 // 5
    conv_scale = jnp.exp2(coded[pl.ds(rows, 1), :])
    embed_scale = jnp.exp2(coded[pl.ds(rows + 1, 1), :])
    return jnp.concatenate(
        [coded[pl.ds(0, conv_rows), :] * conv_scale, coded[pl.ds(conv_rows, rows - conv_rows), :] * embed_scale], axis=0
    )


def scale_kernel(keep, other, embed, own, *coded):
    held = keep[...] + other[...]
    steps = exponent_of(held), exponent_of(embed[...])
    here = lax.axis_index("fsdp")

    def share(z):
        return jnp.concatenate([keep[z] + other[z], embed[z]], axis=0)

    own[...] = share(here)
    for place, target in enumerate(coded):
        store_scaled(target, share(here ^ (place + 1)), steps)


def first_sum_kernel(own, *refs):
    *received, coded = refs
    total = own[...]
    for part in received:
        total = total + load_coded(part, total.shape[0])
    store_coded(coded, total)


def next_sum_kernel(mine, other, coded):
    rows = mine.shape[0] - 8
    store_coded(coded, load_coded(mine, rows) + load_coded(other, rows))


def output_kernel(mine, across, sibling, diagonal, grad_embed, grad_conv):
    rows = mine.shape[0] - 8
    conv_rows, half = rows * 4 // 5, rows // 5
    core_zero = lax.rem(lax.axis_index("dp"), 2) == 0
    own = load_coded(mine, rows) + load_coded(across, rows)
    other = load_coded(sibling, rows) + load_coded(diagonal, rows)
    grad_conv[pl.ds(0, conv_rows), :] = jnp.where(core_zero, own[:conv_rows], other[:conv_rows])
    grad_conv[pl.ds(conv_rows, conv_rows), :] = jnp.where(core_zero, other[:conv_rows], own[:conv_rows])
    embed = own[conv_rows:] + other[conv_rows:]
    grad_embed[pl.ds(0, half), :] = embed[:, :128]
    grad_embed[pl.ds(half, half), :] = embed[:, 128:]


VMEM = pl.BlockSpec(memory_space=pltpu.VMEM)
HBM = pl.BlockSpec(memory_space=pltpu.HBM)
SAVED = (
    ((4, 512, 1024), BF16),
    ((4, 256, 1024), F32),
    ((4, 4, 256, 256), BF16),
    ((4, 256, 256), F32),
)


def forward(facies, prior_draws, recon_grad, w_embed, w_conv, w_head):
    samples = facies.shape[0]
    latent_width = prior_draws.shape[1]
    rows, lanes = samples * PATCH_X, PATCH_Y * PATCH_Z
    operands = (facies.reshape(rows, lanes), prior_draws, recon_grad, w_embed, w_conv, w_head)
    return pl.pallas_call(
        forward_kernel,
        out_shape=(pltpu.VMEM((samples, 2 * latent_width + 256), BF16),)
        + tuple(pltpu.VMEM(shape, kind) for shape, kind in SAVED)
        + (pltpu.VMEM(w_conv.shape, BF16), pltpu.VMEM(w_head.shape, BF16)),
        in_specs=[HBM] * 6,
        out_specs=(VMEM,) * 7,
        scratch_shapes=[
            pltpu.VMEM((rows, lanes), jnp.int32),
            pltpu.VMEM(prior_draws.shape, BF16),
            pltpu.VMEM(recon_grad.shape, BF16),
            pltpu.VMEM(w_embed.shape, BF16),
            pltpu.VMEM((256, 512), BF16),
            pltpu.VMEM((rows, lanes), BF16),
            pltpu.SemaphoreType.DMA((7,)),
        ],
        compiler_params=pltpu.CompilerParams(vmem_limit_bytes=30 * 2**20),
        name="forward",
    )(*(pltpu.with_memory_space_constraint(operand, pltpu.HBM) for operand in operands))


def backward(sizes, gathered, hidden, pre_conv, w_head):
    dp, fsdp = sizes
    payload = pltpu.VMEM((fsdp, 1024 // fsdp // 2, 256), F32)
    return pl.pallas_call(
        lambda *refs: backward_kernel(sizes, *refs),
        out_shape=(
            payload, payload, pltpu.VMEM((4, 256, 256), BF16), jax.ShapeDtypeStruct((256 // fsdp, 512), F32)
        ),
        in_specs=[VMEM] * 4,
        out_specs=(VMEM,) * 4,
        scratch_shapes=[pltpu.VMEM((256, 512), F32)],
        compiler_params=pltpu.CompilerParams(vmem_limit_bytes=24 * 2**20),
        name="backward",
    )(gathered, hidden, pre_conv, w_head)


def embed_gradient(fsdp, grads, w_conv, pre_embed, one_hot):
    return pl.pallas_call(
        embed_kernel,
        out_shape=pltpu.VMEM((fsdp, 256 // fsdp // 2, 256), F32),
        in_specs=[VMEM] * 4,
        out_specs=VMEM,
        compiler_params=pltpu.CompilerParams(vmem_limit_bytes=24 * 2**20),
        cost_estimate=pl.CostEstimate(flops=16 * 10**8, bytes_accessed=10 * 2**20, transcendentals=0),
        name="embed_gradient",
    )(grads, w_conv, pre_embed, one_hot)


def place_of(x, core, z, fsdp):
    return (2 * x + core) * fsdp + z


def exchange(block, dp, fsdp, flip_x, flip_core, flip_z):
    pairs = []
    for x in range(dp // 2):
        for core in range(2):
            for z in range(fsdp):
                pairs.append((place_of(x, core, z, fsdp), place_of(x ^ flip_x, core ^ flip_core, z ^ flip_z, fsdp)))
    return lax.ppermute(block, GROUP, pairs)


def gather_blocks(block, devices):
    copies = jnp.broadcast_to(block[None], (devices,) + block.shape)
    return lax.all_to_all(copies, GROUP, 0, 0, tiled=True).reshape(-1, block.shape[1])


def local_kernel(kernel, outs, name, *operands):
    return pl.pallas_call(
        kernel,
        out_shape=outs,
        in_specs=[VMEM] * len(operands),
        out_specs=(VMEM,) * len(outs),
        compiler_params=pltpu.CompilerParams(vmem_limit_bytes=16 * 2**20),
        name=name,
    )(*operands)


def to_half(coded):
    rounded = lax.reduce_precision(coded, exponent_bits=5, mantissa_bits=10)
    return rounded, rounded.astype(jnp.float16)


def reduce_to_owner(keep, other, embed, dp, fsdp):
    rows, width = keep.shape[1] + embed.shape[1], keep.shape[2]
    plain = jax.ShapeDtypeStruct((rows, width), F32)
    scaled = jax.ShapeDtypeStruct((rows + 8, width), F32)
    own, *coded = local_kernel(scale_kernel, (plain,) + (scaled,) * (fsdp - 1), "scale", keep, other, embed)
    received = [
        exchange(to_half(part)[1], dp, fsdp, 0, 0, place + 1).astype(F32) for place, part in enumerate(coded)
    ]
    (coded,) = local_kernel(first_sum_kernel, (scaled,), "sum_z", own, *received)
    flip = dp // 4
    for bit in range(flip.bit_length() - 1):
        mine, sent = to_half(coded)
        other = exchange(sent, dp, fsdp, 2**bit, 0, 0).astype(F32)
        (coded,) = local_kernel(next_sum_kernel, (scaled,), "sum_x", mine, other)
    mine, sent = to_half(coded)
    flips = (flip, 0), (0, 1), (flip, 1)
    return mine, *(exchange(sent, dp, fsdp, x, core, 0).astype(F32) for x, core in flips)


def shards(facies, prior_draws, recon_grad, w_embed, w_conv, w_head):
    dp, fsdp = lax.axis_size("dp"), lax.axis_size("fsdp")
    block, one_hot, pre_embed, hidden, pre_conv, w_conv, w_head = forward(
        facies, prior_draws, recon_grad, w_embed, w_conv, w_head
    )
    gathered = gather_blocks(block, dp * fsdp)
    keep, send, grads, grad_head = backward((dp, fsdp), gathered, hidden, pre_conv, w_head)
    received = exchange(send, dp, fsdp, 0, 1, 0)
    embed = embed_gradient(fsdp, grads, w_conv, pre_embed, one_hot)
    sums = reduce_to_owner(keep, received, embed, dp, fsdp)
    grad_embed, grad_conv = pl.pallas_call(
        output_kernel,
        out_shape=(
            jax.ShapeDtypeStruct((256 // fsdp, 128), F32),
            jax.ShapeDtypeStruct((1024 // fsdp, 256), F32),
        ),
        in_specs=[VMEM] * 4,
        out_specs=(VMEM,) * 2,
        compiler_params=pltpu.CompilerParams(vmem_limit_bytes=16 * 2**20),
        name="outputs",
    )(*sums)
    return (grad_embed, grad_conv, grad_head)


def solution(mesh):
    return jax.shard_map(
        shards,
        mesh=mesh,
        in_specs=(
            P(("groups", "dp", "fsdp"), None, None),
            P(("groups", "dp", "fsdp"), None),
            P(("groups", "dp", "fsdp"), None),
            P(),
            P(),
            P(),
        ),
        out_specs=(
            P(("groups", "fsdp"), None),
            P(("groups", "fsdp"), None),
            P(("groups", "fsdp"), None),
        ),
        check_vma=False,
    )
```

```python
import jax
import jax.numpy as jnp
from jax import lax
from jax.experimental import pallas as pl
from jax.experimental.pallas import tpu as pltpu
from jax.sharding import PartitionSpec as P

PATCH_X = 64
PATCH_Y = 64
PATCH_Z = 32
LEVELS = 4
GROUP = ("dp", "fsdp")
NT = (((1,), (1,)), ((), ()))
F32 = jnp.float32
BF16 = jnp.bfloat16


def iota(shape, dim):
    return lax.broadcasted_iota(jnp.int32, shape, dim)


def mm(left, right):
    return jnp.dot(left, right, preferred_element_type=F32)


def mm_nt(left, right):
    return lax.dot_general(left, right, NT, preferred_element_type=F32)


def pair_weights(w_embed):
    turned = jnp.transpose(w_embed.astype(F32)).astype(BF16)
    row, lane = iota((256, 512), 0), iota((256, 512), 1)
    same = (row // 64 == lane // 128) & (row % 4 == lane // 32 % 4)
    same = same & (row // 16 % 4 == lane // 8 % 4) & (row // 4 % 4 == lane % 4)
    halves = []
    for half in range(2):
        halves.append(mm(turned, jnp.where(same & (lane // 4 % 2 == half), 1.0, 0.0).astype(BF16)))
    return jnp.concatenate(halves, axis=0).astype(BF16)


def sigmoid(value):
    return pltpu.reciprocal(1.0 + jnp.exp2(value * -1.4426950408889634), approx=True)


def silu_slope(value):
    gate = sigmoid(value)
    return gate * (1.0 + value * (1.0 - gate))


def forward_kernel(
    facies_hbm, prior_hbm, recon_hbm, w_embed_hbm, w_conv_hbm, w_head_hbm,
    block, one_hot, pre_embed, hidden, pre_conv, w_conv, w_head,
    facies, prior, recon, w_embed, packed, sem
):
    blocks = facies.shape[0]
    loads = [
        pltpu.make_async_copy(facies_hbm.at[:, pl.ds(b * 128, 128)], facies.at[b], sem.at[b]) for b in range(blocks)
    ]
    for load in loads:
        load.start()
    others = []
    for source, target in (
        (w_embed_hbm, w_embed), (w_conv_hbm, w_conv), (prior_hbm, prior), (recon_hbm, recon), (w_head_hbm, w_head)
    ):
        others.append(pltpu.make_async_copy(source, target, sem.at[blocks + len(others)]))
    for half in range(2):
        for load in loads[half * blocks // 2 : (half + 1) * blocks // 2]:
            load.wait()
        if half == 0:
            for load in others:
                load.start()
        for t in range(8):
            dx2, dx = t // 4, t % 4
            rows = [
                facies[2 * b2 + dy2, pl.ds(t, 32, stride=8), :]
                for dy2 in range(2)
                for b2 in range(4 * half, 4 * half + 4)
            ]
            turned = jnp.transpose(jnp.concatenate(rows, axis=0).astype(F32))
            for cp in range(4):
                part = jnp.concatenate([turned[dy * 32 + cp * 8 : dy * 32 + cp * 8 + 8] for dy in range(4)], axis=0)
                part = part.astype(BF16)
                for k in range(LEVELS):
                    hot = jnp.where(part == BF16(k), BF16(1.0), BF16(0.0))
                    for dy2 in range(2):
                        at = (2 * dx2 + dy2) * 256 + half * 128
                        one_hot[cp, pl.ds(dx * 128 + k * 32, 32), pl.ds(at, 128)] = hot[:, dy2 * 128 : dy2 * 128 + 128]
    others[0].wait()
    packed[...] = pair_weights(w_embed[...])
    others[1].wait()
    conv_turned = jnp.transpose(w_conv[...].astype(F32)).astype(BF16)
    sums = jnp.zeros((256, 128), F32)
    for cp in range(4):
        for dx2 in range(2):
            at = pl.ds(dx2 * 512, 512)
            pre = mm(packed[...], one_hot[cp, :, at])
            pre_embed[cp, :, at] = pre
            act = (pre * sigmoid(pre)).astype(BF16)
            hidden[cp, 2 * dx2] = act[:, :256]
            hidden[cp, 2 * dx2 + 1] = act[:, 256:]
        pre = mm(conv_turned, hidden[cp].reshape(1024, 256))
        pre_conv[cp] = pre
        act = pre * sigmoid(pre)
        sums = sums + act[:, :128] + act[:, 128:]
    pick = jnp.where(iota((8, 128), 1) // 8 % 4 == iota((8, 128), 0), 1.0, 0.0)
    total = lax.dot_general(pick, sums, NT, precision=lax.Precision.HIGHEST, preferred_element_type=F32)
    for load in others[2:]:
        load.wait()
    block[:, pl.ds(0, 512)] = prior[...]
    block[:, pl.ds(512, 512)] = recon[...]
    block[:, pl.ds(1024, 256)] = (total[:4] / 256.0).astype(BF16)


def pair_kernel(queries, query_square, keys):
    inner = mm_nt(queries, keys)
    key_float = keys.astype(F32)
    count = keys.shape[0]
    key_square = jnp.sum(key_float * key_float, axis=1, keepdims=True)
    key_row = jnp.transpose(jnp.broadcast_to(key_square, (count, 128)))[:1]
    kern = jnp.exp(-(query_square + key_row - 2.0 * inner) / keys.shape[1])
    return jnp.sum(kern, axis=1, keepdims=True), mm(kern.astype(BF16), keys)


def backward_kernel(
    sizes, gathered, hidden, pre_conv, w_head,
    keep, send, grads, grad_head,
    ordered, head_full
):
    dp, fsdp = sizes
    devices = dp * fsdp
    dp_here, fsdp_here = lax.axis_index("dp"), lax.axis_index("fsdp")
    here = dp_here * fsdp + fsdp_here
    for owner in range(devices):
        ordered[owner] = gathered[owner].astype(F32)
    samples = ordered.shape[1]
    count = devices * samples
    full = ordered[...].reshape(count, ordered.shape[2])
    prior = full[:, :512].astype(BF16)
    recon = full[:, 512:1024]
    pooled = full[:, 1024:].astype(BF16)
    latent = mm(pooled, w_head[...]).astype(BF16)
    latent_float = latent.astype(F32)
    square = jnp.sum(latent_float * latent_float, axis=1, keepdims=True)
    self_sum, self_mix = pair_kernel(latent, square, latent)
    cross_sum, cross_mix = pair_kernel(latent, square, prior)
    pull = -32.0 / count * ((self_sum - cross_sum) * latent_float - self_mix + cross_mix)
    cotangent = (recon + pull).astype(BF16)
    turned = jnp.transpose(full[:, 1024:]).astype(BF16)
    head_full[...] = mm(turned, cotangent)
    share = grad_head.shape[0]
    start = pl.multiple_of(fsdp_here * share, share)
    grad_head[...] = head_full[pl.ds(start, share), :]

    lane_sample = iota((128, count), 0) // 8 % 4 + samples * here
    pick = jnp.where(lane_sample == iota((128, count), 1), 1.0, 0.0).astype(BF16)
    lanes = mm(pick, cotangent).astype(BF16)
    back_pool = mm_nt(w_head[...], lanes) / 256.0
    back_pool = jnp.concatenate([back_pool, back_pool], axis=1)
    conv_total = None
    for cp in range(4):
        grads[cp] = (back_pool * silu_slope(pre_conv[cp])).astype(BF16)
        term = mm_nt(hidden[cp].reshape(1024, 256), grads[cp])
        conv_total = term if cp == 0 else conv_total + term
    core_zero = lax.rem(dp_here, 2) == 0
    rows = keep.shape[1]
    for f in range(fsdp):
        at = 2 * f * rows
        first, second = conv_total[at : at + rows], conv_total[at + rows : at + 2 * rows]
        keep[f] = jnp.where(core_zero, first, second)
        send[f] = jnp.where(core_zero, second, first)


def embed_kernel(grads, w_conv, pre_embed, one_hot, embed_out):
    embed_total = None
    for cp in range(4):
        signals = []
        for dx2 in range(2):
            back_rows = mm(w_conv[pl.ds(dx2 * 512, 512), :], grads[cp])
            back_rows = jnp.concatenate([back_rows[:256], back_rows[256:]], axis=1)
            signals.append((back_rows * silu_slope(pre_embed[cp, :, pl.ds(dx2 * 512, 512)])).astype(BF16))
        term = mm_nt(one_hot[cp], jnp.concatenate(signals, axis=1))
        embed_total = term if cp == 0 else embed_total + term
    pairs = embed_total.reshape(64, 8, 256)
    embed = (pairs[:, :4, :128] + pairs[:, 4:, 128:]).reshape(256, 128)
    half = embed_out.shape[1]
    depth = 2 * half // LEVELS
    for f in range(embed_out.shape[0]):
        dx, at = f * 2 * half // 64, f * 2 * half % 64 // LEVELS
        share = jnp.concatenate([embed[dx * 64 + k * 16 + at :][:depth] for k in range(LEVELS)], axis=0)
        for side in range(2):
            embed_out[f, :, pl.ds(side * 128, 128)] = share[side * half : (side + 1) * half]


def exponent_of(part):
    top = jnp.abs(part)
    while top.ndim > 2:
        top = jnp.max(top, axis=0)
    top = jnp.max(jnp.max(top, axis=0, keepdims=True), axis=1, keepdims=True)
    return jnp.clip(jnp.floor(jnp.log2(jnp.maximum(top, 1e-37))) - 14.0, -124.0, 114.0)


def store_coded(coded, part):
    rows = part.shape[0]
    conv_rows = rows * 4 // 5
    conv, embed = part[:conv_rows], part[conv_rows:]
    steps = exponent_of(conv), exponent_of(embed)
    store_scaled(coded, part, steps)


def store_scaled(coded, part, steps):
    rows, spare = part.shape[0], coded.shape[0] - part.shape[0]
    conv_rows = rows * 4 // 5
    coded[pl.ds(0, conv_rows), :] = part[:conv_rows] * jnp.exp2(-steps[0])
    coded[pl.ds(conv_rows, rows - conv_rows), :] = part[conv_rows:] * jnp.exp2(-steps[1])
    tail = jnp.where(iota((spare, coded.shape[1]), 0) == 0, steps[0], steps[1])
    coded[pl.ds(rows, spare), :] = tail


def load_coded(coded, rows):
    conv_rows = rows * 4 // 5
    conv_scale = jnp.exp2(coded[pl.ds(rows, 1), :])
    embed_scale = jnp.exp2(coded[pl.ds(rows + 1, 1), :])
    return jnp.concatenate(
        [coded[pl.ds(0, conv_rows), :] * conv_scale, coded[pl.ds(conv_rows, rows - conv_rows), :] * embed_scale], axis=0
    )


def scale_kernel(keep, other, embed, own, *coded):
    held = keep[...] + other[...]
    steps = exponent_of(held), exponent_of(embed[...])
    here = lax.axis_index("fsdp")

    def share(z):
        return jnp.concatenate([keep[z] + other[z], embed[z]], axis=0)

    own[...] = share(here)
    for place, target in enumerate(coded):
        store_scaled(target, share(here ^ (place + 1)), steps)


def first_sum_kernel(own, *refs):
    *received, coded = refs
    total = own[...]
    for part in received:
        total = total + load_coded(part, total.shape[0])
    store_coded(coded, total)


def next_sum_kernel(mine, other, total, *coded):
    rows = total.shape[0]
    summed = load_coded(mine, rows) + load_coded(other, rows)
    total[...] = summed
    if coded:
        store_coded(coded[0], summed)


def output_kernel(own, other, grad_embed, grad_conv):
    rows = own.shape[0]
    conv_rows, half = rows * 4 // 5, rows // 5
    core_zero = lax.rem(lax.axis_index("dp"), 2) == 0
    grad_conv[pl.ds(0, conv_rows), :] = jnp.where(core_zero, own[pl.ds(0, conv_rows), :], other[pl.ds(0, conv_rows), :])
    grad_conv[pl.ds(conv_rows, conv_rows), :] = jnp.where(
        core_zero, other[pl.ds(0, conv_rows), :], own[pl.ds(0, conv_rows), :]
    )
    embed = own[pl.ds(conv_rows, half), :] + other[pl.ds(conv_rows, half), :]
    embed = jnp.concatenate([embed[:, :128], embed[:, 128:]], axis=0)
    count = 2 * half
    row, lane = iota((count, count), 0), iota((count, count), 1)
    order = jnp.where(lane == row % LEVELS * (count // LEVELS) + row // LEVELS, 1.0, 0.0).astype(BF16)
    result = None
    for _ in range(3):
        term = embed.astype(BF16)
        embed = embed - term.astype(F32)
        result = mm(order, term) if result is None else result + mm(order, term)
    grad_embed[...] = result


VMEM = pl.BlockSpec(memory_space=pltpu.VMEM)
HBM = pl.BlockSpec(memory_space=pltpu.HBM)
SAVED = (
    ((4, 512, 1024), BF16),
    ((4, 256, 1024), F32),
    ((4, 4, 256, 256), BF16),
    ((4, 256, 256), F32),
)


def forward(facies, prior_draws, recon_grad, w_embed, w_conv, w_head):
    samples = facies.shape[0]
    latent_width = prior_draws.shape[1]
    rows, lanes = samples * PATCH_X, PATCH_Y * PATCH_Z
    operands = (facies.reshape(rows, lanes), prior_draws, recon_grad, w_embed, w_conv, w_head)
    return pl.pallas_call(
        forward_kernel,
        out_shape=(pltpu.VMEM((samples, 2 * latent_width + 256), BF16),)
        + tuple(pltpu.VMEM(shape, kind) for shape, kind in SAVED)
        + (pltpu.VMEM(w_conv.shape, BF16), pltpu.VMEM(w_head.shape, BF16)),
        in_specs=[HBM] * 6,
        out_specs=(VMEM,) * 7,
        scratch_shapes=[
            pltpu.VMEM((lanes // 128, rows, 128), jnp.int32),
            pltpu.VMEM(prior_draws.shape, BF16),
            pltpu.VMEM(recon_grad.shape, BF16),
            pltpu.VMEM(w_embed.shape, BF16),
            pltpu.VMEM((256, 512), BF16),
            pltpu.SemaphoreType.DMA((lanes // 128 + 5,)),
        ],
        compiler_params=pltpu.CompilerParams(vmem_limit_bytes=30 * 2**20),
        name="forward",
    )(*(pltpu.with_memory_space_constraint(operand, pltpu.HBM) for operand in operands))


def backward(sizes, gathered, hidden, pre_conv, w_head):
    dp, fsdp = sizes
    devices, samples, width = gathered.shape
    payload = pltpu.VMEM((fsdp, 1024 // fsdp // 2, 256), F32)
    return pl.pallas_call(
        lambda *refs: backward_kernel(sizes, *refs),
        out_shape=(
            payload, payload, pltpu.VMEM((4, 256, 256), BF16), jax.ShapeDtypeStruct((256 // fsdp, 512), F32)
        ),
        in_specs=[VMEM] * 4,
        out_specs=(VMEM,) * 4,
        scratch_shapes=[pltpu.VMEM((devices, samples, width), F32), pltpu.VMEM((256, 512), F32)],
        compiler_params=pltpu.CompilerParams(vmem_limit_bytes=24 * 2**20),
        name="backward",
    )(gathered, hidden, pre_conv, w_head)


def embed_gradient(fsdp, grads, w_conv, pre_embed, one_hot):
    return pl.pallas_call(
        embed_kernel,
        out_shape=pltpu.VMEM((fsdp, 256 // fsdp // 2, 256), F32),
        in_specs=[VMEM] * 4,
        out_specs=VMEM,
        compiler_params=pltpu.CompilerParams(vmem_limit_bytes=24 * 2**20),
        cost_estimate=pl.CostEstimate(flops=16 * 10**8, bytes_accessed=10 * 2**20, transcendentals=0),
        name="embed_gradient",
    )(grads, w_conv, pre_embed, one_hot)


def place_of(x, core, z, fsdp):
    return (2 * x + core) * fsdp + z


def exchange(block, dp, fsdp, flip_x, flip_core, flip_z):
    pairs = []
    for x in range(dp // 2):
        for core in range(2):
            for z in range(fsdp):
                pairs.append((place_of(x, core, z, fsdp), place_of(x ^ flip_x, core ^ flip_core, z ^ flip_z, fsdp)))
    return lax.ppermute(block, GROUP, pairs)


def gather_blocks(block, devices):
    copies = jnp.broadcast_to(block[None], (devices,) + block.shape)
    return lax.all_to_all(copies, GROUP, 0, 0, tiled=True)


def local_kernel(kernel, outs, name, *operands):
    return pl.pallas_call(
        kernel,
        out_shape=outs,
        in_specs=[VMEM] * len(operands),
        out_specs=(VMEM,) * len(outs),
        compiler_params=pltpu.CompilerParams(vmem_limit_bytes=16 * 2**20),
        name=name,
    )(*operands)


def to_half(coded):
    rounded = lax.reduce_precision(coded, exponent_bits=5, mantissa_bits=10)
    return rounded, rounded.astype(jnp.float16)


def reduce_to_owner(keep, other, embed, dp, fsdp):
    rows, width = keep.shape[1] + embed.shape[1], keep.shape[2]
    plain = jax.ShapeDtypeStruct((rows, width), F32)
    scaled = jax.ShapeDtypeStruct((rows + 8, width), F32)
    own, *coded = local_kernel(scale_kernel, (plain,) + (scaled,) * (fsdp - 1), "scale", keep, other, embed)
    received = [
        exchange(to_half(part)[1], dp, fsdp, 0, 0, place + 1).astype(F32) for place, part in enumerate(coded)
    ]
    (coded,) = local_kernel(first_sum_kernel, (scaled,), "sum_z", own, *received)
    flip = 1
    while flip < dp // 2:
        mine, sent = to_half(coded)
        other = exchange(sent, dp, fsdp, flip, 0, 0).astype(F32)
        flip *= 2
        outs = (plain, scaled) if flip < dp // 2 else (plain,)
        total, *rest = local_kernel(next_sum_kernel, outs, "sum_x", mine, other)
        coded = rest[0] if rest else None
    return total, exchange(total, dp, fsdp, 0, 1, 0)


def shards(facies, prior_draws, recon_grad, w_embed, w_conv, w_head):
    dp, fsdp = lax.axis_size("dp"), lax.axis_size("fsdp")
    block, one_hot, pre_embed, hidden, pre_conv, w_conv, w_head = forward(
        facies, prior_draws, recon_grad, w_embed, w_conv, w_head
    )
    gathered = gather_blocks(block, dp * fsdp)
    keep, send, grads, grad_head = backward((dp, fsdp), gathered, hidden, pre_conv, w_head)
    received = exchange(send, dp, fsdp, 0, 1, 0)
    embed = embed_gradient(fsdp, grads, w_conv, pre_embed, one_hot)
    own, other = reduce_to_owner(keep, received, embed, dp, fsdp)
    grad_embed, grad_conv = pl.pallas_call(
        output_kernel,
        out_shape=(
            jax.ShapeDtypeStruct((256 // fsdp, 128), F32),
            jax.ShapeDtypeStruct((1024 // fsdp, 256), F32),
        ),
        in_specs=[VMEM] * 2,
        out_specs=(VMEM,) * 2,
        compiler_params=pltpu.CompilerParams(vmem_limit_bytes=16 * 2**20),
        name="outputs",
    )(own, other)
    return (grad_embed, grad_conv, grad_head)


def solution(mesh):
    return jax.shard_map(
        shards,
        mesh=mesh,
        in_specs=(
            P(("groups", "dp", "fsdp"), None, None),
            P(("groups", "dp", "fsdp"), None),
            P(("groups", "dp", "fsdp"), None),
            P(),
            P(),
            P(),
        ),
        out_specs=(
            P(("groups", "fsdp"), None),
            P(("groups", "fsdp"), None),
            P(("groups", "fsdp"), None),
        ),
        check_vma=False,
    )
```

```python
import jax
import jax.numpy as jnp
from jax import lax
from jax.experimental import pallas as pl
from jax.experimental.pallas import tpu as pltpu
from jax.sharding import PartitionSpec as P

PATCH_X = 64
PATCH_Y = 64
PATCH_Z = 32
LEVELS = 4
GROUP = ("dp", "fsdp")
NT = (((1,), (1,)), ((), ()))
F32 = jnp.float32
BF16 = jnp.bfloat16


def iota(shape, dim):
    return lax.broadcasted_iota(jnp.int32, shape, dim)


def mm(left, right):
    return jnp.dot(left, right, preferred_element_type=F32)


def mm_nt(left, right):
    return lax.dot_general(left, right, NT, preferred_element_type=F32)


def turned_weights(w_embed):
    turned = jnp.transpose(w_embed.astype(F32)).astype(BF16)
    row, lane = iota((256, 256), 0), iota((256, 256), 1)
    same = (row // 64 == lane // 64) & (row % 4 == lane // 16 % 4) & (row // 4 % 16 == lane % 16)
    return mm(turned, jnp.where(same, 1.0, 0.0).astype(BF16)).astype(BF16)


def sigmoid(value):
    return pltpu.reciprocal(1.0 + jnp.exp2(value * -1.4426950408889634), approx=True)


def silu_slope(value):
    gate = sigmoid(value)
    return gate * (1.0 + value * (1.0 - gate))


def forward_kernel(
    facies_hbm, prior_hbm, recon_hbm, w_embed_hbm, w_conv_hbm, w_head_hbm,
    block, one_hot, pre_embed, hidden, pre_conv, w_conv, w_head,
    facies, prior, recon, w_embed, packed, conv_turned, sem
):
    blocks = facies.shape[0]
    loads = [
        pltpu.make_async_copy(facies_hbm.at[:, pl.ds(b * 128, 128)], facies.at[b], sem.at[b]) for b in range(blocks)
    ]
    others = []
    for source, target in (
        (w_embed_hbm, w_embed), (w_conv_hbm, w_conv), (prior_hbm, prior), (recon_hbm, recon), (w_head_hbm, w_head)
    ):
        others.append(pltpu.make_async_copy(source, target, sem.at[blocks + len(others)]))
    for load in others[:2] + loads:
        load.start()
    others[0].wait()
    packed[...] = turned_weights(w_embed[...])
    others[1].wait()
    conv_turned[...] = jnp.transpose(w_conv[...].astype(F32)).astype(BF16)
    low = iota((8, 256), 0) < 4
    for half in range(2):
        for load in loads[half * blocks // 2 : (half + 1) * blocks // 2]:
            load.wait()
        if half == 0:
            for load in others[2:]:
                load.start()
        for t in range(8):
            dx2, dx = t // 4, t % 4
            rows = [
                facies[2 * b2 + dy2, pl.ds(t, 32, stride=8), :]
                for dy2 in range(2)
                for b2 in range(4 * half, 4 * half + 4)
            ]
            turned = jnp.transpose(jnp.concatenate(rows, axis=0).astype(F32))
            for cp in range(4):
                part = [turned[dy * 32 + cp * 8 : dy * 32 + cp * 8 + 8] for dy in range(4)]
                swapped = [pltpu.roll(piece, 4, 0) for piece in part]
                for dz2 in range(2):
                    pieces = [
                        jnp.where(low, part[dy], swapped[dy + 1]) if dz2 == 0 else jnp.where(low, swapped[dy], part[dy + 1])
                        for dy in (0, 2)
                    ]
                    cells = jnp.concatenate(pieces, axis=0).astype(BF16)
                    for k in range(LEVELS):
                        hot = jnp.where(cells == BF16(k), BF16(1.0), BF16(0.0))
                        for dy2 in range(2):
                            at = (2 * dx2 + dy2) * 256 + half * 128
                            one_hot[2 * cp + dz2, pl.ds(dx * 64 + k * 16, 16), pl.ds(at, 128)] = hot[
                                :, dy2 * 128 : dy2 * 128 + 128
                            ]
    sums = jnp.zeros((256, 128), F32)
    for cp in range(4):
        for dz2 in range(2):
            rows = pl.ds(dz2 * 128, 128)
            for dx2 in range(2):
                at = pl.ds(dx2 * 512, 512)
                pre = mm(packed[...], one_hot[2 * cp + dz2, :, at])
                pre_embed[cp, rows, at] = pre
                act = (pre * sigmoid(pre)).astype(BF16)
                hidden[cp, 2 * dx2, rows, :] = act[:, :256]
                hidden[cp, 2 * dx2 + 1, rows, :] = act[:, 256:]
        pre = mm(conv_turned[...], hidden[cp].reshape(1024, 256))
        pre_conv[cp] = pre
        act = pre * sigmoid(pre)
        sums = sums + act[:, :128] + act[:, 128:]
    pick = jnp.where(iota((8, 128), 1) // 8 % 4 == iota((8, 128), 0), 1.0, 0.0)
    total = lax.dot_general(pick, sums, NT, precision=lax.Precision.HIGHEST, preferred_element_type=F32)
    for load in others[2:]:
        load.wait()
    block[:, pl.ds(0, 512)] = prior[...]
    block[:, pl.ds(512, 512)] = recon[...]
    block[:, pl.ds(1024, 256)] = (total[:4] / 256.0).astype(BF16)


def pair_kernel(queries, query_square, keys):
    inner = mm_nt(queries, keys)
    key_float = keys.astype(F32)
    count = keys.shape[0]
    key_square = jnp.sum(key_float * key_float, axis=1, keepdims=True)
    key_row = jnp.transpose(jnp.broadcast_to(key_square, (count, 128)))[:1]
    kern = jnp.exp(-(query_square + key_row - 2.0 * inner) / keys.shape[1])
    return jnp.sum(kern, axis=1, keepdims=True), mm(kern.astype(BF16), keys)


def backward_kernel(
    sizes, gathered, hidden, pre_conv, w_head,
    keep, send, grads, grad_head,
    ordered, head_full
):
    dp, fsdp = sizes
    devices = dp * fsdp
    dp_here, fsdp_here = lax.axis_index("dp"), lax.axis_index("fsdp")
    here = dp_here * fsdp + fsdp_here
    for owner in range(devices):
        ordered[owner] = gathered[owner].astype(F32)
    samples = ordered.shape[1]
    count = devices * samples
    full = ordered[...].reshape(count, ordered.shape[2])
    prior = full[:, :512].astype(BF16)
    recon = full[:, 512:1024]
    pooled = full[:, 1024:].astype(BF16)
    latent = mm(pooled, w_head[...]).astype(BF16)
    latent_float = latent.astype(F32)
    square = jnp.sum(latent_float * latent_float, axis=1, keepdims=True)
    self_sum, self_mix = pair_kernel(latent, square, latent)
    cross_sum, cross_mix = pair_kernel(latent, square, prior)
    pull = -32.0 / count * ((self_sum - cross_sum) * latent_float - self_mix + cross_mix)
    cotangent = (recon + pull).astype(BF16)
    turned = jnp.transpose(full[:, 1024:]).astype(BF16)
    head_full[...] = mm(turned, cotangent)
    share = grad_head.shape[0]
    start = pl.multiple_of(fsdp_here * share, share)
    grad_head[...] = head_full[pl.ds(start, share), :]

    lane_sample = iota((128, count), 0) // 8 % 4 + samples * here
    pick = jnp.where(lane_sample == iota((128, count), 1), 1.0, 0.0).astype(BF16)
    lanes = mm(pick, cotangent).astype(BF16)
    back_pool = mm_nt(w_head[...], lanes) / 256.0
    back_pool = jnp.concatenate([back_pool, back_pool], axis=1)
    conv_total = None
    for cp in range(4):
        grads[cp] = (back_pool * silu_slope(pre_conv[cp])).astype(BF16)
        term = mm_nt(hidden[cp].reshape(1024, 256), grads[cp])
        conv_total = term if cp == 0 else conv_total + term
    core_zero = lax.rem(dp_here, 2) == 0
    rows = keep.shape[1]
    for f in range(fsdp):
        at = 2 * f * rows
        first, second = conv_total[at : at + rows], conv_total[at + rows : at + 2 * rows]
        keep[f] = jnp.where(core_zero, first, second)
        send[f] = jnp.where(core_zero, second, first)


def embed_kernel(grads, w_conv, pre_embed, one_hot, embed_out):
    embed = None
    for cp in range(4):
        signals = []
        for dx2 in range(2):
            back_rows = mm(w_conv[pl.ds(dx2 * 512, 512), :], grads[cp])
            back_rows = jnp.concatenate([back_rows[:256], back_rows[256:]], axis=1)
            signals.append((back_rows * silu_slope(pre_embed[cp, :, pl.ds(dx2 * 512, 512)])).astype(BF16))
        signal = jnp.concatenate(signals, axis=1)
        for dz2 in range(2):
            term = mm_nt(one_hot[2 * cp + dz2], signal[dz2 * 128 : dz2 * 128 + 128])
            embed = term if embed is None else embed + term
    half = embed_out.shape[1]
    depth = 2 * half // LEVELS
    for f in range(embed_out.shape[0]):
        dx, at = f * 2 * half // 64, f * 2 * half % 64 // LEVELS
        share = jnp.concatenate([embed[dx * 64 + k * 16 + at :][:depth] for k in range(LEVELS)], axis=0)
        for side in range(2):
            embed_out[f, :, pl.ds(side * 128, 128)] = share[side * half : (side + 1) * half]


def exponent_of(part):
    top = jnp.abs(part)
    while top.ndim > 2:
        top = jnp.max(top, axis=0)
    top = jnp.max(jnp.max(top, axis=0, keepdims=True), axis=1, keepdims=True)
    return jnp.clip(jnp.floor(jnp.log2(jnp.maximum(top, 1e-37))) - 14.0, -124.0, 114.0)


def store_coded(coded, part):
    rows = part.shape[0]
    conv_rows = rows * 4 // 5
    conv, embed = part[:conv_rows], part[conv_rows:]
    steps = exponent_of(conv), exponent_of(embed)
    store_scaled(coded, part, steps)


def store_scaled(coded, part, steps):
    rows, spare = part.shape[0], coded.shape[0] - part.shape[0]
    conv_rows = rows * 4 // 5
    coded[pl.ds(0, conv_rows), :] = part[:conv_rows] * jnp.exp2(-steps[0])
    coded[pl.ds(conv_rows, rows - conv_rows), :] = part[conv_rows:] * jnp.exp2(-steps[1])
    tail = jnp.where(iota((spare, coded.shape[1]), 0) == 0, steps[0], steps[1])
    coded[pl.ds(rows, spare), :] = tail


def load_coded(coded, rows):
    conv_rows = rows * 4 // 5
    conv_scale = jnp.exp2(coded[pl.ds(rows, 1), :])
    embed_scale = jnp.exp2(coded[pl.ds(rows + 1, 1), :])
    return jnp.concatenate(
        [coded[pl.ds(0, conv_rows), :] * conv_scale, coded[pl.ds(conv_rows, rows - conv_rows), :] * embed_scale], axis=0
    )


def scale_kernel(keep, other, embed, own, *coded):
    held = keep[...] + other[...]
    steps = exponent_of(held), exponent_of(embed[...])
    here = lax.axis_index("fsdp")

    def share(z):
        return jnp.concatenate([keep[z] + other[z], embed[z]], axis=0)

    own[...] = share(here)
    for place, target in enumerate(coded):
        store_scaled(target, share(here ^ (place + 1)), steps)


def first_sum_kernel(own, *refs):
    *received, coded = refs
    total = own[...]
    for part in received:
        total = total + load_coded(part, total.shape[0])
    store_coded(coded, total)


def next_sum_kernel(mine, other, total, *coded):
    rows = total.shape[0]
    summed = load_coded(mine, rows) + load_coded(other, rows)
    total[...] = summed
    if coded:
        store_coded(coded[0], summed)


def output_kernel(own, other, grad_embed, grad_conv):
    rows = own.shape[0]
    conv_rows, half = rows * 4 // 5, rows // 5
    core_zero = lax.rem(lax.axis_index("dp"), 2) == 0
    grad_conv[pl.ds(0, conv_rows), :] = jnp.where(core_zero, own[pl.ds(0, conv_rows), :], other[pl.ds(0, conv_rows), :])
    grad_conv[pl.ds(conv_rows, conv_rows), :] = jnp.where(
        core_zero, other[pl.ds(0, conv_rows), :], own[pl.ds(0, conv_rows), :]
    )
    embed = own[pl.ds(conv_rows, half), :] + other[pl.ds(conv_rows, half), :]
    embed = jnp.concatenate([embed[:, :128], embed[:, 128:]], axis=0)
    count = 2 * half
    row, lane = iota((count, count), 0), iota((count, count), 1)
    order = jnp.where(lane == row % LEVELS * (count // LEVELS) + row // LEVELS, 1.0, 0.0).astype(BF16)
    result = None
    for _ in range(3):
        term = embed.astype(BF16)
        embed = embed - term.astype(F32)
        result = mm(order, term) if result is None else result + mm(order, term)
    grad_embed[...] = result


VMEM = pl.BlockSpec(memory_space=pltpu.VMEM)
HBM = pl.BlockSpec(memory_space=pltpu.HBM)
SAVED = (
    ((8, 256, 1024), BF16),
    ((4, 256, 1024), F32),
    ((4, 4, 256, 256), BF16),
    ((4, 256, 256), F32),
)


def forward(facies, prior_draws, recon_grad, w_embed, w_conv, w_head):
    samples = facies.shape[0]
    latent_width = prior_draws.shape[1]
    rows, lanes = samples * PATCH_X, PATCH_Y * PATCH_Z
    operands = (facies.reshape(rows, lanes), prior_draws, recon_grad, w_embed, w_conv, w_head)
    return pl.pallas_call(
        forward_kernel,
        out_shape=(pltpu.VMEM((samples, 2 * latent_width + 256), BF16),)
        + tuple(pltpu.VMEM(shape, kind) for shape, kind in SAVED)
        + (pltpu.VMEM(w_conv.shape, BF16), pltpu.VMEM(w_head.shape, BF16)),
        in_specs=[HBM] * 6,
        out_specs=(VMEM,) * 7,
        scratch_shapes=[
            pltpu.VMEM((lanes // 128, rows, 128), jnp.int32),
            pltpu.VMEM(prior_draws.shape, BF16),
            pltpu.VMEM(recon_grad.shape, BF16),
            pltpu.VMEM(w_embed.shape, BF16),
            pltpu.VMEM((128, 256), BF16),
            pltpu.VMEM((256, 1024), BF16),
            pltpu.SemaphoreType.DMA((lanes // 128 + 5,)),
        ],
        compiler_params=pltpu.CompilerParams(vmem_limit_bytes=30 * 2**20),
        name="forward",
    )(*(pltpu.with_memory_space_constraint(operand, pltpu.HBM) for operand in operands))


def backward(sizes, gathered, hidden, pre_conv, w_head):
    dp, fsdp = sizes
    devices, samples, width = gathered.shape
    payload = pltpu.VMEM((fsdp, 1024 // fsdp // 2, 256), F32)
    return pl.pallas_call(
        lambda *refs: backward_kernel(sizes, *refs),
        out_shape=(
            payload, payload, pltpu.VMEM((4, 256, 256), BF16), jax.ShapeDtypeStruct((256 // fsdp, 512), F32)
        ),
        in_specs=[VMEM] * 4,
        out_specs=(VMEM,) * 4,
        scratch_shapes=[pltpu.VMEM((devices, samples, width), F32), pltpu.VMEM((256, 512), F32)],
        compiler_params=pltpu.CompilerParams(vmem_limit_bytes=24 * 2**20),
        name="backward",
    )(gathered, hidden, pre_conv, w_head)


def embed_gradient(fsdp, grads, w_conv, pre_embed, one_hot):
    return pl.pallas_call(
        embed_kernel,
        out_shape=pltpu.VMEM((fsdp, 256 // fsdp // 2, 256), F32),
        in_specs=[VMEM] * 4,
        out_specs=VMEM,
        compiler_params=pltpu.CompilerParams(vmem_limit_bytes=24 * 2**20),
        cost_estimate=pl.CostEstimate(flops=16 * 10**8, bytes_accessed=10 * 2**20, transcendentals=0),
        name="embed_gradient",
    )(grads, w_conv, pre_embed, one_hot)


def place_of(x, core, z, fsdp):
    return (2 * x + core) * fsdp + z


def exchange(block, dp, fsdp, flip_x, flip_core, flip_z):
    pairs = []
    for x in range(dp // 2):
        for core in range(2):
            for z in range(fsdp):
                pairs.append((place_of(x, core, z, fsdp), place_of(x ^ flip_x, core ^ flip_core, z ^ flip_z, fsdp)))
    return lax.ppermute(block, GROUP, pairs)


def gather_blocks(block, devices):
    copies = jnp.broadcast_to(block[None], (devices,) + block.shape)
    return lax.all_to_all(copies, GROUP, 0, 0, tiled=True)


def local_kernel(kernel, outs, name, *operands):
    return pl.pallas_call(
        kernel,
        out_shape=outs,
        in_specs=[VMEM] * len(operands),
        out_specs=(VMEM,) * len(outs),
        compiler_params=pltpu.CompilerParams(vmem_limit_bytes=16 * 2**20),
        name=name,
    )(*operands)


def to_half(coded):
    rounded = lax.reduce_precision(coded, exponent_bits=5, mantissa_bits=10)
    return rounded, rounded.astype(jnp.float16)


def reduce_to_owner(keep, other, embed, dp, fsdp):
    rows, width = keep.shape[1] + embed.shape[1], keep.shape[2]
    plain = jax.ShapeDtypeStruct((rows, width), F32)
    scaled = jax.ShapeDtypeStruct((rows + 8, width), F32)
    own, *coded = local_kernel(scale_kernel, (plain,) + (scaled,) * (fsdp - 1), "scale", keep, other, embed)
    received = [
        exchange(to_half(part)[1], dp, fsdp, 0, 0, place + 1).astype(F32) for place, part in enumerate(coded)
    ]
    (coded,) = local_kernel(first_sum_kernel, (scaled,), "sum_z", own, *received)
    flip = 1
    while flip < dp // 2:
        mine, sent = to_half(coded)
        other = exchange(sent, dp, fsdp, flip, 0, 0).astype(F32)
        flip *= 2
        outs = (plain, scaled) if flip < dp // 2 else (plain,)
        total, *rest = local_kernel(next_sum_kernel, outs, "sum_x", mine, other)
        coded = rest[0] if rest else None
    return total, exchange(total, dp, fsdp, 0, 1, 0)


def shards(facies, prior_draws, recon_grad, w_embed, w_conv, w_head):
    dp, fsdp = lax.axis_size("dp"), lax.axis_size("fsdp")
    block, one_hot, pre_embed, hidden, pre_conv, w_conv, w_head = forward(
        facies, prior_draws, recon_grad, w_embed, w_conv, w_head
    )
    gathered = gather_blocks(block, dp * fsdp)
    keep, send, grads, grad_head = backward((dp, fsdp), gathered, hidden, pre_conv, w_head)
    received = exchange(send, dp, fsdp, 0, 1, 0)
    embed = embed_gradient(fsdp, grads, w_conv, pre_embed, one_hot)
    own, other = reduce_to_owner(keep, received, embed, dp, fsdp)
    grad_embed, grad_conv = pl.pallas_call(
        output_kernel,
        out_shape=(
            jax.ShapeDtypeStruct((256 // fsdp, 128), F32),
            jax.ShapeDtypeStruct((1024 // fsdp, 256), F32),
        ),
        in_specs=[VMEM] * 2,
        out_specs=(VMEM,) * 2,
        compiler_params=pltpu.CompilerParams(vmem_limit_bytes=16 * 2**20),
        name="outputs",
    )(own, other)
    return (grad_embed, grad_conv, grad_head)


def solution(mesh):
    return jax.shard_map(
        shards,
        mesh=mesh,
        in_specs=(
            P(("groups", "dp", "fsdp"), None, None),
            P(("groups", "dp", "fsdp"), None),
            P(("groups", "dp", "fsdp"), None),
            P(),
            P(),
            P(),
        ),
        out_specs=(
            P(("groups", "fsdp"), None),
            P(("groups", "fsdp"), None),
            P(("groups", "fsdp"), None),
        ),
        check_vma=False,
    )
```

```python
import functools

import jax
import jax.numpy as jnp
from jax import lax
from jax.experimental import pallas as pl
from jax.experimental.pallas import tpu as pltpu
from jax.sharding import PartitionSpec as P

PATCH_X = 64
PATCH_Y = 64
PATCH_Z = 32
LEVELS = 4
GROUP = ("dp", "fsdp")
NT = (((1,), (1,)), ((), ()))
F32 = jnp.float32
BF16 = jnp.bfloat16


def iota(shape, dim):
    return lax.broadcasted_iota(jnp.int32, shape, dim)


def mm(left, right):
    return jnp.dot(left, right, preferred_element_type=F32)


def mm_nt(left, right):
    return lax.dot_general(left, right, NT, preferred_element_type=F32)


def turned_weights(w_embed):
    turned = jnp.transpose(w_embed.astype(F32)).astype(BF16)
    row, lane = iota((256, 256), 0), iota((256, 256), 1)
    dx, k = row // 64, row % 4
    same = lane == jnp.where(k < 3, dx * 48 + k * 16, 192 + dx * 16) + row // 4 % 16
    return mm(turned, jnp.where(same, 1.0, 0.0).astype(BF16)).astype(BF16)


def sigmoid(value):
    return pltpu.reciprocal(1.0 + jnp.exp2(value * -1.4426950408889634), approx=True)


def silu_slope(value):
    gate = sigmoid(value)
    return gate * (1.0 + value * (1.0 - gate))


def forward_kernel(
    facies_hbm, prior_hbm, recon_hbm, w_embed_hbm, w_conv_hbm, w_head_hbm,
    block, one_hot, pre_embed, hidden, pre_conv, w_conv, w_head,
    facies, prior, recon, w_embed, packed, conv_turned, sem
):
    blocks = facies.shape[0]
    loads = [
        pltpu.make_async_copy(facies_hbm.at[:, pl.ds(b * 128, 128)], facies.at[b], sem.at[b]) for b in range(blocks)
    ]
    others = []
    for source, target in (
        (w_embed_hbm, w_embed), (w_conv_hbm, w_conv), (prior_hbm, prior), (recon_hbm, recon), (w_head_hbm, w_head)
    ):
        others.append(pltpu.make_async_copy(source, target, sem.at[blocks + len(others)]))
    for load in others[:2] + loads:
        load.start()
    others[0].wait()
    packed[...] = turned_weights(w_embed[...])
    others[1].wait()
    conv_turned[...] = jnp.transpose(w_conv[...].astype(F32)).astype(BF16)
    low = iota((8, 256), 0) < 4
    for half in range(2):
        for load in loads[half * blocks // 2 : (half + 1) * blocks // 2]:
            load.wait()
        if half == 0:
            for load in others[2:]:
                load.start()
        for t in range(8):
            dx2, dx = t // 4, t % 4
            rows = [
                facies[2 * b2 + dy2, pl.ds(t, 32, stride=8), :]
                for dy2 in range(2)
                for b2 in range(4 * half, 4 * half + 4)
            ]
            turned = jnp.transpose(jnp.concatenate(rows, axis=0).astype(F32))
            for cp in range(4):
                part = [turned[dy * 32 + cp * 8 : dy * 32 + cp * 8 + 8] for dy in range(4)]
                swapped = [pltpu.roll(piece, 4, 0) for piece in part]
                for dz2 in range(2):
                    pieces = [
                        jnp.where(low, part[dy], swapped[dy + 1]) if dz2 == 0 else jnp.where(low, swapped[dy], part[dy + 1])
                        for dy in (0, 2)
                    ]
                    cells = jnp.concatenate(pieces, axis=0).astype(BF16)
                    for k in range(LEVELS):
                        hot = jnp.where(cells == BF16(k), BF16(1.0), BF16(0.0))
                        first = dx * 48 + k * 16 if k < 3 else 192 + dx * 16
                        for dy2 in range(2):
                            at = (2 * dx2 + dy2) * 256 + half * 128
                            one_hot[2 * cp + dz2, pl.ds(first, 16), pl.ds(at, 128)] = hot[:, dy2 * 128 : dy2 * 128 + 128]
    sums = jnp.zeros((256, 128), F32)
    for cp in range(4):
        for dz2 in range(2):
            rows = pl.ds(dz2 * 128, 128)
            for dx2 in range(2):
                at = pl.ds(dx2 * 512, 512)
                pre = mm(packed[...], one_hot[2 * cp + dz2, :, at])
                pre_embed[cp, rows, at] = pre
                act = (pre * sigmoid(pre)).astype(BF16)
                hidden[cp, 2 * dx2, rows, :] = act[:, :256]
                hidden[cp, 2 * dx2 + 1, rows, :] = act[:, 256:]
        pre = mm(conv_turned[...], hidden[cp].reshape(1024, 256))
        pre_conv[cp] = pre
        act = pre * sigmoid(pre)
        sums = sums + act[:, :128] + act[:, 128:]
    pick = jnp.where(iota((8, 128), 1) // 8 % 4 == iota((8, 128), 0), 1.0, 0.0)
    total = lax.dot_general(pick, sums, NT, precision=lax.Precision.HIGHEST, preferred_element_type=F32)
    for load in others[2:]:
        load.wait()
    block[:, pl.ds(0, 512)] = prior[...]
    block[:, pl.ds(512, 512)] = recon[...]
    block[:, pl.ds(1024, 256)] = (total[:4] / 256.0).astype(BF16)


def pair_kernel(queries, query_square, keys):
    inner = mm_nt(queries, keys)
    key_float = keys.astype(F32)
    count = keys.shape[0]
    key_square = jnp.sum(key_float * key_float, axis=1, keepdims=True)
    key_row = jnp.transpose(jnp.broadcast_to(key_square, (count, 128)))[:1]
    kern = jnp.exp(-(query_square + key_row - 2.0 * inner) / keys.shape[1])
    return jnp.sum(kern, axis=1, keepdims=True), mm(kern.astype(BF16), keys)


def backward_kernel(
    sizes, gathered, hidden, pre_conv, w_head,
    keep, send, grads, grad_head,
    ordered, head_full
):
    dp, fsdp = sizes
    devices = dp * fsdp
    dp_here, fsdp_here = lax.axis_index("dp"), lax.axis_index("fsdp")
    here = dp_here * fsdp + fsdp_here
    for owner in range(devices):
        ordered[owner] = gathered[owner].astype(F32)
    samples = ordered.shape[1]
    count = devices * samples
    full = ordered[...].reshape(count, ordered.shape[2])
    prior = full[:, :512].astype(BF16)
    recon = full[:, 512:1024]
    pooled = full[:, 1024:].astype(BF16)
    latent = mm(pooled, w_head[...]).astype(BF16)
    latent_float = latent.astype(F32)
    square = jnp.sum(latent_float * latent_float, axis=1, keepdims=True)
    self_sum, self_mix = pair_kernel(latent, square, latent)
    cross_sum, cross_mix = pair_kernel(latent, square, prior)
    pull = -32.0 / count * ((self_sum - cross_sum) * latent_float - self_mix + cross_mix)
    cotangent = (recon + pull).astype(BF16)
    turned = jnp.transpose(full[:, 1024:]).astype(BF16)
    head_full[...] = mm(turned, cotangent)
    share = grad_head.shape[0]
    start = pl.multiple_of(fsdp_here * share, share)
    grad_head[...] = head_full[pl.ds(start, share), :]

    lane_sample = iota((128, count), 0) // 8 % 4 + samples * here
    pick = jnp.where(lane_sample == iota((128, count), 1), 1.0, 0.0).astype(BF16)
    lanes = mm(pick, cotangent).astype(BF16)
    back_pool = mm_nt(w_head[...], lanes) / 256.0
    back_pool = jnp.concatenate([back_pool, back_pool], axis=1)
    conv_total = None
    for cp in range(4):
        grads[cp] = (back_pool * silu_slope(pre_conv[cp])).astype(BF16)
        term = mm_nt(hidden[cp].reshape(1024, 256), grads[cp])
        conv_total = term if cp == 0 else conv_total + term
    core_zero = lax.rem(dp_here, 2) == 0
    rows = keep.shape[1]
    for f in range(fsdp):
        at = 2 * f * rows
        first, second = conv_total[at : at + rows], conv_total[at + rows : at + 2 * rows]
        keep[f] = jnp.where(core_zero, first, second)
        send[f] = jnp.where(core_zero, second, first)


def embed_kernel(grads, w_conv, pre_embed, one_hot, embed_out):
    embed = None
    ones = jnp.ones((16, 1024), BF16)
    for cp in range(4):
        signals = []
        for dx2 in range(2):
            back_rows = mm(w_conv[pl.ds(dx2 * 512, 512), :], grads[cp])
            back_rows = jnp.concatenate([back_rows[:256], back_rows[256:]], axis=1)
            signals.append((back_rows * silu_slope(pre_embed[cp, :, pl.ds(dx2 * 512, 512)])).astype(BF16))
        signal = jnp.concatenate(signals, axis=1)
        for dz2 in range(2):
            rows = jnp.concatenate([one_hot[2 * cp + dz2, pl.ds(0, 192), :], ones], axis=0)
            term = mm_nt(rows, signal[dz2 * 128 : dz2 * 128 + 128])
            embed = term if embed is None else embed + term
    shares = embed_out.shape[0]
    depth = 64 // shares
    half = 3 * depth // 2
    embed_out[...] = jnp.zeros(embed_out.shape, F32)
    for f in range(shares):
        dx, at = f * 4 // shares, f * depth % 16
        share = jnp.concatenate([embed[dx * 48 + k * 16 + at :][:depth] for k in range(3)], axis=0)
        for side in range(2):
            embed_out[f, pl.ds(0, half), pl.ds(side * 128, 128)] = share[side * half : (side + 1) * half]
        embed_out[f, pl.ds(embed_out.shape[1] - 8, 8), pl.ds(0, 128)] = embed[192:200]


def exponent_of(part):
    top = jnp.abs(part)
    while top.ndim > 2:
        top = jnp.max(top, axis=0)
    top = jnp.max(jnp.max(top, axis=0, keepdims=True), axis=1, keepdims=True)
    return jnp.clip(jnp.floor(jnp.log2(jnp.maximum(top, 1e-37))) - 14.0, -124.0, 114.0)


def store_coded(coded, part, conv_rows):
    store_scaled(coded, part, (exponent_of(part[:conv_rows]), exponent_of(part[conv_rows:])), conv_rows)


def store_scaled(coded, part, steps, conv_rows):
    last = part.shape[0] - 8
    coded[pl.ds(0, conv_rows), :] = part[:conv_rows] * jnp.exp2(-steps[0])
    coded[pl.ds(conv_rows, last - conv_rows), :] = part[conv_rows:last] * jnp.exp2(-steps[1])
    total = part[last:, :128] * jnp.exp2(-steps[1])
    high = total.astype(BF16).astype(F32)
    row = iota((8, 256), 0)
    tail = jnp.where(row == 1, steps[0], steps[1])
    coded[pl.ds(last, 8), :] = jnp.where(row == 0, jnp.concatenate([high, total - high], axis=1), tail)


def load_coded(coded, conv_rows):
    last = coded.shape[0] - 8
    embed_scale = jnp.exp2(coded[pl.ds(last + 2, 1), :])
    total = coded[pl.ds(last, 8), pl.ds(0, 128)] + coded[pl.ds(last, 8), pl.ds(128, 128)]
    total = jnp.where(iota((8, 256), 0) == 0, jnp.concatenate([total, jnp.zeros((8, 128), F32)], axis=1), 0.0)
    embed = jnp.concatenate([coded[pl.ds(conv_rows, last - conv_rows), :], total], axis=0) * embed_scale
    return jnp.concatenate([coded[pl.ds(0, conv_rows), :] * jnp.exp2(coded[pl.ds(last + 1, 1), :]), embed], axis=0)


def scale_kernel(keep, other, embed, own, *coded):
    held = keep[...] + other[...]
    steps = exponent_of(held), exponent_of(embed[...])
    here = lax.axis_index("fsdp")

    def share(z):
        return jnp.concatenate([keep[z] + other[z], embed[z]], axis=0)

    own[...] = share(here)
    for place, target in enumerate(coded):
        store_scaled(target, share(here ^ (place + 1)), steps, keep.shape[1])


def first_sum_kernel(conv_rows, own, *refs):
    *received, coded = refs
    total = own[...]
    for part in received:
        total = total + load_coded(part, conv_rows)
    store_coded(coded, total, conv_rows)


def next_sum_kernel(conv_rows, mine, other, total, *coded):
    summed = load_coded(mine, conv_rows) + load_coded(other, conv_rows)
    total[...] = summed
    if coded:
        store_coded(coded[0], summed, conv_rows)


def output_kernel(own, other, grad_embed, grad_conv):
    conv_rows, count = grad_conv.shape[0] // 2, grad_embed.shape[0]
    core_zero = lax.rem(lax.axis_index("dp"), 2) == 0
    grad_conv[pl.ds(0, conv_rows), :] = jnp.where(core_zero, own[pl.ds(0, conv_rows), :], other[pl.ds(0, conv_rows), :])
    grad_conv[pl.ds(conv_rows, conv_rows), :] = jnp.where(
        core_zero, other[pl.ds(0, conv_rows), :], own[pl.ds(0, conv_rows), :]
    )
    half, depth = 3 * count // 8, count // LEVELS
    embed = own[pl.ds(conv_rows, half), :] + other[pl.ds(conv_rows, half), :]
    embed = jnp.concatenate([embed[:, :128], embed[:, 128:]], axis=0)
    last = own.shape[0] - 8
    total = own[pl.ds(last, 1), pl.ds(0, 128)] + other[pl.ds(last, 1), pl.ds(0, 128)]
    fourth = total - (embed[:depth] + embed[depth : 2 * depth] + embed[2 * depth :])
    embed = jnp.concatenate([embed, fourth], axis=0)
    row, lane = iota((count, count), 0), iota((count, count), 1)
    order = jnp.where(lane == row % LEVELS * depth + row // LEVELS, 1.0, 0.0).astype(BF16)
    result = None
    for _ in range(3):
        term = embed.astype(BF16)
        embed = embed - term.astype(F32)
        result = mm(order, term) if result is None else result + mm(order, term)
    grad_embed[...] = result


VMEM = pl.BlockSpec(memory_space=pltpu.VMEM)
HBM = pl.BlockSpec(memory_space=pltpu.HBM)
SAVED = (
    ((8, 256, 1024), BF16),
    ((4, 256, 1024), F32),
    ((4, 4, 256, 256), BF16),
    ((4, 256, 256), F32),
)


def forward(facies, prior_draws, recon_grad, w_embed, w_conv, w_head):
    samples = facies.shape[0]
    latent_width = prior_draws.shape[1]
    rows, lanes = samples * PATCH_X, PATCH_Y * PATCH_Z
    operands = (facies.reshape(rows, lanes), prior_draws, recon_grad, w_embed, w_conv, w_head)
    return pl.pallas_call(
        forward_kernel,
        out_shape=(pltpu.VMEM((samples, 2 * latent_width + 256), BF16),)
        + tuple(pltpu.VMEM(shape, kind) for shape, kind in SAVED)
        + (pltpu.VMEM(w_conv.shape, BF16), pltpu.VMEM(w_head.shape, BF16)),
        in_specs=[HBM] * 6,
        out_specs=(VMEM,) * 7,
        scratch_shapes=[
            pltpu.VMEM((lanes // 128, rows, 128), jnp.int32),
            pltpu.VMEM(prior_draws.shape, BF16),
            pltpu.VMEM(recon_grad.shape, BF16),
            pltpu.VMEM(w_embed.shape, BF16),
            pltpu.VMEM((128, 256), BF16),
            pltpu.VMEM((256, 1024), BF16),
            pltpu.SemaphoreType.DMA((lanes // 128 + 5,)),
        ],
        compiler_params=pltpu.CompilerParams(vmem_limit_bytes=30 * 2**20),
        name="forward",
    )(*(pltpu.with_memory_space_constraint(operand, pltpu.HBM) for operand in operands))


def backward(sizes, gathered, hidden, pre_conv, w_head):
    dp, fsdp = sizes
    devices, samples, width = gathered.shape
    payload = pltpu.VMEM((fsdp, 1024 // fsdp // 2, 256), F32)
    return pl.pallas_call(
        lambda *refs: backward_kernel(sizes, *refs),
        out_shape=(
            payload, payload, pltpu.VMEM((4, 256, 256), BF16), jax.ShapeDtypeStruct((256 // fsdp, 512), F32)
        ),
        in_specs=[VMEM] * 4,
        out_specs=(VMEM,) * 4,
        scratch_shapes=[pltpu.VMEM((devices, samples, width), F32), pltpu.VMEM((256, 512), F32)],
        compiler_params=pltpu.CompilerParams(vmem_limit_bytes=24 * 2**20),
        name="backward",
    )(gathered, hidden, pre_conv, w_head)


def embed_gradient(fsdp, grads, w_conv, pre_embed, one_hot):
    return pl.pallas_call(
        embed_kernel,
        out_shape=pltpu.VMEM((fsdp, (96 // fsdp + 7) // 8 * 8 + 8, 256), F32),
        in_specs=[VMEM] * 4,
        out_specs=VMEM,
        compiler_params=pltpu.CompilerParams(vmem_limit_bytes=24 * 2**20),
        cost_estimate=pl.CostEstimate(flops=16 * 10**8, bytes_accessed=10 * 2**20, transcendentals=0),
        name="embed_gradient",
    )(grads, w_conv, pre_embed, one_hot)


def place_of(x, core, z, fsdp):
    return (2 * x + core) * fsdp + z


def exchange(block, dp, fsdp, flip_x, flip_core, flip_z):
    pairs = []
    for x in range(dp // 2):
        for core in range(2):
            for z in range(fsdp):
                pairs.append((place_of(x, core, z, fsdp), place_of(x ^ flip_x, core ^ flip_core, z ^ flip_z, fsdp)))
    return lax.ppermute(block, GROUP, pairs)


def gather_blocks(block, devices):
    copies = jnp.broadcast_to(block[None], (devices,) + block.shape)
    return lax.all_to_all(copies, GROUP, 0, 0, tiled=True)


def local_kernel(kernel, outs, name, *operands):
    return pl.pallas_call(
        kernel,
        out_shape=outs,
        in_specs=[VMEM] * len(operands),
        out_specs=(VMEM,) * len(outs),
        compiler_params=pltpu.CompilerParams(vmem_limit_bytes=16 * 2**20),
        name=name,
    )(*operands)


def to_half(coded):
    rounded = lax.reduce_precision(coded, exponent_bits=5, mantissa_bits=10)
    return rounded, rounded.astype(jnp.float16)


def reduce_to_owner(keep, other, embed, dp, fsdp):
    conv_rows, width = keep.shape[1:]
    rows = conv_rows + embed.shape[1]
    plain = jax.ShapeDtypeStruct((rows, width), F32)
    own, *coded = local_kernel(scale_kernel, (plain,) + (plain,) * (fsdp - 1), "scale", keep, other, embed)
    received = [
        exchange(to_half(part)[1], dp, fsdp, 0, 0, place + 1).astype(F32) for place, part in enumerate(coded)
    ]
    (coded,) = local_kernel(functools.partial(first_sum_kernel, conv_rows), (plain,), "sum_z", own, *received)
    flip = 1
    while flip < dp // 2:
        mine, sent = to_half(coded)
        other = exchange(sent, dp, fsdp, flip, 0, 0).astype(F32)
        flip *= 2
        outs = (plain,) * (2 if flip < dp // 2 else 1)
        total, *rest = local_kernel(functools.partial(next_sum_kernel, conv_rows), outs, "sum_x", mine, other)
        coded = rest[0] if rest else None
    return total, exchange(total, dp, fsdp, 0, 1, 0)


def shards(facies, prior_draws, recon_grad, w_embed, w_conv, w_head):
    dp, fsdp = lax.axis_size("dp"), lax.axis_size("fsdp")
    block, one_hot, pre_embed, hidden, pre_conv, w_conv, w_head = forward(
        facies, prior_draws, recon_grad, w_embed, w_conv, w_head
    )
    gathered = gather_blocks(block, dp * fsdp)
    keep, send, grads, grad_head = backward((dp, fsdp), gathered, hidden, pre_conv, w_head)
    received = exchange(send, dp, fsdp, 0, 1, 0)
    embed = embed_gradient(fsdp, grads, w_conv, pre_embed, one_hot)
    own, other = reduce_to_owner(keep, received, embed, dp, fsdp)
    grad_embed, grad_conv = pl.pallas_call(
        output_kernel,
        out_shape=(
            jax.ShapeDtypeStruct((256 // fsdp, 128), F32),
            jax.ShapeDtypeStruct((1024 // fsdp, 256), F32),
        ),
        in_specs=[VMEM] * 2,
        out_specs=(VMEM,) * 2,
        compiler_params=pltpu.CompilerParams(vmem_limit_bytes=16 * 2**20),
        name="outputs",
    )(own, other)
    return (grad_embed, grad_conv, grad_head)


def solution(mesh):
    return jax.shard_map(
        shards,
        mesh=mesh,
        in_specs=(
            P(("groups", "dp", "fsdp"), None, None),
            P(("groups", "dp", "fsdp"), None),
            P(("groups", "dp", "fsdp"), None),
            P(),
            P(),
            P(),
        ),
        out_specs=(
            P(("groups", "fsdp"), None),
            P(("groups", "fsdp"), None),
            P(("groups", "fsdp"), None),
        ),
        check_vma=False,
    )
```

```python
import functools

import jax
import jax.numpy as jnp
from jax import lax
from jax.experimental import pallas as pl
from jax.experimental.pallas import tpu as pltpu
from jax.sharding import PartitionSpec as P

PATCH_X = 64
PATCH_Y = 64
PATCH_Z = 32
LEVELS = 4
GROUP = ("dp", "fsdp")
NT = (((1,), (1,)), ((), ()))
F32 = jnp.float32
BF16 = jnp.bfloat16


def iota(shape, dim):
    return lax.broadcasted_iota(jnp.int32, shape, dim)


def mm(left, right):
    return jnp.dot(left, right, preferred_element_type=F32)


def mm_nt(left, right):
    return lax.dot_general(left, right, NT, preferred_element_type=F32)


def turned_weights(w_embed):
    turned = jnp.transpose(w_embed.astype(F32)).astype(BF16)
    row, lane = iota((256, 256), 0), iota((256, 256), 1)
    dx, k = row // 64, row % 4
    same = lane == jnp.where(k < 3, dx * 48 + k * 16, 192 + dx * 16) + row // 4 % 16
    return mm(turned, jnp.where(same, 1.0, 0.0).astype(BF16)).astype(BF16)


def sigmoid(value):
    return pltpu.reciprocal(1.0 + jnp.exp2(value * -1.4426950408889634), approx=True)


def silu_slope(value):
    gate = sigmoid(value)
    return gate * (1.0 + value * (1.0 - gate))


def forward_kernel(
    facies_hbm, prior_hbm, recon_hbm, w_embed_hbm, w_conv_hbm, w_head_hbm,
    block, one_hot, pre_embed, hidden, pre_conv, w_conv, w_head,
    facies, prior, recon, w_embed, packed, conv_turned, sem
):
    blocks = facies.shape[0]
    loads = [
        pltpu.make_async_copy(facies_hbm.at[:, pl.ds(b * 128, 128)], facies.at[b], sem.at[b]) for b in range(blocks)
    ]
    others = []
    for source, target in (
        (w_embed_hbm, w_embed), (w_conv_hbm, w_conv), (prior_hbm, prior), (recon_hbm, recon), (w_head_hbm, w_head)
    ):
        others.append(pltpu.make_async_copy(source, target, sem.at[blocks + len(others)]))
    for load in others[:2] + loads:
        load.start()
    others[0].wait()
    packed[...] = turned_weights(w_embed[...])
    others[1].wait()
    conv_turned[...] = jnp.transpose(w_conv[...].astype(F32)).astype(BF16)
    low = iota((8, 256), 0) < 4
    for half in range(2):
        for load in loads[half * blocks // 2 : (half + 1) * blocks // 2]:
            load.wait()
        if half == 0:
            for load in others[2:]:
                load.start()
        for t in range(8):
            dx2, dx = t // 4, t % 4
            rows = [
                facies[2 * b2 + dy2, pl.ds(t, 32, stride=8), :]
                for dy2 in range(2)
                for b2 in range(4 * half, 4 * half + 4)
            ]
            turned = jnp.transpose(jnp.concatenate(rows, axis=0).astype(F32))
            for cp in range(4):
                part = [turned[dy * 32 + cp * 8 : dy * 32 + cp * 8 + 8] for dy in range(4)]
                swapped = [pltpu.roll(piece, 4, 0) for piece in part]
                for dz2 in range(2):
                    pieces = [
                        jnp.where(low, part[dy], swapped[dy + 1]) if dz2 == 0 else jnp.where(low, swapped[dy], part[dy + 1])
                        for dy in (0, 2)
                    ]
                    cells = jnp.concatenate(pieces, axis=0).astype(BF16)
                    for k in range(LEVELS):
                        hot = jnp.where(cells == BF16(k), BF16(1.0), BF16(0.0))
                        first = dx * 48 + k * 16 if k < 3 else 192 + dx * 16
                        for dy2 in range(2):
                            at = (2 * dx2 + dy2) * 256 + half * 128
                            one_hot[2 * cp + dz2, pl.ds(first, 16), pl.ds(at, 128)] = hot[:, dy2 * 128 : dy2 * 128 + 128]
    sums = jnp.zeros((256, 128), F32)
    for cp in range(4):
        for dz2 in range(2):
            rows = pl.ds(dz2 * 128, 128)
            for dx2 in range(2):
                at = pl.ds(dx2 * 512, 512)
                pre = mm(packed[...], one_hot[2 * cp + dz2, :, at])
                pre_embed[cp, rows, at] = pre
                act = (pre * sigmoid(pre)).astype(BF16)
                hidden[cp, 2 * dx2, rows, :] = act[:, :256]
                hidden[cp, 2 * dx2 + 1, rows, :] = act[:, 256:]
        pre = mm(conv_turned[...], hidden[cp].reshape(1024, 256))
        pre_conv[cp] = pre
        act = pre * sigmoid(pre)
        sums = sums + act[:, :128] + act[:, 128:]
    pick = jnp.where(iota((8, 128), 1) // 8 % 4 == iota((8, 128), 0), 1.0, 0.0)
    total = lax.dot_general(pick, sums, NT, precision=lax.Precision.HIGHEST, preferred_element_type=F32)
    for load in others[2:]:
        load.wait()
    block[:, pl.ds(0, 512)] = prior[...]
    block[:, pl.ds(512, 512)] = recon[...]
    block[:, pl.ds(1024, 256)] = (total[:4] / 256.0).astype(BF16)


def pair_kernel(queries, query_square, keys):
    inner = mm_nt(queries, keys)
    key_float = keys.astype(F32)
    count = keys.shape[0]
    key_square = jnp.sum(key_float * key_float, axis=1, keepdims=True)
    key_row = jnp.transpose(jnp.broadcast_to(key_square, (count, 128)))[:1]
    kern = jnp.exp(-(query_square + key_row - 2.0 * inner) / keys.shape[1])
    return jnp.sum(kern, axis=1, keepdims=True), mm(kern.astype(BF16), keys)


def backward_kernel(
    sizes, gathered, gathered_other, hidden, pre_conv, w_head,
    keep, send, grads, grad_head,
    ordered, head_full
):
    dp, fsdp = sizes
    devices = dp * fsdp
    dp_here, fsdp_here = lax.axis_index("dp"), lax.axis_index("fsdp")
    here = (lax.rem(dp_here, 2) * (dp // 2) + dp_here // 2) * fsdp + fsdp_here
    core = lax.rem(dp_here, 2)
    for place in range(devices // 2):
        ordered[core * (devices // 2) + place] = gathered[place].astype(F32)
        ordered[(1 - core) * (devices // 2) + place] = gathered_other[place].astype(F32)
    samples = ordered.shape[1]
    count = devices * samples
    full = ordered[...].reshape(count, ordered.shape[2])
    prior = full[:, :512].astype(BF16)
    recon = full[:, 512:1024]
    pooled = full[:, 1024:].astype(BF16)
    latent = mm(pooled, w_head[...]).astype(BF16)
    latent_float = latent.astype(F32)
    square = jnp.sum(latent_float * latent_float, axis=1, keepdims=True)
    self_sum, self_mix = pair_kernel(latent, square, latent)
    cross_sum, cross_mix = pair_kernel(latent, square, prior)
    pull = -32.0 / count * ((self_sum - cross_sum) * latent_float - self_mix + cross_mix)
    cotangent = (recon + pull).astype(BF16)
    turned = jnp.transpose(full[:, 1024:]).astype(BF16)
    head_full[...] = mm(turned, cotangent)
    share = grad_head.shape[0]
    start = pl.multiple_of(fsdp_here * share, share)
    grad_head[...] = head_full[pl.ds(start, share), :]

    lane_sample = iota((128, count), 0) // 8 % 4 + samples * here
    pick = jnp.where(lane_sample == iota((128, count), 1), 1.0, 0.0).astype(BF16)
    lanes = mm(pick, cotangent).astype(BF16)
    back_pool = mm_nt(w_head[...], lanes) / 256.0
    back_pool = jnp.concatenate([back_pool, back_pool], axis=1)
    conv_total = None
    for cp in range(4):
        grads[cp] = (back_pool * silu_slope(pre_conv[cp])).astype(BF16)
        term = mm_nt(hidden[cp].reshape(1024, 256), grads[cp])
        conv_total = term if cp == 0 else conv_total + term
    core_zero = lax.rem(dp_here, 2) == 0
    rows = keep.shape[1]
    for f in range(fsdp):
        at = 2 * f * rows
        first, second = conv_total[at : at + rows], conv_total[at + rows : at + 2 * rows]
        keep[f] = jnp.where(core_zero, first, second)
        send[f] = jnp.where(core_zero, second, first)


def embed_kernel(grads, w_conv, pre_embed, one_hot, embed_out):
    embed = None
    ones = jnp.ones((16, 1024), BF16)
    for cp in range(4):
        signals = []
        for dx2 in range(2):
            back_rows = mm(w_conv[pl.ds(dx2 * 512, 512), :], grads[cp])
            back_rows = jnp.concatenate([back_rows[:256], back_rows[256:]], axis=1)
            signals.append((back_rows * silu_slope(pre_embed[cp, :, pl.ds(dx2 * 512, 512)])).astype(BF16))
        signal = jnp.concatenate(signals, axis=1)
        for dz2 in range(2):
            rows = jnp.concatenate([one_hot[2 * cp + dz2, pl.ds(0, 192), :], ones], axis=0)
            term = mm_nt(rows, signal[dz2 * 128 : dz2 * 128 + 128])
            embed = term if embed is None else embed + term
    shares = embed_out.shape[0]
    depth = 64 // shares
    half = 3 * depth // 2
    embed_out[...] = jnp.zeros(embed_out.shape, F32)
    for f in range(shares):
        dx, at = f * 4 // shares, f * depth % 16
        share = jnp.concatenate([embed[dx * 48 + k * 16 + at :][:depth] for k in range(3)], axis=0)
        for side in range(2):
            embed_out[f, pl.ds(0, half), pl.ds(side * 128, 128)] = share[side * half : (side + 1) * half]
        embed_out[f, pl.ds(embed_out.shape[1] - 8, 8), pl.ds(0, 128)] = embed[192:200]


def exponent_of(part):
    top = jnp.abs(part)
    while top.ndim > 2:
        top = jnp.max(top, axis=0)
    top = jnp.max(jnp.max(top, axis=0, keepdims=True), axis=1, keepdims=True)
    return jnp.clip(jnp.floor(jnp.log2(jnp.maximum(top, 1e-37))) - 14.0, -124.0, 114.0)


def store_coded(coded, part, conv_rows):
    store_scaled(coded, part, (exponent_of(part[:conv_rows]), exponent_of(part[conv_rows:])), conv_rows)


def store_scaled(coded, part, steps, conv_rows):
    last = part.shape[0] - 8
    coded[pl.ds(0, conv_rows), :] = part[:conv_rows] * jnp.exp2(-steps[0])
    coded[pl.ds(conv_rows, last - conv_rows), :] = part[conv_rows:last] * jnp.exp2(-steps[1])
    total = part[last:, :128] * jnp.exp2(-steps[1])
    high = total.astype(BF16).astype(F32)
    row = iota((8, 256), 0)
    tail = jnp.where(row == 1, steps[0], steps[1])
    coded[pl.ds(last, 8), :] = jnp.where(row == 0, jnp.concatenate([high, total - high], axis=1), tail)


def load_coded(coded, conv_rows):
    last = coded.shape[0] - 8
    embed_scale = jnp.exp2(coded[pl.ds(last + 2, 1), :])
    total = coded[pl.ds(last, 8), pl.ds(0, 128)] + coded[pl.ds(last, 8), pl.ds(128, 128)]
    total = jnp.where(iota((8, 256), 0) == 0, jnp.concatenate([total, jnp.zeros((8, 128), F32)], axis=1), 0.0)
    embed = jnp.concatenate([coded[pl.ds(conv_rows, last - conv_rows), :], total], axis=0) * embed_scale
    return jnp.concatenate([coded[pl.ds(0, conv_rows), :] * jnp.exp2(coded[pl.ds(last + 1, 1), :]), embed], axis=0)


def scale_kernel(keep, other, embed, own, *coded):
    held = keep[...] + other[...]
    steps = exponent_of(held), exponent_of(embed[...])
    here = lax.axis_index("fsdp")

    def share(z):
        return jnp.concatenate([keep[z] + other[z], embed[z]], axis=0)

    own[...] = share(here)
    for place, target in enumerate(coded):
        store_scaled(target, share(here ^ (place + 1)), steps, keep.shape[1])


def first_sum_kernel(conv_rows, own, *refs):
    *received, coded = refs
    total = own[...]
    for part in received:
        total = total + load_coded(part, conv_rows)
    store_coded(coded, total, conv_rows)


def next_sum_kernel(conv_rows, mine, other, total, *coded):
    summed = load_coded(mine, conv_rows) + load_coded(other, conv_rows)
    total[...] = summed
    if coded:
        store_coded(coded[0], summed, conv_rows)


def output_kernel(own, other, head, grad_embed, grad_conv, grad_head):
    grad_head[...] = head[...]
    conv_rows, count = grad_conv.shape[0] // 2, grad_embed.shape[0]
    core_zero = lax.rem(lax.axis_index("dp"), 2) == 0
    grad_conv[pl.ds(0, conv_rows), :] = jnp.where(core_zero, own[pl.ds(0, conv_rows), :], other[pl.ds(0, conv_rows), :])
    grad_conv[pl.ds(conv_rows, conv_rows), :] = jnp.where(
        core_zero, other[pl.ds(0, conv_rows), :], own[pl.ds(0, conv_rows), :]
    )
    half, depth = 3 * count // 8, count // LEVELS
    embed = own[pl.ds(conv_rows, half), :] + other[pl.ds(conv_rows, half), :]
    embed = jnp.concatenate([embed[:, :128], embed[:, 128:]], axis=0)
    last = own.shape[0] - 8
    total = own[pl.ds(last, 1), pl.ds(0, 128)] + other[pl.ds(last, 1), pl.ds(0, 128)]
    fourth = total - (embed[:depth] + embed[depth : 2 * depth] + embed[2 * depth :])
    embed = jnp.concatenate([embed, fourth], axis=0)
    row, lane = iota((count, count), 0), iota((count, count), 1)
    order = jnp.where(lane == row % LEVELS * depth + row // LEVELS, 1.0, 0.0).astype(BF16)
    result = None
    for _ in range(3):
        term = embed.astype(BF16)
        embed = embed - term.astype(F32)
        result = mm(order, term) if result is None else result + mm(order, term)
    grad_embed[...] = result


VMEM = pl.BlockSpec(memory_space=pltpu.VMEM)
HBM = pl.BlockSpec(memory_space=pltpu.HBM)
SAVED = (
    ((8, 256, 1024), BF16),
    ((4, 256, 1024), F32),
    ((4, 4, 256, 256), BF16),
    ((4, 256, 256), F32),
)


def forward(facies, prior_draws, recon_grad, w_embed, w_conv, w_head):
    samples = facies.shape[0]
    latent_width = prior_draws.shape[1]
    rows, lanes = samples * PATCH_X, PATCH_Y * PATCH_Z
    operands = (facies.reshape(rows, lanes), prior_draws, recon_grad, w_embed, w_conv, w_head)
    return pl.pallas_call(
        forward_kernel,
        out_shape=(pltpu.VMEM((samples, 2 * latent_width + 256), BF16),)
        + tuple(pltpu.VMEM(shape, kind) for shape, kind in SAVED)
        + (pltpu.VMEM(w_conv.shape, BF16), pltpu.VMEM(w_head.shape, BF16)),
        in_specs=[HBM] * 6,
        out_specs=(VMEM,) * 7,
        scratch_shapes=[
            pltpu.VMEM((lanes // 128, rows, 128), jnp.int32),
            pltpu.VMEM(prior_draws.shape, BF16),
            pltpu.VMEM(recon_grad.shape, BF16),
            pltpu.VMEM(w_embed.shape, BF16),
            pltpu.VMEM((128, 256), BF16),
            pltpu.VMEM((256, 1024), BF16),
            pltpu.SemaphoreType.DMA((lanes // 128 + 5,)),
        ],
        compiler_params=pltpu.CompilerParams(vmem_limit_bytes=30 * 2**20),
        name="forward",
    )(*(pltpu.with_memory_space_constraint(operand, pltpu.HBM) for operand in operands))


def backward(sizes, gathered, hidden, pre_conv, w_head):
    dp, fsdp = sizes
    _, samples, width = gathered[0].shape
    devices = dp * fsdp
    payload = pltpu.VMEM((fsdp, 1024 // fsdp // 2, 256), F32)
    return pl.pallas_call(
        lambda *refs: backward_kernel(sizes, *refs),
        out_shape=(
            payload, payload, pltpu.VMEM((4, 256, 256), BF16), pltpu.VMEM((256 // fsdp, 512), F32)
        ),
        in_specs=[VMEM] * 5,
        out_specs=(VMEM,) * 4,
        scratch_shapes=[pltpu.VMEM((devices, samples, width), F32), pltpu.VMEM((256, 512), F32)],
        compiler_params=pltpu.CompilerParams(vmem_limit_bytes=24 * 2**20),
        name="backward",
    )(*gathered, hidden, pre_conv, w_head)


def embed_gradient(fsdp, grads, w_conv, pre_embed, one_hot):
    return pl.pallas_call(
        embed_kernel,
        out_shape=pltpu.VMEM((fsdp, (96 // fsdp + 7) // 8 * 8 + 8, 256), F32),
        in_specs=[VMEM] * 4,
        out_specs=VMEM,
        compiler_params=pltpu.CompilerParams(vmem_limit_bytes=24 * 2**20),
        cost_estimate=pl.CostEstimate(flops=16 * 10**8, bytes_accessed=10 * 2**20, transcendentals=0),
        name="embed_gradient",
    )(grads, w_conv, pre_embed, one_hot)


def place_of(x, core, z, fsdp):
    return (2 * x + core) * fsdp + z


def exchange(block, dp, fsdp, flip_x, flip_core, flip_z):
    pairs = []
    for x in range(dp // 2):
        for core in range(2):
            for z in range(fsdp):
                pairs.append((place_of(x, core, z, fsdp), place_of(x ^ flip_x, core ^ flip_core, z ^ flip_z, fsdp)))
    return lax.ppermute(block, GROUP, pairs)


def gather_blocks(block, dp, fsdp):
    peers = dp // 2 * fsdp
    groups = [[place_of(x, core, z, fsdp) for x in range(dp // 2) for z in range(fsdp)] for core in range(2)]
    copies = jnp.broadcast_to(block[None], (peers,) + block.shape)
    own = lax.all_to_all(copies, GROUP, 0, 0, axis_index_groups=groups, tiled=True)
    return own, exchange(own, dp, fsdp, 0, 1, 0)


def local_kernel(kernel, outs, name, *operands):
    return pl.pallas_call(
        kernel,
        out_shape=outs,
        in_specs=[VMEM] * len(operands),
        out_specs=(VMEM,) * len(outs),
        compiler_params=pltpu.CompilerParams(vmem_limit_bytes=16 * 2**20),
        name=name,
    )(*operands)


def to_half(coded):
    rounded = lax.reduce_precision(coded, exponent_bits=5, mantissa_bits=10)
    return rounded, rounded.astype(jnp.float16)


def reduce_to_owner(keep, other, embed, dp, fsdp):
    conv_rows, width = keep.shape[1:]
    rows = conv_rows + embed.shape[1]
    plain = jax.ShapeDtypeStruct((rows, width), F32)
    own, *coded = local_kernel(scale_kernel, (plain,) + (plain,) * (fsdp - 1), "scale", keep, other, embed)
    received = [
        exchange(to_half(part)[1], dp, fsdp, 0, 0, place + 1).astype(F32) for place, part in enumerate(coded)
    ]
    (coded,) = local_kernel(functools.partial(first_sum_kernel, conv_rows), (plain,), "sum_z", own, *received)
    flip = 1
    while flip < dp // 2:
        mine, sent = to_half(coded)
        other = exchange(sent, dp, fsdp, flip, 0, 0).astype(F32)
        flip *= 2
        outs = (plain,) * (2 if flip < dp // 2 else 1)
        total, *rest = local_kernel(functools.partial(next_sum_kernel, conv_rows), outs, "sum_x", mine, other)
        coded = rest[0] if rest else None
    return total, exchange(total, dp, fsdp, 0, 1, 0)


def shards(facies, prior_draws, recon_grad, w_embed, w_conv, w_head):
    dp, fsdp = lax.axis_size("dp"), lax.axis_size("fsdp")
    block, one_hot, pre_embed, hidden, pre_conv, w_conv, w_head = forward(
        facies, prior_draws, recon_grad, w_embed, w_conv, w_head
    )
    gathered = gather_blocks(block, dp, fsdp)
    keep, send, grads, grad_head = backward((dp, fsdp), gathered, hidden, pre_conv, w_head)
    received = exchange(send, dp, fsdp, 0, 1, 0)
    embed = embed_gradient(fsdp, grads, w_conv, pre_embed, one_hot)
    own, other = reduce_to_owner(keep, received, embed, dp, fsdp)
    outs = (
        jax.ShapeDtypeStruct((256 // fsdp, 128), F32),
        jax.ShapeDtypeStruct((1024 // fsdp, 256), F32),
        jax.ShapeDtypeStruct(grad_head.shape, F32),
    )
    return local_kernel(output_kernel, outs, "outputs", own, other, grad_head)


def solution(mesh):
    return jax.shard_map(
        shards,
        mesh=mesh,
        in_specs=(
            P(("groups", "dp", "fsdp"), None, None),
            P(("groups", "dp", "fsdp"), None),
            P(("groups", "dp", "fsdp"), None),
            P(),
            P(),
            P(),
        ),
        out_specs=(
            P(("groups", "fsdp"), None),
            P(("groups", "fsdp"), None),
            P(("groups", "fsdp"), None),
        ),
        check_vma=False,
    )
```

```python
import functools

import jax
import jax.numpy as jnp
from jax import lax
from jax.experimental import pallas as pl
from jax.experimental.pallas import tpu as pltpu
from jax.sharding import PartitionSpec as P

PATCH_X = 64
PATCH_Y = 64
PATCH_Z = 32
LEVELS = 4
GROUP = ("dp", "fsdp")
NT = (((1,), (1,)), ((), ()))
F32 = jnp.float32
BF16 = jnp.bfloat16


def iota(shape, dim):
    return lax.broadcasted_iota(jnp.int32, shape, dim)


def mm(left, right):
    return jnp.dot(left, right, preferred_element_type=F32)


def mm_nt(left, right):
    return lax.dot_general(left, right, NT, preferred_element_type=F32)


def turned_weights(w_embed):
    turned = jnp.transpose(w_embed.astype(F32)).astype(BF16)
    row, lane = iota((256, 256), 0), iota((256, 256), 1)
    dx, k = row // 64, row % 4
    same = lane == jnp.where(k < 3, dx * 48 + k * 16, 192 + dx * 16) + row // 4 % 16
    return mm(turned, jnp.where(same, 1.0, 0.0).astype(BF16)).astype(BF16)


def sigmoid(value):
    return pltpu.reciprocal(1.0 + jnp.exp2(value * -1.4426950408889634), approx=True)


def silu_slope(value):
    gate = sigmoid(value)
    return gate * (1.0 + value * (1.0 - gate))


def forward_kernel(
    facies_hbm, prior_hbm, recon_hbm, w_embed_hbm, w_conv_hbm, w_head_hbm,
    block, one_hot, pre_embed, hidden, pre_conv, w_conv, w_head,
    facies, prior, recon, w_embed, packed, conv_turned, sem
):
    blocks = facies.shape[0]
    loads = [
        pltpu.make_async_copy(facies_hbm.at[:, pl.ds(b * 128, 128)], facies.at[b], sem.at[b]) for b in range(blocks)
    ]
    others = []
    for source, target in (
        (w_embed_hbm, w_embed), (w_conv_hbm, w_conv), (prior_hbm, prior), (recon_hbm, recon), (w_head_hbm, w_head)
    ):
        others.append(pltpu.make_async_copy(source, target, sem.at[blocks + len(others)]))
    for load in others[:2] + loads:
        load.start()
    others[0].wait()
    packed[...] = turned_weights(w_embed[...])
    others[1].wait()
    conv_turned[...] = jnp.transpose(w_conv[...].astype(F32)).astype(BF16)
    low = iota((8, 256), 0) < 4
    for half in range(2):
        for load in loads[half * blocks // 2 : (half + 1) * blocks // 2]:
            load.wait()
        if half == 0:
            for load in others[2:]:
                load.start()
        for t in range(8):
            dx2, dx = t // 4, t % 4
            rows = [
                facies[2 * b2 + dy2, pl.ds(t, 32, stride=8), :]
                for dy2 in range(2)
                for b2 in range(4 * half, 4 * half + 4)
            ]
            turned = jnp.transpose(jnp.concatenate(rows, axis=0).astype(F32))
            for cp in range(4):
                part = [turned[dy * 32 + cp * 8 : dy * 32 + cp * 8 + 8] for dy in range(4)]
                swapped = [pltpu.roll(piece, 4, 0) for piece in part]
                for dz2 in range(2):
                    pieces = [
                        jnp.where(low, part[dy], swapped[dy + 1]) if dz2 == 0 else jnp.where(low, swapped[dy], part[dy + 1])
                        for dy in (0, 2)
                    ]
                    cells = jnp.concatenate(pieces, axis=0).astype(BF16)
                    for k in range(LEVELS):
                        hot = jnp.where(cells == BF16(k), BF16(1.0), BF16(0.0))
                        first = dx * 48 + k * 16 if k < 3 else 192 + dx * 16
                        for dy2 in range(2):
                            at = (2 * dx2 + dy2) * 256 + half * 128
                            one_hot[2 * cp + dz2, pl.ds(first, 16), pl.ds(at, 128)] = hot[:, dy2 * 128 : dy2 * 128 + 128]
    sums = jnp.zeros((256, 128), F32)
    for cp in range(4):
        for dz2 in range(2):
            rows = pl.ds(dz2 * 128, 128)
            for dx2 in range(2):
                at = pl.ds(dx2 * 512, 512)
                pre = mm(packed[...], one_hot[2 * cp + dz2, :, at])
                pre_embed[cp, rows, at] = pre
                act = (pre * sigmoid(pre)).astype(BF16)
                hidden[cp, 2 * dx2, rows, :] = act[:, :256]
                hidden[cp, 2 * dx2 + 1, rows, :] = act[:, 256:]
        pre = mm(conv_turned[...], hidden[cp].reshape(1024, 256))
        pre_conv[cp] = pre
        act = pre * sigmoid(pre)
        sums = sums + act[:, :128] + act[:, 128:]
    pick = jnp.where(iota((8, 128), 1) // 8 % 4 == iota((8, 128), 0), 1.0, 0.0)
    total = lax.dot_general(pick, sums, NT, precision=lax.Precision.HIGHEST, preferred_element_type=F32)
    for load in others[2:]:
        load.wait()
    block[:, pl.ds(0, 512)] = prior[...]
    block[:, pl.ds(512, 512)] = recon[...]
    block[:, pl.ds(1024, 256)] = (total[:4] / 256.0).astype(BF16)


def pair_kernel(queries, query_square, keys):
    inner = mm_nt(queries, keys)
    key_float = keys.astype(F32)
    count = keys.shape[0]
    key_square = jnp.sum(key_float * key_float, axis=1, keepdims=True)
    key_row = jnp.transpose(jnp.broadcast_to(key_square, (count, 128)))[:1]
    kern = jnp.exp(-(query_square + key_row - 2.0 * inner) / keys.shape[1])
    return jnp.sum(kern, axis=1, keepdims=True), mm(kern.astype(BF16), keys)


def backward_kernel(
    sizes, gathered, gathered_other, hidden, pre_conv, w_head,
    keep, send, grads, grad_head,
    ordered, head_full
):
    dp, fsdp = sizes
    devices = dp * fsdp
    dp_here, fsdp_here = lax.axis_index("dp"), lax.axis_index("fsdp")
    here = (lax.rem(dp_here, 2) * (dp // 2) + dp_here // 2) * fsdp + fsdp_here
    core = lax.rem(dp_here, 2)
    for place in range(devices // 2):
        ordered[core * (devices // 2) + place] = gathered[place].astype(F32)
        ordered[(1 - core) * (devices // 2) + place] = gathered_other[place].astype(F32)
    samples = ordered.shape[1]
    count = devices * samples
    full = ordered[...].reshape(count, ordered.shape[2])
    prior = full[:, :512].astype(BF16)
    recon = full[:, 512:1024]
    pooled = full[:, 1024:].astype(BF16)
    latent = mm(pooled, w_head[...]).astype(BF16)
    latent_float = latent.astype(F32)
    square = jnp.sum(latent_float * latent_float, axis=1, keepdims=True)
    self_sum, self_mix = pair_kernel(latent, square, latent)
    cross_sum, cross_mix = pair_kernel(latent, square, prior)
    pull = -32.0 / count * ((self_sum - cross_sum) * latent_float - self_mix + cross_mix)
    cotangent = (recon + pull).astype(BF16)
    turned = jnp.transpose(full[:, 1024:]).astype(BF16)
    head_full[...] = mm(turned, cotangent)
    share = grad_head.shape[0]
    start = pl.multiple_of(fsdp_here * share, share)
    grad_head[...] = head_full[pl.ds(start, share), :]

    lane_sample = iota((128, count), 0) // 8 % 4 + samples * here
    pick = jnp.where(lane_sample == iota((128, count), 1), 1.0, 0.0).astype(BF16)
    lanes = mm(pick, cotangent).astype(BF16)
    back_pool = mm_nt(w_head[...], lanes) / 256.0
    back_pool = jnp.concatenate([back_pool, back_pool], axis=1)
    conv_total = None
    for cp in range(4):
        grads[cp] = (back_pool * silu_slope(pre_conv[cp])).astype(BF16)
        term = mm_nt(hidden[cp].reshape(1024, 256), grads[cp])
        conv_total = term if cp == 0 else conv_total + term
    core_zero = lax.rem(dp_here, 2) == 0
    rows = keep.shape[1]
    for f in range(fsdp):
        at = 2 * f * rows
        first, second = conv_total[at : at + rows], conv_total[at + rows : at + 2 * rows]
        keep[f] = jnp.where(core_zero, first, second)
        send[f] = jnp.where(core_zero, second, first)


def embed_kernel(grads, w_conv, pre_embed, one_hot, embed_out):
    embed = None
    ones = jnp.ones((16, 1024), BF16)
    for cp in range(4):
        signals = []
        for dx2 in range(2):
            back_rows = mm(w_conv[pl.ds(dx2 * 512, 512), :], grads[cp])
            back_rows = jnp.concatenate([back_rows[:256], back_rows[256:]], axis=1)
            signals.append((back_rows * silu_slope(pre_embed[cp, :, pl.ds(dx2 * 512, 512)])).astype(BF16))
        signal = jnp.concatenate(signals, axis=1)
        for dz2 in range(2):
            rows = jnp.concatenate([one_hot[2 * cp + dz2, pl.ds(0, 192), :], ones], axis=0)
            term = mm_nt(rows, signal[dz2 * 128 : dz2 * 128 + 128])
            embed = term if embed is None else embed + term
    shares = embed_out.shape[0]
    depth = 64 // shares
    half = 3 * depth // 2
    embed_out[...] = jnp.zeros(embed_out.shape, F32)
    for f in range(shares):
        dx, at = f * 4 // shares, f * depth % 16
        share = jnp.concatenate([embed[dx * 48 + k * 16 + at :][:depth] for k in range(3)], axis=0)
        for side in range(2):
            embed_out[f, pl.ds(0, half), pl.ds(side * 128, 128)] = share[side * half : (side + 1) * half]
        embed_out[f, pl.ds(embed_out.shape[1] - 8, 8), pl.ds(0, 128)] = embed[192:200]


def exponent_of(part):
    top = jnp.abs(part)
    while top.ndim > 2:
        top = jnp.max(top, axis=0)
    top = jnp.max(jnp.max(top, axis=0, keepdims=True), axis=1, keepdims=True)
    return jnp.clip(jnp.floor(jnp.log2(jnp.maximum(top, 1e-37))) - 14.0, -124.0, 114.0)


def store_coded(coded, part, conv_rows):
    store_scaled(coded, part, (exponent_of(part[:conv_rows]), exponent_of(part[conv_rows:])), conv_rows)


def store_scaled(coded, part, steps, conv_rows):
    last = part.shape[0] - 8
    coded[pl.ds(0, conv_rows), :] = part[:conv_rows] * jnp.exp2(-steps[0])
    coded[pl.ds(conv_rows, last - conv_rows), :] = part[conv_rows:last] * jnp.exp2(-steps[1])
    total = part[last:, :128] * jnp.exp2(-steps[1])
    high = total.astype(BF16).astype(F32)
    row = iota((8, 256), 0)
    tail = jnp.where(row == 1, steps[0], steps[1])
    coded[pl.ds(last, 8), :] = jnp.where(row == 0, jnp.concatenate([high, total - high], axis=1), tail)


def load_coded(coded, conv_rows):
    last = coded.shape[0] - 8
    embed_scale = jnp.exp2(coded[pl.ds(last + 2, 1), :])
    total = coded[pl.ds(last, 8), pl.ds(0, 128)] + coded[pl.ds(last, 8), pl.ds(128, 128)]
    total = jnp.where(iota((8, 256), 0) == 0, jnp.concatenate([total, jnp.zeros((8, 128), F32)], axis=1), 0.0)
    embed = jnp.concatenate([coded[pl.ds(conv_rows, last - conv_rows), :], total], axis=0) * embed_scale
    return jnp.concatenate([coded[pl.ds(0, conv_rows), :] * jnp.exp2(coded[pl.ds(last + 1, 1), :]), embed], axis=0)


def scale_kernel(keep, other, embed, own, *coded):
    held = keep[...] + other[...]
    steps = exponent_of(held), exponent_of(embed[...])
    here = lax.axis_index("fsdp")

    def share(z):
        return jnp.concatenate([keep[z] + other[z], embed[z]], axis=0)

    own[...] = share(here)
    for place, target in enumerate(coded):
        store_scaled(target, share(lax.rem(here + (len(coded) - place), keep.shape[0])), steps, keep.shape[1])


def first_sum_kernel(conv_rows, own, *refs):
    *received, coded = refs
    total = own[...]
    for part in received:
        total = total + load_coded(part, conv_rows)
    store_coded(coded, total, conv_rows)


def next_sum_kernel(conv_rows, mine, other, total, *coded):
    summed = load_coded(mine, conv_rows) + load_coded(other, conv_rows)
    total[...] = summed
    if coded:
        store_coded(coded[0], summed, conv_rows)


def output_kernel(own, other, head, grad_embed, grad_conv, grad_head):
    grad_head[...] = head[...]
    conv_rows, count = grad_conv.shape[0] // 2, grad_embed.shape[0]
    core_zero = lax.rem(lax.axis_index("dp"), 2) == 0
    grad_conv[pl.ds(0, conv_rows), :] = jnp.where(core_zero, own[pl.ds(0, conv_rows), :], other[pl.ds(0, conv_rows), :])
    grad_conv[pl.ds(conv_rows, conv_rows), :] = jnp.where(
        core_zero, other[pl.ds(0, conv_rows), :], own[pl.ds(0, conv_rows), :]
    )
    half, depth = 3 * count // 8, count // LEVELS
    embed = own[pl.ds(conv_rows, half), :] + other[pl.ds(conv_rows, half), :]
    embed = jnp.concatenate([embed[:, :128], embed[:, 128:]], axis=0)
    last = own.shape[0] - 8
    total = own[pl.ds(last, 1), pl.ds(0, 128)] + other[pl.ds(last, 1), pl.ds(0, 128)]
    fourth = total - (embed[:depth] + embed[depth : 2 * depth] + embed[2 * depth :])
    embed = jnp.concatenate([embed, fourth], axis=0)
    row, lane = iota((count, count), 0), iota((count, count), 1)
    order = jnp.where(lane == row % LEVELS * depth + row // LEVELS, 1.0, 0.0).astype(BF16)
    result = None
    for _ in range(3):
        term = embed.astype(BF16)
        embed = embed - term.astype(F32)
        result = mm(order, term) if result is None else result + mm(order, term)
    grad_embed[...] = result


VMEM = pl.BlockSpec(memory_space=pltpu.VMEM)
HBM = pl.BlockSpec(memory_space=pltpu.HBM)
SAVED = (
    ((8, 256, 1024), BF16),
    ((4, 256, 1024), F32),
    ((4, 4, 256, 256), BF16),
    ((4, 256, 256), F32),
)


def forward(facies, prior_draws, recon_grad, w_embed, w_conv, w_head):
    samples = facies.shape[0]
    latent_width = prior_draws.shape[1]
    rows, lanes = samples * PATCH_X, PATCH_Y * PATCH_Z
    operands = (facies.reshape(rows, lanes), prior_draws, recon_grad, w_embed, w_conv, w_head)
    return pl.pallas_call(
        forward_kernel,
        out_shape=(pltpu.VMEM((samples, 2 * latent_width + 256), BF16),)
        + tuple(pltpu.VMEM(shape, kind) for shape, kind in SAVED)
        + (pltpu.VMEM(w_conv.shape, BF16), pltpu.VMEM(w_head.shape, BF16)),
        in_specs=[HBM] * 6,
        out_specs=(VMEM,) * 7,
        scratch_shapes=[
            pltpu.VMEM((lanes // 128, rows, 128), jnp.int32),
            pltpu.VMEM(prior_draws.shape, BF16),
            pltpu.VMEM(recon_grad.shape, BF16),
            pltpu.VMEM(w_embed.shape, BF16),
            pltpu.VMEM((128, 256), BF16),
            pltpu.VMEM((256, 1024), BF16),
            pltpu.SemaphoreType.DMA((lanes // 128 + 5,)),
        ],
        compiler_params=pltpu.CompilerParams(vmem_limit_bytes=30 * 2**20),
        name="forward",
    )(*(pltpu.with_memory_space_constraint(operand, pltpu.HBM) for operand in operands))


def backward(sizes, gathered, hidden, pre_conv, w_head):
    dp, fsdp = sizes
    _, samples, width = gathered[0].shape
    devices = dp * fsdp
    payload = pltpu.VMEM((fsdp, 1024 // fsdp // 2, 256), F32)
    return pl.pallas_call(
        lambda *refs: backward_kernel(sizes, *refs),
        out_shape=(
            payload, payload, pltpu.VMEM((4, 256, 256), BF16), pltpu.VMEM((256 // fsdp, 512), F32)
        ),
        in_specs=[VMEM] * 5,
        out_specs=(VMEM,) * 4,
        scratch_shapes=[pltpu.VMEM((devices, samples, width), F32), pltpu.VMEM((256, 512), F32)],
        compiler_params=pltpu.CompilerParams(vmem_limit_bytes=24 * 2**20),
        name="backward",
    )(*gathered, hidden, pre_conv, w_head)


def embed_gradient(fsdp, grads, w_conv, pre_embed, one_hot):
    return pl.pallas_call(
        embed_kernel,
        out_shape=pltpu.VMEM((fsdp, (96 // fsdp + 7) // 8 * 8 + 8, 256), F32),
        in_specs=[VMEM] * 4,
        out_specs=VMEM,
        compiler_params=pltpu.CompilerParams(vmem_limit_bytes=24 * 2**20),
        cost_estimate=pl.CostEstimate(flops=16 * 10**8, bytes_accessed=10 * 2**20, transcendentals=0),
        name="embed_gradient",
    )(grads, w_conv, pre_embed, one_hot)


def place_of(x, core, z, fsdp):
    return (2 * x + core) * fsdp + z


def exchange(block, dp, fsdp, flip_x, flip_core, step_z):
    pairs = []
    for x in range(dp // 2):
        for core in range(2):
            for z in range(fsdp):
                to = place_of(x ^ flip_x, core ^ flip_core, (z + step_z) % fsdp, fsdp)
                pairs.append((place_of(x, core, z, fsdp), to))
    return lax.ppermute(block, GROUP, pairs)


def gather_blocks(block, dp, fsdp):
    peers = dp // 2 * fsdp
    groups = [[place_of(x, core, z, fsdp) for x in range(dp // 2) for z in range(fsdp)] for core in range(2)]
    copies = jnp.broadcast_to(block[None], (peers,) + block.shape)
    own = lax.all_to_all(copies, GROUP, 0, 0, axis_index_groups=groups, tiled=True)
    return own, exchange(own, dp, fsdp, 0, 1, 0)


def local_kernel(kernel, outs, name, *operands):
    return pl.pallas_call(
        kernel,
        out_shape=outs,
        in_specs=[VMEM] * len(operands),
        out_specs=(VMEM,) * len(outs),
        compiler_params=pltpu.CompilerParams(vmem_limit_bytes=16 * 2**20),
        name=name,
    )(*operands)


def to_half(coded):
    rounded = lax.reduce_precision(coded, exponent_bits=5, mantissa_bits=10)
    return rounded, rounded.astype(jnp.float16)


def reduce_to_owner(keep, other, embed, dp, fsdp):
    conv_rows, width = keep.shape[1:]
    rows = conv_rows + embed.shape[1]
    plain = jax.ShapeDtypeStruct((rows, width), F32)
    own, *coded = local_kernel(scale_kernel, (plain,) + (plain,) * (fsdp - 1), "scale", keep, other, embed)
    received = [
        exchange(to_half(part)[1], dp, fsdp, 0, 0, fsdp - 1 - place).astype(F32) for place, part in enumerate(coded)
    ]
    (coded,) = local_kernel(functools.partial(first_sum_kernel, conv_rows), (plain,), "sum_z", own, *received)
    flip = 1
    while flip < dp // 2:
        mine, sent = to_half(coded)
        other = exchange(sent, dp, fsdp, flip, 0, 0).astype(F32)
        flip *= 2
        outs = (plain,) * (2 if flip < dp // 2 else 1)
        total, *rest = local_kernel(functools.partial(next_sum_kernel, conv_rows), outs, "sum_x", mine, other)
        coded = rest[0] if rest else None
    return total, exchange(total, dp, fsdp, 0, 1, 0)


def shards(facies, prior_draws, recon_grad, w_embed, w_conv, w_head):
    dp, fsdp = lax.axis_size("dp"), lax.axis_size("fsdp")
    block, one_hot, pre_embed, hidden, pre_conv, w_conv, w_head = forward(
        facies, prior_draws, recon_grad, w_embed, w_conv, w_head
    )
    gathered = gather_blocks(block, dp, fsdp)
    keep, send, grads, grad_head = backward((dp, fsdp), gathered, hidden, pre_conv, w_head)
    received = exchange(send, dp, fsdp, 0, 1, 0)
    embed = embed_gradient(fsdp, grads, w_conv, pre_embed, one_hot)
    own, other = reduce_to_owner(keep, received, embed, dp, fsdp)
    outs = (
        jax.ShapeDtypeStruct((256 // fsdp, 128), F32),
        jax.ShapeDtypeStruct((1024 // fsdp, 256), F32),
        jax.ShapeDtypeStruct(grad_head.shape, F32),
    )
    return local_kernel(output_kernel, outs, "outputs", own, other, grad_head)


def solution(mesh):
    return jax.shard_map(
        shards,
        mesh=mesh,
        in_specs=(
            P(("groups", "dp", "fsdp"), None, None),
            P(("groups", "dp", "fsdp"), None),
            P(("groups", "dp", "fsdp"), None),
            P(),
            P(),
            P(),
        ),
        out_specs=(
            P(("groups", "fsdp"), None),
            P(("groups", "fsdp"), None),
            P(("groups", "fsdp"), None),
        ),
        check_vma=False,
    )
```

```python
import functools

import jax
import jax.numpy as jnp
from jax import lax
from jax.experimental import pallas as pl
from jax.experimental.pallas import tpu as pltpu
from jax.sharding import PartitionSpec as P

PATCH_X = 64
PATCH_Y = 64
PATCH_Z = 32
LEVELS = 4
GROUP = ("dp", "fsdp")
NT = (((1,), (1,)), ((), ()))
F32 = jnp.float32
BF16 = jnp.bfloat16


def iota(shape, dim):
    return lax.broadcasted_iota(jnp.int32, shape, dim)


def mm(left, right):
    return jnp.dot(left, right, preferred_element_type=F32)


def mm_nt(left, right):
    return lax.dot_general(left, right, NT, preferred_element_type=F32)


def turned_weights(w_embed):
    turned = jnp.transpose(w_embed.astype(F32)).astype(BF16)
    row, lane = iota((256, 256), 0), iota((256, 256), 1)
    dx, k = row // 64, row % 4
    same = lane == jnp.where(k < 3, dx * 48 + k * 16, 192 + dx * 16) + row // 4 % 16
    return mm(turned, jnp.where(same, 1.0, 0.0).astype(BF16)).astype(BF16)


def sigmoid(value):
    return pltpu.reciprocal(1.0 + jnp.exp2(value * -1.4426950408889634), approx=True)


def silu_slope(value):
    gate = sigmoid(value)
    return gate * (1.0 + value * (1.0 - gate))


def forward_kernel(
    facies_hbm, prior_hbm, recon_hbm, w_embed_hbm, w_conv_hbm, w_head_hbm,
    block, pooled_lanes, recon_lanes, one_hot, pre_embed, hidden, pre_conv, w_conv, w_head,
    facies, prior, recon, w_embed, packed, conv_turned, sem
):
    blocks = facies.shape[0]
    loads = [
        pltpu.make_async_copy(facies_hbm.at[:, pl.ds(b * 128, 128)], facies.at[b], sem.at[b]) for b in range(blocks)
    ]
    others = []
    for source, target in (
        (w_embed_hbm, w_embed), (w_conv_hbm, w_conv), (prior_hbm, prior), (recon_hbm, recon), (w_head_hbm, w_head)
    ):
        others.append(pltpu.make_async_copy(source, target, sem.at[blocks + len(others)]))
    for load in others[:2] + loads:
        load.start()
    others[0].wait()
    packed[...] = turned_weights(w_embed[...])
    others[1].wait()
    conv_turned[...] = jnp.transpose(w_conv[...].astype(F32)).astype(BF16)
    low = iota((8, 256), 0) < 4
    for half in range(2):
        for load in loads[half * blocks // 2 : (half + 1) * blocks // 2]:
            load.wait()
        if half == 0:
            for load in others[2:]:
                load.start()
        for t in range(8):
            dx2, dx = t // 4, t % 4
            rows = [
                facies[2 * b2 + dy2, pl.ds(t, 32, stride=8), :]
                for dy2 in range(2)
                for b2 in range(4 * half, 4 * half + 4)
            ]
            turned = jnp.transpose(jnp.concatenate(rows, axis=0).astype(F32))
            for cp in range(4):
                part = [turned[dy * 32 + cp * 8 : dy * 32 + cp * 8 + 8] for dy in range(4)]
                swapped = [pltpu.roll(piece, 4, 0) for piece in part]
                for dz2 in range(2):
                    pieces = [
                        jnp.where(low, part[dy], swapped[dy + 1]) if dz2 == 0 else jnp.where(low, swapped[dy], part[dy + 1])
                        for dy in (0, 2)
                    ]
                    cells = jnp.concatenate(pieces, axis=0).astype(BF16)
                    for k in range(LEVELS):
                        hot = jnp.where(cells == BF16(k), BF16(1.0), BF16(0.0))
                        first = dx * 48 + k * 16 if k < 3 else 192 + dx * 16
                        for dy2 in range(2):
                            at = (2 * dx2 + dy2) * 256 + half * 128
                            one_hot[2 * cp + dz2, pl.ds(first, 16), pl.ds(at, 128)] = hot[:, dy2 * 128 : dy2 * 128 + 128]
    sums = jnp.zeros((256, 128), F32)
    for cp in range(4):
        for dz2 in range(2):
            rows = pl.ds(dz2 * 128, 128)
            for dx2 in range(2):
                at = pl.ds(dx2 * 512, 512)
                pre = mm(packed[...], one_hot[2 * cp + dz2, :, at])
                pre_embed[cp, rows, at] = pre
                act = (pre * sigmoid(pre)).astype(BF16)
                hidden[cp, 2 * dx2, rows, :] = act[:, :256]
                hidden[cp, 2 * dx2 + 1, rows, :] = act[:, 256:]
        pre = mm(conv_turned[...], hidden[cp].reshape(1024, 256))
        pre_conv[cp] = pre
        act = pre * sigmoid(pre)
        sums = sums + act[:, :128] + act[:, 128:]
    for rows, every in ((8, 1), (128, 8)):
        pick = iota((rows, 128), 1) // 8 % 4 == iota((rows, 128), 0) // every % 4
        total = lax.dot_general(
            jnp.where(pick, 1.0, 0.0), sums, NT, precision=lax.Precision.HIGHEST, preferred_element_type=F32
        )
        mean = (total / 256.0).astype(BF16)
        if rows == 8:
            block[:, pl.ds(1024, 256)] = mean[:4]
        else:
            pooled_lanes[...] = mean
    for load in others[2:]:
        load.wait()
    block[:, pl.ds(0, 512)] = prior[...]
    block[:, pl.ds(512, 512)] = recon[...]
    recon_float = recon[...].astype(F32)
    for place in range(16):
        recon_lanes[pl.ds(place * 8, 8), :] = jnp.broadcast_to(recon_float[place % 4 : place % 4 + 1], (8, recon.shape[1]))


def pair_kernel(queries, query_square, keys):
    inner = mm_nt(queries, keys)
    key_float = keys.astype(F32)
    count = keys.shape[0]
    key_square = jnp.sum(key_float * key_float, axis=1, keepdims=True)
    key_row = jnp.transpose(jnp.broadcast_to(key_square, (count, 128)))[:1]
    kern = jnp.exp(-(query_square + key_row - 2.0 * inner) / keys.shape[1])
    return jnp.sum(kern, axis=1, keepdims=True), mm(kern.astype(BF16), keys)


def group_rows(gathered, ordered):
    for owner in range(gathered.shape[0]):
        ordered[owner] = gathered[owner].astype(F32)
    return ordered[...].reshape(gathered.shape[0] * gathered.shape[1], gathered.shape[2])


def latent_rows(pooled, w_head):
    return mm(pooled, w_head[...]).astype(BF16)


def cotangent_rows(queries, keys, prior, recon):
    query_float = queries.astype(F32)
    square = jnp.sum(query_float * query_float, axis=1, keepdims=True)
    self_sum, self_mix = pair_kernel(queries, square, keys)
    cross_sum, cross_mix = pair_kernel(queries, square, prior)
    pull = -32.0 / keys.shape[0] * ((self_sum - cross_sum) * query_float - self_mix + cross_mix)
    return (recon + pull).astype(BF16)


def head_kernel(gathered, w_head, after, grad_head, token, ordered, head_full):
    token[...] = jnp.zeros(token.shape, F32)
    full = group_rows(gathered, ordered)
    latent = latent_rows(full[:, 1024:].astype(BF16), w_head)
    cotangent = cotangent_rows(latent, latent, full[:, :512].astype(BF16), full[:, 512:1024])
    head_full[...] = mm(jnp.transpose(full[:, 1024:]).astype(BF16), cotangent)
    share = grad_head.shape[0]
    start = pl.multiple_of(lax.axis_index("fsdp") * share, share)
    grad_head[...] = head_full[pl.ds(start, share), :]


def backward_kernel(gathered, pooled_lanes, recon_lanes, hidden, pre_conv, w_head, keep, send, grads, ordered):
    full = group_rows(gathered, ordered)
    queries = latent_rows(pooled_lanes[...], w_head)
    keys = latent_rows(full[:, 1024:].astype(BF16), w_head)
    cotangent = cotangent_rows(queries, keys, full[:, :512].astype(BF16), recon_lanes[...])
    back_pool = mm_nt(w_head[...], cotangent) / 256.0
    back_pool = jnp.concatenate([back_pool, back_pool], axis=1)
    fsdp = keep.shape[0]
    conv_total = None
    for cp in range(4):
        grads[cp] = (back_pool * silu_slope(pre_conv[cp])).astype(BF16)
        term = mm_nt(hidden[cp].reshape(1024, 256), grads[cp])
        conv_total = term if cp == 0 else conv_total + term
    core_zero = lax.rem(lax.axis_index("dp"), 2) == 0
    rows = keep.shape[1]
    for f in range(fsdp):
        at = 2 * f * rows
        first, second = conv_total[at : at + rows], conv_total[at + rows : at + 2 * rows]
        keep[f] = jnp.where(core_zero, first, second)
        send[f] = jnp.where(core_zero, second, first)


def embed_kernel(grads, w_conv, pre_embed, one_hot, embed_out):
    embed = None
    ones = jnp.ones((16, 1024), BF16)
    for cp in range(4):
        signals = []
        for dx2 in range(2):
            back_rows = mm(w_conv[pl.ds(dx2 * 512, 512), :], grads[cp])
            back_rows = jnp.concatenate([back_rows[:256], back_rows[256:]], axis=1)
            signals.append((back_rows * silu_slope(pre_embed[cp, :, pl.ds(dx2 * 512, 512)])).astype(BF16))
        signal = jnp.concatenate(signals, axis=1)
        for dz2 in range(2):
            rows = jnp.concatenate([one_hot[2 * cp + dz2, pl.ds(0, 192), :], ones], axis=0)
            term = mm_nt(rows, signal[dz2 * 128 : dz2 * 128 + 128])
            embed = term if embed is None else embed + term
    shares = embed_out.shape[0]
    depth = 64 // shares
    half = 3 * depth // 2
    embed_out[...] = jnp.zeros(embed_out.shape, F32)
    for f in range(shares):
        dx, at = f * 4 // shares, f * depth % 16
        share = jnp.concatenate([embed[dx * 48 + k * 16 + at :][:depth] for k in range(3)], axis=0)
        for side in range(2):
            embed_out[f, pl.ds(0, half), pl.ds(side * 128, 128)] = share[side * half : (side + 1) * half]
        embed_out[f, pl.ds(embed_out.shape[1] - 8, 8), pl.ds(0, 128)] = embed[192:200]


def exponent_of(part):
    top = jnp.abs(part)
    while top.ndim > 2:
        top = jnp.max(top, axis=0)
    top = jnp.max(jnp.max(top, axis=0, keepdims=True), axis=1, keepdims=True)
    return jnp.clip(jnp.floor(jnp.log2(jnp.maximum(top, 1e-37))) - 14.0, -124.0, 114.0)


def store_coded(coded, part, conv_rows):
    store_scaled(coded, part, (exponent_of(part[:conv_rows]), exponent_of(part[conv_rows:])), conv_rows)


def store_scaled(coded, part, steps, conv_rows):
    last = part.shape[0] - 8
    coded[pl.ds(0, conv_rows), :] = part[:conv_rows] * jnp.exp2(-steps[0])
    coded[pl.ds(conv_rows, last - conv_rows), :] = part[conv_rows:last] * jnp.exp2(-steps[1])
    total = part[last:, :128] * jnp.exp2(-steps[1])
    high = total.astype(BF16).astype(F32)
    row = iota((8, 256), 0)
    tail = jnp.where(row == 1, steps[0], steps[1])
    coded[pl.ds(last, 8), :] = jnp.where(row == 0, jnp.concatenate([high, total - high], axis=1), tail)


def load_coded(coded, conv_rows):
    last = coded.shape[0] - 8
    embed_scale = jnp.exp2(coded[pl.ds(last + 2, 1), :])
    total = coded[pl.ds(last, 8), pl.ds(0, 128)] + coded[pl.ds(last, 8), pl.ds(128, 128)]
    total = jnp.where(iota((8, 256), 0) == 0, jnp.concatenate([total, jnp.zeros((8, 128), F32)], axis=1), 0.0)
    embed = jnp.concatenate([coded[pl.ds(conv_rows, last - conv_rows), :], total], axis=0) * embed_scale
    return jnp.concatenate([coded[pl.ds(0, conv_rows), :] * jnp.exp2(coded[pl.ds(last + 1, 1), :]), embed], axis=0)


def scale_kernel(keep, other, embed, own, *coded):
    held = keep[...] + other[...]
    steps = exponent_of(held), exponent_of(embed[...])
    here = lax.axis_index("fsdp")

    def share(z):
        return jnp.concatenate([keep[z] + other[z], embed[z]], axis=0)

    own[...] = share(here)
    for place, target in enumerate(coded):
        store_scaled(target, share(here ^ (place + 1)), steps, keep.shape[1])


def first_sum_kernel(conv_rows, own, *refs):
    *received, coded = refs
    total = own[...]
    for part in received:
        total = total + load_coded(part, conv_rows)
    store_coded(coded, total, conv_rows)


def next_sum_kernel(conv_rows, mine, other, total, *coded):
    summed = load_coded(mine, conv_rows) + load_coded(other, conv_rows)
    total[...] = summed
    if coded:
        store_coded(coded[0], summed, conv_rows)


def output_kernel(own, other, grad_embed, grad_conv):
    conv_rows, count = grad_conv.shape[0] // 2, grad_embed.shape[0]
    core_zero = lax.rem(lax.axis_index("dp"), 2) == 0
    grad_conv[pl.ds(0, conv_rows), :] = jnp.where(core_zero, own[pl.ds(0, conv_rows), :], other[pl.ds(0, conv_rows), :])
    grad_conv[pl.ds(conv_rows, conv_rows), :] = jnp.where(
        core_zero, other[pl.ds(0, conv_rows), :], own[pl.ds(0, conv_rows), :]
    )
    half, depth = 3 * count // 8, count // LEVELS
    embed = own[pl.ds(conv_rows, half), :] + other[pl.ds(conv_rows, half), :]
    embed = jnp.concatenate([embed[:, :128], embed[:, 128:]], axis=0)
    last = own.shape[0] - 8
    total = own[pl.ds(last, 1), pl.ds(0, 128)] + other[pl.ds(last, 1), pl.ds(0, 128)]
    fourth = total - (embed[:depth] + embed[depth : 2 * depth] + embed[2 * depth :])
    embed = jnp.concatenate([embed, fourth], axis=0)
    row, lane = iota((count, count), 0), iota((count, count), 1)
    order = jnp.where(lane == row % LEVELS * depth + row // LEVELS, 1.0, 0.0).astype(BF16)
    result = None
    for _ in range(3):
        term = embed.astype(BF16)
        embed = embed - term.astype(F32)
        result = mm(order, term) if result is None else result + mm(order, term)
    grad_embed[...] = result


VMEM = pl.BlockSpec(memory_space=pltpu.VMEM)
HBM = pl.BlockSpec(memory_space=pltpu.HBM)
SAVED = (
    ((8, 256, 1024), BF16),
    ((4, 256, 1024), F32),
    ((4, 4, 256, 256), BF16),
    ((4, 256, 256), F32),
)


def forward(facies, prior_draws, recon_grad, w_embed, w_conv, w_head):
    samples = facies.shape[0]
    latent_width = prior_draws.shape[1]
    rows, lanes = samples * PATCH_X, PATCH_Y * PATCH_Z
    operands = (facies.reshape(rows, lanes), prior_draws, recon_grad, w_embed, w_conv, w_head)
    return pl.pallas_call(
        forward_kernel,
        out_shape=(pltpu.VMEM((samples, 2 * latent_width + 256), BF16),)
        + (pltpu.VMEM((128, 256), BF16), pltpu.VMEM((128, latent_width), F32))
        + tuple(pltpu.VMEM(shape, kind) for shape, kind in SAVED)
        + (pltpu.VMEM(w_conv.shape, BF16), pltpu.VMEM(w_head.shape, BF16)),
        in_specs=[HBM] * 6,
        out_specs=(VMEM,) * 9,
        scratch_shapes=[
            pltpu.VMEM((lanes // 128, rows, 128), jnp.int32),
            pltpu.VMEM(prior_draws.shape, BF16),
            pltpu.VMEM(recon_grad.shape, BF16),
            pltpu.VMEM(w_embed.shape, BF16),
            pltpu.VMEM((128, 256), BF16),
            pltpu.VMEM((256, 1024), BF16),
            pltpu.SemaphoreType.DMA((lanes // 128 + 5,)),
        ],
        compiler_params=pltpu.CompilerParams(vmem_limit_bytes=30 * 2**20),
        name="forward",
    )(*(pltpu.with_memory_space_constraint(operand, pltpu.HBM) for operand in operands))


def backward(fsdp, gathered, *operands):
    devices, samples, width = gathered.shape
    payload = pltpu.VMEM((fsdp, 1024 // fsdp // 2, 256), F32)
    return pl.pallas_call(
        backward_kernel,
        out_shape=(payload, payload, pltpu.VMEM((4, 256, 256), BF16)),
        in_specs=[VMEM] * 6,
        out_specs=(VMEM,) * 3,
        scratch_shapes=[pltpu.VMEM((devices, samples, width), F32)],
        compiler_params=pltpu.CompilerParams(vmem_limit_bytes=24 * 2**20),
        name="backward",
    )(gathered, *operands)


def head_gradient(fsdp, gathered, w_head, after):
    devices, samples, width = gathered.shape
    return pl.pallas_call(
        head_kernel,
        out_shape=(jax.ShapeDtypeStruct((256 // fsdp, 512), F32), pltpu.VMEM((8, 128), F32)),
        in_specs=[VMEM] * 2 + [HBM],
        out_specs=(VMEM,) * 2,
        scratch_shapes=[pltpu.VMEM((devices, samples, width), F32), pltpu.VMEM((256, 512), F32)],
        compiler_params=pltpu.CompilerParams(vmem_limit_bytes=16 * 2**20),
        cost_estimate=pl.CostEstimate(flops=2 * 10**9, bytes_accessed=2 * 2**20, transcendentals=10000),
        name="head_gradient",
    )(gathered, w_head, after)


def embed_gradient(fsdp, grads, w_conv, pre_embed, one_hot):
    return pl.pallas_call(
        embed_kernel,
        out_shape=pltpu.VMEM((fsdp, (96 // fsdp + 7) // 8 * 8 + 8, 256), F32),
        in_specs=[VMEM] * 4,
        out_specs=VMEM,
        compiler_params=pltpu.CompilerParams(vmem_limit_bytes=24 * 2**20),
        cost_estimate=pl.CostEstimate(flops=16 * 10**8, bytes_accessed=10 * 2**20, transcendentals=0),
        name="embed_gradient",
    )(grads, w_conv, pre_embed, one_hot)


def place_of(x, core, z, fsdp):
    return (2 * x + core) * fsdp + z


def exchange(block, dp, fsdp, flip_x, flip_core, flip_z):
    pairs = []
    for x in range(dp // 2):
        for core in range(2):
            for z in range(fsdp):
                pairs.append((place_of(x, core, z, fsdp), place_of(x ^ flip_x, core ^ flip_core, z ^ flip_z, fsdp)))
    return lax.ppermute(block, GROUP, pairs)


def gather_blocks(block, devices):
    copies = jnp.broadcast_to(block[None], (devices,) + block.shape)
    return lax.all_to_all(copies, GROUP, 0, 0, tiled=True)


def local_kernel(kernel, outs, name, *operands, unread=()):
    return pl.pallas_call(
        lambda *refs: kernel(*refs[: len(operands)], *refs[len(operands) + len(unread) :]),
        out_shape=outs,
        in_specs=[VMEM] * (len(operands) + len(unread)),
        out_specs=(VMEM,) * len(outs),
        compiler_params=pltpu.CompilerParams(vmem_limit_bytes=16 * 2**20),
        name=name,
    )(*operands, *unread)


def to_half(coded):
    rounded = lax.reduce_precision(coded, exponent_bits=5, mantissa_bits=10)
    return rounded, rounded.astype(jnp.float16)


def reduce_to_owner(keep, other, embed, gathered, w_head, dp, fsdp):
    conv_rows, width = keep.shape[1:]
    rows = conv_rows + embed.shape[1]
    plain = jax.ShapeDtypeStruct((rows, width), F32)
    own, *coded = local_kernel(scale_kernel, (plain,) + (plain,) * (fsdp - 1), "scale", keep, other, embed)
    received = [
        exchange(to_half(part)[1], dp, fsdp, 0, 0, place + 1).astype(F32) for place, part in enumerate(coded)
    ]
    grad_head, token = head_gradient(fsdp, gathered, w_head, own)
    (coded,) = local_kernel(
        functools.partial(first_sum_kernel, conv_rows), (plain,), "sum_z", own, *received, unread=(token,)
    )
    flip = 1
    while flip < dp // 2:
        mine, sent = to_half(coded)
        other = exchange(sent, dp, fsdp, flip, 0, 0).astype(F32)
        flip *= 2
        outs = (plain,) * (2 if flip < dp // 2 else 1)
        total, *rest = local_kernel(functools.partial(next_sum_kernel, conv_rows), outs, "sum_x", mine, other)
        coded = rest[0] if rest else None
    return total, exchange(total, dp, fsdp, 0, 1, 0), grad_head


def shards(facies, prior_draws, recon_grad, w_embed, w_conv, w_head):
    dp, fsdp = lax.axis_size("dp"), lax.axis_size("fsdp")
    block, pooled_lanes, recon_lanes, one_hot, pre_embed, hidden, pre_conv, w_conv, w_head = forward(
        facies, prior_draws, recon_grad, w_embed, w_conv, w_head
    )
    gathered = gather_blocks(block, dp * fsdp)
    keep, send, grads = backward(fsdp, gathered, pooled_lanes, recon_lanes, hidden, pre_conv, w_head)
    received = exchange(send, dp, fsdp, 0, 1, 0)
    embed = embed_gradient(fsdp, grads, w_conv, pre_embed, one_hot)
    own, other, grad_head = reduce_to_owner(keep, received, embed, gathered, w_head, dp, fsdp)
    grad_embed, grad_conv = pl.pallas_call(
        output_kernel,
        out_shape=(
            jax.ShapeDtypeStruct((256 // fsdp, 128), F32),
            jax.ShapeDtypeStruct((1024 // fsdp, 256), F32),
        ),
        in_specs=[VMEM] * 2,
        out_specs=(VMEM,) * 2,
        compiler_params=pltpu.CompilerParams(vmem_limit_bytes=16 * 2**20),
        name="outputs",
    )(own, other)
    return (grad_embed, grad_conv, grad_head)


def solution(mesh):
    return jax.shard_map(
        shards,
        mesh=mesh,
        in_specs=(
            P(("groups", "dp", "fsdp"), None, None),
            P(("groups", "dp", "fsdp"), None),
            P(("groups", "dp", "fsdp"), None),
            P(),
            P(),
            P(),
        ),
        out_specs=(
            P(("groups", "fsdp"), None),
            P(("groups", "fsdp"), None),
            P(("groups", "fsdp"), None),
        ),
        check_vma=False,
    )
```

```python
import functools

import jax
import jax.numpy as jnp
from jax import lax
from jax.experimental import pallas as pl
from jax.experimental.pallas import tpu as pltpu
from jax.sharding import PartitionSpec as P

PATCH_X = 64
PATCH_Y = 64
PATCH_Z = 32
LEVELS = 4
GROUP = ("dp", "fsdp")
NT = (((1,), (1,)), ((), ()))
F32 = jnp.float32
BF16 = jnp.bfloat16


def iota(shape, dim):
    return lax.broadcasted_iota(jnp.int32, shape, dim)


def mm(left, right):
    return jnp.dot(left, right, preferred_element_type=F32)


def mm_nt(left, right):
    return lax.dot_general(left, right, NT, preferred_element_type=F32)


def turned_weights(w_embed):
    turned = jnp.transpose(w_embed.astype(F32)).astype(BF16)
    row, lane = iota((256, 256), 0), iota((256, 256), 1)
    dx, k = row // 64, row % 4
    same = lane == jnp.where(k < 3, dx * 48 + k * 16, 192 + dx * 16) + row // 4 % 16
    return mm(turned, jnp.where(same, 1.0, 0.0).astype(BF16)).astype(BF16)


def sigmoid(value):
    return pltpu.reciprocal(1.0 + jnp.exp2(value * -1.4426950408889634), approx=True)


def silu_slope(value):
    gate = sigmoid(value)
    return gate * (1.0 + value * (1.0 - gate))


def forward_kernel(
    facies_hbm, prior_hbm, recon_hbm, w_embed_hbm, w_conv_hbm, w_head_hbm,
    block, one_hot, pre_embed, hidden, pre_conv, w_conv, w_head,
    facies, prior, recon, w_embed, packed, conv_turned, sem
):
    blocks = facies.shape[0]
    loads = [
        pltpu.make_async_copy(facies_hbm.at[:, pl.ds(b * 128, 128)], facies.at[b], sem.at[b]) for b in range(blocks)
    ]
    others = []
    for source, target in (
        (w_embed_hbm, w_embed), (w_conv_hbm, w_conv), (prior_hbm, prior), (recon_hbm, recon), (w_head_hbm, w_head)
    ):
        others.append(pltpu.make_async_copy(source, target, sem.at[blocks + len(others)]))
    for load in others[:2] + loads:
        load.start()
    others[0].wait()
    packed[...] = turned_weights(w_embed[...])
    others[1].wait()
    conv_turned[...] = jnp.transpose(w_conv[...].astype(F32)).astype(BF16)
    low = iota((8, 256), 0) < 4
    for half in range(2):
        for load in loads[half * blocks // 2 : (half + 1) * blocks // 2]:
            load.wait()
        if half == 0:
            for load in others[2:]:
                load.start()
        for t in range(8):
            dx2, dx = t // 4, t % 4
            rows = [
                facies[2 * b2 + dy2, pl.ds(t, 32, stride=8), :]
                for dy2 in range(2)
                for b2 in range(4 * half, 4 * half + 4)
            ]
            turned = jnp.transpose(jnp.concatenate(rows, axis=0).astype(F32))
            for cp in range(4):
                part = [turned[dy * 32 + cp * 8 : dy * 32 + cp * 8 + 8] for dy in range(4)]
                swapped = [pltpu.roll(piece, 4, 0) for piece in part]
                for dz2 in range(2):
                    pieces = [
                        jnp.where(low, part[dy], swapped[dy + 1]) if dz2 == 0 else jnp.where(low, swapped[dy], part[dy + 1])
                        for dy in (0, 2)
                    ]
                    cells = jnp.concatenate(pieces, axis=0).astype(BF16)
                    for k in range(LEVELS):
                        hot = jnp.where(cells == BF16(k), BF16(1.0), BF16(0.0))
                        first = dx * 48 + k * 16 if k < 3 else 192 + dx * 16
                        for dy2 in range(2):
                            at = (2 * dx2 + dy2) * 256 + half * 128
                            one_hot[2 * cp + dz2, pl.ds(first, 16), pl.ds(at, 128)] = hot[:, dy2 * 128 : dy2 * 128 + 128]
    sums = jnp.zeros((256, 128), F32)
    for cp in range(4):
        for dz2 in range(2):
            rows = pl.ds(dz2 * 128, 128)
            for dx2 in range(2):
                at = pl.ds(dx2 * 512, 512)
                pre = mm(packed[...], one_hot[2 * cp + dz2, :, at])
                pre_embed[cp, rows, at] = pre
                act = (pre * sigmoid(pre)).astype(BF16)
                hidden[cp, 2 * dx2, rows, :] = act[:, :256]
                hidden[cp, 2 * dx2 + 1, rows, :] = act[:, 256:]
        pre = mm(conv_turned[...], hidden[cp].reshape(1024, 256))
        pre_conv[cp] = pre
        act = pre * sigmoid(pre)
        sums = sums + act[:, :128] + act[:, 128:]
    pick = jnp.where(iota((8, 128), 1) // 8 % 4 == iota((8, 128), 0), 1.0, 0.0)
    total = lax.dot_general(pick, sums, NT, precision=lax.Precision.HIGHEST, preferred_element_type=F32)
    for load in others[2:]:
        load.wait()
    block[:, pl.ds(0, 512)] = prior[...]
    block[:, pl.ds(512, 512)] = recon[...]
    block[:, pl.ds(1024, 256)] = (total[:4] / 256.0).astype(BF16)


def pair_kernel(queries, query_square, keys):
    inner = mm_nt(queries, keys)
    key_float = keys.astype(F32)
    count = keys.shape[0]
    key_square = jnp.sum(key_float * key_float, axis=1, keepdims=True)
    key_row = jnp.transpose(jnp.broadcast_to(key_square, (count, 128)))[:1]
    kern = jnp.exp(-(query_square + key_row - 2.0 * inner) / keys.shape[1])
    return jnp.sum(kern, axis=1, keepdims=True), mm(kern.astype(BF16), keys)


def backward_kernel(
    sizes, gathered, hidden, pre_conv, w_head,
    keep, send, grads, grad_head,
    ordered, head_full
):
    dp, fsdp = sizes
    devices = dp * fsdp
    dp_here, fsdp_here = lax.axis_index("dp"), lax.axis_index("fsdp")
    here = dp_here * fsdp + fsdp_here
    for owner in range(devices):
        ordered[owner] = gathered[owner].astype(F32)
    samples = ordered.shape[1]
    count = devices * samples
    full = ordered[...].reshape(count, ordered.shape[2])
    prior = full[:, :512].astype(BF16)
    recon = full[:, 512:1024]
    pooled = full[:, 1024:].astype(BF16)
    latent = mm(pooled, w_head[...]).astype(BF16)
    latent_float = latent.astype(F32)
    square = jnp.sum(latent_float * latent_float, axis=1, keepdims=True)
    self_sum, self_mix = pair_kernel(latent, square, latent)
    cross_sum, cross_mix = pair_kernel(latent, square, prior)
    pull = -32.0 / count * ((self_sum - cross_sum) * latent_float - self_mix + cross_mix)
    cotangent = (recon + pull).astype(BF16)
    turned = jnp.transpose(full[:, 1024:]).astype(BF16)
    head_full[...] = mm(turned, cotangent)
    share = grad_head.shape[0]
    start = pl.multiple_of(fsdp_here * share, share)
    grad_head[...] = head_full[pl.ds(start, share), :]

    lane_sample = iota((128, count), 0) // 8 % 4 + samples * here
    pick = jnp.where(lane_sample == iota((128, count), 1), 1.0, 0.0).astype(BF16)
    lanes = mm(pick, cotangent).astype(BF16)
    back_pool = mm_nt(w_head[...], lanes) / 256.0
    back_pool = jnp.concatenate([back_pool, back_pool], axis=1)
    conv_total = None
    for cp in range(4):
        grads[cp] = (back_pool * silu_slope(pre_conv[cp])).astype(BF16)
        term = mm_nt(hidden[cp].reshape(1024, 256), grads[cp])
        conv_total = term if cp == 0 else conv_total + term
    core_zero = lax.rem(dp_here, 2) == 0
    rows = keep.shape[1]
    for f in range(fsdp):
        at = 2 * f * rows
        first, second = conv_total[at : at + rows], conv_total[at + rows : at + 2 * rows]
        keep[f] = jnp.where(core_zero, first, second)
        send[f] = jnp.where(core_zero, second, first)


def embed_kernel(grads, w_conv, pre_embed, one_hot, embed_out):
    embed = None
    ones = jnp.ones((16, 1024), BF16)
    for cp in range(4):
        signals = []
        for dx2 in range(2):
            back_rows = mm(w_conv[pl.ds(dx2 * 512, 512), :], grads[cp])
            back_rows = jnp.concatenate([back_rows[:256], back_rows[256:]], axis=1)
            signals.append((back_rows * silu_slope(pre_embed[cp, :, pl.ds(dx2 * 512, 512)])).astype(BF16))
        signal = jnp.concatenate(signals, axis=1)
        for dz2 in range(2):
            rows = jnp.concatenate([one_hot[2 * cp + dz2, pl.ds(0, 192), :], ones], axis=0)
            term = mm_nt(rows, signal[dz2 * 128 : dz2 * 128 + 128])
            embed = term if embed is None else embed + term
    shares = embed_out.shape[0]
    depth = 64 // shares
    half = 3 * depth // 2
    embed_out[...] = jnp.zeros(embed_out.shape, F32)
    for f in range(shares):
        dx, at = f * 4 // shares, f * depth % 16
        share = jnp.concatenate([embed[dx * 48 + k * 16 + at :][:depth] for k in range(3)], axis=0)
        for side in range(2):
            embed_out[f, pl.ds(0, half), pl.ds(side * 128, 128)] = share[side * half : (side + 1) * half]
        embed_out[f, pl.ds(embed_out.shape[1] - 8, 8), pl.ds(0, 128)] = embed[192:200]


def exponent_of(part):
    top = jnp.abs(part)
    while top.ndim > 2:
        top = jnp.max(top, axis=0)
    top = jnp.max(jnp.max(top, axis=0, keepdims=True), axis=1, keepdims=True)
    return jnp.clip(jnp.floor(jnp.log2(jnp.maximum(top, 1e-37))) - 14.0, -124.0, 114.0)


def store_coded(coded, part, conv_rows):
    store_scaled(coded, part, (exponent_of(part[:conv_rows]), exponent_of(part[conv_rows:])), conv_rows)


def store_scaled(coded, part, steps, conv_rows):
    last = part.shape[0] - 8
    coded[pl.ds(0, conv_rows), :] = part[:conv_rows] * jnp.exp2(-steps[0])
    coded[pl.ds(conv_rows, last - conv_rows), :] = part[conv_rows:last] * jnp.exp2(-steps[1])
    total = part[last:, :128] * jnp.exp2(-steps[1])
    high = total.astype(BF16).astype(F32)
    row = iota((8, 256), 0)
    tail = jnp.where(row == 1, steps[0], steps[1])
    coded[pl.ds(last, 8), :] = jnp.where(row == 0, jnp.concatenate([high, total - high], axis=1), tail)


def load_coded(coded, conv_rows):
    last = coded.shape[0] - 8
    embed_scale = jnp.exp2(coded[pl.ds(last + 2, 1), :])
    total = coded[pl.ds(last, 8), pl.ds(0, 128)] + coded[pl.ds(last, 8), pl.ds(128, 128)]
    total = jnp.where(iota((8, 256), 0) == 0, jnp.concatenate([total, jnp.zeros((8, 128), F32)], axis=1), 0.0)
    embed = jnp.concatenate([coded[pl.ds(conv_rows, last - conv_rows), :], total], axis=0) * embed_scale
    return jnp.concatenate([coded[pl.ds(0, conv_rows), :] * jnp.exp2(coded[pl.ds(last + 1, 1), :]), embed], axis=0)


def scale_kernel(keep, other, embed, own, *coded):
    held = keep[...] + other[...]
    steps = exponent_of(held), exponent_of(embed[...])
    here = lax.axis_index("fsdp")

    def share(z):
        return jnp.concatenate([keep[z] + other[z], embed[z]], axis=0)

    own[...] = share(here)
    for place, target in enumerate(coded):
        store_scaled(target, share(here ^ (place % (keep.shape[0] - 1) + 1)), steps, keep.shape[1])


def first_sum_kernel(conv_rows, own, *refs):
    *received, coded = refs
    total = own[...]
    for part in received:
        total = total + load_coded(part, conv_rows)
    store_coded(coded, total, conv_rows)


def next_sum_kernel(conv_rows, mine, other, total, *coded):
    summed = load_coded(mine, conv_rows) + load_coded(other, conv_rows)
    total[...] = summed
    if coded:
        store_coded(coded[0], summed, conv_rows)


def output_kernel(own, other, grad_embed, grad_conv):
    conv_rows, count = grad_conv.shape[0] // 2, grad_embed.shape[0]
    core_zero = lax.rem(lax.axis_index("dp"), 2) == 0
    grad_conv[pl.ds(0, conv_rows), :] = jnp.where(core_zero, own[pl.ds(0, conv_rows), :], other[pl.ds(0, conv_rows), :])
    grad_conv[pl.ds(conv_rows, conv_rows), :] = jnp.where(
        core_zero, other[pl.ds(0, conv_rows), :], own[pl.ds(0, conv_rows), :]
    )
    half, depth = 3 * count // 8, count // LEVELS
    embed = own[pl.ds(conv_rows, half), :] + other[pl.ds(conv_rows, half), :]
    embed = jnp.concatenate([embed[:, :128], embed[:, 128:]], axis=0)
    last = own.shape[0] - 8
    total = own[pl.ds(last, 1), pl.ds(0, 128)] + other[pl.ds(last, 1), pl.ds(0, 128)]
    fourth = total - (embed[:depth] + embed[depth : 2 * depth] + embed[2 * depth :])
    embed = jnp.concatenate([embed, fourth], axis=0)
    row, lane = iota((count, count), 0), iota((count, count), 1)
    order = jnp.where(lane == row % LEVELS * depth + row // LEVELS, 1.0, 0.0).astype(BF16)
    result = None
    for _ in range(3):
        term = embed.astype(BF16)
        embed = embed - term.astype(F32)
        result = mm(order, term) if result is None else result + mm(order, term)
    grad_embed[...] = result


VMEM = pl.BlockSpec(memory_space=pltpu.VMEM)
HBM = pl.BlockSpec(memory_space=pltpu.HBM)
SAVED = (
    ((8, 256, 1024), BF16),
    ((4, 256, 1024), F32),
    ((4, 4, 256, 256), BF16),
    ((4, 256, 256), F32),
)


def forward(facies, prior_draws, recon_grad, w_embed, w_conv, w_head):
    samples = facies.shape[0]
    latent_width = prior_draws.shape[1]
    rows, lanes = samples * PATCH_X, PATCH_Y * PATCH_Z
    operands = (facies.reshape(rows, lanes), prior_draws, recon_grad, w_embed, w_conv, w_head)
    return pl.pallas_call(
        forward_kernel,
        out_shape=(pltpu.VMEM((samples, 2 * latent_width + 256), BF16),)
        + tuple(pltpu.VMEM(shape, kind) for shape, kind in SAVED)
        + (pltpu.VMEM(w_conv.shape, BF16), pltpu.VMEM(w_head.shape, BF16)),
        in_specs=[HBM] * 6,
        out_specs=(VMEM,) * 7,
        scratch_shapes=[
            pltpu.VMEM((lanes // 128, rows, 128), jnp.int32),
            pltpu.VMEM(prior_draws.shape, BF16),
            pltpu.VMEM(recon_grad.shape, BF16),
            pltpu.VMEM(w_embed.shape, BF16),
            pltpu.VMEM((128, 256), BF16),
            pltpu.VMEM((256, 1024), BF16),
            pltpu.SemaphoreType.DMA((lanes // 128 + 5,)),
        ],
        compiler_params=pltpu.CompilerParams(vmem_limit_bytes=30 * 2**20),
        name="forward",
    )(*(pltpu.with_memory_space_constraint(operand, pltpu.HBM) for operand in operands))


def backward(sizes, gathered, hidden, pre_conv, w_head):
    dp, fsdp = sizes
    devices, samples, width = gathered.shape
    payload = pltpu.VMEM((fsdp, 1024 // fsdp // 2, 256), F32)
    return pl.pallas_call(
        lambda *refs: backward_kernel(sizes, *refs),
        out_shape=(
            payload, payload, pltpu.VMEM((4, 256, 256), BF16), jax.ShapeDtypeStruct((256 // fsdp, 512), F32)
        ),
        in_specs=[VMEM] * 4,
        out_specs=(VMEM,) * 4,
        scratch_shapes=[pltpu.VMEM((devices, samples, width), F32), pltpu.VMEM((256, 512), F32)],
        compiler_params=pltpu.CompilerParams(vmem_limit_bytes=24 * 2**20),
        name="backward",
    )(gathered, hidden, pre_conv, w_head)


def embed_gradient(fsdp, grads, w_conv, pre_embed, one_hot):
    return pl.pallas_call(
        embed_kernel,
        out_shape=pltpu.VMEM((fsdp, (96 // fsdp + 7) // 8 * 8 + 8, 256), F32),
        in_specs=[VMEM] * 4,
        out_specs=VMEM,
        compiler_params=pltpu.CompilerParams(vmem_limit_bytes=24 * 2**20),
        cost_estimate=pl.CostEstimate(flops=16 * 10**8, bytes_accessed=10 * 2**20, transcendentals=0),
        name="embed_gradient",
    )(grads, w_conv, pre_embed, one_hot)


def place_of(x, core, z, fsdp):
    return (2 * x + core) * fsdp + z


def exchange(block, dp, fsdp, flip_x, flip_core, flip_z, among=None):
    pairs = []
    for x in range(dp // 2):
        for core in range(2):
            for z in range(fsdp):
                to = place_of(x ^ flip_x, core ^ flip_core, z ^ flip_z, fsdp)
                if among is None or z in among:
                    pairs.append((place_of(x, core, z, fsdp), to))
    return lax.ppermute(block, GROUP, pairs)


def gather_blocks(block, devices):
    copies = jnp.broadcast_to(block[None], (devices,) + block.shape)
    return lax.all_to_all(copies, GROUP, 0, 0, tiled=True)


def local_kernel(kernel, outs, name, *operands):
    return pl.pallas_call(
        kernel,
        out_shape=outs,
        in_specs=[VMEM] * len(operands),
        out_specs=(VMEM,) * len(outs),
        compiler_params=pltpu.CompilerParams(vmem_limit_bytes=16 * 2**20),
        name=name,
    )(*operands)


def to_half(coded):
    rounded = lax.reduce_precision(coded, exponent_bits=5, mantissa_bits=10)
    return rounded, rounded.astype(jnp.float16)


def reduce_to_owner(keep, other, embed, dp, fsdp):
    conv_rows, width = keep.shape[1:]
    rows = conv_rows + embed.shape[1]
    plain = jax.ShapeDtypeStruct((rows, width), F32)
    own, *coded = local_kernel(scale_kernel, (plain,) + (plain,) * (2 * fsdp - 2), "scale", keep, other, embed)
    received = []
    for place, part in enumerate(coded):
        flip = place % (fsdp - 1) + 1
        late = [0, flip]
        among = late if place < fsdp - 1 else [z for z in range(fsdp) if z not in late]
        received.append(exchange(part.astype(jnp.float16), dp, fsdp, 0, 0, flip, among).astype(F32))
    (coded,) = local_kernel(functools.partial(first_sum_kernel, conv_rows), (plain,), "sum_z", own, *received)
    flip = 1
    while flip < dp // 2:
        mine, sent = to_half(coded)
        other = exchange(sent, dp, fsdp, flip, 0, 0).astype(F32)
        flip *= 2
        outs = (plain,) * (2 if flip < dp // 2 else 1)
        total, *rest = local_kernel(functools.partial(next_sum_kernel, conv_rows), outs, "sum_x", mine, other)
        coded = rest[0] if rest else None
    return total, exchange(total, dp, fsdp, 0, 1, 0)


def shards(facies, prior_draws, recon_grad, w_embed, w_conv, w_head):
    dp, fsdp = lax.axis_size("dp"), lax.axis_size("fsdp")
    block, one_hot, pre_embed, hidden, pre_conv, w_conv, w_head = forward(
        facies, prior_draws, recon_grad, w_embed, w_conv, w_head
    )
    gathered = gather_blocks(block, dp * fsdp)
    keep, send, grads, grad_head = backward((dp, fsdp), gathered, hidden, pre_conv, w_head)
    received = exchange(send, dp, fsdp, 0, 1, 0)
    embed = embed_gradient(fsdp, grads, w_conv, pre_embed, one_hot)
    own, other = reduce_to_owner(keep, received, embed, dp, fsdp)
    grad_embed, grad_conv = pl.pallas_call(
        output_kernel,
        out_shape=(
            jax.ShapeDtypeStruct((256 // fsdp, 128), F32),
            jax.ShapeDtypeStruct((1024 // fsdp, 256), F32),
        ),
        in_specs=[VMEM] * 2,
        out_specs=(VMEM,) * 2,
        compiler_params=pltpu.CompilerParams(vmem_limit_bytes=16 * 2**20),
        name="outputs",
    )(own, other)
    return (grad_embed, grad_conv, grad_head)


def solution(mesh):
    return jax.shard_map(
        shards,
        mesh=mesh,
        in_specs=(
            P(("groups", "dp", "fsdp"), None, None),
            P(("groups", "dp", "fsdp"), None),
            P(("groups", "dp", "fsdp"), None),
            P(),
            P(),
            P(),
        ),
        out_specs=(
            P(("groups", "fsdp"), None),
            P(("groups", "fsdp"), None),
            P(("groups", "fsdp"), None),
        ),
        check_vma=False,
    )
```

```python
import functools

import jax
import jax.numpy as jnp
from jax import lax
from jax.experimental import pallas as pl
from jax.experimental.pallas import tpu as pltpu
from jax.sharding import PartitionSpec as P

PATCH_X = 64
PATCH_Y = 64
PATCH_Z = 32
LEVELS = 4
GROUP = ("dp", "fsdp")
NT = (((1,), (1,)), ((), ()))
F32 = jnp.float32
BF16 = jnp.bfloat16


def iota(shape, dim):
    return lax.broadcasted_iota(jnp.int32, shape, dim)


def mm(left, right):
    return jnp.dot(left, right, preferred_element_type=F32)


def mm_nt(left, right):
    return lax.dot_general(left, right, NT, preferred_element_type=F32)


def turned_weights(w_embed):
    turned = jnp.transpose(w_embed.astype(F32)).astype(BF16)
    row, lane = iota((256, 256), 0), iota((256, 256), 1)
    dx, k = row // 64, row % 4
    same = lane == jnp.where(k < 3, dx * 48 + k * 16, 192 + dx * 16) + row // 4 % 16
    return mm(turned, jnp.where(same, 1.0, 0.0).astype(BF16)).astype(BF16)


def sigmoid(value):
    return pltpu.reciprocal(1.0 + jnp.exp2(value * -1.4426950408889634), approx=True)


def silu_slope(value):
    gate = sigmoid(value)
    return gate * (1.0 + value * (1.0 - gate))


def forward_kernel(
    facies_hbm, prior_hbm, recon_hbm, w_embed_hbm, w_conv_hbm, w_head_hbm,
    block, pooled_lanes, recon, one_hot, pre_embed, hidden, pre_conv, w_conv, w_head,
    facies, prior, w_embed, packed, conv_turned, sem
):
    blocks = facies.shape[0]
    loads = [
        pltpu.make_async_copy(facies_hbm.at[:, pl.ds(b * 128, 128)], facies.at[b], sem.at[b]) for b in range(blocks)
    ]
    others = []
    for source, target in (
        (w_embed_hbm, w_embed), (w_conv_hbm, w_conv), (prior_hbm, prior), (recon_hbm, recon), (w_head_hbm, w_head)
    ):
        others.append(pltpu.make_async_copy(source, target, sem.at[blocks + len(others)]))
    for load in others[:2] + loads:
        load.start()
    others[0].wait()
    packed[...] = turned_weights(w_embed[...])
    others[1].wait()
    conv_turned[...] = jnp.transpose(w_conv[...].astype(F32)).astype(BF16)
    low = iota((8, 256), 0) < 4

    def build(half, dx2):
        for dx in range(4):
            rows = [
                facies[2 * b2 + dy2, pl.ds(4 * dx2 + dx, 32, stride=8), :]
                for dy2 in range(2)
                for b2 in range(4 * half, 4 * half + 4)
            ]
            turned = jnp.transpose(jnp.concatenate(rows, axis=0).astype(F32))
            for cp in range(4):
                part = [turned[dy * 32 + cp * 8 : dy * 32 + cp * 8 + 8] for dy in range(4)]
                swapped = [pltpu.roll(piece, 4, 0) for piece in part]
                for dz2 in range(2):
                    pieces = [
                        jnp.where(low, part[dy], swapped[dy + 1]) if dz2 == 0 else jnp.where(low, swapped[dy], part[dy + 1])
                        for dy in (0, 2)
                    ]
                    cells = jnp.concatenate(pieces, axis=0).astype(BF16)
                    for k in range(LEVELS):
                        hot = jnp.where(cells == BF16(k), BF16(1.0), BF16(0.0))
                        first = dx * 48 + k * 16 if k < 3 else 192 + dx * 16
                        for dy2 in range(2):
                            at = (2 * dx2 + dy2) * 256 + half * 128
                            one_hot[2 * cp + dz2, pl.ds(first, 16), pl.ds(at, 128)] = hot[:, dy2 * 128 : dy2 * 128 + 128]

    def embed(cp, dx2):
        for dz2 in range(2):
            rows, at = pl.ds(dz2 * 128, 128), pl.ds(dx2 * 512, 512)
            pre = mm(packed[...], one_hot[2 * cp + dz2, :, at])
            pre_embed[cp, rows, at] = pre
            act = (pre * sigmoid(pre)).astype(BF16)
            hidden[cp, 2 * dx2, rows, :] = act[:, :256]
            hidden[cp, 2 * dx2 + 1, rows, :] = act[:, 256:]

    for half in range(2):
        for load in loads[half * blocks // 2 : (half + 1) * blocks // 2]:
            load.wait()
        if half == 0:
            for load in others[2:]:
                load.start()
            build(0, 0)
            build(0, 1)
    build(1, 0)
    for cp in range(4):
        embed(cp, 0)
    build(1, 1)
    sums = jnp.zeros((256, 128), F32)
    for cp in range(4):
        embed(cp, 1)
        pre = mm(conv_turned[...], hidden[cp].reshape(1024, 256))
        pre_conv[cp] = pre
        act = pre * sigmoid(pre)
        sums = sums + act[:, :128] + act[:, 128:]
    pick = jnp.where(iota((128, 128), 1) // 8 % 4 == iota((128, 128), 0) // 8 % 4, 1.0, 0.0)
    total = lax.dot_general(pick, sums, NT, precision=lax.Precision.HIGHEST, preferred_element_type=F32) / 256.0
    pooled_lanes[...] = total.astype(BF16)
    block[:, pl.ds(1024, 256)] = jnp.concatenate([total[8 * s : 8 * s + 1] for s in range(4)], axis=0).astype(BF16)
    for load in others[2:]:
        load.wait()
    block[:, pl.ds(0, 512)] = prior[...]
    block[:, pl.ds(512, 512)] = recon[...]


def pair_kernel(queries, query_square, keys):
    inner = mm_nt(queries, keys)
    key_float = keys.astype(F32)
    count = keys.shape[0]
    key_square = jnp.sum(key_float * key_float, axis=1, keepdims=True)
    key_row = jnp.transpose(jnp.broadcast_to(key_square, (count, 128)))[:1]
    kern = jnp.exp(-(query_square + key_row - 2.0 * inner) / keys.shape[1])
    return jnp.sum(kern, axis=1, keepdims=True), mm(kern.astype(BF16), keys)


def group_rows(gathered, ordered):
    for owner in range(gathered.shape[0]):
        ordered[owner] = gathered[owner].astype(F32)
    return ordered[...].reshape(gathered.shape[0] * gathered.shape[1], gathered.shape[2])


def latent_rows(pooled, w_head):
    return mm(pooled, w_head[...]).astype(BF16)


def cotangent_rows(queries, keys, prior, recon):
    query_float = queries.astype(F32)
    square = jnp.sum(query_float * query_float, axis=1, keepdims=True)
    self_sum, self_mix = pair_kernel(queries, square, keys)
    cross_sum, cross_mix = pair_kernel(queries, square, prior)
    pull = -32.0 / keys.shape[0] * ((self_sum - cross_sum) * query_float - self_mix + cross_mix)
    return (recon + pull).astype(BF16)


def head_kernel(gathered, w_head, after, grad_head, token, ordered, head_full):
    token[...] = jnp.zeros(token.shape, F32)
    full = group_rows(gathered, ordered)
    latent = latent_rows(full[:, 1024:].astype(BF16), w_head)
    cotangent = cotangent_rows(latent, latent, full[:, :512].astype(BF16), full[:, 512:1024])
    head_full[...] = mm(jnp.transpose(full[:, 1024:]).astype(BF16), cotangent)
    share = grad_head.shape[0]
    start = pl.multiple_of(lax.axis_index("fsdp") * share, share)
    grad_head[...] = head_full[pl.ds(start, share), :]


def backward_kernel(gathered, pooled_lanes, recon, hidden, pre_conv, w_head, keep, send, grads, ordered):
    full = group_rows(gathered, ordered)
    queries = latent_rows(pooled_lanes[...], w_head)
    keys = latent_rows(full[:, 1024:].astype(BF16), w_head)
    recon_float = recon[...].astype(F32)
    recon_lanes = jnp.concatenate(
        [jnp.broadcast_to(recon_float[s : s + 1], (8, recon.shape[1])) for s in range(4)] * 4, axis=0
    )
    cotangent = cotangent_rows(queries, keys, full[:, :512].astype(BF16), recon_lanes)
    back_pool = mm_nt(w_head[...], cotangent) / 256.0
    back_pool = jnp.concatenate([back_pool, back_pool], axis=1)
    fsdp = keep.shape[0]
    conv_total = None
    for cp in range(4):
        grads[cp] = (back_pool * silu_slope(pre_conv[cp])).astype(BF16)
        term = mm_nt(hidden[cp].reshape(1024, 256), grads[cp])
        conv_total = term if cp == 0 else conv_total + term
    core_zero = lax.rem(lax.axis_index("dp"), 2) == 0
    rows = keep.shape[1]
    for f in range(fsdp):
        at = 2 * f * rows
        first, second = conv_total[at : at + rows], conv_total[at + rows : at + 2 * rows]
        keep[f] = jnp.where(core_zero, first, second)
        send[f] = jnp.where(core_zero, second, first)


def embed_kernel(grads, w_conv, pre_embed, one_hot, embed_out):
    embed = None
    ones = jnp.ones((16, 1024), BF16)
    for cp in range(4):
        signals = []
        for dx2 in range(2):
            back_rows = mm(w_conv[pl.ds(dx2 * 512, 512), :], grads[cp])
            back_rows = jnp.concatenate([back_rows[:256], back_rows[256:]], axis=1)
            signals.append((back_rows * silu_slope(pre_embed[cp, :, pl.ds(dx2 * 512, 512)])).astype(BF16))
        signal = jnp.concatenate(signals, axis=1)
        for dz2 in range(2):
            rows = jnp.concatenate([one_hot[2 * cp + dz2, pl.ds(0, 192), :], ones], axis=0)
            term = mm_nt(rows, signal[dz2 * 128 : dz2 * 128 + 128])
            embed = term if embed is None else embed + term
    shares = embed_out.shape[0]
    depth = 64 // shares
    half = 3 * depth // 2
    embed_out[...] = jnp.zeros(embed_out.shape, F32)
    for f in range(shares):
        dx, at = f * 4 // shares, f * depth % 16
        share = jnp.concatenate([embed[dx * 48 + k * 16 + at :][:depth] for k in range(3)], axis=0)
        for side in range(2):
            embed_out[f, pl.ds(0, half), pl.ds(side * 128, 128)] = share[side * half : (side + 1) * half]
        embed_out[f, pl.ds(embed_out.shape[1] - 8, 8), pl.ds(0, 128)] = embed[192:200]


def exponent_of(part):
    top = jnp.abs(part)
    while top.ndim > 2:
        top = jnp.max(top, axis=0)
    top = jnp.max(jnp.max(top, axis=0, keepdims=True), axis=1, keepdims=True)
    return jnp.clip(jnp.floor(jnp.log2(jnp.maximum(top, 1e-37))) - 14.0, -124.0, 114.0)


def store_coded(coded, part, conv_rows):
    store_scaled(coded, part, (exponent_of(part[:conv_rows]), exponent_of(part[conv_rows:])), conv_rows)


def store_scaled(coded, part, steps, conv_rows):
    last = part.shape[0] - 8
    coded[pl.ds(0, conv_rows), :] = part[:conv_rows] * jnp.exp2(-steps[0])
    coded[pl.ds(conv_rows, last - conv_rows), :] = part[conv_rows:last] * jnp.exp2(-steps[1])
    total = part[last:, :128] * jnp.exp2(-steps[1])
    high = total.astype(BF16).astype(F32)
    row = iota((8, 256), 0)
    tail = jnp.where(row == 1, steps[0], steps[1])
    coded[pl.ds(last, 8), :] = jnp.where(row == 0, jnp.concatenate([high, total - high], axis=1), tail)


def load_coded(coded, conv_rows):
    last = coded.shape[0] - 8
    embed_scale = jnp.exp2(coded[pl.ds(last + 2, 1), :])
    total = coded[pl.ds(last, 8), pl.ds(0, 128)] + coded[pl.ds(last, 8), pl.ds(128, 128)]
    total = jnp.where(iota((8, 256), 0) == 0, jnp.concatenate([total, jnp.zeros((8, 128), F32)], axis=1), 0.0)
    embed = jnp.concatenate([coded[pl.ds(conv_rows, last - conv_rows), :], total], axis=0) * embed_scale
    return jnp.concatenate([coded[pl.ds(0, conv_rows), :] * jnp.exp2(coded[pl.ds(last + 1, 1), :]), embed], axis=0)


def scale_kernel(keep, other, embed, own, *coded):
    held = keep[...] + other[...]
    steps = exponent_of(held), exponent_of(embed[...])
    here = lax.axis_index("fsdp")

    def share(z):
        return jnp.concatenate([keep[z] + other[z], embed[z]], axis=0)

    own[...] = share(here)
    for place, target in enumerate(coded):
        store_scaled(target, share(here ^ (place + 1)), steps, keep.shape[1])


def first_sum_kernel(conv_rows, own, *refs):
    *received, coded = refs
    total = own[...]
    for part in received:
        total = total + load_coded(part, conv_rows)
    store_coded(coded, total, conv_rows)


def next_sum_kernel(conv_rows, mine, other, total, *coded):
    summed = load_coded(mine, conv_rows) + load_coded(other, conv_rows)
    total[...] = summed
    if coded:
        store_coded(coded[0], summed, conv_rows)


def output_kernel(own, other, grad_embed, grad_conv):
    conv_rows, count = grad_conv.shape[0] // 2, grad_embed.shape[0]
    core_zero = lax.rem(lax.axis_index("dp"), 2) == 0
    grad_conv[pl.ds(0, conv_rows), :] = jnp.where(core_zero, own[pl.ds(0, conv_rows), :], other[pl.ds(0, conv_rows), :])
    grad_conv[pl.ds(conv_rows, conv_rows), :] = jnp.where(
        core_zero, other[pl.ds(0, conv_rows), :], own[pl.ds(0, conv_rows), :]
    )
    half, depth = 3 * count // 8, count // LEVELS
    embed = own[pl.ds(conv_rows, half), :] + other[pl.ds(conv_rows, half), :]
    embed = jnp.concatenate([embed[:, :128], embed[:, 128:]], axis=0)
    last = own.shape[0] - 8
    total = own[pl.ds(last, 1), pl.ds(0, 128)] + other[pl.ds(last, 1), pl.ds(0, 128)]
    fourth = total - (embed[:depth] + embed[depth : 2 * depth] + embed[2 * depth :])
    embed = jnp.concatenate([embed, fourth], axis=0)
    row, lane = iota((count, count), 0), iota((count, count), 1)
    order = jnp.where(lane == row % LEVELS * depth + row // LEVELS, 1.0, 0.0).astype(BF16)
    result = None
    for _ in range(3):
        term = embed.astype(BF16)
        embed = embed - term.astype(F32)
        result = mm(order, term) if result is None else result + mm(order, term)
    grad_embed[...] = result


VMEM = pl.BlockSpec(memory_space=pltpu.VMEM)
HBM = pl.BlockSpec(memory_space=pltpu.HBM)
SAVED = (
    ((8, 256, 1024), BF16),
    ((4, 256, 1024), F32),
    ((4, 4, 256, 256), BF16),
    ((4, 256, 256), F32),
)


def forward(facies, prior_draws, recon_grad, w_embed, w_conv, w_head):
    samples = facies.shape[0]
    latent_width = prior_draws.shape[1]
    rows, lanes = samples * PATCH_X, PATCH_Y * PATCH_Z
    operands = (facies.reshape(rows, lanes), prior_draws, recon_grad, w_embed, w_conv, w_head)
    return pl.pallas_call(
        forward_kernel,
        out_shape=(pltpu.VMEM((samples, 2 * latent_width + 256), BF16),)
        + (pltpu.VMEM((128, 256), BF16), pltpu.VMEM(recon_grad.shape, BF16))
        + tuple(pltpu.VMEM(shape, kind) for shape, kind in SAVED)
        + (pltpu.VMEM(w_conv.shape, BF16), pltpu.VMEM(w_head.shape, BF16)),
        in_specs=[HBM] * 6,
        out_specs=(VMEM,) * 9,
        scratch_shapes=[
            pltpu.VMEM((lanes // 128, rows, 128), jnp.int32),
            pltpu.VMEM(prior_draws.shape, BF16),
            pltpu.VMEM(w_embed.shape, BF16),
            pltpu.VMEM((128, 256), BF16),
            pltpu.VMEM((256, 1024), BF16),
            pltpu.SemaphoreType.DMA((lanes // 128 + 5,)),
        ],
        compiler_params=pltpu.CompilerParams(vmem_limit_bytes=30 * 2**20),
        name="forward",
    )(*(pltpu.with_memory_space_constraint(operand, pltpu.HBM) for operand in operands))


def backward(fsdp, gathered, *operands):
    devices, samples, width = gathered.shape
    payload = pltpu.VMEM((fsdp, 1024 // fsdp // 2, 256), F32)
    return pl.pallas_call(
        backward_kernel,
        out_shape=(payload, payload, pltpu.VMEM((4, 256, 256), BF16)),
        in_specs=[VMEM] * 6,
        out_specs=(VMEM,) * 3,
        scratch_shapes=[pltpu.VMEM((devices, samples, width), F32)],
        compiler_params=pltpu.CompilerParams(vmem_limit_bytes=24 * 2**20),
        name="backward",
    )(gathered, *operands)


def head_gradient(fsdp, gathered, w_head, after):
    devices, samples, width = gathered.shape
    return pl.pallas_call(
        head_kernel,
        out_shape=(jax.ShapeDtypeStruct((256 // fsdp, 512), F32), pltpu.VMEM((8, 128), F32)),
        in_specs=[VMEM] * 2 + [HBM],
        out_specs=(VMEM,) * 2,
        scratch_shapes=[pltpu.VMEM((devices, samples, width), F32), pltpu.VMEM((256, 512), F32)],
        compiler_params=pltpu.CompilerParams(vmem_limit_bytes=16 * 2**20),
        cost_estimate=pl.CostEstimate(flops=2 * 10**9, bytes_accessed=2 * 2**20, transcendentals=10000),
        name="head_gradient",
    )(gathered, w_head, after)


def embed_gradient(fsdp, grads, w_conv, pre_embed, one_hot):
    return pl.pallas_call(
        embed_kernel,
        out_shape=pltpu.VMEM((fsdp, (96 // fsdp + 7) // 8 * 8 + 8, 256), F32),
        in_specs=[VMEM] * 4,
        out_specs=VMEM,
        compiler_params=pltpu.CompilerParams(vmem_limit_bytes=24 * 2**20),
        cost_estimate=pl.CostEstimate(flops=16 * 10**8, bytes_accessed=10 * 2**20, transcendentals=0),
        name="embed_gradient",
    )(grads, w_conv, pre_embed, one_hot)


def place_of(x, core, z, fsdp):
    return (2 * x + core) * fsdp + z


def exchange(block, dp, fsdp, flip_x, flip_core, flip_z):
    pairs = []
    for x in range(dp // 2):
        for core in range(2):
            for z in range(fsdp):
                pairs.append((place_of(x, core, z, fsdp), place_of(x ^ flip_x, core ^ flip_core, z ^ flip_z, fsdp)))
    return lax.ppermute(block, GROUP, pairs)


def gather_blocks(block, devices):
    copies = jnp.broadcast_to(block[None], (devices,) + block.shape)
    return lax.all_to_all(copies, GROUP, 0, 0, tiled=True)


def local_kernel(kernel, outs, name, *operands, unread=()):
    return pl.pallas_call(
        lambda *refs: kernel(*refs[: len(operands)], *refs[len(operands) + len(unread) :]),
        out_shape=outs,
        in_specs=[VMEM] * (len(operands) + len(unread)),
        out_specs=(VMEM,) * len(outs),
        compiler_params=pltpu.CompilerParams(vmem_limit_bytes=16 * 2**20),
        name=name,
    )(*operands, *unread)


def to_half(coded):
    rounded = lax.reduce_precision(coded, exponent_bits=5, mantissa_bits=10)
    return rounded, rounded.astype(jnp.float16)


def reduce_to_owner(keep, other, embed, gathered, w_head, dp, fsdp):
    conv_rows, width = keep.shape[1:]
    rows = conv_rows + embed.shape[1]
    plain = jax.ShapeDtypeStruct((rows, width), F32)
    own, *coded = local_kernel(scale_kernel, (plain,) + (plain,) * (fsdp - 1), "scale", keep, other, embed)
    received = [
        exchange(to_half(part)[1], dp, fsdp, 0, 0, place + 1).astype(F32) for place, part in enumerate(coded)
    ]
    grad_head, token = head_gradient(fsdp, gathered, w_head, own)
    (coded,) = local_kernel(
        functools.partial(first_sum_kernel, conv_rows), (plain,), "sum_z", own, *received, unread=(token,)
    )
    flip = 1
    while flip < dp // 2:
        mine, sent = to_half(coded)
        other = exchange(sent, dp, fsdp, flip, 0, 0).astype(F32)
        flip *= 2
        outs = (plain,) * (2 if flip < dp // 2 else 1)
        total, *rest = local_kernel(functools.partial(next_sum_kernel, conv_rows), outs, "sum_x", mine, other)
        coded = rest[0] if rest else None
    return total, exchange(total, dp, fsdp, 0, 1, 0), grad_head


def shards(facies, prior_draws, recon_grad, w_embed, w_conv, w_head):
    dp, fsdp = lax.axis_size("dp"), lax.axis_size("fsdp")
    block, pooled_lanes, recon, one_hot, pre_embed, hidden, pre_conv, w_conv, w_head = forward(
        facies, prior_draws, recon_grad, w_embed, w_conv, w_head
    )
    gathered = gather_blocks(block, dp * fsdp)
    keep, send, grads = backward(fsdp, gathered, pooled_lanes, recon, hidden, pre_conv, w_head)
    received = exchange(send, dp, fsdp, 0, 1, 0)
    embed = embed_gradient(fsdp, grads, w_conv, pre_embed, one_hot)
    own, other, grad_head = reduce_to_owner(keep, received, embed, gathered, w_head, dp, fsdp)
    grad_embed, grad_conv = pl.pallas_call(
        output_kernel,
        out_shape=(
            jax.ShapeDtypeStruct((256 // fsdp, 128), F32),
            jax.ShapeDtypeStruct((1024 // fsdp, 256), F32),
        ),
        in_specs=[VMEM] * 2,
        out_specs=(VMEM,) * 2,
        compiler_params=pltpu.CompilerParams(vmem_limit_bytes=16 * 2**20),
        name="outputs",
    )(own, other)
    return (grad_embed, grad_conv, grad_head)


def solution(mesh):
    return jax.shard_map(
        shards,
        mesh=mesh,
        in_specs=(
            P(("groups", "dp", "fsdp"), None, None),
            P(("groups", "dp", "fsdp"), None),
            P(("groups", "dp", "fsdp"), None),
            P(),
            P(),
            P(),
        ),
        out_specs=(
            P(("groups", "fsdp"), None),
            P(("groups", "fsdp"), None),
            P(("groups", "fsdp"), None),
        ),
        check_vma=False,
    )
```

```python
import functools

import jax
import jax.numpy as jnp
from jax import lax
from jax.experimental import pallas as pl
from jax.experimental.pallas import tpu as pltpu
from jax.sharding import PartitionSpec as P

PATCH_X = 64
PATCH_Y = 64
PATCH_Z = 32
LEVELS = 4
GROUP = ("dp", "fsdp")
NT = (((1,), (1,)), ((), ()))
F32 = jnp.float32
BF16 = jnp.bfloat16


def iota(shape, dim):
    return lax.broadcasted_iota(jnp.int32, shape, dim)


def mm(left, right):
    return jnp.dot(left, right, preferred_element_type=F32)


def mm_nt(left, right):
    return lax.dot_general(left, right, NT, preferred_element_type=F32)


def turned_weights(w_embed):
    turned = jnp.transpose(w_embed.astype(F32)).astype(BF16)
    row, lane = iota((256, 256), 0), iota((256, 256), 1)
    dx, k = row // 64, row % 4
    same = lane == jnp.where(k < 3, dx * 48 + k * 16, 192 + dx * 16) + row // 4 % 16
    return mm(turned, jnp.where(same, 1.0, 0.0).astype(BF16)).astype(BF16)


def sigmoid(value):
    return pltpu.reciprocal(1.0 + jnp.exp2(value * -1.4426950408889634), approx=True)


def silu_slope(value):
    gate = sigmoid(value)
    return gate * (1.0 + value * (1.0 - gate))


def forward_kernel(
    facies_hbm, prior_hbm, recon_hbm, w_embed_hbm, w_conv_hbm, w_head_hbm,
    block, pooled_lanes, recon, one_hot, pre_embed, hidden, pre_conv, w_conv, w_head,
    facies, prior, w_embed, packed, conv_turned, sem
):
    blocks = facies.shape[0]
    loads = [
        pltpu.make_async_copy(facies_hbm.at[:, pl.ds(b * 128, 128)], facies.at[b], sem.at[b]) for b in range(blocks)
    ]
    others = []
    for source, target in (
        (w_embed_hbm, w_embed), (w_conv_hbm, w_conv), (prior_hbm, prior), (recon_hbm, recon), (w_head_hbm, w_head)
    ):
        others.append(pltpu.make_async_copy(source, target, sem.at[blocks + len(others)]))
    for load in others[:2] + loads:
        load.start()
    others[0].wait()
    packed[...] = turned_weights(w_embed[...])
    others[1].wait()
    conv_turned[...] = jnp.transpose(w_conv[...].astype(F32)).astype(BF16)
    low = iota((8, 256), 0) < 4

    def build(half, dx2):
        for dx in range(4):
            rows = [
                facies[2 * b2 + dy2, pl.ds(4 * dx2 + dx, 32, stride=8), :]
                for dy2 in range(2)
                for b2 in range(4 * half, 4 * half + 4)
            ]
            turned = jnp.transpose(jnp.concatenate(rows, axis=0).astype(F32))
            for cp in range(4):
                part = [turned[dy * 32 + cp * 8 : dy * 32 + cp * 8 + 8] for dy in range(4)]
                swapped = [pltpu.roll(piece, 4, 0) for piece in part]
                for dz2 in range(2):
                    pieces = [
                        jnp.where(low, part[dy], swapped[dy + 1]) if dz2 == 0 else jnp.where(low, swapped[dy], part[dy + 1])
                        for dy in (0, 2)
                    ]
                    cells = jnp.concatenate(pieces, axis=0).astype(BF16)
                    for k in range(LEVELS):
                        hot = jnp.where(cells == BF16(k), BF16(1.0), BF16(0.0))
                        first = dx * 48 + k * 16 if k < 3 else 192 + dx * 16
                        for dy2 in range(2):
                            at = (2 * dx2 + dy2) * 256 + half * 128
                            one_hot[2 * cp + dz2, pl.ds(first, 16), pl.ds(at, 128)] = hot[:, dy2 * 128 : dy2 * 128 + 128]

    def embed(cp, dx2):
        for dz2 in range(2):
            rows, at = pl.ds(dz2 * 128, 128), pl.ds(dx2 * 512, 512)
            pre = mm(packed[...], one_hot[2 * cp + dz2, :, at])
            pre_embed[cp, rows, at] = pre
            act = (pre * sigmoid(pre)).astype(BF16)
            hidden[cp, 2 * dx2, rows, :] = act[:, :256]
            hidden[cp, 2 * dx2 + 1, rows, :] = act[:, 256:]

    for half in range(2):
        for load in loads[half * blocks // 2 : (half + 1) * blocks // 2]:
            load.wait()
        if half == 0:
            for load in others[2:]:
                load.start()
            build(0, 0)
            build(0, 1)
    build(1, 0)
    for cp in range(4):
        embed(cp, 0)
    build(1, 1)
    sums = jnp.zeros((256, 128), F32)
    for cp in range(4):
        embed(cp, 1)
        pre = mm(conv_turned[...], hidden[cp].reshape(1024, 256))
        pre_conv[cp] = pre
        act = pre * sigmoid(pre)
        sums = sums + act[:, :128] + act[:, 128:]
    pick = jnp.where(iota((128, 128), 1) // 8 % 4 == iota((128, 128), 0) // 8 % 4, 1.0, 0.0)
    total = lax.dot_general(pick, sums, NT, precision=lax.Precision.HIGHEST, preferred_element_type=F32) / 256.0
    pooled_lanes[...] = total.astype(BF16)
    block[:, pl.ds(1024, 256)] = jnp.concatenate([total[8 * s : 8 * s + 1] for s in range(4)], axis=0).astype(BF16)
    for load in others[2:]:
        load.wait()
    block[:, pl.ds(0, 512)] = prior[...]
    block[:, pl.ds(512, 512)] = recon[...]


def pair_kernel(queries, query_square, keys):
    inner = mm_nt(queries, keys)
    key_float = keys.astype(F32)
    count = keys.shape[0]
    key_square = jnp.sum(key_float * key_float, axis=1, keepdims=True)
    key_row = jnp.transpose(jnp.broadcast_to(key_square, (count, 128)))[:1]
    kern = jnp.exp(-(query_square + key_row - 2.0 * inner) / keys.shape[1])
    return jnp.sum(kern, axis=1, keepdims=True), mm(kern.astype(BF16), keys)


def group_rows(gathered, ordered):
    for owner in range(gathered.shape[0]):
        ordered[owner] = gathered[owner].astype(F32)
    return ordered[...].reshape(gathered.shape[0] * gathered.shape[1], gathered.shape[2])


def latent_rows(pooled, w_head):
    return mm(pooled, w_head[...]).astype(BF16)


def cotangent_rows(queries, keys, prior, recon):
    query_float = queries.astype(F32)
    square = jnp.sum(query_float * query_float, axis=1, keepdims=True)
    self_sum, self_mix = pair_kernel(queries, square, keys)
    cross_sum, cross_mix = pair_kernel(queries, square, prior)
    pull = -32.0 / keys.shape[0] * ((self_sum - cross_sum) * query_float - self_mix + cross_mix)
    return (recon + pull).astype(BF16)


def head_kernel(gathered, w_head, after, grad_head, token, ordered, head_full):
    token[...] = jnp.zeros(token.shape, F32)
    full = group_rows(gathered, ordered)
    latent = latent_rows(full[:, 1024:].astype(BF16), w_head)
    cotangent = cotangent_rows(latent, latent, full[:, :512].astype(BF16), full[:, 512:1024])
    head_full[...] = mm(jnp.transpose(full[:, 1024:]).astype(BF16), cotangent)
    share = grad_head.shape[0]
    start = pl.multiple_of(lax.axis_index("fsdp") * share, share)
    grad_head[...] = head_full[pl.ds(start, share), :]


def backward_kernel(gathered, pooled_lanes, recon, hidden, pre_conv, w_head, keep, send, grads, ordered):
    full = group_rows(gathered, ordered)
    queries = latent_rows(pooled_lanes[...], w_head)
    keys = latent_rows(full[:, 1024:].astype(BF16), w_head)
    recon_float = recon[...].astype(F32)
    recon_lanes = jnp.concatenate(
        [jnp.broadcast_to(recon_float[s : s + 1], (8, recon.shape[1])) for s in range(4)] * 4, axis=0
    )
    cotangent = cotangent_rows(queries, keys, full[:, :512].astype(BF16), recon_lanes)
    back_pool = mm_nt(w_head[...], cotangent) / 256.0
    back_pool = jnp.concatenate([back_pool, back_pool], axis=1)
    fsdp = keep.shape[0]
    conv_total = None
    for cp in range(4):
        grads[cp] = (back_pool * silu_slope(pre_conv[cp])).astype(BF16)
        term = mm_nt(hidden[cp].reshape(1024, 256), grads[cp])
        conv_total = term if cp == 0 else conv_total + term
    core_zero = lax.rem(lax.axis_index("dp"), 2) == 0
    rows = keep.shape[1]
    for f in range(fsdp):
        at = 2 * f * rows
        first, second = conv_total[at : at + rows], conv_total[at + rows : at + 2 * rows]
        keep[f] = jnp.where(core_zero, first, second)
        send[f] = jnp.where(core_zero, second, first)


def embed_kernel(grads, w_conv, pre_embed, one_hot, embed_out):
    embed = None
    ones = jnp.ones((16, 1024), BF16)
    for cp in range(4):
        signals = []
        for dx2 in range(2):
            back_rows = mm(w_conv[pl.ds(dx2 * 512, 512), :], grads[cp])
            back_rows = jnp.concatenate([back_rows[:256], back_rows[256:]], axis=1)
            signals.append((back_rows * silu_slope(pre_embed[cp, :, pl.ds(dx2 * 512, 512)])).astype(BF16))
        signal = jnp.concatenate(signals, axis=1)
        for dz2 in range(2):
            rows = jnp.concatenate([one_hot[2 * cp + dz2, pl.ds(0, 192), :], ones], axis=0)
            term = mm_nt(rows, signal[dz2 * 128 : dz2 * 128 + 128])
            embed = term if embed is None else embed + term
    shares = embed_out.shape[0]
    depth = 64 // shares
    half = 3 * depth // 2
    embed_out[...] = jnp.zeros(embed_out.shape, F32)
    for f in range(shares):
        dx, at = f * 4 // shares, f * depth % 16
        share = jnp.concatenate([embed[dx * 48 + k * 16 + at :][:depth] for k in range(3)], axis=0)
        for side in range(2):
            embed_out[f, pl.ds(0, half), pl.ds(side * 128, 128)] = share[side * half : (side + 1) * half]
        embed_out[f, pl.ds(embed_out.shape[1] - 8, 8), pl.ds(0, 128)] = embed[192:200]


def exponent_of(part):
    top = jnp.abs(part)
    while top.ndim > 2:
        top = jnp.max(top, axis=0)
    top = jnp.max(jnp.max(top, axis=0, keepdims=True), axis=1, keepdims=True)
    return jnp.clip(jnp.floor(jnp.log2(jnp.maximum(top, 1e-37))) - 14.0, -124.0, 114.0)


def store_coded(coded, part, conv_rows):
    store_scaled(coded, part, (exponent_of(part[:conv_rows]), exponent_of(part[conv_rows:])), conv_rows)


def store_scaled(coded, part, steps, conv_rows):
    last = part.shape[0] - 8
    coded[pl.ds(0, conv_rows), :] = part[:conv_rows] * jnp.exp2(-steps[0])
    coded[pl.ds(conv_rows, last - conv_rows), :] = part[conv_rows:last] * jnp.exp2(-steps[1])
    total = part[last:, :128] * jnp.exp2(-steps[1])
    high = total.astype(BF16).astype(F32)
    row = iota((8, 256), 0)
    tail = jnp.where(row == 1, steps[0], steps[1])
    coded[pl.ds(last, 8), :] = jnp.where(row == 0, jnp.concatenate([high, total - high], axis=1), tail)


def load_coded(coded, conv_rows):
    last = coded.shape[0] - 8
    embed_scale = jnp.exp2(coded[pl.ds(last + 2, 1), :])
    total = coded[pl.ds(last, 8), pl.ds(0, 128)] + coded[pl.ds(last, 8), pl.ds(128, 128)]
    total = jnp.where(iota((8, 256), 0) == 0, jnp.concatenate([total, jnp.zeros((8, 128), F32)], axis=1), 0.0)
    embed = jnp.concatenate([coded[pl.ds(conv_rows, last - conv_rows), :], total], axis=0) * embed_scale
    return jnp.concatenate([coded[pl.ds(0, conv_rows), :] * jnp.exp2(coded[pl.ds(last + 1, 1), :]), embed], axis=0)


def scale_kernel(keep, other, embed, own, *coded):
    held = keep[...] + other[...]
    steps = exponent_of(held), exponent_of(embed[...])
    here = lax.axis_index("fsdp")

    def share(z):
        return jnp.concatenate([keep[z] + other[z], embed[z]], axis=0)

    own[...] = share(here)
    for place, target in enumerate(coded):
        store_scaled(target, share(here ^ (place + 1)), steps, keep.shape[1])


def first_sum_kernel(conv_rows, own, *refs):
    *received, coded = refs
    total = own[...]
    for part in received:
        total = total + load_coded(part, conv_rows)
    store_coded(coded, total, conv_rows)


def next_sum_kernel(conv_rows, mine, other, total, *coded):
    summed = load_coded(mine, conv_rows) + load_coded(other, conv_rows)
    total[...] = summed
    if coded:
        store_coded(coded[0], summed, conv_rows)


def output_kernel(own, other, grad_embed, grad_conv):
    conv_rows, count = grad_conv.shape[0] // 2, grad_embed.shape[0]
    core_zero = lax.rem(lax.axis_index("dp"), 2) == 0
    grad_conv[pl.ds(0, conv_rows), :] = jnp.where(core_zero, own[pl.ds(0, conv_rows), :], other[pl.ds(0, conv_rows), :])
    grad_conv[pl.ds(conv_rows, conv_rows), :] = jnp.where(
        core_zero, other[pl.ds(0, conv_rows), :], own[pl.ds(0, conv_rows), :]
    )
    half, depth = 3 * count // 8, count // LEVELS
    embed = own[pl.ds(conv_rows, half), :] + other[pl.ds(conv_rows, half), :]
    embed = jnp.concatenate([embed[:, :128], embed[:, 128:]], axis=0)
    last = own.shape[0] - 8
    total = own[pl.ds(last, 1), pl.ds(0, 128)] + other[pl.ds(last, 1), pl.ds(0, 128)]
    fourth = total - (embed[:depth] + embed[depth : 2 * depth] + embed[2 * depth :])
    embed = jnp.concatenate([embed, fourth], axis=0)
    row, lane = iota((count, count), 0), iota((count, count), 1)
    order = jnp.where(lane == row % LEVELS * depth + row // LEVELS, 1.0, 0.0).astype(BF16)
    result = None
    for _ in range(3):
        term = embed.astype(BF16)
        embed = embed - term.astype(F32)
        result = mm(order, term) if result is None else result + mm(order, term)
    grad_embed[...] = result


VMEM = pl.BlockSpec(memory_space=pltpu.VMEM)
HBM = pl.BlockSpec(memory_space=pltpu.HBM)
SAVED = (
    ((8, 256, 1024), BF16),
    ((4, 256, 1024), F32),
    ((4, 4, 256, 256), BF16),
    ((4, 256, 256), F32),
)


def forward(facies, prior_draws, recon_grad, w_embed, w_conv, w_head):
    samples = facies.shape[0]
    latent_width = prior_draws.shape[1]
    rows, lanes = samples * PATCH_X, PATCH_Y * PATCH_Z
    operands = (facies.reshape(rows, lanes), prior_draws, recon_grad, w_embed, w_conv, w_head)
    return pl.pallas_call(
        forward_kernel,
        out_shape=(pltpu.VMEM((samples, 2 * latent_width + 256), BF16),)
        + (pltpu.VMEM((128, 256), BF16), pltpu.VMEM(recon_grad.shape, BF16))
        + tuple(pltpu.VMEM(shape, kind) for shape, kind in SAVED)
        + (pltpu.VMEM(w_conv.shape, BF16), pltpu.VMEM(w_head.shape, BF16)),
        in_specs=[HBM] * 6,
        out_specs=(VMEM,) * 9,
        scratch_shapes=[
            pltpu.VMEM((lanes // 128, rows, 128), jnp.int32),
            pltpu.VMEM(prior_draws.shape, BF16),
            pltpu.VMEM(w_embed.shape, BF16),
            pltpu.VMEM((128, 256), BF16),
            pltpu.VMEM((256, 1024), BF16),
            pltpu.SemaphoreType.DMA((lanes // 128 + 5,)),
        ],
        compiler_params=pltpu.CompilerParams(vmem_limit_bytes=30 * 2**20),
        name="forward",
    )(*(pltpu.with_memory_space_constraint(operand, pltpu.HBM) for operand in operands))


def backward(fsdp, gathered, *operands):
    devices, samples, width = gathered.shape
    payload = pltpu.VMEM((fsdp, 1024 // fsdp // 2, 256), F32)
    return pl.pallas_call(
        backward_kernel,
        out_shape=(payload, payload, pltpu.VMEM((4, 256, 256), BF16)),
        in_specs=[VMEM] * 6,
        out_specs=(VMEM,) * 3,
        scratch_shapes=[pltpu.VMEM((devices, samples, width), F32)],
        compiler_params=pltpu.CompilerParams(vmem_limit_bytes=24 * 2**20),
        name="backward",
    )(gathered, *operands)


def head_gradient(fsdp, gathered, w_head, after):
    devices, samples, width = gathered.shape
    return pl.pallas_call(
        head_kernel,
        out_shape=(jax.ShapeDtypeStruct((256 // fsdp, 512), F32), pltpu.VMEM((8, 128), F32)),
        in_specs=[VMEM] * 2 + [HBM],
        out_specs=(VMEM,) * 2,
        scratch_shapes=[pltpu.VMEM((devices, samples, width), F32), pltpu.VMEM((256, 512), F32)],
        compiler_params=pltpu.CompilerParams(vmem_limit_bytes=16 * 2**20),
        cost_estimate=pl.CostEstimate(flops=2 * 10**9, bytes_accessed=2 * 2**20, transcendentals=10000),
        name="head_gradient",
    )(gathered, w_head, after)


def embed_gradient(fsdp, grads, w_conv, pre_embed, one_hot):
    return pl.pallas_call(
        embed_kernel,
        out_shape=pltpu.VMEM((fsdp, (96 // fsdp + 7) // 8 * 8 + 8, 256), F32),
        in_specs=[VMEM] * 4,
        out_specs=VMEM,
        compiler_params=pltpu.CompilerParams(vmem_limit_bytes=24 * 2**20),
        cost_estimate=pl.CostEstimate(flops=16 * 10**8, bytes_accessed=10 * 2**20, transcendentals=0),
        name="embed_gradient",
    )(grads, w_conv, pre_embed, one_hot)


def place_of(x, core, z, fsdp):
    return (2 * x + core) * fsdp + z


def exchange(block, dp, fsdp, flip_x, flip_core, flip_z):
    pairs = []
    for x in range(dp // 2):
        for core in range(2):
            for z in range(fsdp):
                pairs.append((place_of(x, core, z, fsdp), place_of(x ^ flip_x, core ^ flip_core, z ^ flip_z, fsdp)))
    return lax.ppermute(block, GROUP, pairs)


def gather_blocks(block, dp, fsdp):
    devices = dp * fsdp
    order = [row * fsdp + z for z in reversed(range(fsdp)) for row in range(dp)]
    copies = jnp.broadcast_to(block[None], (devices,) + block.shape)
    return lax.all_to_all(copies, GROUP, 0, 0, axis_index_groups=[order], tiled=True)


def local_kernel(kernel, outs, name, *operands, unread=()):
    return pl.pallas_call(
        lambda *refs: kernel(*refs[: len(operands)], *refs[len(operands) + len(unread) :]),
        out_shape=outs,
        in_specs=[VMEM] * (len(operands) + len(unread)),
        out_specs=(VMEM,) * len(outs),
        compiler_params=pltpu.CompilerParams(vmem_limit_bytes=16 * 2**20),
        name=name,
    )(*operands, *unread)


def to_half(coded):
    rounded = lax.reduce_precision(coded, exponent_bits=5, mantissa_bits=10)
    return rounded, rounded.astype(jnp.float16)


def reduce_to_owner(keep, other, embed, gathered, w_head, dp, fsdp):
    conv_rows, width = keep.shape[1:]
    rows = conv_rows + embed.shape[1]
    plain = jax.ShapeDtypeStruct((rows, width), F32)
    own, *coded = local_kernel(scale_kernel, (plain,) + (plain,) * (fsdp - 1), "scale", keep, other, embed)
    received = [
        exchange(to_half(part)[1], dp, fsdp, 0, 0, place + 1).astype(F32) for place, part in enumerate(coded)
    ]
    grad_head, token = head_gradient(fsdp, gathered, w_head, own)
    (coded,) = local_kernel(
        functools.partial(first_sum_kernel, conv_rows), (plain,), "sum_z", own, *received, unread=(token,)
    )
    flip = 1
    while flip < dp // 2:
        mine, sent = to_half(coded)
        other = exchange(sent, dp, fsdp, flip, 0, 0).astype(F32)
        flip *= 2
        outs = (plain,) * (2 if flip < dp // 2 else 1)
        total, *rest = local_kernel(functools.partial(next_sum_kernel, conv_rows), outs, "sum_x", mine, other)
        coded = rest[0] if rest else None
    return total, exchange(total, dp, fsdp, 0, 1, 0), grad_head


def shards(facies, prior_draws, recon_grad, w_embed, w_conv, w_head):
    dp, fsdp = lax.axis_size("dp"), lax.axis_size("fsdp")
    block, pooled_lanes, recon, one_hot, pre_embed, hidden, pre_conv, w_conv, w_head = forward(
        facies, prior_draws, recon_grad, w_embed, w_conv, w_head
    )
    gathered = gather_blocks(block, dp, fsdp)
    keep, send, grads = backward(fsdp, gathered, pooled_lanes, recon, hidden, pre_conv, w_head)
    received = exchange(send, dp, fsdp, 0, 1, 0)
    embed = embed_gradient(fsdp, grads, w_conv, pre_embed, one_hot)
    own, other, grad_head = reduce_to_owner(keep, received, embed, gathered, w_head, dp, fsdp)
    grad_embed, grad_conv = pl.pallas_call(
        output_kernel,
        out_shape=(
            jax.ShapeDtypeStruct((256 // fsdp, 128), F32),
            jax.ShapeDtypeStruct((1024 // fsdp, 256), F32),
        ),
        in_specs=[VMEM] * 2,
        out_specs=(VMEM,) * 2,
        compiler_params=pltpu.CompilerParams(vmem_limit_bytes=16 * 2**20),
        name="outputs",
    )(own, other)
    return (grad_embed, grad_conv, grad_head)


def solution(mesh):
    return jax.shard_map(
        shards,
        mesh=mesh,
        in_specs=(
            P(("groups", "dp", "fsdp"), None, None),
            P(("groups", "dp", "fsdp"), None),
            P(("groups", "dp", "fsdp"), None),
            P(),
            P(),
            P(),
        ),
        out_specs=(
            P(("groups", "fsdp"), None),
            P(("groups", "fsdp"), None),
            P(("groups", "fsdp"), None),
        ),
        check_vma=False,
    )
```

```python
import functools

import jax
import jax.numpy as jnp
from jax import lax
from jax.experimental import pallas as pl
from jax.experimental.pallas import tpu as pltpu
from jax.sharding import PartitionSpec as P

PATCH_X = 64
PATCH_Y = 64
PATCH_Z = 32
LEVELS = 4
GROUP = ("dp", "fsdp")
NT = (((1,), (1,)), ((), ()))
F32 = jnp.float32
BF16 = jnp.bfloat16


def iota(shape, dim):
    return lax.broadcasted_iota(jnp.int32, shape, dim)


def mm(left, right):
    return jnp.dot(left, right, preferred_element_type=F32)


def mm_nt(left, right):
    return lax.dot_general(left, right, NT, preferred_element_type=F32)


def turned_weights(w_embed):
    turned = jnp.transpose(w_embed.astype(F32)).astype(BF16)
    row, lane = iota((256, 256), 0), iota((256, 256), 1)
    dx, k = row // 64, row % 4
    same = lane == jnp.where(k < 3, dx * 48 + k * 16, 192 + dx * 16) + row // 4 % 16
    return mm(turned, jnp.where(same, 1.0, 0.0).astype(BF16)).astype(BF16)


def sigmoid(value):
    return pltpu.reciprocal(1.0 + jnp.exp2(value * -1.4426950408889634), approx=True)


def silu_slope(value):
    gate = sigmoid(value)
    return gate * (1.0 + value * (1.0 - gate))


def forward_kernel(
    facies_hbm, prior_hbm, recon_hbm, w_embed_hbm, w_conv_hbm, w_head_hbm,
    block, pooled_lanes, recon, one_hot, pre_embed, hidden, pre_conv, w_conv, w_head,
    facies, prior, w_embed, packed, conv_turned, sem
):
    blocks = facies.shape[0]
    loads = [
        pltpu.make_async_copy(facies_hbm.at[:, pl.ds(b * 128, 128)], facies.at[b], sem.at[b]) for b in range(blocks)
    ]
    others = []
    for source, target in (
        (w_embed_hbm, w_embed), (w_conv_hbm, w_conv), (prior_hbm, prior), (recon_hbm, recon), (w_head_hbm, w_head)
    ):
        others.append(pltpu.make_async_copy(source, target, sem.at[blocks + len(others)]))
    for load in others[:2] + loads:
        load.start()
    others[0].wait()
    packed[...] = turned_weights(w_embed[...])
    others[1].wait()
    conv_turned[...] = jnp.transpose(w_conv[...].astype(F32)).astype(BF16)
    low = iota((8, 256), 0) < 4

    def build(half, dx2):
        for dx in range(4):
            rows = [
                facies[2 * b2 + dy2, pl.ds(4 * dx2 + dx, 32, stride=8), :]
                for dy2 in range(2)
                for b2 in range(4 * half, 4 * half + 4)
            ]
            turned = jnp.transpose(jnp.concatenate(rows, axis=0).astype(F32))
            for cp in range(4):
                part = [turned[dy * 32 + cp * 8 : dy * 32 + cp * 8 + 8] for dy in range(4)]
                swapped = [pltpu.roll(piece, 4, 0) for piece in part]
                for dz2 in range(2):
                    pieces = [
                        jnp.where(low, part[dy], swapped[dy + 1]) if dz2 == 0 else jnp.where(low, swapped[dy], part[dy + 1])
                        for dy in (0, 2)
                    ]
                    cells = jnp.concatenate(pieces, axis=0).astype(BF16)
                    for k in range(LEVELS):
                        hot = jnp.where(cells == BF16(k), BF16(1.0), BF16(0.0))
                        first = dx * 48 + k * 16 if k < 3 else 192 + dx * 16
                        for dy2 in range(2):
                            at = (2 * dx2 + dy2) * 256 + half * 128
                            one_hot[2 * cp + dz2, pl.ds(first, 16), pl.ds(at, 128)] = hot[:, dy2 * 128 : dy2 * 128 + 128]

    def embed(cp, dx2):
        for dz2 in range(2):
            rows, at = pl.ds(dz2 * 128, 128), pl.ds(dx2 * 512, 512)
            pre = mm(packed[...], one_hot[2 * cp + dz2, :, at])
            pre_embed[cp, rows, at] = pre
            act = (pre * sigmoid(pre)).astype(BF16)
            hidden[cp, 2 * dx2, rows, :] = act[:, :256]
            hidden[cp, 2 * dx2 + 1, rows, :] = act[:, 256:]

    for half in range(2):
        for load in loads[half * blocks // 2 : (half + 1) * blocks // 2]:
            load.wait()
        if half == 0:
            for load in others[2:]:
                load.start()
            build(0, 0)
            build(0, 1)
    build(1, 0)
    for cp in range(4):
        embed(cp, 0)
    build(1, 1)
    sums = jnp.zeros((256, 128), F32)
    for cp in range(4):
        embed(cp, 1)
        pre = mm(conv_turned[...], hidden[cp].reshape(1024, 256))
        pre_conv[cp] = pre
        act = pre * sigmoid(pre)
        sums = sums + act[:, :128] + act[:, 128:]
    pick = jnp.where(iota((128, 128), 1) // 8 % 4 == iota((128, 128), 0) // 8 % 4, 1.0, 0.0)
    total = lax.dot_general(pick, sums, NT, precision=lax.Precision.HIGHEST, preferred_element_type=F32) / 256.0
    pooled_lanes[...] = total.astype(BF16)
    block[:, pl.ds(1024, 256)] = jnp.concatenate([total[8 * s : 8 * s + 1] for s in range(4)], axis=0).astype(BF16)
    for load in others[2:]:
        load.wait()
    block[:, pl.ds(0, 512)] = prior[...]
    block[:, pl.ds(512, 512)] = recon[...]


def pair_kernel(queries, query_square, keys):
    inner = mm_nt(queries, keys)
    key_float = keys.astype(F32)
    count = keys.shape[0]
    key_square = jnp.sum(key_float * key_float, axis=1, keepdims=True)
    key_row = jnp.transpose(jnp.broadcast_to(key_square, (count, 128)))[:1]
    kern = jnp.exp(-(query_square + key_row - 2.0 * inner) / keys.shape[1])
    return jnp.sum(kern, axis=1, keepdims=True), mm(kern.astype(BF16), keys)


def group_rows(gathered, ordered):
    for owner in range(gathered.shape[0]):
        ordered[owner] = gathered[owner].astype(F32)
    return ordered[...].reshape(gathered.shape[0] * gathered.shape[1], gathered.shape[2])


def latent_rows(pooled, w_head):
    return mm(pooled, w_head[...]).astype(BF16)


def cotangent_rows(queries, keys, prior, recon):
    query_float = queries.astype(F32)
    square = jnp.sum(query_float * query_float, axis=1, keepdims=True)
    self_sum, self_mix = pair_kernel(queries, square, keys)
    cross_sum, cross_mix = pair_kernel(queries, square, prior)
    pull = -32.0 / keys.shape[0] * ((self_sum - cross_sum) * query_float - self_mix + cross_mix)
    return (recon + pull).astype(BF16)


def head_kernel(gathered, w_head, after, grad_head, token, ordered, head_full):
    token[...] = jnp.zeros(token.shape, F32)
    full = group_rows(gathered, ordered)
    latent = latent_rows(full[:, 1024:].astype(BF16), w_head)
    cotangent = cotangent_rows(latent, latent, full[:, :512].astype(BF16), full[:, 512:1024])
    head_full[...] = mm(jnp.transpose(full[:, 1024:]).astype(BF16), cotangent)
    share = grad_head.shape[0]
    start = pl.multiple_of(lax.axis_index("fsdp") * share, share)
    grad_head[...] = head_full[pl.ds(start, share), :]


def backward_kernel(gathered, pooled_lanes, recon, hidden, pre_conv, w_head, keep, send, grads, ordered):
    full = group_rows(gathered, ordered)
    queries = latent_rows(pooled_lanes[...], w_head)
    keys = latent_rows(full[:, 1024:].astype(BF16), w_head)
    recon_float = recon[...].astype(F32)
    recon_lanes = jnp.concatenate(
        [jnp.broadcast_to(recon_float[s : s + 1], (8, recon.shape[1])) for s in range(4)] * 4, axis=0
    )
    cotangent = cotangent_rows(queries, keys, full[:, :512].astype(BF16), recon_lanes)
    back_pool = mm_nt(w_head[...], cotangent) / 256.0
    back_pool = jnp.concatenate([back_pool, back_pool], axis=1)
    fsdp = keep.shape[0]
    conv_total = None
    for cp in range(4):
        grads[cp] = (back_pool * silu_slope(pre_conv[cp])).astype(BF16)
        term = mm_nt(hidden[cp].reshape(1024, 256), grads[cp])
        conv_total = term if cp == 0 else conv_total + term
    core_zero = lax.rem(lax.axis_index("dp"), 2) == 0
    rows = keep.shape[1]
    for f in range(fsdp):
        at = 2 * f * rows
        first, second = conv_total[at : at + rows], conv_total[at + rows : at + 2 * rows]
        keep[f] = jnp.where(core_zero, first, second)
        send[f] = jnp.where(core_zero, second, first)


def embed_kernel(grads, w_conv, pre_embed, one_hot, embed_out):
    embed = None
    ones = jnp.ones((16, 1024), BF16)
    for cp in range(4):
        signals = []
        for dx2 in range(2):
            back_rows = mm(w_conv[pl.ds(dx2 * 512, 512), :], grads[cp])
            back_rows = jnp.concatenate([back_rows[:256], back_rows[256:]], axis=1)
            signals.append((back_rows * silu_slope(pre_embed[cp, :, pl.ds(dx2 * 512, 512)])).astype(BF16))
        signal = jnp.concatenate(signals, axis=1)
        for dz2 in range(2):
            rows = jnp.concatenate([one_hot[2 * cp + dz2, pl.ds(0, 192), :], ones], axis=0)
            term = mm_nt(rows, signal[dz2 * 128 : dz2 * 128 + 128])
            embed = term if embed is None else embed + term
    shares = embed_out.shape[0]
    depth = 64 // shares
    half = 3 * depth // 2
    embed_out[...] = jnp.zeros(embed_out.shape, F32)
    for f in range(shares):
        dx, at = f * 4 // shares, f * depth % 16
        share = jnp.concatenate([embed[dx * 48 + k * 16 + at :][:depth] for k in range(3)], axis=0)
        for side in range(2):
            embed_out[f, pl.ds(0, half), pl.ds(side * 128, 128)] = share[side * half : (side + 1) * half]
        embed_out[f, pl.ds(embed_out.shape[1] - 8, 8), pl.ds(0, 128)] = embed[192:200]


def exponent_of(part):
    top = jnp.abs(part)
    while top.ndim > 2:
        top = jnp.max(top, axis=0)
    top = jnp.max(jnp.max(top, axis=0, keepdims=True), axis=1, keepdims=True)
    return jnp.clip(jnp.floor(jnp.log2(jnp.maximum(top, 1e-37))) - 14.0, -124.0, 114.0)


def store_coded(coded, part, conv_rows):
    store_scaled(coded, part, (exponent_of(part[:conv_rows]), exponent_of(part[conv_rows:])), conv_rows)


def store_scaled(coded, part, steps, conv_rows):
    last = part.shape[0] - 8
    coded[pl.ds(0, conv_rows), :] = part[:conv_rows] * jnp.exp2(-steps[0])
    coded[pl.ds(conv_rows, last - conv_rows), :] = part[conv_rows:last] * jnp.exp2(-steps[1])
    total = part[last:, :128] * jnp.exp2(-steps[1])
    high = total.astype(BF16).astype(F32)
    row = iota((8, 256), 0)
    tail = jnp.where(row == 1, steps[0], steps[1])
    coded[pl.ds(last, 8), :] = jnp.where(row == 0, jnp.concatenate([high, total - high], axis=1), tail)


def load_coded(coded, conv_rows):
    last = coded.shape[0] - 8
    embed_scale = jnp.exp2(coded[pl.ds(last + 2, 1), :])
    total = coded[pl.ds(last, 8), pl.ds(0, 128)] + coded[pl.ds(last, 8), pl.ds(128, 128)]
    total = jnp.where(iota((8, 256), 0) == 0, jnp.concatenate([total, jnp.zeros((8, 128), F32)], axis=1), 0.0)
    embed = jnp.concatenate([coded[pl.ds(conv_rows, last - conv_rows), :], total], axis=0) * embed_scale
    return jnp.concatenate([coded[pl.ds(0, conv_rows), :] * jnp.exp2(coded[pl.ds(last + 1, 1), :]), embed], axis=0)


def scale_kernel(keep, other, embed, own, *coded):
    held = keep[...] + other[...]
    steps = exponent_of(held), exponent_of(embed[...])
    here = lax.axis_index("fsdp")

    def share(z):
        return jnp.concatenate([keep[z] + other[z], embed[z]], axis=0)

    own[...] = share(here)
    for place, target in enumerate(coded):
        store_scaled(target, share(here ^ (place + 1)), steps, keep.shape[1])


def first_sum_kernel(conv_rows, own, *refs):
    *received, coded = refs
    total = own[...]
    for part in received:
        total = total + load_coded(part, conv_rows)
    store_coded(coded, total, conv_rows)


def next_sum_kernel(conv_rows, mine, other, total, *coded):
    summed = load_coded(mine, conv_rows) + load_coded(other, conv_rows)
    total[...] = summed
    if coded:
        store_coded(coded[0], summed, conv_rows)


def output_kernel(own, other, grad_embed, grad_conv):
    conv_rows, count = grad_conv.shape[0] // 2, grad_embed.shape[0]
    core_zero = lax.rem(lax.axis_index("dp"), 2) == 0
    grad_conv[pl.ds(0, conv_rows), :] = jnp.where(core_zero, own[pl.ds(0, conv_rows), :], other[pl.ds(0, conv_rows), :])
    grad_conv[pl.ds(conv_rows, conv_rows), :] = jnp.where(
        core_zero, other[pl.ds(0, conv_rows), :], own[pl.ds(0, conv_rows), :]
    )
    half, depth = 3 * count // 8, count // LEVELS
    embed = own[pl.ds(conv_rows, half), :] + other[pl.ds(conv_rows, half), :]
    embed = jnp.concatenate([embed[:, :128], embed[:, 128:]], axis=0)
    last = own.shape[0] - 8
    total = own[pl.ds(last, 1), pl.ds(0, 128)] + other[pl.ds(last, 1), pl.ds(0, 128)]
    fourth = total - (embed[:depth] + embed[depth : 2 * depth] + embed[2 * depth :])
    embed = jnp.concatenate([embed, fourth], axis=0)
    row, lane = iota((count, count), 0), iota((count, count), 1)
    order = jnp.where(lane == row % LEVELS * depth + row // LEVELS, 1.0, 0.0).astype(BF16)
    result = None
    for _ in range(3):
        term = embed.astype(BF16)
        embed = embed - term.astype(F32)
        result = mm(order, term) if result is None else result + mm(order, term)
    grad_embed[...] = result


VMEM = pl.BlockSpec(memory_space=pltpu.VMEM)
HBM = pl.BlockSpec(memory_space=pltpu.HBM)
SAVED = (
    ((8, 256, 1024), BF16),
    ((4, 256, 1024), F32),
    ((4, 4, 256, 256), BF16),
    ((4, 256, 256), F32),
)


def forward(facies, prior_draws, recon_grad, w_embed, w_conv, w_head):
    samples = facies.shape[0]
    latent_width = prior_draws.shape[1]
    rows, lanes = samples * PATCH_X, PATCH_Y * PATCH_Z
    operands = (facies.reshape(rows, lanes), prior_draws, recon_grad, w_embed, w_conv, w_head)
    return pl.pallas_call(
        forward_kernel,
        out_shape=(pltpu.VMEM((samples, 2 * latent_width + 256), BF16),)
        + (pltpu.VMEM((128, 256), BF16), pltpu.VMEM(recon_grad.shape, BF16))
        + tuple(pltpu.VMEM(shape, kind) for shape, kind in SAVED)
        + (pltpu.VMEM(w_conv.shape, BF16), pltpu.VMEM(w_head.shape, BF16)),
        in_specs=[HBM] * 6,
        out_specs=(VMEM,) * 9,
        scratch_shapes=[
            pltpu.VMEM((lanes // 128, rows, 128), jnp.int32),
            pltpu.VMEM(prior_draws.shape, BF16),
            pltpu.VMEM(w_embed.shape, BF16),
            pltpu.VMEM((128, 256), BF16),
            pltpu.VMEM((256, 1024), BF16),
            pltpu.SemaphoreType.DMA((lanes // 128 + 5,)),
        ],
        compiler_params=pltpu.CompilerParams(vmem_limit_bytes=30 * 2**20),
        name="forward",
    )(*(pltpu.with_memory_space_constraint(operand, pltpu.HBM) for operand in operands))


def backward(fsdp, gathered, *operands):
    devices, samples, width = gathered.shape
    payload = pltpu.VMEM((fsdp, 1024 // fsdp // 2, 256), F32)
    return pl.pallas_call(
        backward_kernel,
        out_shape=(payload, payload, pltpu.VMEM((4, 256, 256), BF16)),
        in_specs=[VMEM] * 6,
        out_specs=(VMEM,) * 3,
        scratch_shapes=[pltpu.VMEM((devices, samples, width), F32)],
        compiler_params=pltpu.CompilerParams(vmem_limit_bytes=24 * 2**20),
        name="backward",
    )(gathered, *operands)


def head_gradient(fsdp, gathered, w_head, after):
    devices, samples, width = gathered.shape
    return pl.pallas_call(
        head_kernel,
        out_shape=(jax.ShapeDtypeStruct((256 // fsdp, 512), F32), pltpu.VMEM((8, 128), F32)),
        in_specs=[VMEM] * 2 + [HBM],
        out_specs=(VMEM,) * 2,
        scratch_shapes=[pltpu.VMEM((devices, samples, width), F32), pltpu.VMEM((256, 512), F32)],
        compiler_params=pltpu.CompilerParams(vmem_limit_bytes=16 * 2**20),
        cost_estimate=pl.CostEstimate(flops=2 * 10**9, bytes_accessed=2 * 2**20, transcendentals=10000),
        name="head_gradient",
    )(gathered, w_head, after)


def embed_gradient(fsdp, grads, w_conv, pre_embed, one_hot):
    return pl.pallas_call(
        embed_kernel,
        out_shape=pltpu.VMEM((fsdp, (96 // fsdp + 7) // 8 * 8 + 8, 256), F32),
        in_specs=[VMEM] * 4,
        out_specs=VMEM,
        compiler_params=pltpu.CompilerParams(vmem_limit_bytes=24 * 2**20),
        cost_estimate=pl.CostEstimate(flops=16 * 10**8, bytes_accessed=10 * 2**20, transcendentals=0),
        name="embed_gradient",
    )(grads, w_conv, pre_embed, one_hot)


def place_of(x, core, z, fsdp):
    return (2 * x + core) * fsdp + z


def exchange(block, dp, fsdp, flip_x, flip_core, flip_z):
    pairs = []
    for x in range(dp // 2):
        for core in range(2):
            for z in range(fsdp):
                pairs.append((place_of(x, core, z, fsdp), place_of(x ^ flip_x, core ^ flip_core, z ^ flip_z, fsdp)))
    return lax.ppermute(block, GROUP, pairs)


def gather_blocks(block, dp, fsdp):
    devices = dp * fsdp
    order = [
        place_of(x, core, z, fsdp) for z in reversed(range(fsdp)) for x in reversed(range(dp // 2)) for core in range(2)
    ]
    copies = jnp.broadcast_to(block[None], (devices,) + block.shape)
    return lax.all_to_all(copies, GROUP, 0, 0, axis_index_groups=[order], tiled=True)


def local_kernel(kernel, outs, name, *operands, unread=()):
    return pl.pallas_call(
        lambda *refs: kernel(*refs[: len(operands)], *refs[len(operands) + len(unread) :]),
        out_shape=outs,
        in_specs=[VMEM] * (len(operands) + len(unread)),
        out_specs=(VMEM,) * len(outs),
        compiler_params=pltpu.CompilerParams(vmem_limit_bytes=16 * 2**20),
        name=name,
    )(*operands, *unread)


def to_half(coded):
    rounded = lax.reduce_precision(coded, exponent_bits=5, mantissa_bits=10)
    return rounded, rounded.astype(jnp.float16)


def reduce_to_owner(keep, other, embed, gathered, w_head, dp, fsdp):
    conv_rows, width = keep.shape[1:]
    rows = conv_rows + embed.shape[1]
    plain = jax.ShapeDtypeStruct((rows, width), F32)
    own, *coded = local_kernel(scale_kernel, (plain,) + (plain,) * (fsdp - 1), "scale", keep, other, embed)
    received = [
        exchange(to_half(part)[1], dp, fsdp, 0, 0, place + 1).astype(F32) for place, part in enumerate(coded)
    ]
    grad_head, token = head_gradient(fsdp, gathered, w_head, own)
    (coded,) = local_kernel(
        functools.partial(first_sum_kernel, conv_rows), (plain,), "sum_z", own, *received, unread=(token,)
    )
    flip = 1
    while flip < dp // 2:
        mine, sent = to_half(coded)
        other = exchange(sent, dp, fsdp, flip, 0, 0).astype(F32)
        flip *= 2
        outs = (plain,) * (2 if flip < dp // 2 else 1)
        total, *rest = local_kernel(functools.partial(next_sum_kernel, conv_rows), outs, "sum_x", mine, other)
        coded = rest[0] if rest else None
    return total, exchange(total, dp, fsdp, 0, 1, 0), grad_head


def shards(facies, prior_draws, recon_grad, w_embed, w_conv, w_head):
    dp, fsdp = lax.axis_size("dp"), lax.axis_size("fsdp")
    block, pooled_lanes, recon, one_hot, pre_embed, hidden, pre_conv, w_conv, w_head = forward(
        facies, prior_draws, recon_grad, w_embed, w_conv, w_head
    )
    gathered = gather_blocks(block, dp, fsdp)
    keep, send, grads = backward(fsdp, gathered, pooled_lanes, recon, hidden, pre_conv, w_head)
    received = exchange(send, dp, fsdp, 0, 1, 0)
    embed = embed_gradient(fsdp, grads, w_conv, pre_embed, one_hot)
    own, other, grad_head = reduce_to_owner(keep, received, embed, gathered, w_head, dp, fsdp)
    grad_embed, grad_conv = pl.pallas_call(
        output_kernel,
        out_shape=(
            jax.ShapeDtypeStruct((256 // fsdp, 128), F32),
            jax.ShapeDtypeStruct((1024 // fsdp, 256), F32),
        ),
        in_specs=[VMEM] * 2,
        out_specs=(VMEM,) * 2,
        compiler_params=pltpu.CompilerParams(vmem_limit_bytes=16 * 2**20),
        name="outputs",
    )(own, other)
    return (grad_embed, grad_conv, grad_head)


def solution(mesh):
    return jax.shard_map(
        shards,
        mesh=mesh,
        in_specs=(
            P(("groups", "dp", "fsdp"), None, None),
            P(("groups", "dp", "fsdp"), None),
            P(("groups", "dp", "fsdp"), None),
            P(),
            P(),
            P(),
        ),
        out_specs=(
            P(("groups", "fsdp"), None),
            P(("groups", "fsdp"), None),
            P(("groups", "fsdp"), None),
        ),
        check_vma=False,
    )
```

```python
import functools

import jax
import jax.numpy as jnp
from jax import lax
from jax.experimental import pallas as pl
from jax.experimental.pallas import tpu as pltpu
from jax.sharding import PartitionSpec as P

PATCH_X = 64
PATCH_Y = 64
PATCH_Z = 32
LEVELS = 4
GROUP = ("dp", "fsdp")
NT = (((1,), (1,)), ((), ()))
F32 = jnp.float32
BF16 = jnp.bfloat16


def iota(shape, dim):
    return lax.broadcasted_iota(jnp.int32, shape, dim)


def mm(left, right):
    return jnp.dot(left, right, preferred_element_type=F32)


def mm_nt(left, right):
    return lax.dot_general(left, right, NT, preferred_element_type=F32)


def turned_weights(w_embed):
    turned = jnp.transpose(w_embed.astype(F32)).astype(BF16)
    row, lane = iota((256, 256), 0), iota((256, 256), 1)
    dx, k = row // 64, row % 4
    same = lane == jnp.where(k < 3, dx * 48 + k * 16, 192 + dx * 16) + row // 4 % 16
    return mm(turned, jnp.where(same, 1.0, 0.0).astype(BF16)).astype(BF16)


def sigmoid(value):
    return pltpu.reciprocal(1.0 + jnp.exp2(value * -1.4426950408889634), approx=True)


def silu_slope(value):
    gate = sigmoid(value)
    return gate * (1.0 + value * (1.0 - gate))


def forward_kernel(
    facies_hbm, prior_hbm, recon_hbm, w_embed_hbm, w_conv_hbm, w_head_hbm,
    block, pooled_lanes, recon, one_hot, pre_embed, hidden, pre_conv, w_conv, w_head,
    facies, prior, w_embed, packed, conv_turned, sem
):
    blocks = facies.shape[0]
    loads = [
        pltpu.make_async_copy(facies_hbm.at[:, pl.ds(b * 128, 128)], facies.at[b], sem.at[b]) for b in range(blocks)
    ]
    others = []
    for source, target in (
        (w_embed_hbm, w_embed), (w_conv_hbm, w_conv), (prior_hbm, prior), (recon_hbm, recon), (w_head_hbm, w_head)
    ):
        others.append(pltpu.make_async_copy(source, target, sem.at[blocks + len(others)]))
    for load in others[:2] + loads:
        load.start()
    others[0].wait()
    packed[...] = turned_weights(w_embed[...])
    others[1].wait()
    conv_turned[...] = jnp.transpose(w_conv[...].astype(F32)).astype(BF16)
    low = iota((8, 256), 0) < 4

    def build(half, dx2):
        for dx in range(4):
            rows = [
                facies[2 * b2 + dy2, pl.ds(4 * dx2 + dx, 32, stride=8), :]
                for dy2 in range(2)
                for b2 in range(4 * half, 4 * half + 4)
            ]
            turned = jnp.transpose(jnp.concatenate(rows, axis=0).astype(F32))
            for cp in range(4):
                part = [turned[dy * 32 + cp * 8 : dy * 32 + cp * 8 + 8] for dy in range(4)]
                swapped = [pltpu.roll(piece, 4, 0) for piece in part]
                for dz2 in range(2):
                    pieces = [
                        jnp.where(low, part[dy], swapped[dy + 1]) if dz2 == 0 else jnp.where(low, swapped[dy], part[dy + 1])
                        for dy in (0, 2)
                    ]
                    cells = jnp.concatenate(pieces, axis=0).astype(BF16)
                    for k in range(LEVELS):
                        hot = jnp.where(cells == BF16(k), BF16(1.0), BF16(0.0))
                        first = dx * 48 + k * 16 if k < 3 else 192 + dx * 16
                        for dy2 in range(2):
                            at = (2 * dx2 + dy2) * 256 + half * 128
                            one_hot[2 * cp + dz2, pl.ds(first, 16), pl.ds(at, 128)] = hot[:, dy2 * 128 : dy2 * 128 + 128]

    def embed(cp, dx2):
        for dz2 in range(2):
            rows, at = pl.ds(dz2 * 128, 128), pl.ds(dx2 * 512, 512)
            pre = mm(packed[...], one_hot[2 * cp + dz2, :, at])
            pre_embed[cp, rows, at] = pre
            act = (pre * sigmoid(pre)).astype(BF16)
            hidden[cp, 2 * dx2, rows, :] = act[:, :256]
            hidden[cp, 2 * dx2 + 1, rows, :] = act[:, 256:]

    for half in range(2):
        for load in loads[half * blocks // 2 : (half + 1) * blocks // 2]:
            load.wait()
        if half == 0:
            for load in others[2:]:
                load.start()
            build(0, 0)
            build(0, 1)
    build(1, 0)
    for cp in range(4):
        embed(cp, 0)
    build(1, 1)
    sums = jnp.zeros((256, 128), F32)
    for cp in range(4):
        embed(cp, 1)
        pre = mm(conv_turned[...], hidden[cp].reshape(1024, 256))
        pre_conv[cp] = pre
        act = pre * sigmoid(pre)
        sums = sums + act[:, :128] + act[:, 128:]
    pick = jnp.where(iota((128, 128), 1) // 8 % 4 == iota((128, 128), 0) // 8 % 4, 1.0, 0.0)
    total = lax.dot_general(pick, sums, NT, precision=lax.Precision.HIGHEST, preferred_element_type=F32) / 256.0
    pooled_lanes[...] = total.astype(BF16)
    block[:, pl.ds(1024, 256)] = jnp.concatenate([total[8 * s : 8 * s + 1] for s in range(4)], axis=0).astype(BF16)
    for load in others[2:]:
        load.wait()
    block[:, pl.ds(0, 512)] = prior[...]
    block[:, pl.ds(512, 512)] = recon[...]


def pair_kernel(queries, query_square, keys):
    inner = mm_nt(queries, keys)
    key_float = keys.astype(F32)
    count = keys.shape[0]
    key_square = jnp.sum(key_float * key_float, axis=1, keepdims=True)
    key_row = jnp.transpose(jnp.broadcast_to(key_square, (count, 128)))[:1]
    kern = jnp.exp(-(query_square + key_row - 2.0 * inner) / keys.shape[1])
    return jnp.sum(kern, axis=1, keepdims=True), mm(kern.astype(BF16), keys)


def group_rows(gathered, ordered):
    for owner in range(gathered.shape[0]):
        ordered[owner] = gathered[owner].astype(F32)
    return ordered[...].reshape(gathered.shape[0] * gathered.shape[1], gathered.shape[2])


def latent_rows(pooled, w_head):
    return mm(pooled, w_head[...]).astype(BF16)


def cotangent_rows(queries, keys, prior, recon):
    query_float = queries.astype(F32)
    square = jnp.sum(query_float * query_float, axis=1, keepdims=True)
    self_sum, self_mix = pair_kernel(queries, square, keys)
    cross_sum, cross_mix = pair_kernel(queries, square, prior)
    pull = -32.0 / keys.shape[0] * ((self_sum - cross_sum) * query_float - self_mix + cross_mix)
    return (recon + pull).astype(BF16)


def head_kernel(gathered, w_head, after, grad_head, token, ordered, head_full):
    token[...] = jnp.zeros(token.shape, F32)
    full = group_rows(gathered, ordered)
    latent = latent_rows(full[:, 1024:].astype(BF16), w_head)
    cotangent = cotangent_rows(latent, latent, full[:, :512].astype(BF16), full[:, 512:1024])
    head_full[...] = mm(jnp.transpose(full[:, 1024:]).astype(BF16), cotangent)
    share = grad_head.shape[0]
    start = pl.multiple_of(lax.axis_index("fsdp") * share, share)
    grad_head[...] = head_full[pl.ds(start, share), :]


def backward_kernel(gathered, pooled_lanes, recon, hidden, pre_conv, w_head, keep, send, grads, ordered):
    full = group_rows(gathered, ordered)
    queries = latent_rows(pooled_lanes[...], w_head)
    keys = latent_rows(full[:, 1024:].astype(BF16), w_head)
    recon_float = recon[...].astype(F32)
    recon_lanes = jnp.concatenate(
        [jnp.broadcast_to(recon_float[s : s + 1], (8, recon.shape[1])) for s in range(4)] * 4, axis=0
    )
    cotangent = cotangent_rows(queries, keys, full[:, :512].astype(BF16), recon_lanes)
    back_pool = mm_nt(w_head[...], cotangent) / 256.0
    back_pool = jnp.concatenate([back_pool, back_pool], axis=1)
    fsdp = keep.shape[0]
    conv_total = None
    for cp in range(4):
        grads[cp] = (back_pool * silu_slope(pre_conv[cp])).astype(BF16)
        term = mm_nt(hidden[cp].reshape(1024, 256), grads[cp])
        conv_total = term if cp == 0 else conv_total + term
    core_zero = lax.rem(lax.axis_index("dp"), 2) == 0
    rows = keep.shape[1]
    for f in range(fsdp):
        at = 2 * f * rows
        first, second = conv_total[at : at + rows], conv_total[at + rows : at + 2 * rows]
        keep[f] = jnp.where(core_zero, first, second)
        send[f] = jnp.where(core_zero, second, first)


def embed_kernel(grads, w_conv, pre_embed, one_hot, embed_out):
    embed = None
    ones = jnp.ones((16, 1024), BF16)
    for cp in range(4):
        signals = []
        for dx2 in range(2):
            back_rows = mm(w_conv[pl.ds(dx2 * 512, 512), :], grads[cp])
            back_rows = jnp.concatenate([back_rows[:256], back_rows[256:]], axis=1)
            signals.append((back_rows * silu_slope(pre_embed[cp, :, pl.ds(dx2 * 512, 512)])).astype(BF16))
        signal = jnp.concatenate(signals, axis=1)
        for dz2 in range(2):
            rows = jnp.concatenate([one_hot[2 * cp + dz2, pl.ds(0, 192), :], ones], axis=0)
            term = mm_nt(rows, signal[dz2 * 128 : dz2 * 128 + 128])
            embed = term if embed is None else embed + term
    shares = embed_out.shape[0]
    depth = 64 // shares
    half = 3 * depth // 2
    embed_out[...] = jnp.zeros(embed_out.shape, F32)
    for f in range(shares):
        dx, at = f * 4 // shares, f * depth % 16
        share = jnp.concatenate([embed[dx * 48 + k * 16 + at :][:depth] for k in range(3)], axis=0)
        for side in range(2):
            embed_out[f, pl.ds(0, half), pl.ds(side * 128, 128)] = share[side * half : (side + 1) * half]
        embed_out[f, pl.ds(embed_out.shape[1] - 8, 8), pl.ds(0, 128)] = embed[192:200]


def exponent_of(part):
    top = jnp.abs(part)
    while top.ndim > 2:
        top = jnp.max(top, axis=0)
    top = jnp.max(jnp.max(top, axis=0, keepdims=True), axis=1, keepdims=True)
    return jnp.clip(jnp.floor(jnp.log2(jnp.maximum(top, 1e-37))) - 14.0, -124.0, 114.0)


def store_coded(coded, part, conv_rows):
    store_scaled(coded, part, (exponent_of(part[:conv_rows]), exponent_of(part[conv_rows:])), conv_rows)


def store_scaled(coded, part, steps, conv_rows):
    last = part.shape[0] - 8
    coded[pl.ds(0, conv_rows), :] = part[:conv_rows] * jnp.exp2(-steps[0])
    coded[pl.ds(conv_rows, last - conv_rows), :] = part[conv_rows:last] * jnp.exp2(-steps[1])
    total = part[last:, :128] * jnp.exp2(-steps[1])
    high = total.astype(BF16).astype(F32)
    row = iota((8, 256), 0)
    tail = jnp.where(row == 1, steps[0], steps[1])
    coded[pl.ds(last, 8), :] = jnp.where(row == 0, jnp.concatenate([high, total - high], axis=1), tail)


def load_coded(coded, conv_rows):
    last = coded.shape[0] - 8
    embed_scale = jnp.exp2(coded[pl.ds(last + 2, 1), :])
    total = coded[pl.ds(last, 8), pl.ds(0, 128)] + coded[pl.ds(last, 8), pl.ds(128, 128)]
    total = jnp.where(iota((8, 256), 0) == 0, jnp.concatenate([total, jnp.zeros((8, 128), F32)], axis=1), 0.0)
    embed = jnp.concatenate([coded[pl.ds(conv_rows, last - conv_rows), :], total], axis=0) * embed_scale
    return jnp.concatenate([coded[pl.ds(0, conv_rows), :] * jnp.exp2(coded[pl.ds(last + 1, 1), :]), embed], axis=0)


def z_flips(fsdp):
    return [flip for flip in range(1, fsdp) if flip != fsdp // 2] + [fsdp // 2]


def scale_kernel(keep, other, embed, own, *coded):
    held = keep[...] + other[...]
    steps = exponent_of(held), exponent_of(embed[...])
    here = lax.axis_index("fsdp")

    def share(z):
        return jnp.concatenate([keep[z] + other[z], embed[z]], axis=0)

    own[...] = share(here)
    for flip, target in zip(z_flips(keep.shape[0]), coded):
        store_scaled(target, share(here ^ flip), steps, keep.shape[1])


def first_sum_kernel(conv_rows, own, *refs):
    *received, coded = refs
    total = own[...]
    for part in received:
        total = total + load_coded(part, conv_rows)
    store_coded(coded, total, conv_rows)


def next_sum_kernel(conv_rows, mine, other, total, *coded):
    summed = load_coded(mine, conv_rows) + load_coded(other, conv_rows)
    total[...] = summed
    if coded:
        store_coded(coded[0], summed, conv_rows)


def output_kernel(own, other, grad_embed, grad_conv):
    conv_rows, count = grad_conv.shape[0] // 2, grad_embed.shape[0]
    core_zero = lax.rem(lax.axis_index("dp"), 2) == 0
    grad_conv[pl.ds(0, conv_rows), :] = jnp.where(core_zero, own[pl.ds(0, conv_rows), :], other[pl.ds(0, conv_rows), :])
    grad_conv[pl.ds(conv_rows, conv_rows), :] = jnp.where(
        core_zero, other[pl.ds(0, conv_rows), :], own[pl.ds(0, conv_rows), :]
    )
    half, depth = 3 * count // 8, count // LEVELS
    embed = own[pl.ds(conv_rows, half), :] + other[pl.ds(conv_rows, half), :]
    embed = jnp.concatenate([embed[:, :128], embed[:, 128:]], axis=0)
    last = own.shape[0] - 8
    total = own[pl.ds(last, 1), pl.ds(0, 128)] + other[pl.ds(last, 1), pl.ds(0, 128)]
    fourth = total - (embed[:depth] + embed[depth : 2 * depth] + embed[2 * depth :])
    embed = jnp.concatenate([embed, fourth], axis=0)
    row, lane = iota((count, count), 0), iota((count, count), 1)
    order = jnp.where(lane == row % LEVELS * depth + row // LEVELS, 1.0, 0.0).astype(BF16)
    result = None
    for _ in range(3):
        term = embed.astype(BF16)
        embed = embed - term.astype(F32)
        result = mm(order, term) if result is None else result + mm(order, term)
    grad_embed[...] = result


VMEM = pl.BlockSpec(memory_space=pltpu.VMEM)
HBM = pl.BlockSpec(memory_space=pltpu.HBM)
SAVED = (
    ((8, 256, 1024), BF16),
    ((4, 256, 1024), F32),
    ((4, 4, 256, 256), BF16),
    ((4, 256, 256), F32),
)


def forward(facies, prior_draws, recon_grad, w_embed, w_conv, w_head):
    samples = facies.shape[0]
    latent_width = prior_draws.shape[1]
    rows, lanes = samples * PATCH_X, PATCH_Y * PATCH_Z
    operands = (facies.reshape(rows, lanes), prior_draws, recon_grad, w_embed, w_conv, w_head)
    return pl.pallas_call(
        forward_kernel,
        out_shape=(pltpu.VMEM((samples, 2 * latent_width + 256), BF16),)
        + (pltpu.VMEM((128, 256), BF16), pltpu.VMEM(recon_grad.shape, BF16))
        + tuple(pltpu.VMEM(shape, kind) for shape, kind in SAVED)
        + (pltpu.VMEM(w_conv.shape, BF16), pltpu.VMEM(w_head.shape, BF16)),
        in_specs=[HBM] * 6,
        out_specs=(VMEM,) * 9,
        scratch_shapes=[
            pltpu.VMEM((lanes // 128, rows, 128), jnp.int32),
            pltpu.VMEM(prior_draws.shape, BF16),
            pltpu.VMEM(w_embed.shape, BF16),
            pltpu.VMEM((128, 256), BF16),
            pltpu.VMEM((256, 1024), BF16),
            pltpu.SemaphoreType.DMA((lanes // 128 + 5,)),
        ],
        compiler_params=pltpu.CompilerParams(vmem_limit_bytes=30 * 2**20),
        name="forward",
    )(*(pltpu.with_memory_space_constraint(operand, pltpu.HBM) for operand in operands))


def backward(fsdp, gathered, *operands):
    devices, samples, width = gathered.shape
    payload = pltpu.VMEM((fsdp, 1024 // fsdp // 2, 256), F32)
    return pl.pallas_call(
        backward_kernel,
        out_shape=(payload, payload, pltpu.VMEM((4, 256, 256), BF16)),
        in_specs=[VMEM] * 6,
        out_specs=(VMEM,) * 3,
        scratch_shapes=[pltpu.VMEM((devices, samples, width), F32)],
        compiler_params=pltpu.CompilerParams(vmem_limit_bytes=24 * 2**20),
        name="backward",
    )(gathered, *operands)


def head_gradient(fsdp, gathered, w_head, after):
    devices, samples, width = gathered.shape
    return pl.pallas_call(
        head_kernel,
        out_shape=(jax.ShapeDtypeStruct((256 // fsdp, 512), F32), pltpu.VMEM((8, 128), F32)),
        in_specs=[VMEM] * 2 + [HBM],
        out_specs=(VMEM,) * 2,
        scratch_shapes=[pltpu.VMEM((devices, samples, width), F32), pltpu.VMEM((256, 512), F32)],
        compiler_params=pltpu.CompilerParams(vmem_limit_bytes=16 * 2**20),
        cost_estimate=pl.CostEstimate(flops=2 * 10**9, bytes_accessed=2 * 2**20, transcendentals=10000),
        name="head_gradient",
    )(gathered, w_head, after)


def embed_gradient(fsdp, grads, w_conv, pre_embed, one_hot):
    return pl.pallas_call(
        embed_kernel,
        out_shape=pltpu.VMEM((fsdp, (96 // fsdp + 7) // 8 * 8 + 8, 256), F32),
        in_specs=[VMEM] * 4,
        out_specs=VMEM,
        compiler_params=pltpu.CompilerParams(vmem_limit_bytes=24 * 2**20),
        cost_estimate=pl.CostEstimate(flops=16 * 10**8, bytes_accessed=10 * 2**20, transcendentals=0),
        name="embed_gradient",
    )(grads, w_conv, pre_embed, one_hot)


def place_of(x, core, z, fsdp):
    return (2 * x + core) * fsdp + z


def exchange(block, dp, fsdp, flip_x, flip_core, flip_z):
    pairs = []
    for x in range(dp // 2):
        for core in range(2):
            for z in range(fsdp):
                pairs.append((place_of(x, core, z, fsdp), place_of(x ^ flip_x, core ^ flip_core, z ^ flip_z, fsdp)))
    return lax.ppermute(block, GROUP, pairs)


def gather_blocks(block, dp, fsdp):
    devices = dp * fsdp
    order = [
        place_of(x, core, z, fsdp) for z in reversed(range(fsdp)) for x in reversed(range(dp // 2)) for core in range(2)
    ]
    copies = jnp.broadcast_to(block[None], (devices,) + block.shape)
    return lax.all_to_all(copies, GROUP, 0, 0, axis_index_groups=[order], tiled=True)


def local_kernel(kernel, outs, name, *operands, unread=()):
    return pl.pallas_call(
        lambda *refs: kernel(*refs[: len(operands)], *refs[len(operands) + len(unread) :]),
        out_shape=outs,
        in_specs=[VMEM] * (len(operands) + len(unread)),
        out_specs=(VMEM,) * len(outs),
        compiler_params=pltpu.CompilerParams(vmem_limit_bytes=16 * 2**20),
        name=name,
    )(*operands, *unread)


def to_half(coded):
    rounded = lax.reduce_precision(coded, exponent_bits=5, mantissa_bits=10)
    return rounded, rounded.astype(jnp.float16)


def reduce_to_owner(keep, other, embed, gathered, w_head, dp, fsdp):
    conv_rows, width = keep.shape[1:]
    rows = conv_rows + embed.shape[1]
    plain = jax.ShapeDtypeStruct((rows, width), F32)
    own, *coded = local_kernel(scale_kernel, (plain,) + (plain,) * (fsdp - 1), "scale", keep, other, embed)
    received = [
        exchange(to_half(part)[1], dp, fsdp, 0, 0, flip).astype(F32) for flip, part in zip(z_flips(fsdp), coded)
    ]
    grad_head, token = head_gradient(fsdp, gathered, w_head, own)
    (coded,) = local_kernel(
        functools.partial(first_sum_kernel, conv_rows), (plain,), "sum_z", own, *received, unread=(token,)
    )
    flip = 1
    while flip < dp // 2:
        mine, sent = to_half(coded)
        other = exchange(sent, dp, fsdp, flip, 0, 0).astype(F32)
        flip *= 2
        outs = (plain,) * (2 if flip < dp // 2 else 1)
        total, *rest = local_kernel(functools.partial(next_sum_kernel, conv_rows), outs, "sum_x", mine, other)
        coded = rest[0] if rest else None
    return total, exchange(total, dp, fsdp, 0, 1, 0), grad_head


def shards(facies, prior_draws, recon_grad, w_embed, w_conv, w_head):
    dp, fsdp = lax.axis_size("dp"), lax.axis_size("fsdp")
    block, pooled_lanes, recon, one_hot, pre_embed, hidden, pre_conv, w_conv, w_head = forward(
        facies, prior_draws, recon_grad, w_embed, w_conv, w_head
    )
    gathered = gather_blocks(block, dp, fsdp)
    keep, send, grads = backward(fsdp, gathered, pooled_lanes, recon, hidden, pre_conv, w_head)
    received = exchange(send, dp, fsdp, 0, 1, 0)
    embed = embed_gradient(fsdp, grads, w_conv, pre_embed, one_hot)
    own, other, grad_head = reduce_to_owner(keep, received, embed, gathered, w_head, dp, fsdp)
    grad_embed, grad_conv = pl.pallas_call(
        output_kernel,
        out_shape=(
            jax.ShapeDtypeStruct((256 // fsdp, 128), F32),
            jax.ShapeDtypeStruct((1024 // fsdp, 256), F32),
        ),
        in_specs=[VMEM] * 2,
        out_specs=(VMEM,) * 2,
        compiler_params=pltpu.CompilerParams(vmem_limit_bytes=16 * 2**20),
        name="outputs",
    )(own, other)
    return (grad_embed, grad_conv, grad_head)


def solution(mesh):
    return jax.shard_map(
        shards,
        mesh=mesh,
        in_specs=(
            P(("groups", "dp", "fsdp"), None, None),
            P(("groups", "dp", "fsdp"), None),
            P(("groups", "dp", "fsdp"), None),
            P(),
            P(),
            P(),
        ),
        out_specs=(
            P(("groups", "fsdp"), None),
            P(("groups", "fsdp"), None),
            P(("groups", "fsdp"), None),
        ),
        check_vma=False,
    )
```

```python
import functools

import jax
import jax.numpy as jnp
from jax import lax
from jax.experimental import pallas as pl
from jax.experimental.pallas import tpu as pltpu
from jax.sharding import PartitionSpec as P

PATCH_X = 64
PATCH_Y = 64
PATCH_Z = 32
LEVELS = 4
GROUP = ("dp", "fsdp")
NT = (((1,), (1,)), ((), ()))
F32 = jnp.float32
BF16 = jnp.bfloat16


def iota(shape, dim):
    return lax.broadcasted_iota(jnp.int32, shape, dim)


def mm(left, right):
    return jnp.dot(left, right, preferred_element_type=F32)


def mm_nt(left, right):
    return lax.dot_general(left, right, NT, preferred_element_type=F32)


def turned_weights(w_embed):
    turned = jnp.transpose(w_embed.astype(F32)).astype(BF16)
    row, lane = iota((256, 256), 0), iota((256, 256), 1)
    dx, k = row // 64, row % 4
    same = lane == jnp.where(k < 3, dx * 48 + k * 16, 192 + dx * 16) + row // 4 % 16
    return mm(turned, jnp.where(same, 1.0, 0.0).astype(BF16)).astype(BF16)


def sigmoid(value):
    return pltpu.reciprocal(1.0 + jnp.exp2(value * -1.4426950408889634), approx=True)


def silu_slope(value):
    gate = sigmoid(value)
    return gate * (1.0 + value * (1.0 - gate))


def forward_kernel(
    facies_hbm, prior_hbm, recon_hbm, w_embed_hbm, w_conv_hbm, w_head_hbm,
    block, pooled_lanes, recon, one_hot, pre_embed, hidden, pre_conv, w_conv, w_head,
    facies, prior, w_embed, packed, conv_turned, sem
):
    blocks = facies.shape[0]
    loads = [
        pltpu.make_async_copy(facies_hbm.at[:, pl.ds(b * 128, 128)], facies.at[b], sem.at[b]) for b in range(blocks)
    ]
    others = []
    for source, target in (
        (w_embed_hbm, w_embed), (w_conv_hbm, w_conv), (prior_hbm, prior), (recon_hbm, recon), (w_head_hbm, w_head)
    ):
        others.append(pltpu.make_async_copy(source, target, sem.at[blocks + len(others)]))
    for load in others[:2] + loads:
        load.start()
    others[0].wait()
    packed[...] = turned_weights(w_embed[...])
    others[1].wait()
    conv_turned[...] = jnp.transpose(w_conv[...].astype(F32)).astype(BF16)
    low = iota((8, 256), 0) < 4

    def build(half, dx2):
        for dx in range(4):
            rows = [
                facies[2 * b2 + dy2, pl.ds(4 * dx2 + dx, 32, stride=8), :]
                for dy2 in range(2)
                for b2 in range(4 * half, 4 * half + 4)
            ]
            turned = jnp.transpose(jnp.concatenate(rows, axis=0).astype(F32))
            for cp in range(4):
                part = [turned[dy * 32 + cp * 8 : dy * 32 + cp * 8 + 8] for dy in range(4)]
                swapped = [pltpu.roll(piece, 4, 0) for piece in part]
                for dz2 in range(2):
                    pieces = [
                        jnp.where(low, part[dy], swapped[dy + 1]) if dz2 == 0 else jnp.where(low, swapped[dy], part[dy + 1])
                        for dy in (0, 2)
                    ]
                    cells = jnp.concatenate(pieces, axis=0).astype(BF16)
                    for k in range(LEVELS):
                        hot = jnp.where(cells == BF16(k), BF16(1.0), BF16(0.0))
                        first = dx * 48 + k * 16 if k < 3 else 192 + dx * 16
                        for dy2 in range(2):
                            at = (2 * dx2 + dy2) * 256 + half * 128
                            one_hot[2 * cp + dz2, pl.ds(first, 16), pl.ds(at, 128)] = hot[:, dy2 * 128 : dy2 * 128 + 128]

    def embed(cp, dx2):
        for dz2 in range(2):
            rows, at = pl.ds(dz2 * 128, 128), pl.ds(dx2 * 512, 512)
            pre = mm(packed[...], one_hot[2 * cp + dz2, :, at])
            pre_embed[cp, rows, at] = pre
            act = (pre * sigmoid(pre)).astype(BF16)
            hidden[cp, 2 * dx2, rows, :] = act[:, :256]
            hidden[cp, 2 * dx2 + 1, rows, :] = act[:, 256:]

    for half in range(2):
        for load in loads[half * blocks // 2 : (half + 1) * blocks // 2]:
            load.wait()
        if half == 0:
            for load in others[2:]:
                load.start()
            build(0, 0)
            build(0, 1)
    build(1, 0)
    for cp in range(4):
        embed(cp, 0)
    build(1, 1)
    sums = jnp.zeros((256, 128), F32)
    for cp in range(4):
        embed(cp, 1)
        pre = mm(conv_turned[...], hidden[cp].reshape(1024, 256))
        pre_conv[cp] = pre
        act = pre * sigmoid(pre)
        sums = sums + act[:, :128] + act[:, 128:]
    pick = jnp.where(iota((8, 128), 1) // 8 % 4 == iota((8, 128), 0), 1.0, 0.0)
    total = lax.dot_general(pick, sums, NT, precision=lax.Precision.HIGHEST, preferred_element_type=F32) / 256.0
    block[:, pl.ds(1024, 256)] = total[:4].astype(BF16)
    lanes = [jnp.broadcast_to(total[s : s + 1], (8, total.shape[1])) for s in range(4)] * 4
    pooled_lanes[...] = jnp.concatenate(lanes, axis=0).astype(BF16)
    for load in others[2:]:
        load.wait()
    block[:, pl.ds(0, 512)] = prior[...]
    block[:, pl.ds(512, 512)] = recon[...]


def pair_kernel(queries, query_square, keys):
    inner = mm_nt(queries, keys)
    key_float = keys.astype(F32)
    count = keys.shape[0]
    key_square = jnp.sum(key_float * key_float, axis=1, keepdims=True)
    key_row = jnp.transpose(jnp.broadcast_to(key_square, (count, 128)))[:1]
    kern = jnp.exp(-(query_square + key_row - 2.0 * inner) / keys.shape[1])
    return jnp.sum(kern, axis=1, keepdims=True), mm(kern.astype(BF16), keys)


def group_rows(gathered, gathered_other, ordered):
    peers = gathered.shape[0]
    core = lax.rem(lax.axis_index("dp"), 2)
    for place in range(peers):
        ordered[core * peers + place] = gathered[place].astype(F32)
        ordered[(1 - core) * peers + place] = gathered_other[place].astype(F32)
    return ordered[...].reshape(2 * peers * gathered.shape[1], gathered.shape[2])


def latent_rows(pooled, w_head):
    return mm(pooled, w_head[...]).astype(BF16)


def cotangent_rows(queries, keys, prior, recon):
    query_float = queries.astype(F32)
    square = jnp.sum(query_float * query_float, axis=1, keepdims=True)
    self_sum, self_mix = pair_kernel(queries, square, keys)
    cross_sum, cross_mix = pair_kernel(queries, square, prior)
    pull = -32.0 / keys.shape[0] * ((self_sum - cross_sum) * query_float - self_mix + cross_mix)
    return (recon + pull).astype(BF16)


def head_kernel(gathered, gathered_other, w_head, after, grad_head, token, ordered, head_full):
    token[...] = jnp.zeros(token.shape, F32)
    full = group_rows(gathered, gathered_other, ordered)
    latent = latent_rows(full[:, 1024:].astype(BF16), w_head)
    cotangent = cotangent_rows(latent, latent, full[:, :512].astype(BF16), full[:, 512:1024])
    head_full[...] = mm(jnp.transpose(full[:, 1024:]).astype(BF16), cotangent)
    share = grad_head.shape[0]
    start = pl.multiple_of(lax.axis_index("fsdp") * share, share)
    grad_head[...] = head_full[pl.ds(start, share), :]


def backward_kernel(gathered, gathered_other, pooled_lanes, recon, hidden, pre_conv, w_head, keep, send, grads, ordered):
    full = group_rows(gathered, gathered_other, ordered)
    queries = latent_rows(pooled_lanes[...], w_head)
    keys = latent_rows(full[:, 1024:].astype(BF16), w_head)
    recon_float = recon[...].astype(F32)
    recon_lanes = jnp.concatenate(
        [jnp.broadcast_to(recon_float[s : s + 1], (8, recon.shape[1])) for s in range(4)] * 4, axis=0
    )
    cotangent = cotangent_rows(queries, keys, full[:, :512].astype(BF16), recon_lanes)
    back_pool = mm_nt(w_head[...], cotangent) / 256.0
    back_pool = jnp.concatenate([back_pool, back_pool], axis=1)
    fsdp = keep.shape[0]
    conv_total = None
    for cp in range(4):
        grads[cp] = (back_pool * silu_slope(pre_conv[cp])).astype(BF16)
        term = mm_nt(hidden[cp].reshape(1024, 256), grads[cp])
        conv_total = term if cp == 0 else conv_total + term
    core_zero = lax.rem(lax.axis_index("dp"), 2) == 0
    rows = keep.shape[1]
    for f in range(fsdp):
        at = 2 * f * rows
        first, second = conv_total[at : at + rows], conv_total[at + rows : at + 2 * rows]
        keep[f] = jnp.where(core_zero, first, second)
        send[f] = jnp.where(core_zero, second, first)


def embed_kernel(grads, w_conv, pre_embed, one_hot, embed_out):
    embed = None
    ones = jnp.ones((16, 1024), BF16)
    for cp in range(4):
        signals = []
        for dx2 in range(2):
            back_rows = mm(w_conv[pl.ds(dx2 * 512, 512), :], grads[cp])
            back_rows = jnp.concatenate([back_rows[:256], back_rows[256:]], axis=1)
            signals.append((back_rows * silu_slope(pre_embed[cp, :, pl.ds(dx2 * 512, 512)])).astype(BF16))
        signal = jnp.concatenate(signals, axis=1)
        for dz2 in range(2):
            rows = jnp.concatenate([one_hot[2 * cp + dz2, pl.ds(0, 192), :], ones], axis=0)
            term = mm_nt(rows, signal[dz2 * 128 : dz2 * 128 + 128])
            embed = term if embed is None else embed + term
    shares = embed_out.shape[0]
    depth = 64 // shares
    half = 3 * depth // 2
    embed_out[...] = jnp.zeros(embed_out.shape, F32)
    for f in range(shares):
        dx, at = f * 4 // shares, f * depth % 16
        share = jnp.concatenate([embed[dx * 48 + k * 16 + at :][:depth] for k in range(3)], axis=0)
        for side in range(2):
            embed_out[f, pl.ds(0, half), pl.ds(side * 128, 128)] = share[side * half : (side + 1) * half]
        embed_out[f, pl.ds(embed_out.shape[1] - 8, 8), pl.ds(0, 128)] = embed[192:200]


def exponent_of(part):
    top = jnp.abs(part)
    while top.ndim > 2:
        top = jnp.max(top, axis=0)
    top = jnp.max(jnp.max(top, axis=0, keepdims=True), axis=1, keepdims=True)
    return jnp.clip(jnp.floor(jnp.log2(jnp.maximum(top, 1e-37))) - 14.0, -124.0, 114.0)


def store_coded(coded, part, conv_rows):
    store_scaled(coded, part, (exponent_of(part[:conv_rows]), exponent_of(part[conv_rows:])), conv_rows)


def store_scaled(coded, part, steps, conv_rows):
    last = part.shape[0] - 8
    coded[pl.ds(0, conv_rows), :] = part[:conv_rows] * jnp.exp2(-steps[0])
    coded[pl.ds(conv_rows, last - conv_rows), :] = part[conv_rows:last] * jnp.exp2(-steps[1])
    total = part[last:, :128] * jnp.exp2(-steps[1])
    high = total.astype(BF16).astype(F32)
    row = iota((8, 256), 0)
    tail = jnp.where(row == 1, steps[0], steps[1])
    coded[pl.ds(last, 8), :] = jnp.where(row == 0, jnp.concatenate([high, total - high], axis=1), tail)


def load_coded(coded, conv_rows):
    last = coded.shape[0] - 8
    embed_scale = jnp.exp2(coded[pl.ds(last + 2, 1), :])
    total = coded[pl.ds(last, 8), pl.ds(0, 128)] + coded[pl.ds(last, 8), pl.ds(128, 128)]
    total = jnp.where(iota((8, 256), 0) == 0, jnp.concatenate([total, jnp.zeros((8, 128), F32)], axis=1), 0.0)
    embed = jnp.concatenate([coded[pl.ds(conv_rows, last - conv_rows), :], total], axis=0) * embed_scale
    return jnp.concatenate([coded[pl.ds(0, conv_rows), :] * jnp.exp2(coded[pl.ds(last + 1, 1), :]), embed], axis=0)


def scale_kernel(keep, other, embed, own, *coded):
    held = keep[...] + other[...]
    steps = exponent_of(held), exponent_of(embed[...])
    here = lax.axis_index("fsdp")

    def share(z):
        return jnp.concatenate([keep[z] + other[z], embed[z]], axis=0)

    own[...] = share(here)
    for place, target in enumerate(coded):
        store_scaled(target, share(here ^ (place + 1)), steps, keep.shape[1])


def first_sum_kernel(conv_rows, own, *refs):
    *received, coded = refs
    total = own[...]
    for part in received:
        total = total + load_coded(part, conv_rows)
    store_coded(coded, total, conv_rows)


def next_sum_kernel(conv_rows, mine, other, total, *coded):
    summed = load_coded(mine, conv_rows) + load_coded(other, conv_rows)
    total[...] = summed
    if coded:
        store_coded(coded[0], summed, conv_rows)


def output_kernel(own, other, grad_embed, grad_conv):
    conv_rows, count = grad_conv.shape[0] // 2, grad_embed.shape[0]
    core_zero = lax.rem(lax.axis_index("dp"), 2) == 0
    grad_conv[pl.ds(0, conv_rows), :] = jnp.where(core_zero, own[pl.ds(0, conv_rows), :], other[pl.ds(0, conv_rows), :])
    grad_conv[pl.ds(conv_rows, conv_rows), :] = jnp.where(
        core_zero, other[pl.ds(0, conv_rows), :], own[pl.ds(0, conv_rows), :]
    )
    half, depth = 3 * count // 8, count // LEVELS
    embed = own[pl.ds(conv_rows, half), :] + other[pl.ds(conv_rows, half), :]
    embed = jnp.concatenate([embed[:, :128], embed[:, 128:]], axis=0)
    last = own.shape[0] - 8
    total = own[pl.ds(last, 1), pl.ds(0, 128)] + other[pl.ds(last, 1), pl.ds(0, 128)]
    fourth = total - (embed[:depth] + embed[depth : 2 * depth] + embed[2 * depth :])
    embed = jnp.concatenate([embed, fourth], axis=0)
    row, lane = iota((count, count), 0), iota((count, count), 1)
    order = jnp.where(lane == row % LEVELS * depth + row // LEVELS, 1.0, 0.0).astype(BF16)
    result = None
    for _ in range(3):
        term = embed.astype(BF16)
        embed = embed - term.astype(F32)
        result = mm(order, term) if result is None else result + mm(order, term)
    grad_embed[...] = result


VMEM = pl.BlockSpec(memory_space=pltpu.VMEM)
HBM = pl.BlockSpec(memory_space=pltpu.HBM)
SAVED = (
    ((8, 256, 1024), BF16),
    ((4, 256, 1024), F32),
    ((4, 4, 256, 256), BF16),
    ((4, 256, 256), F32),
)


def forward(facies, prior_draws, recon_grad, w_embed, w_conv, w_head):
    samples = facies.shape[0]
    latent_width = prior_draws.shape[1]
    rows, lanes = samples * PATCH_X, PATCH_Y * PATCH_Z
    operands = (facies.reshape(rows, lanes), prior_draws, recon_grad, w_embed, w_conv, w_head)
    return pl.pallas_call(
        forward_kernel,
        out_shape=(pltpu.VMEM((samples, 2 * latent_width + 256), BF16),)
        + (pltpu.VMEM((128, 256), BF16), pltpu.VMEM(recon_grad.shape, BF16))
        + tuple(pltpu.VMEM(shape, kind) for shape, kind in SAVED)
        + (pltpu.VMEM(w_conv.shape, BF16), pltpu.VMEM(w_head.shape, BF16)),
        in_specs=[HBM] * 6,
        out_specs=(VMEM,) * 9,
        scratch_shapes=[
            pltpu.VMEM((lanes // 128, rows, 128), jnp.int32),
            pltpu.VMEM(prior_draws.shape, BF16),
            pltpu.VMEM(w_embed.shape, BF16),
            pltpu.VMEM((128, 256), BF16),
            pltpu.VMEM((256, 1024), BF16),
            pltpu.SemaphoreType.DMA((lanes // 128 + 5,)),
        ],
        compiler_params=pltpu.CompilerParams(vmem_limit_bytes=30 * 2**20),
        name="forward",
    )(*(pltpu.with_memory_space_constraint(operand, pltpu.HBM) for operand in operands))


def backward(fsdp, gathered, *operands):
    peers, samples, width = gathered[0].shape
    payload = pltpu.VMEM((fsdp, 1024 // fsdp // 2, 256), F32)
    return pl.pallas_call(
        backward_kernel,
        out_shape=(payload, payload, pltpu.VMEM((4, 256, 256), BF16)),
        in_specs=[VMEM] * 7,
        out_specs=(VMEM,) * 3,
        scratch_shapes=[pltpu.VMEM((2 * peers, samples, width), F32)],
        compiler_params=pltpu.CompilerParams(vmem_limit_bytes=24 * 2**20),
        name="backward",
    )(*gathered, *operands)


def head_gradient(fsdp, gathered, w_head, after):
    peers, samples, width = gathered[0].shape
    return pl.pallas_call(
        head_kernel,
        out_shape=(jax.ShapeDtypeStruct((256 // fsdp, 512), F32), pltpu.VMEM((8, 128), F32)),
        in_specs=[VMEM] * 3 + [HBM],
        out_specs=(VMEM,) * 2,
        scratch_shapes=[pltpu.VMEM((2 * peers, samples, width), F32), pltpu.VMEM((256, 512), F32)],
        compiler_params=pltpu.CompilerParams(vmem_limit_bytes=16 * 2**20),
        cost_estimate=pl.CostEstimate(flops=2 * 10**9, bytes_accessed=2 * 2**20, transcendentals=10000),
        name="head_gradient",
    )(*gathered, w_head, after)


def embed_gradient(fsdp, grads, w_conv, pre_embed, one_hot):
    return pl.pallas_call(
        embed_kernel,
        out_shape=pltpu.VMEM((fsdp, (96 // fsdp + 7) // 8 * 8 + 8, 256), F32),
        in_specs=[VMEM] * 4,
        out_specs=VMEM,
        compiler_params=pltpu.CompilerParams(vmem_limit_bytes=24 * 2**20),
        cost_estimate=pl.CostEstimate(flops=16 * 10**8, bytes_accessed=10 * 2**20, transcendentals=0),
        name="embed_gradient",
    )(grads, w_conv, pre_embed, one_hot)


def place_of(x, core, z, fsdp):
    return (2 * x + core) * fsdp + z


def exchange(block, dp, fsdp, flip_x, flip_core, flip_z):
    pairs = []
    for x in range(dp // 2):
        for core in range(2):
            for z in range(fsdp):
                pairs.append((place_of(x, core, z, fsdp), place_of(x ^ flip_x, core ^ flip_core, z ^ flip_z, fsdp)))
    return lax.ppermute(block, GROUP, pairs)


def gather_blocks(block, dp, fsdp):
    backward = [(x, z) for z in reversed(range(fsdp)) for x in reversed(range(dp // 2))]
    groups = [[place_of(x, core, z, fsdp) for x, z in backward] for core in range(2)]
    copies = jnp.broadcast_to(block[None], (len(backward),) + block.shape)
    own = lax.all_to_all(copies, GROUP, 0, 0, axis_index_groups=groups, tiled=True)
    return own, exchange(own, dp, fsdp, 0, 1, 0)


def local_kernel(kernel, outs, name, *operands, unread=()):
    return pl.pallas_call(
        lambda *refs: kernel(*refs[: len(operands)], *refs[len(operands) + len(unread) :]),
        out_shape=outs,
        in_specs=[VMEM] * (len(operands) + len(unread)),
        out_specs=(VMEM,) * len(outs),
        compiler_params=pltpu.CompilerParams(vmem_limit_bytes=16 * 2**20),
        name=name,
    )(*operands, *unread)


def to_half(coded):
    rounded = lax.reduce_precision(coded, exponent_bits=5, mantissa_bits=10)
    return rounded, rounded.astype(jnp.float16)


def reduce_to_owner(keep, other, embed, gathered, w_head, dp, fsdp):
    conv_rows, width = keep.shape[1:]
    rows = conv_rows + embed.shape[1]
    plain = jax.ShapeDtypeStruct((rows, width), F32)
    own, *coded = local_kernel(scale_kernel, (plain,) + (plain,) * (fsdp - 1), "scale", keep, other, embed)
    received = [
        exchange(to_half(part)[1], dp, fsdp, 0, 0, place + 1).astype(F32) for place, part in enumerate(coded)
    ]
    grad_head, token = head_gradient(fsdp, gathered, w_head, own)
    (coded,) = local_kernel(
        functools.partial(first_sum_kernel, conv_rows), (plain,), "sum_z", own, *received, unread=(token,)
    )
    flip = 1
    while flip < dp // 2:
        mine, sent = to_half(coded)
        other = exchange(sent, dp, fsdp, flip, 0, 0).astype(F32)
        flip *= 2
        outs = (plain,) * (2 if flip < dp // 2 else 1)
        total, *rest = local_kernel(functools.partial(next_sum_kernel, conv_rows), outs, "sum_x", mine, other)
        coded = rest[0] if rest else None
    return total, exchange(total, dp, fsdp, 0, 1, 0), grad_head


def shards(facies, prior_draws, recon_grad, w_embed, w_conv, w_head):
    dp, fsdp = lax.axis_size("dp"), lax.axis_size("fsdp")
    block, pooled_lanes, recon, one_hot, pre_embed, hidden, pre_conv, w_conv, w_head = forward(
        facies, prior_draws, recon_grad, w_embed, w_conv, w_head
    )
    gathered = gather_blocks(block, dp, fsdp)
    keep, send, grads = backward(fsdp, gathered, pooled_lanes, recon, hidden, pre_conv, w_head)
    received = exchange(send, dp, fsdp, 0, 1, 0)
    embed = embed_gradient(fsdp, grads, w_conv, pre_embed, one_hot)
    own, other, grad_head = reduce_to_owner(keep, received, embed, gathered, w_head, dp, fsdp)
    grad_embed, grad_conv = pl.pallas_call(
        output_kernel,
        out_shape=(
            jax.ShapeDtypeStruct((256 // fsdp, 128), F32),
            jax.ShapeDtypeStruct((1024 // fsdp, 256), F32),
        ),
        in_specs=[VMEM] * 2,
        out_specs=(VMEM,) * 2,
        compiler_params=pltpu.CompilerParams(vmem_limit_bytes=16 * 2**20),
        name="outputs",
    )(own, other)
    return (grad_embed, grad_conv, grad_head)


def solution(mesh):
    return jax.shard_map(
        shards,
        mesh=mesh,
        in_specs=(
            P(("groups", "dp", "fsdp"), None, None),
            P(("groups", "dp", "fsdp"), None),
            P(("groups", "dp", "fsdp"), None),
            P(),
            P(),
            P(),
        ),
        out_specs=(
            P(("groups", "fsdp"), None),
            P(("groups", "fsdp"), None),
            P(("groups", "fsdp"), None),
        ),
        check_vma=False,
    )
```

```python
import functools

import jax
import jax.numpy as jnp
from jax import lax
from jax.experimental import pallas as pl
from jax.experimental.pallas import tpu as pltpu
from jax.sharding import PartitionSpec as P

PATCH_X = 64
PATCH_Y = 64
PATCH_Z = 32
LEVELS = 4
GROUP = ("dp", "fsdp")
NT = (((1,), (1,)), ((), ()))
F32 = jnp.float32
BF16 = jnp.bfloat16


def iota(shape, dim):
    return lax.broadcasted_iota(jnp.int32, shape, dim)


def mm(left, right):
    return jnp.dot(left, right, preferred_element_type=F32)


def mm_nt(left, right):
    return lax.dot_general(left, right, NT, preferred_element_type=F32)


def turned_weights(w_embed):
    turned = jnp.transpose(w_embed.astype(F32)).astype(BF16)
    row, lane = iota((256, 256), 0), iota((256, 256), 1)
    dx, k = row // 64, row % 4
    same = lane == jnp.where(k < 3, dx * 48 + k * 16, 192 + dx * 16) + row // 4 % 16
    return mm(turned, jnp.where(same, 1.0, 0.0).astype(BF16)).astype(BF16)


def sigmoid(value):
    return pltpu.reciprocal(1.0 + jnp.exp2(value * -1.4426950408889634), approx=True)


def silu_slope(value):
    gate = sigmoid(value)
    return gate * (1.0 + value * (1.0 - gate))


def forward_kernel(
    facies_hbm, prior_hbm, recon_hbm, w_embed_hbm, w_conv_hbm, w_head_hbm,
    block, pooled_lanes, recon, one_hot, pre_embed, hidden, pre_conv, w_conv, w_head,
    facies, prior, w_embed, packed, conv_turned, sem
):
    blocks = facies.shape[0]
    loads = [
        pltpu.make_async_copy(facies_hbm.at[:, pl.ds(b * 128, 128)], facies.at[b], sem.at[b]) for b in range(blocks)
    ]
    others = []
    for source, target in (
        (w_embed_hbm, w_embed), (w_conv_hbm, w_conv), (prior_hbm, prior), (recon_hbm, recon), (w_head_hbm, w_head)
    ):
        others.append(pltpu.make_async_copy(source, target, sem.at[blocks + len(others)]))
    for load in others[:2] + loads:
        load.start()
    others[0].wait()
    packed[...] = turned_weights(w_embed[...])
    others[1].wait()
    conv_turned[...] = jnp.transpose(w_conv[...].astype(F32)).astype(BF16)
    low = iota((8, 256), 0) < 4

    def build(half, dx2):
        for dx in range(4):
            rows = [
                facies[2 * b2 + dy2, pl.ds(4 * dx2 + dx, 32, stride=8), :]
                for dy2 in range(2)
                for b2 in range(4 * half, 4 * half + 4)
            ]
            turned = jnp.transpose(jnp.concatenate(rows, axis=0).astype(F32))
            for cp in range(4):
                part = [turned[dy * 32 + cp * 8 : dy * 32 + cp * 8 + 8] for dy in range(4)]
                swapped = [pltpu.roll(piece, 4, 0) for piece in part]
                for dz2 in range(2):
                    pieces = [
                        jnp.where(low, part[dy], swapped[dy + 1]) if dz2 == 0 else jnp.where(low, swapped[dy], part[dy + 1])
                        for dy in (0, 2)
                    ]
                    cells = jnp.concatenate(pieces, axis=0).astype(BF16)
                    for k in range(LEVELS):
                        hot = jnp.where(cells == BF16(k), BF16(1.0), BF16(0.0))
                        first = dx * 48 + k * 16 if k < 3 else 192 + dx * 16
                        for dy2 in range(2):
                            at = (2 * dx2 + dy2) * 256 + half * 128
                            one_hot[2 * cp + dz2, pl.ds(first, 16), pl.ds(at, 128)] = hot[:, dy2 * 128 : dy2 * 128 + 128]

    def embed(cp, dx2):
        for dz2 in range(2):
            rows, at = pl.ds(dz2 * 128, 128), pl.ds(dx2 * 512, 512)
            pre = mm(packed[...], one_hot[2 * cp + dz2, :, at])
            pre_embed[cp, rows, at] = pre
            act = (pre * sigmoid(pre)).astype(BF16)
            hidden[cp, 2 * dx2, rows, :] = act[:, :256]
            hidden[cp, 2 * dx2 + 1, rows, :] = act[:, 256:]

    for half in range(2):
        for load in loads[half * blocks // 2 : (half + 1) * blocks // 2]:
            load.wait()
        if half == 0:
            for load in others[2:]:
                load.start()
            build(0, 0)
            build(0, 1)
    build(1, 0)
    build(1, 1)
    sums = jnp.zeros((256, 128), F32)
    for cp in range(4):
        embed(cp, 0)
        embed(cp, 1)
        pre = mm(conv_turned[...], hidden[cp].reshape(1024, 256))
        pre_conv[cp] = pre
        act = pre * sigmoid(pre)
        sums = sums + act[:, :128] + act[:, 128:]
    pick = jnp.where(iota((8, 128), 1) // 8 % 4 == iota((8, 128), 0), 1.0, 0.0)
    total = lax.dot_general(pick, sums, NT, precision=lax.Precision.HIGHEST, preferred_element_type=F32) / 256.0
    block[:, pl.ds(1024, 256)] = total[:4].astype(BF16)
    lanes = [jnp.broadcast_to(total[s : s + 1], (8, total.shape[1])) for s in range(4)] * 4
    pooled_lanes[...] = jnp.concatenate(lanes, axis=0).astype(BF16)
    for load in others[2:]:
        load.wait()
    block[:, pl.ds(0, 512)] = prior[...]
    block[:, pl.ds(512, 512)] = recon[...]


def pair_kernel(queries, query_square, keys):
    inner = mm_nt(queries, keys)
    key_float = keys.astype(F32)
    count = keys.shape[0]
    key_square = jnp.sum(key_float * key_float, axis=1, keepdims=True)
    key_row = jnp.transpose(jnp.broadcast_to(key_square, (count, 128)))[:1]
    kern = jnp.exp(-(query_square + key_row - 2.0 * inner) / keys.shape[1])
    return jnp.sum(kern, axis=1, keepdims=True), mm(kern.astype(BF16), keys)


def group_rows(gathered, gathered_other, ordered):
    peers = gathered.shape[0]
    core = lax.rem(lax.axis_index("dp"), 2)
    for place in range(peers):
        ordered[core * peers + place] = gathered[place].astype(F32)
        ordered[(1 - core) * peers + place] = gathered_other[place].astype(F32)
    return ordered[...].reshape(2 * peers * gathered.shape[1], gathered.shape[2])


def latent_rows(pooled, w_head):
    return mm(pooled, w_head[...]).astype(BF16)


def cotangent_rows(queries, keys, prior, recon):
    query_float = queries.astype(F32)
    square = jnp.sum(query_float * query_float, axis=1, keepdims=True)
    self_sum, self_mix = pair_kernel(queries, square, keys)
    cross_sum, cross_mix = pair_kernel(queries, square, prior)
    pull = -32.0 / keys.shape[0] * ((self_sum - cross_sum) * query_float - self_mix + cross_mix)
    return (recon + pull).astype(BF16)


def head_kernel(gathered, gathered_other, w_head, after, grad_head, token, ordered, head_full):
    token[...] = jnp.zeros(token.shape, F32)
    full = group_rows(gathered, gathered_other, ordered)
    latent = latent_rows(full[:, 1024:].astype(BF16), w_head)
    cotangent = cotangent_rows(latent, latent, full[:, :512].astype(BF16), full[:, 512:1024])
    head_full[...] = mm(jnp.transpose(full[:, 1024:]).astype(BF16), cotangent)
    share = grad_head.shape[0]
    start = pl.multiple_of(lax.axis_index("fsdp") * share, share)
    grad_head[...] = head_full[pl.ds(start, share), :]


def backward_kernel(gathered, gathered_other, pooled_lanes, recon, hidden, pre_conv, w_head, keep, send, grads, ordered):
    full = group_rows(gathered, gathered_other, ordered)
    queries = latent_rows(pooled_lanes[...], w_head)
    keys = latent_rows(full[:, 1024:].astype(BF16), w_head)
    recon_float = recon[...].astype(F32)
    recon_lanes = jnp.concatenate(
        [jnp.broadcast_to(recon_float[s : s + 1], (8, recon.shape[1])) for s in range(4)] * 4, axis=0
    )
    cotangent = cotangent_rows(queries, keys, full[:, :512].astype(BF16), recon_lanes)
    back_pool = mm_nt(w_head[...], cotangent) / 256.0
    back_pool = jnp.concatenate([back_pool, back_pool], axis=1)
    fsdp = keep.shape[0]
    conv_total = None
    for cp in range(4):
        grads[cp] = (back_pool * silu_slope(pre_conv[cp])).astype(BF16)
        term = mm_nt(hidden[cp].reshape(1024, 256), grads[cp])
        conv_total = term if cp == 0 else conv_total + term
    core_zero = lax.rem(lax.axis_index("dp"), 2) == 0
    rows = keep.shape[1]
    for f in range(fsdp):
        at = 2 * f * rows
        first, second = conv_total[at : at + rows], conv_total[at + rows : at + 2 * rows]
        keep[f] = jnp.where(core_zero, first, second)
        send[f] = jnp.where(core_zero, second, first)


def embed_kernel(grads, w_conv, pre_embed, one_hot, embed_out):
    embed = None
    ones = jnp.ones((16, 1024), BF16)
    for cp in range(4):
        signals = []
        for dx2 in range(2):
            back_rows = mm(w_conv[pl.ds(dx2 * 512, 512), :], grads[cp])
            back_rows = jnp.concatenate([back_rows[:256], back_rows[256:]], axis=1)
            signals.append((back_rows * silu_slope(pre_embed[cp, :, pl.ds(dx2 * 512, 512)])).astype(BF16))
        signal = jnp.concatenate(signals, axis=1)
        for dz2 in range(2):
            rows = jnp.concatenate([one_hot[2 * cp + dz2, pl.ds(0, 192), :], ones], axis=0)
            term = mm_nt(rows, signal[dz2 * 128 : dz2 * 128 + 128])
            embed = term if embed is None else embed + term
    shares = embed_out.shape[0]
    depth = 64 // shares
    half = 3 * depth // 2
    embed_out[...] = jnp.zeros(embed_out.shape, F32)
    for f in range(shares):
        dx, at = f * 4 // shares, f * depth % 16
        share = jnp.concatenate([embed[dx * 48 + k * 16 + at :][:depth] for k in range(3)], axis=0)
        for side in range(2):
            embed_out[f, pl.ds(0, half), pl.ds(side * 128, 128)] = share[side * half : (side + 1) * half]
        embed_out[f, pl.ds(embed_out.shape[1] - 8, 8), pl.ds(0, 128)] = embed[192:200]


def exponent_of(part):
    top = jnp.abs(part)
    while top.ndim > 2:
        top = jnp.max(top, axis=0)
    top = jnp.max(jnp.max(top, axis=0, keepdims=True), axis=1, keepdims=True)
    return jnp.clip(jnp.floor(jnp.log2(jnp.maximum(top, 1e-37))) - 14.0, -124.0, 114.0)


def store_coded(coded, part, conv_rows):
    store_scaled(coded, part, (exponent_of(part[:conv_rows]), exponent_of(part[conv_rows:])), conv_rows)


def store_scaled(coded, part, steps, conv_rows):
    last = part.shape[0] - 8
    coded[pl.ds(0, conv_rows), :] = part[:conv_rows] * jnp.exp2(-steps[0])
    coded[pl.ds(conv_rows, last - conv_rows), :] = part[conv_rows:last] * jnp.exp2(-steps[1])
    total = part[last:, :128] * jnp.exp2(-steps[1])
    high = total.astype(BF16).astype(F32)
    row = iota((8, 256), 0)
    tail = jnp.where(row == 1, steps[0], steps[1])
    coded[pl.ds(last, 8), :] = jnp.where(row == 0, jnp.concatenate([high, total - high], axis=1), tail)


def load_coded(coded, conv_rows):
    last = coded.shape[0] - 8
    embed_scale = jnp.exp2(coded[pl.ds(last + 2, 1), :])
    total = coded[pl.ds(last, 8), pl.ds(0, 128)] + coded[pl.ds(last, 8), pl.ds(128, 128)]
    total = jnp.where(iota((8, 256), 0) == 0, jnp.concatenate([total, jnp.zeros((8, 128), F32)], axis=1), 0.0)
    embed = jnp.concatenate([coded[pl.ds(conv_rows, last - conv_rows), :], total], axis=0) * embed_scale
    return jnp.concatenate([coded[pl.ds(0, conv_rows), :] * jnp.exp2(coded[pl.ds(last + 1, 1), :]), embed], axis=0)


def scale_kernel(keep, other, embed, own, *coded):
    held = keep[...] + other[...]
    steps = exponent_of(held), exponent_of(embed[...])
    here = lax.axis_index("fsdp")

    def share(z):
        return jnp.concatenate([keep[z] + other[z], embed[z]], axis=0)

    own[...] = share(here)
    for place, target in enumerate(coded):
        store_scaled(target, share(here ^ (place + 1)), steps, keep.shape[1])


def first_sum_kernel(conv_rows, own, *refs):
    *received, coded = refs
    total = own[...]
    for part in received:
        total = total + load_coded(part, conv_rows)
    store_coded(coded, total, conv_rows)


def next_sum_kernel(conv_rows, mine, other, total, *coded):
    summed = load_coded(mine, conv_rows) + load_coded(other, conv_rows)
    total[...] = summed
    if coded:
        store_coded(coded[0], summed, conv_rows)


def output_kernel(own, other, grad_embed, grad_conv):
    conv_rows, count = grad_conv.shape[0] // 2, grad_embed.shape[0]
    core_zero = lax.rem(lax.axis_index("dp"), 2) == 0
    grad_conv[pl.ds(0, conv_rows), :] = jnp.where(core_zero, own[pl.ds(0, conv_rows), :], other[pl.ds(0, conv_rows), :])
    grad_conv[pl.ds(conv_rows, conv_rows), :] = jnp.where(
        core_zero, other[pl.ds(0, conv_rows), :], own[pl.ds(0, conv_rows), :]
    )
    half, depth = 3 * count // 8, count // LEVELS
    embed = own[pl.ds(conv_rows, half), :] + other[pl.ds(conv_rows, half), :]
    embed = jnp.concatenate([embed[:, :128], embed[:, 128:]], axis=0)
    last = own.shape[0] - 8
    total = own[pl.ds(last, 1), pl.ds(0, 128)] + other[pl.ds(last, 1), pl.ds(0, 128)]
    fourth = total - (embed[:depth] + embed[depth : 2 * depth] + embed[2 * depth :])
    embed = jnp.concatenate([embed, fourth], axis=0)
    row, lane = iota((count, count), 0), iota((count, count), 1)
    order = jnp.where(lane == row % LEVELS * depth + row // LEVELS, 1.0, 0.0).astype(BF16)
    result = None
    for _ in range(3):
        term = embed.astype(BF16)
        embed = embed - term.astype(F32)
        result = mm(order, term) if result is None else result + mm(order, term)
    grad_embed[...] = result


VMEM = pl.BlockSpec(memory_space=pltpu.VMEM)
HBM = pl.BlockSpec(memory_space=pltpu.HBM)
SAVED = (
    ((8, 256, 1024), BF16),
    ((4, 256, 1024), F32),
    ((4, 4, 256, 256), BF16),
    ((4, 256, 256), F32),
)


def forward(facies, prior_draws, recon_grad, w_embed, w_conv, w_head):
    samples = facies.shape[0]
    latent_width = prior_draws.shape[1]
    rows, lanes = samples * PATCH_X, PATCH_Y * PATCH_Z
    operands = (facies.reshape(rows, lanes), prior_draws, recon_grad, w_embed, w_conv, w_head)
    return pl.pallas_call(
        forward_kernel,
        out_shape=(pltpu.VMEM((samples, 2 * latent_width + 256), BF16),)
        + (pltpu.VMEM((128, 256), BF16), pltpu.VMEM(recon_grad.shape, BF16))
        + tuple(pltpu.VMEM(shape, kind) for shape, kind in SAVED)
        + (pltpu.VMEM(w_conv.shape, BF16), pltpu.VMEM(w_head.shape, BF16)),
        in_specs=[HBM] * 6,
        out_specs=(VMEM,) * 9,
        scratch_shapes=[
            pltpu.VMEM((lanes // 128, rows, 128), jnp.int32),
            pltpu.VMEM(prior_draws.shape, BF16),
            pltpu.VMEM(w_embed.shape, BF16),
            pltpu.VMEM((128, 256), BF16),
            pltpu.VMEM((256, 1024), BF16),
            pltpu.SemaphoreType.DMA((lanes // 128 + 5,)),
        ],
        compiler_params=pltpu.CompilerParams(vmem_limit_bytes=30 * 2**20),
        name="forward",
    )(*(pltpu.with_memory_space_constraint(operand, pltpu.HBM) for operand in operands))


def backward(fsdp, gathered, *operands):
    peers, samples, width = gathered[0].shape
    payload = pltpu.VMEM((fsdp, 1024 // fsdp // 2, 256), F32)
    return pl.pallas_call(
        backward_kernel,
        out_shape=(payload, payload, pltpu.VMEM((4, 256, 256), BF16)),
        in_specs=[VMEM] * 7,
        out_specs=(VMEM,) * 3,
        scratch_shapes=[pltpu.VMEM((2 * peers, samples, width), F32)],
        compiler_params=pltpu.CompilerParams(vmem_limit_bytes=24 * 2**20),
        name="backward",
    )(*gathered, *operands)


def head_gradient(fsdp, gathered, w_head, after):
    peers, samples, width = gathered[0].shape
    return pl.pallas_call(
        head_kernel,
        out_shape=(jax.ShapeDtypeStruct((256 // fsdp, 512), F32), pltpu.VMEM((8, 128), F32)),
        in_specs=[VMEM] * 3 + [HBM],
        out_specs=(VMEM,) * 2,
        scratch_shapes=[pltpu.VMEM((2 * peers, samples, width), F32), pltpu.VMEM((256, 512), F32)],
        compiler_params=pltpu.CompilerParams(vmem_limit_bytes=16 * 2**20),
        cost_estimate=pl.CostEstimate(flops=2 * 10**9, bytes_accessed=2 * 2**20, transcendentals=10000),
        name="head_gradient",
    )(*gathered, w_head, after)


def embed_gradient(fsdp, grads, w_conv, pre_embed, one_hot):
    return pl.pallas_call(
        embed_kernel,
        out_shape=pltpu.VMEM((fsdp, (96 // fsdp + 7) // 8 * 8 + 8, 256), F32),
        in_specs=[VMEM] * 4,
        out_specs=VMEM,
        compiler_params=pltpu.CompilerParams(vmem_limit_bytes=24 * 2**20),
        cost_estimate=pl.CostEstimate(flops=16 * 10**8, bytes_accessed=10 * 2**20, transcendentals=0),
        name="embed_gradient",
    )(grads, w_conv, pre_embed, one_hot)


def place_of(x, core, z, fsdp):
    return (2 * x + core) * fsdp + z


def exchange(block, dp, fsdp, flip_x, flip_core, flip_z):
    pairs = []
    for x in range(dp // 2):
        for core in range(2):
            for z in range(fsdp):
                pairs.append((place_of(x, core, z, fsdp), place_of(x ^ flip_x, core ^ flip_core, z ^ flip_z, fsdp)))
    return lax.ppermute(block, GROUP, pairs)


def gather_blocks(block, dp, fsdp):
    backward = [(x, z) for z in reversed(range(fsdp)) for x in reversed(range(dp // 2))]
    groups = [[place_of(x, core, z, fsdp) for x, z in backward] for core in range(2)]
    copies = jnp.broadcast_to(block[None], (len(backward),) + block.shape)
    own = lax.all_to_all(copies, GROUP, 0, 0, axis_index_groups=groups, tiled=True)
    return own, exchange(own, dp, fsdp, 0, 1, 0)


def local_kernel(kernel, outs, name, *operands, unread=()):
    return pl.pallas_call(
        lambda *refs: kernel(*refs[: len(operands)], *refs[len(operands) + len(unread) :]),
        out_shape=outs,
        in_specs=[VMEM] * (len(operands) + len(unread)),
        out_specs=(VMEM,) * len(outs),
        compiler_params=pltpu.CompilerParams(vmem_limit_bytes=16 * 2**20),
        name=name,
    )(*operands, *unread)


def to_half(coded):
    rounded = lax.reduce_precision(coded, exponent_bits=5, mantissa_bits=10)
    return rounded, rounded.astype(jnp.float16)


def reduce_to_owner(keep, other, embed, gathered, w_head, dp, fsdp):
    conv_rows, width = keep.shape[1:]
    rows = conv_rows + embed.shape[1]
    plain = jax.ShapeDtypeStruct((rows, width), F32)
    own, *coded = local_kernel(scale_kernel, (plain,) + (plain,) * (fsdp - 1), "scale", keep, other, embed)
    received = [
        exchange(to_half(part)[1], dp, fsdp, 0, 0, place + 1).astype(F32) for place, part in enumerate(coded)
    ]
    grad_head, token = head_gradient(fsdp, gathered, w_head, own)
    (coded,) = local_kernel(
        functools.partial(first_sum_kernel, conv_rows), (plain,), "sum_z", own, *received, unread=(token,)
    )
    flip = 1
    while flip < dp // 2:
        mine, sent = to_half(coded)
        other = exchange(sent, dp, fsdp, flip, 0, 0).astype(F32)
        flip *= 2
        outs = (plain,) * (2 if flip < dp // 2 else 1)
        total, *rest = local_kernel(functools.partial(next_sum_kernel, conv_rows), outs, "sum_x", mine, other)
        coded = rest[0] if rest else None
    return total, exchange(total, dp, fsdp, 0, 1, 0), grad_head


def shards(facies, prior_draws, recon_grad, w_embed, w_conv, w_head):
    dp, fsdp = lax.axis_size("dp"), lax.axis_size("fsdp")
    block, pooled_lanes, recon, one_hot, pre_embed, hidden, pre_conv, w_conv, w_head = forward(
        facies, prior_draws, recon_grad, w_embed, w_conv, w_head
    )
    gathered = gather_blocks(block, dp, fsdp)
    keep, send, grads = backward(fsdp, gathered, pooled_lanes, recon, hidden, pre_conv, w_head)
    received = exchange(send, dp, fsdp, 0, 1, 0)
    embed = embed_gradient(fsdp, grads, w_conv, pre_embed, one_hot)
    own, other, grad_head = reduce_to_owner(keep, received, embed, gathered, w_head, dp, fsdp)
    grad_embed, grad_conv = pl.pallas_call(
        output_kernel,
        out_shape=(
            jax.ShapeDtypeStruct((256 // fsdp, 128), F32),
            jax.ShapeDtypeStruct((1024 // fsdp, 256), F32),
        ),
        in_specs=[VMEM] * 2,
        out_specs=(VMEM,) * 2,
        compiler_params=pltpu.CompilerParams(vmem_limit_bytes=16 * 2**20),
        name="outputs",
    )(own, other)
    return (grad_embed, grad_conv, grad_head)


def solution(mesh):
    return jax.shard_map(
        shards,
        mesh=mesh,
        in_specs=(
            P(("groups", "dp", "fsdp"), None, None),
            P(("groups", "dp", "fsdp"), None),
            P(("groups", "dp", "fsdp"), None),
            P(),
            P(),
            P(),
        ),
        out_specs=(
            P(("groups", "fsdp"), None),
            P(("groups", "fsdp"), None),
            P(("groups", "fsdp"), None),
        ),
        check_vma=False,
    )
```

```python
import functools

import jax
import jax.numpy as jnp
from jax import lax
from jax.experimental import pallas as pl
from jax.experimental.pallas import tpu as pltpu
from jax.sharding import PartitionSpec as P

PATCH_X = 64
PATCH_Y = 64
PATCH_Z = 32
LEVELS = 4
GROUP = ("dp", "fsdp")
NT = (((1,), (1,)), ((), ()))
F32 = jnp.float32
BF16 = jnp.bfloat16


def iota(shape, dim):
    return lax.broadcasted_iota(jnp.int32, shape, dim)


def mm(left, right):
    return jnp.dot(left, right, preferred_element_type=F32)


def mm_nt(left, right):
    return lax.dot_general(left, right, NT, preferred_element_type=F32)


def turned_weights(w_embed):
    turned = jnp.transpose(w_embed.astype(F32)).astype(BF16)
    row, lane = iota((256, 256), 0), iota((256, 256), 1)
    dx, k = row // 64, row % 4
    same = lane == jnp.where(k < 3, dx * 48 + k * 16, 192 + dx * 16) + row // 4 % 16
    return mm(turned, jnp.where(same, 1.0, 0.0).astype(BF16)).astype(BF16)


def sigmoid(value):
    return pltpu.reciprocal(1.0 + jnp.exp2(value * -1.4426950408889634), approx=True)


def silu_slope(value):
    gate = sigmoid(value)
    return gate * (1.0 + value * (1.0 - gate))


def forward_kernel(
    facies_hbm, prior_hbm, recon_hbm, w_embed_hbm, w_conv_hbm, w_head_hbm,
    block, pooled_lanes, recon, one_hot, pre_embed, hidden, pre_conv, w_conv, w_head,
    facies, prior, w_embed, packed, conv_turned, sem
):
    blocks = facies.shape[0]
    loads = [
        pltpu.make_async_copy(facies_hbm.at[:, pl.ds(b * 128, 128)], facies.at[b], sem.at[b]) for b in range(blocks)
    ]
    others = []
    for source, target in (
        (w_embed_hbm, w_embed), (w_conv_hbm, w_conv), (prior_hbm, prior), (recon_hbm, recon), (w_head_hbm, w_head)
    ):
        others.append(pltpu.make_async_copy(source, target, sem.at[blocks + len(others)]))
    for load in others[:2] + loads:
        load.start()
    others[0].wait()
    packed[...] = turned_weights(w_embed[...])
    others[1].wait()
    conv_turned[...] = jnp.transpose(w_conv[...].astype(F32)).astype(BF16)
    low = iota((8, 256), 0) < 4

    def build(half, dx2):
        for dx in range(4):
            rows = [
                facies[2 * b2 + dy2, pl.ds(4 * dx2 + dx, 32, stride=8), :]
                for dy2 in range(2)
                for b2 in range(4 * half, 4 * half + 4)
            ]
            turned = jnp.transpose(jnp.concatenate(rows, axis=0).astype(F32))
            for cp in range(4):
                part = [turned[dy * 32 + cp * 8 : dy * 32 + cp * 8 + 8] for dy in range(4)]
                swapped = [pltpu.roll(piece, 4, 0) for piece in part]
                for dz2 in range(2):
                    pieces = [
                        jnp.where(low, part[dy], swapped[dy + 1]) if dz2 == 0 else jnp.where(low, swapped[dy], part[dy + 1])
                        for dy in (0, 2)
                    ]
                    cells = jnp.concatenate(pieces, axis=0).astype(BF16)
                    for k in range(LEVELS):
                        hot = jnp.where(cells == BF16(k), BF16(1.0), BF16(0.0))
                        first = dx * 48 + k * 16 if k < 3 else 192 + dx * 16
                        for dy2 in range(2):
                            at = (2 * dx2 + dy2) * 256 + half * 128
                            one_hot[2 * cp + dz2, pl.ds(first, 16), pl.ds(at, 128)] = hot[:, dy2 * 128 : dy2 * 128 + 128]

    def embed(cp, dx2):
        for dz2 in range(2):
            rows, at = pl.ds(dz2 * 128, 128), pl.ds(dx2 * 512, 512)
            pre = mm(packed[...], one_hot[2 * cp + dz2, :, at])
            pre_embed[cp, rows, at] = pre
            act = (pre * sigmoid(pre)).astype(BF16)
            hidden[cp, 2 * dx2, rows, :] = act[:, :256]
            hidden[cp, 2 * dx2 + 1, rows, :] = act[:, 256:]

    for half in range(2):
        for load in loads[half * blocks // 2 : (half + 1) * blocks // 2]:
            load.wait()
        if half == 0:
            for load in others[2:]:
                load.start()
            build(0, 0)
            build(0, 1)
    build(1, 0)
    build(1, 1)
    sums = jnp.zeros((256, 128), F32)
    for cp in range(4):
        embed(cp, 0)
        embed(cp, 1)
        pre = mm(conv_turned[...], hidden[cp].reshape(1024, 256))
        pre_conv[cp] = pre
        act = pre * sigmoid(pre)
        sums = sums + act[:, :128] + act[:, 128:]
    pick = jnp.where(iota((8, 128), 1) // 8 % 4 == iota((8, 128), 0), 1.0, 0.0)
    total = lax.dot_general(pick, sums, NT, precision=lax.Precision.HIGHEST, preferred_element_type=F32) / 256.0
    block[:, pl.ds(1024, 256)] = total[:4].astype(BF16)
    lanes = [jnp.broadcast_to(total[s : s + 1], (8, total.shape[1])) for s in range(4)] * 4
    pooled_lanes[...] = jnp.concatenate(lanes, axis=0).astype(BF16)
    for load in others[2:]:
        load.wait()
    block[:, pl.ds(0, 512)] = prior[...]
    block[:, pl.ds(512, 512)] = recon[...]


def pair_kernel(queries, query_square, keys):
    inner = mm_nt(queries, keys)
    key_float = keys.astype(F32)
    count = keys.shape[0]
    key_square = jnp.sum(key_float * key_float, axis=1, keepdims=True)
    key_row = jnp.transpose(jnp.broadcast_to(key_square, (count, 128)))[:1]
    kern = jnp.exp(-(query_square + key_row - 2.0 * inner) / keys.shape[1])
    return jnp.sum(kern, axis=1, keepdims=True), mm(kern.astype(BF16), keys)


def group_rows(gathered, gathered_other, ordered):
    peers = gathered.shape[0]
    core = lax.rem(lax.axis_index("dp"), 2)
    for place in range(peers):
        ordered[core * peers + place] = gathered[place].astype(F32)
        ordered[(1 - core) * peers + place] = gathered_other[place].astype(F32)
    return ordered[...].reshape(2 * peers * gathered.shape[1], gathered.shape[2])


def latent_rows(pooled, w_head):
    return mm(pooled, w_head[...]).astype(BF16)


def cotangent_rows(queries, keys, prior, recon):
    query_float = queries.astype(F32)
    square = jnp.sum(query_float * query_float, axis=1, keepdims=True)
    self_sum, self_mix = pair_kernel(queries, square, keys)
    cross_sum, cross_mix = pair_kernel(queries, square, prior)
    pull = -32.0 / keys.shape[0] * ((self_sum - cross_sum) * query_float - self_mix + cross_mix)
    return (recon + pull).astype(BF16)


def head_kernel(gathered, gathered_other, w_head, after, grad_head, token, ordered, head_full):
    token[...] = jnp.zeros(token.shape, F32)
    full = group_rows(gathered, gathered_other, ordered)
    latent = latent_rows(full[:, 1024:].astype(BF16), w_head)
    cotangent = cotangent_rows(latent, latent, full[:, :512].astype(BF16), full[:, 512:1024])
    head_full[...] = mm(jnp.transpose(full[:, 1024:]).astype(BF16), cotangent)
    share = grad_head.shape[0]
    start = pl.multiple_of(lax.axis_index("fsdp") * share, share)
    grad_head[...] = head_full[pl.ds(start, share), :]


def backward_kernel(gathered, gathered_other, pooled_lanes, recon, hidden, pre_conv, w_head, keep, send, grads, ordered):
    full = group_rows(gathered, gathered_other, ordered)
    queries = latent_rows(pooled_lanes[...], w_head)
    keys = latent_rows(full[:, 1024:].astype(BF16), w_head)
    recon_float = recon[...].astype(F32)
    recon_lanes = jnp.concatenate(
        [jnp.broadcast_to(recon_float[s : s + 1], (8, recon.shape[1])) for s in range(4)] * 4, axis=0
    )
    cotangent = cotangent_rows(queries, keys, full[:, :512].astype(BF16), recon_lanes)
    back_pool = mm_nt(w_head[...], cotangent) / 256.0
    back_pool = jnp.concatenate([back_pool, back_pool], axis=1)
    fsdp = keep.shape[0]
    conv_total = None
    for cp in range(4):
        grads[cp] = (back_pool * silu_slope(pre_conv[cp])).astype(BF16)
        term = mm_nt(hidden[cp].reshape(1024, 256), grads[cp])
        conv_total = term if cp == 0 else conv_total + term
    core_zero = lax.rem(lax.axis_index("dp"), 2) == 0
    rows = keep.shape[1]
    for f in range(fsdp):
        at = 2 * f * rows
        first, second = conv_total[at : at + rows], conv_total[at + rows : at + 2 * rows]
        keep[f] = jnp.where(core_zero, first, second)
        send[f] = jnp.where(core_zero, second, first)


def embed_kernel(grads, w_conv, pre_embed, one_hot, embed_out):
    embed = None
    ones = jnp.ones((16, 1024), BF16)
    for cp in range(4):
        signals = []
        for dx2 in range(2):
            back_rows = mm(w_conv[pl.ds(dx2 * 512, 512), :], grads[cp])
            back_rows = jnp.concatenate([back_rows[:256], back_rows[256:]], axis=1)
            signals.append((back_rows * silu_slope(pre_embed[cp, :, pl.ds(dx2 * 512, 512)])).astype(BF16))
        signal = jnp.concatenate(signals, axis=1)
        for dz2 in range(2):
            rows = jnp.concatenate([one_hot[2 * cp + dz2, pl.ds(0, 192), :], ones], axis=0)
            term = mm_nt(rows, signal[dz2 * 128 : dz2 * 128 + 128])
            embed = term if embed is None else embed + term
    shares = embed_out.shape[0]
    depth = 64 // shares
    half = 3 * depth // 2
    embed_out[...] = jnp.zeros(embed_out.shape, F32)
    for f in range(shares):
        dx, at = f * 4 // shares, f * depth % 16
        share = jnp.concatenate([embed[dx * 48 + k * 16 + at :][:depth] for k in range(3)], axis=0)
        for side in range(2):
            embed_out[f, pl.ds(0, half), pl.ds(side * 128, 128)] = share[side * half : (side + 1) * half]
        embed_out[f, pl.ds(embed_out.shape[1] - 8, 8), pl.ds(0, 128)] = embed[192:200]


def exponent_of(part):
    top = jnp.abs(part)
    while top.ndim > 2:
        top = jnp.max(top, axis=0)
    top = jnp.max(jnp.max(top, axis=0, keepdims=True), axis=1, keepdims=True)
    return jnp.clip(jnp.floor(jnp.log2(jnp.maximum(top, 1e-37))) - 14.0, -124.0, 114.0)


def store_coded(coded, part, conv_rows):
    store_scaled(coded, part, (exponent_of(part[:conv_rows]), exponent_of(part[conv_rows:])), conv_rows)


def store_scaled(coded, part, steps, conv_rows):
    last = part.shape[0] - 8
    coded[pl.ds(0, conv_rows), :] = part[:conv_rows] * jnp.exp2(-steps[0])
    coded[pl.ds(conv_rows, last - conv_rows), :] = part[conv_rows:last] * jnp.exp2(-steps[1])
    total = part[last:, :128] * jnp.exp2(-steps[1])
    high = total.astype(BF16).astype(F32)
    row = iota((8, 256), 0)
    tail = jnp.where(row == 1, steps[0], steps[1])
    coded[pl.ds(last, 8), :] = jnp.where(row == 0, jnp.concatenate([high, total - high], axis=1), tail)


def load_coded(coded, conv_rows):
    last = coded.shape[0] - 8
    embed_scale = jnp.exp2(coded[pl.ds(last + 2, 1), :])
    total = coded[pl.ds(last, 8), pl.ds(0, 128)] + coded[pl.ds(last, 8), pl.ds(128, 128)]
    total = jnp.where(iota((8, 256), 0) == 0, jnp.concatenate([total, jnp.zeros((8, 128), F32)], axis=1), 0.0)
    embed = jnp.concatenate([coded[pl.ds(conv_rows, last - conv_rows), :], total], axis=0) * embed_scale
    return jnp.concatenate([coded[pl.ds(0, conv_rows), :] * jnp.exp2(coded[pl.ds(last + 1, 1), :]), embed], axis=0)


def scale_kernel(keep, other, embed, own, *coded):
    held = keep[...] + other[...]
    steps = exponent_of(held), exponent_of(embed[...])
    here = lax.axis_index("fsdp")

    def share(z):
        return jnp.concatenate([keep[z] + other[z], embed[z]], axis=0)

    own[...] = share(here)
    for place, target in enumerate(coded):
        store_scaled(target, share(here ^ (place + 1)), steps, keep.shape[1])


def first_sum_kernel(conv_rows, own, *refs):
    *received, coded = refs
    total = own[...]
    for part in received:
        total = total + load_coded(part, conv_rows)
    store_coded(coded, total, conv_rows)


def next_sum_kernel(conv_rows, mine, other, total, *coded):
    summed = load_coded(mine, conv_rows) + load_coded(other, conv_rows)
    total[...] = summed
    if coded:
        store_coded(coded[0], summed, conv_rows)


def output_kernel(own, other, grad_embed, grad_conv):
    conv_rows, count = grad_conv.shape[0] // 2, grad_embed.shape[0]
    core_zero = lax.rem(lax.axis_index("dp"), 2) == 0
    grad_conv[pl.ds(0, conv_rows), :] = jnp.where(core_zero, own[pl.ds(0, conv_rows), :], other[pl.ds(0, conv_rows), :])
    grad_conv[pl.ds(conv_rows, conv_rows), :] = jnp.where(
        core_zero, other[pl.ds(0, conv_rows), :], own[pl.ds(0, conv_rows), :]
    )
    half, depth = 3 * count // 8, count // LEVELS
    embed = own[pl.ds(conv_rows, half), :] + other[pl.ds(conv_rows, half), :]
    embed = jnp.concatenate([embed[:, :128], embed[:, 128:]], axis=0)
    last = own.shape[0] - 8
    total = own[pl.ds(last, 1), pl.ds(0, 128)] + other[pl.ds(last, 1), pl.ds(0, 128)]
    fourth = total - (embed[:depth] + embed[depth : 2 * depth] + embed[2 * depth :])
    embed = jnp.concatenate([embed, fourth], axis=0)
    row, lane = iota((count, count), 0), iota((count, count), 1)
    order = jnp.where(lane == row % LEVELS * depth + row // LEVELS, 1.0, 0.0).astype(BF16)
    result = None
    for _ in range(3):
        term = embed.astype(BF16)
        embed = embed - term.astype(F32)
        result = mm(order, term) if result is None else result + mm(order, term)
    grad_embed[...] = result


VMEM = pl.BlockSpec(memory_space=pltpu.VMEM)
HBM = pl.BlockSpec(memory_space=pltpu.HBM)
SAVED = (
    ((8, 256, 1024), BF16),
    ((4, 256, 1024), F32),
    ((4, 4, 256, 256), BF16),
    ((4, 256, 256), F32),
)


def forward(facies, prior_draws, recon_grad, w_embed, w_conv, w_head):
    samples = facies.shape[0]
    latent_width = prior_draws.shape[1]
    rows, lanes = samples * PATCH_X, PATCH_Y * PATCH_Z
    operands = (facies.reshape(rows, lanes), prior_draws, recon_grad, w_embed, w_conv, w_head)
    return pl.pallas_call(
        forward_kernel,
        out_shape=(pltpu.VMEM((samples, 2 * latent_width + 256), BF16),)
        + (pltpu.VMEM((128, 256), BF16), pltpu.VMEM(recon_grad.shape, BF16))
        + tuple(pltpu.VMEM(shape, kind) for shape, kind in SAVED)
        + (pltpu.VMEM(w_conv.shape, BF16), pltpu.VMEM(w_head.shape, BF16)),
        in_specs=[HBM] * 6,
        out_specs=(VMEM,) * 9,
        scratch_shapes=[
            pltpu.VMEM((lanes // 128, rows, 128), jnp.int32),
            pltpu.VMEM(prior_draws.shape, BF16),
            pltpu.VMEM(w_embed.shape, BF16),
            pltpu.VMEM((128, 256), BF16),
            pltpu.VMEM((256, 1024), BF16),
            pltpu.SemaphoreType.DMA((lanes // 128 + 5,)),
        ],
        compiler_params=pltpu.CompilerParams(vmem_limit_bytes=30 * 2**20),
        name="forward",
    )(*(pltpu.with_memory_space_constraint(operand, pltpu.HBM) for operand in operands))


def backward(fsdp, gathered, *operands):
    peers, samples, width = gathered[0].shape
    payload = pltpu.VMEM((fsdp, 1024 // fsdp // 2, 256), F32)
    return pl.pallas_call(
        backward_kernel,
        out_shape=(payload, payload, pltpu.VMEM((4, 256, 256), BF16)),
        in_specs=[VMEM] * 7,
        out_specs=(VMEM,) * 3,
        scratch_shapes=[pltpu.VMEM((2 * peers, samples, width), F32)],
        compiler_params=pltpu.CompilerParams(vmem_limit_bytes=24 * 2**20),
        name="backward",
    )(*gathered, *operands)


def head_gradient(fsdp, gathered, w_head, after):
    peers, samples, width = gathered[0].shape
    return pl.pallas_call(
        head_kernel,
        out_shape=(jax.ShapeDtypeStruct((256 // fsdp, 512), F32), pltpu.VMEM((8, 128), F32)),
        in_specs=[VMEM] * 3 + [HBM],
        out_specs=(VMEM,) * 2,
        scratch_shapes=[pltpu.VMEM((2 * peers, samples, width), F32), pltpu.VMEM((256, 512), F32)],
        compiler_params=pltpu.CompilerParams(vmem_limit_bytes=16 * 2**20),
        cost_estimate=pl.CostEstimate(flops=2 * 10**9, bytes_accessed=2 * 2**20, transcendentals=10000),
        name="head_gradient",
    )(*gathered, w_head, after)


def embed_gradient(fsdp, grads, w_conv, pre_embed, one_hot):
    return pl.pallas_call(
        embed_kernel,
        out_shape=pltpu.VMEM((fsdp, (96 // fsdp + 7) // 8 * 8 + 8, 256), F32),
        in_specs=[VMEM] * 4,
        out_specs=VMEM,
        compiler_params=pltpu.CompilerParams(vmem_limit_bytes=24 * 2**20),
        cost_estimate=pl.CostEstimate(flops=16 * 10**8, bytes_accessed=10 * 2**20, transcendentals=0),
        name="embed_gradient",
    )(grads, w_conv, pre_embed, one_hot)


def place_of(x, core, z, fsdp):
    return (2 * x + core) * fsdp + z


def exchange(block, dp, fsdp, flip_x, flip_core, flip_z):
    pairs = []
    for x in range(dp // 2):
        for core in range(2):
            for z in range(fsdp):
                pairs.append((place_of(x, core, z, fsdp), place_of(x ^ flip_x, core ^ flip_core, z ^ flip_z, fsdp)))
    return lax.ppermute(block, GROUP, pairs)


def gather_blocks(block, dp, fsdp):
    backward = [(x, z) for z in reversed(range(fsdp)) for x in reversed(range(dp // 2))]
    groups = [[place_of(x, core, z, fsdp) for x, z in backward] for core in range(2)]
    copies = jnp.broadcast_to(block[None], (len(backward),) + block.shape)
    own = lax.all_to_all(copies, GROUP, 0, 0, axis_index_groups=groups, tiled=True)
    return own, exchange(own, dp, fsdp, 0, 1, 0)


def local_kernel(kernel, outs, name, *operands, unread=()):
    return pl.pallas_call(
        lambda *refs: kernel(*refs[: len(operands)], *refs[len(operands) + len(unread) :]),
        out_shape=outs,
        in_specs=[VMEM] * (len(operands) + len(unread)),
        out_specs=(VMEM,) * len(outs),
        compiler_params=pltpu.CompilerParams(vmem_limit_bytes=16 * 2**20),
        name=name,
    )(*operands, *unread)


def to_half(coded):
    rounded = lax.reduce_precision(coded, exponent_bits=5, mantissa_bits=10)
    return rounded, rounded.astype(jnp.float16)


def reduce_to_owner(keep, other, embed, gathered, w_head, dp, fsdp):
    conv_rows, width = keep.shape[1:]
    rows = conv_rows + embed.shape[1]
    plain = jax.ShapeDtypeStruct((rows, width), F32)
    own, *coded = local_kernel(scale_kernel, (plain,) + (plain,) * (fsdp - 1), "scale", keep, other, embed)
    received = [
        exchange(part.astype(jnp.float16), dp, fsdp, 0, 0, place + 1).astype(F32) for place, part in enumerate(coded)
    ]
    grad_head, token = head_gradient(fsdp, gathered, w_head, own)
    (coded,) = local_kernel(
        functools.partial(first_sum_kernel, conv_rows), (plain,), "sum_z", own, *received, unread=(token,)
    )
    flip = 1
    while flip < dp // 2:
        mine, sent = to_half(coded)
        other = exchange(sent, dp, fsdp, flip, 0, 0).astype(F32)
        flip *= 2
        outs = (plain,) * (2 if flip < dp // 2 else 1)
        total, *rest = local_kernel(functools.partial(next_sum_kernel, conv_rows), outs, "sum_x", mine, other)
        coded = rest[0] if rest else None
    return total, exchange(total, dp, fsdp, 0, 1, 0), grad_head


def shards(facies, prior_draws, recon_grad, w_embed, w_conv, w_head):
    dp, fsdp = lax.axis_size("dp"), lax.axis_size("fsdp")
    block, pooled_lanes, recon, one_hot, pre_embed, hidden, pre_conv, w_conv, w_head = forward(
        facies, prior_draws, recon_grad, w_embed, w_conv, w_head
    )
    gathered = gather_blocks(block, dp, fsdp)
    keep, send, grads = backward(fsdp, gathered, pooled_lanes, recon, hidden, pre_conv, w_head)
    received = exchange(send, dp, fsdp, 0, 1, 0)
    embed = embed_gradient(fsdp, grads, w_conv, pre_embed, one_hot)
    own, other, grad_head = reduce_to_owner(keep, received, embed, gathered, w_head, dp, fsdp)
    grad_embed, grad_conv = pl.pallas_call(
        output_kernel,
        out_shape=(
            jax.ShapeDtypeStruct((256 // fsdp, 128), F32),
            jax.ShapeDtypeStruct((1024 // fsdp, 256), F32),
        ),
        in_specs=[VMEM] * 2,
        out_specs=(VMEM,) * 2,
        compiler_params=pltpu.CompilerParams(vmem_limit_bytes=16 * 2**20),
        name="outputs",
    )(own, other)
    return (grad_embed, grad_conv, grad_head)


def solution(mesh):
    return jax.shard_map(
        shards,
        mesh=mesh,
        in_specs=(
            P(("groups", "dp", "fsdp"), None, None),
            P(("groups", "dp", "fsdp"), None),
            P(("groups", "dp", "fsdp"), None),
            P(),
            P(),
            P(),
        ),
        out_specs=(
            P(("groups", "fsdp"), None),
            P(("groups", "fsdp"), None),
            P(("groups", "fsdp"), None),
        ),
        check_vma=False,
    )
```
